32 devices in a mesh: rows: 8 (over y, x, core), seq: 4 (over z).
Axes of the slice: x: 2, y: 2, z: 4, core: 2. Of those that a mesh axis runs over, the one named last changes fastest.
Arguments:
- tokens_in: bfloat16 [8, 2048, 2048], P('rows', 'seq'), may hold values from -6 to 6
- corpus: int32 [8], P('rows'), may hold values from 0 to 7
- corpus_weight: int32 [8], replicated, may hold values from 16 to 64
- w_qkv: bfloat16 [2048, 1920], P(('rows', 'seq')), may hold values from -0.125 to 0.125
- w_out: bfloat16 [1280, 2048], P(None, ('rows', 'seq')), may hold values from -2 to 2
- w_gate: bfloat16 [2048, 4608], P(('rows', 'seq')), may hold values from -0.125 to 0.125
- w_up: bfloat16 [2048, 4608], P(('rows', 'seq')), may hold values from -0.125 to 0.125
- w_down: bfloat16 [4608, 2048], P(('rows', 'seq')), may hold values from -0.09375 to 0.09375
- attn_gain: bfloat16 [2048], P(('rows', 'seq')), may hold values from 0.5 to 1.5
- ffn_gain: bfloat16 [2048], P(('rows', 'seq')), may hold values from 0.5 to 1.5
- q_gain: bfloat16 [64], replicated, may hold values from 0.099609375 to 1.8984375
- k_gain: bfloat16 [64], replicated, may hold values from 0.099609375 to 1.8984375
- upstream: bfloat16 [8, 2048, 2048], P('rows', 'seq'), may hold values from -6 to 6
Outputs:
- output: bfloat16 [8, 2048, 2048], P('rows', 'seq')
- input_grad: bfloat16 [8, 2048, 2048], P('rows', 'seq')
- grad_qkv: float32 [2048, 1920], P(('rows', 'seq'))
- grad_out: float32 [1280, 2048], P(None, ('rows', 'seq'))
- grad_gate: float32 [2048, 4608], P(('rows', 'seq'))
- grad_up: float32 [2048, 4608], P(('rows', 'seq'))
- grad_down: float32 [4608, 2048], P(('rows', 'seq'))
- grad_attn_gain: float32 [2048], P(('rows', 'seq'))
- grad_ffn_gain: float32 [2048], P(('rows', 'seq'))
- grad_q_gain: float32 [64], replicated
- grad_k_gain: float32 [64], replicated
The draws below stay inside these ranges and needn't reach their ends.
All inputs are finite; a program needn't handle non-finite values.
Results may differ from the reference program's by a relative error of at most 0.018.
Values may be sent and summed in bfloat16 or wider, within the bound.
No kernel may reach another device: no remote copies, remote signals or barrier semaphores. Data moves between devices by JAX's collectives and lax.ppermute only.
A program may use at most 320 MiB of HBM per device.

```python
import jax
import jax.numpy as jnp
from jax import lax

D = 2048
QUERY_HEADS = 20
KEY_VALUE_HEADS = 5
HEAD_SIZE = 64
FF = 4608
SEQ_LEN = 2048
CORPORA = 8
DENOM = 64
QKV = 1920
BATCH = 8


def touch_ends(result, own_key, least, high):
    index_at = [jax.random.randint(jax.random.fold_in(own_key, axis), (), 0, length) for axis, length in enumerate(result.shape)]
    longest = result.shape.index(max(result.shape))
    next_to = index_at[:longest] + [(index_at[longest] + 1) % result.shape[longest]] + index_at[longest + 1:]
    return result.at[tuple(index_at)].set(least).at[tuple(next_to)].set(high)


def steps_of(key, extent, split, smallest, largest):
    factor_of, own = 1.0, jax.random.fold_in(key, 6)
    for dim, blocks in split:
        heights = jnp.exp(jax.random.uniform(jax.random.fold_in(own, dim), (blocks,), jnp.float32, smallest / len(split), largest / len(split)))
        factor_of = factor_of * jnp.repeat(heights, extent[dim] // blocks).reshape([-1 if axis == dim else 1 for axis in range(len(extent))])
    return factor_of


def centred(rng, shape, spread, limit, split=(), held_as=jnp.bfloat16):
    values = jax.random.normal(rng, shape, jnp.float32) * spread
    if len(split) > 0:
        values = steps_of(rng, shape, split, -0.22, 0.18) * values
    return jnp.clip(values, min=-limit, max=limit).astype(held_as)


def setup_inputs(seed: int = 0) -> dict:
    arg_keys = jax.random.split(jax.random.key(seed), 14)
    return {
        "tokens_in": centred(arg_keys[0], (BATCH, SEQ_LEN, D), 1.0, 6.0, ((0, 8), (1, 4))),
        "corpus": touch_ends(jax.random.randint(arg_keys[1], (BATCH,), 0, CORPORA), jax.random.fold_in(arg_keys[1], 1), 0, CORPORA - 1).astype(jnp.int32),
        "corpus_weight": touch_ends(jax.random.randint(arg_keys[2], (CORPORA,), DENOM // 4, DENOM + 1), jax.random.fold_in(arg_keys[2], 1), DENOM // 4, DENOM).astype(jnp.int32),
        "w_qkv": centred(arg_keys[3], (D, QKV), D ** -0.5, 0.125, ((0, 32),)),
        "w_out": centred(arg_keys[4], (QUERY_HEADS * HEAD_SIZE, D), (max(QUERY_HEADS * HEAD_SIZE * 16 // SEQ_LEN, 1)) ** -0.5, 2.0, ((1, 32),)),
        "w_gate": centred(arg_keys[5], (D, FF), D ** -0.5, 0.125, ((0, 32),)),
        "w_up": centred(arg_keys[6], (D, FF), D ** -0.5, 0.125, ((0, 32),)),
        "w_down": centred(arg_keys[7], (FF, D), FF ** -0.5, 0.09375, ((0, 32),)),
        "attn_gain": jnp.clip(1.0 + 0.1 * jax.random.normal(arg_keys[8], (D,), jnp.float32), 0.5, 1.5).astype(jnp.bfloat16),
        "ffn_gain": jnp.clip(1.0 + 0.1 * jax.random.normal(arg_keys[9], (D,), jnp.float32), 0.5, 1.5).astype(jnp.bfloat16),
        "q_gain": jnp.clip(1.0 + 0.18 * jax.random.normal(arg_keys[10], (HEAD_SIZE,), jnp.float32), 0.099609375, 1.8984375).astype(jnp.bfloat16),
        "k_gain": jnp.clip(1.0 + 0.18 * jax.random.normal(arg_keys[11], (HEAD_SIZE,), jnp.float32), 0.099609375, 1.8984375).astype(jnp.bfloat16),
        "upstream": centred(arg_keys[12], (BATCH, SEQ_LEN, D), 1.0, 6.0, ((0, 8), (1, 4))),
    }


EPSILON = 1e-06
ROPE_BASE = 10000.0
FULL_PRECISION = lax.Precision.HIGHEST

@jax.custom_vjp
def low(v):
    return lax.optimization_barrier(v.astype(jnp.bfloat16)).astype(jnp.float32)

@jax.custom_vjp
def low_back(v):
    return v

def low_keep(v):
    return (low(v), None)

def low_pass(kept, grad):
    return (grad,)

def back_keep(v):
    return (v, None)

def back_low(kept, grad):
    return (low(grad),)
low.defvjp(low_keep, low_pass)
low_back.defvjp(back_keep, back_low)

def rms_scale(values, gain_vector):
    mean_square = lax.optimization_barrier(jnp.mean(values * values, axis=-1, keepdims=True))
    return values * lax.rsqrt(mean_square + EPSILON) * gain_vector

def rotate(values, position):
    half_width = values.shape[-1] // 2
    exponent = jnp.arange(half_width, dtype=jnp.float32) * (-2.0 / values.shape[-1])
    frequency = jnp.power(ROPE_BASE, exponent)
    angles = position[:, None] * frequency[None, :]
    cosine = jnp.cos(angles)[:, None, :]
    sine_part = jnp.sin(angles)[:, None, :]
    first_half = values[..., :half_width]
    second_half = values[..., half_width:]
    return jnp.concatenate([first_half * cosine - second_half * sine_part, second_half * cosine + first_half * sine_part], axis=-1)

def heads_piece(joint_query_key_value, q_gain, k_gain, position):
    leading_axis = joint_query_key_value.shape[:-1]
    query_column_width = QUERY_HEADS * HEAD_SIZE
    key_column_width = KEY_VALUE_HEADS * HEAD_SIZE
    queries = joint_query_key_value[..., :query_column_width].reshape(leading_axis + (QUERY_HEADS, HEAD_SIZE))
    key_head_rows = joint_query_key_value[..., query_column_width:query_column_width + key_column_width].reshape(leading_axis + (KEY_VALUE_HEADS, HEAD_SIZE))
    value_head_rows = joint_query_key_value[..., query_column_width + key_column_width:].reshape(leading_axis + (KEY_VALUE_HEADS, HEAD_SIZE))
    queries = rotate(rms_scale(queries, q_gain), position)
    key_head_rows = rotate(rms_scale(key_head_rows, k_gain), position)
    return (queries, key_head_rows, value_head_rows)

def activate(gate_values, up_values):
    return jax.nn.silu(gate_values) * up_values

def attention(queries, key_copy, value_copy):
    length = queries.shape[0]
    block_rows = min(512, length)
    block_count = length // block_rows
    score_scale = queries.shape[-1] ** (-0.5)
    key_place = jnp.arange(length, dtype=jnp.int32)

    def one_block(operands):
        query_block, start_row = operands
        scores = jnp.einsum('qhd,khd->hqk', query_block, key_copy, precision=FULL_PRECISION) * score_scale
        scores = low_back(scores)
        query_place = start_row + jnp.arange(block_rows, dtype=jnp.int32)
        allowed = key_place[None, None, :] <= query_place[None, :, None]
        scores = jnp.where(allowed, scores, -jnp.inf)
        highest = lax.optimization_barrier(jnp.max(scores, axis=-1, keepdims=True))
        weights = jnp.exp(scores - highest)
        probability = low(weights / lax.optimization_barrier(jnp.sum(weights, axis=-1, keepdims=True)))
        return jnp.einsum('hqk,khd->qhd', probability, value_copy, precision=FULL_PRECISION)
    pieces = queries.reshape(block_count, block_rows, queries.shape[1], queries.shape[2])
    starts = jnp.arange(block_count, dtype=jnp.int32) * block_rows
    mixed_heads = lax.map(jax.checkpoint(one_block), (pieces, starts))
    return mixed_heads.reshape(queries.shape)

def matmul(left, right):
    return jnp.dot(left, right, precision=FULL_PRECISION, preferred_element_type=jnp.float32)

def layer(inputs, params):
    w_qkv, w_out, w_gate, w_up, w_down, attn_gain, ffn_gain, q_gain, k_gain = params
    length = inputs.shape[0]
    position = jnp.arange(length, dtype=jnp.float32)
    normed = low(rms_scale(inputs, attn_gain))
    joint_query_key_value = low_back(matmul(normed, w_qkv))
    queries, key_head_rows, value_head_rows = heads_piece(joint_query_key_value, q_gain, k_gain, position)
    group_width = QUERY_HEADS // KEY_VALUE_HEADS
    queries = low_back(low(queries))
    key_copy = low_back(low(jnp.repeat(key_head_rows, group_width, axis=1)))
    value_copy = low_back(low(jnp.repeat(value_head_rows, group_width, axis=1)))
    mixed_heads = low_back(low(attention(queries, key_copy, value_copy)))
    branch = low_back(matmul(mixed_heads.reshape(length, QUERY_HEADS * HEAD_SIZE), w_out))
    middle = inputs + branch
    normed_ffn = low(rms_scale(middle, ffn_gain))
    gate_values = low_back(matmul(normed_ffn, w_gate))
    up_values = low_back(matmul(normed_ffn, w_up))
    hidden = low(activate(gate_values, up_values))
    return middle + low_back(matmul(hidden, w_down))

def reference(tokens_in, corpus, corpus_weight, w_qkv, w_out, w_gate, w_up, w_down, attn_gain, ffn_gain, q_gain, k_gain, upstream):
    params = tuple((weight_array.astype(jnp.float32) for weight_array in (w_qkv, w_out, w_gate, w_up, w_down, attn_gain, ffn_gain, q_gain, k_gain)))
    inputs = tokens_in.astype(jnp.float32)

    def forward(inputs_all, params_all):
        return lax.map(lambda row_values: layer(row_values, params_all), inputs_all)
    output, pull_back = jax.vjp(forward, inputs, params)
    corpus_table = (corpus[:, None] == jnp.arange(CORPORA, dtype=jnp.int32)[None, :]).astype(jnp.float32)
    counts = lax.optimization_barrier(jnp.sum(corpus_table, axis=0)) * SEQ_LEN
    all_tokens = jnp.sum(counts)
    weight_row = lax.optimization_barrier(jnp.sum(corpus_table * corpus_weight.astype(jnp.float32)[None, :], axis=1))
    count_row = lax.optimization_barrier(jnp.sum(corpus_table * counts[None, :], axis=1))
    factor = weight_row / DENOM * (all_tokens / (CORPORA * count_row))
    cotangent = upstream.astype(jnp.float32) * factor[:, None, None]
    input_grad, param_grads = pull_back(cotangent)
    return (output.astype(jnp.bfloat16), input_grad.astype(jnp.bfloat16), param_grads[0], param_grads[1], param_grads[2], param_grads[3], param_grads[4], param_grads[5], param_grads[6], param_grads[7], param_grads[8])
```

```python
from functools import partial

import jax
import jax.numpy as jnp
from jax import lax
from jax.experimental import pallas as pl
from jax.experimental.pallas import tpu as pltpu
from jax.sharding import PartitionSpec as P

QUERY_HEADS = 20
KEY_VALUE_HEADS = 5
HEAD_SIZE = 64
CORPORA = 8
DENOM = 64
EPSILON = 1e-06
ROPE_BASE = 10000.0
QUERY_COLUMNS = QUERY_HEADS * HEAD_SIZE
KEY_COLUMNS = KEY_VALUE_HEADS * HEAD_SIZE
LANES = 128
SCORE_EXPONENT = 1.4426950408889634 * HEAD_SIZE**-0.5
VMEM_LIMIT = 48 * 1024 * 1024

f32, bf16 = jnp.float32, jnp.bfloat16


def dot_nn(a, b):
    return lax.dot_general(a, b, (((1,), (0,)), ((), ())), preferred_element_type=f32)


def dot_nt(a, b):
    return lax.dot_general(a, b, (((1,), (1,)), ((), ())), preferred_element_type=f32)


def dot_tn(a, b):
    return lax.dot_general(a, b, (((0,), (0,)), ((), ())), preferred_element_type=f32)


def lanes_of(shape):
    return lax.broadcasted_iota(jnp.int32, shape, len(shape) - 1)


def head_sum(values):
    row = lax.broadcasted_iota(jnp.int32, (LANES, LANES), 0) // HEAD_SIZE
    column = lax.broadcasted_iota(jnp.int32, (LANES, LANES), 1) // HEAD_SIZE
    ones = jnp.where(row == column, 1.0, 0.0).astype(bf16)
    high = values.astype(bf16)
    low = (values - high.astype(f32)).astype(bf16)
    return dot_nn(high, ones) + dot_nn(low, ones)


def partner(values):
    first = lanes_of(values.shape) % HEAD_SIZE < HEAD_SIZE // 2
    return jnp.where(
        first,
        pltpu.roll(values, LANES - HEAD_SIZE // 2, 1),
        pltpu.roll(values, HEAD_SIZE // 2, 1),
    )


def heads_forward_kernel(norm_columns, joint_ref, gain_ref, cos_ref, sin_ref, out_ref):
    values = joint_ref[...]
    scale = lax.rsqrt(head_sum(values * values) * (1.0 / HEAD_SIZE) + EPSILON)
    normed = values * scale * gain_ref[0:1, :]
    turned = normed * cos_ref[...] + partner(normed) * sin_ref[...]
    place = pl.program_id(0) * LANES + lanes_of(values.shape)
    out_ref[...] = jnp.where(place < norm_columns, turned, values).astype(bf16)


def heads_forward(joint, gain, cos, sin, norm_columns):
    tokens, columns = joint.shape
    return pl.pallas_call(
        partial(heads_forward_kernel, norm_columns),
        grid=(columns // LANES,),
        in_specs=[
            pl.BlockSpec((tokens, LANES), lambda i: (0, i)),
            pl.BlockSpec((8, LANES), lambda i: (0, i)),
            pl.BlockSpec((tokens, LANES), lambda i: (0, 0)),
            pl.BlockSpec((tokens, LANES), lambda i: (0, 0)),
        ],
        out_specs=pl.BlockSpec((tokens, LANES), lambda i: (0, i)),
        out_shape=jax.ShapeDtypeStruct((tokens, columns), bf16),
        name="heads_forward",
        cost_estimate=pl.CostEstimate(
            flops=tokens * columns * 256, bytes_accessed=tokens * columns * 6, transcendentals=0
        ),
    )(joint, gain, cos, sin)


def heads_backward_kernel(
    norm_columns, grad_ref, joint_ref, gain_ref, cos_ref, sin_ref, out_ref, gain_out_ref
):
    grad = grad_ref[...].astype(f32)
    values = joint_ref[...]
    gain = gain_ref[0:1, :]
    turned = grad * cos_ref[...] - partner(grad) * sin_ref[...]
    scale = lax.rsqrt(head_sum(values * values) * (1.0 / HEAD_SIZE) + EPSILON)
    gained = turned * gain
    inner = head_sum(values * gained) * (1.0 / HEAD_SIZE)
    result = scale * gained - values * (scale * scale * scale) * inner
    place = pl.program_id(0) * LANES + lanes_of(values.shape)
    out_ref[...] = jnp.where(place < norm_columns, result, grad).astype(bf16)
    gain_out_ref[...] = jnp.broadcast_to(
        jnp.sum(turned * values * scale, axis=0, keepdims=True), gain_out_ref.shape
    )


def heads_backward(grad, joint, gain, cos, sin, norm_columns):
    tokens, columns = joint.shape
    return pl.pallas_call(
        partial(heads_backward_kernel, norm_columns),
        grid=(columns // LANES,),
        in_specs=[
            pl.BlockSpec((tokens, LANES), lambda i: (0, i)),
            pl.BlockSpec((tokens, LANES), lambda i: (0, i)),
            pl.BlockSpec((8, LANES), lambda i: (0, i)),
            pl.BlockSpec((tokens, LANES), lambda i: (0, 0)),
            pl.BlockSpec((tokens, LANES), lambda i: (0, 0)),
        ],
        out_specs=[
            pl.BlockSpec((tokens, LANES), lambda i: (0, i)),
            pl.BlockSpec((8, LANES), lambda i: (0, i)),
        ],
        out_shape=[
            jax.ShapeDtypeStruct((tokens, columns), bf16),
            jax.ShapeDtypeStruct((8, columns), f32),
        ],
        name="heads_backward",
        cost_estimate=pl.CostEstimate(
            flops=tokens * columns * 512, bytes_accessed=tokens * columns * 10, transcendentals=0
        ),
    )(grad, joint, gain, cos, sin)


def both_halves(pair, odd):
    wide = pair.astype(f32)
    first = lanes_of(wide.shape) < HEAD_SIZE
    keep = jnp.where(odd == 1, jnp.where(first, 0, 1), jnp.where(first, 1, 0)) == 1
    return jnp.where(keep, wide, pltpu.roll(wide, HEAD_SIZE, 1))


def attend_forward_kernel(place_ref, q_ref, k_ref, v_ref, out_ref, log_ref):
    group = pl.program_id(0) // 2
    place = place_ref[0]
    tokens = q_ref.shape[0]
    first = lanes_of((tokens, LANES)) < HEAD_SIZE
    pair = q_ref[...].astype(f32)
    queries = (jnp.where(first, pair, 0.0).astype(bf16), jnp.where(first, 0.0, pair).astype(bf16))

    def step(j, totals, diagonal):
        rows = pl.ds(pl.multiple_of(j * tokens, tokens), tokens)
        keys = both_halves(k_ref[rows, :], group % 2).astype(bf16)
        values = both_halves(v_ref[rows, :], (KEY_VALUE_HEADS + group) % 2)
        sides = (
            jnp.where(first, values, 1.0).astype(bf16),
            jnp.where(first, 1.0, values).astype(bf16),
        )
        result = []
        for head in range(2):
            weights = jnp.exp2(dot_nt(queries[head], keys) * SCORE_EXPONENT)
            if diagonal:
                row = lax.broadcasted_iota(jnp.int32, weights.shape, 0)
                weights = jnp.where(lanes_of(weights.shape) <= row, weights, 0.0)
            result.append(totals[head] + dot_nn(weights.astype(bf16), sides[head]))
        return tuple(result)

    zero = jnp.zeros((tokens, LANES), f32)
    totals = lax.fori_loop(0, place, lambda j, c: step(j, c, False), (zero, zero))
    totals = step(place, totals, True)
    numerator = jnp.where(first, totals[0], totals[1])
    swapped = jnp.where(first, totals[1], totals[0])
    out_ref[...] = (numerator / pltpu.roll(swapped, HEAD_SIZE, 1)).astype(bf16)
    log_ref[...] = jnp.log2(swapped)


def attend_forward(place, queries, keys_values):
    tokens = queries.shape[0]
    length = keys_values.shape[0]
    pairs = QUERY_COLUMNS // LANES
    return pl.pallas_call(
        attend_forward_kernel,
        grid_spec=pltpu.PrefetchScalarGridSpec(
            num_scalar_prefetch=1,
            grid=(pairs,),
            in_specs=[
                pl.BlockSpec((tokens, LANES), lambda i, s: (0, i)),
                pl.BlockSpec((length, LANES), lambda i, s: (0, (i // 2) // 2)),
                pl.BlockSpec((length, LANES), lambda i, s: (0, (KEY_VALUE_HEADS + i // 2) // 2)),
            ],
            out_specs=[
                pl.BlockSpec((tokens, LANES), lambda i, s: (0, i)),
                pl.BlockSpec((tokens, LANES), lambda i, s: (0, i)),
            ],
        ),
        out_shape=[
            jax.ShapeDtypeStruct((tokens, QUERY_COLUMNS), bf16),
            jax.ShapeDtypeStruct((tokens, QUERY_COLUMNS), f32),
        ],
        compiler_params=pltpu.CompilerParams(vmem_limit_bytes=VMEM_LIMIT),
        name="attend_forward",
        cost_estimate=pl.CostEstimate(
            flops=QUERY_HEADS * tokens * length * 800,
            bytes_accessed=tokens * QUERY_COLUMNS * 8 + length * 1280,
            transcendentals=QUERY_HEADS * tokens * length,
        ),
    )(place, queries, keys_values, keys_values)


def three_parts(values, lane):
    high = values.astype(bf16).astype(f32)
    rest = values - high
    middle = rest.astype(bf16).astype(f32)
    low = rest - middle
    return jnp.where(
        lane == 0, high, jnp.where(lane == 1, middle, jnp.where(lane == 2, low, 0.0))
    )


def attend_backward_kernel(
    place_ref, q_ref, k_ref, v_ref, out_ref, log_ref, grad_ref, dq_ref, dkv_ref, dk_sum, dv_sum
):
    pair_index = pl.program_id(0)
    group = pair_index // 2
    place = place_ref[0]
    tokens = q_ref.shape[0]
    lane = lanes_of((tokens, LANES))
    first = lane < HEAD_SIZE
    inside = lane % HEAD_SIZE
    pair = q_ref[...].astype(f32)
    grad = grad_ref[...].astype(f32)
    delta = pltpu.roll(head_sum(grad * out_ref[...].astype(f32)), HEAD_SIZE, 1)
    logs = three_parts(log_ref[...] * (1.0 / SCORE_EXPONENT), inside)
    deltas = three_parts(delta, inside)
    minus = jnp.where(inside < 3, -1.0, 0.0)

    def sides(own, other):
        return (
            jnp.where(first, own, other).astype(bf16),
            jnp.where(first, other, own).astype(bf16),
        )

    queries = sides(pair, 0.0)
    grads = sides(grad, 0.0)
    queries_log = sides(pair, logs)
    grads_delta = sides(grad, deltas)

    @pl.when(pair_index % 2 == 0)
    def _():
        dk_sum[...] = jnp.zeros_like(dk_sum)
        dv_sum[...] = jnp.zeros_like(dv_sum)

    def step(j, dq, diagonal):
        rows = pl.ds(pl.multiple_of(j * tokens, tokens), tokens)
        key_wide = both_halves(k_ref[rows, :], group % 2)
        value_wide = both_halves(v_ref[rows, :], (KEY_VALUE_HEADS + group) % 2)
        keys = sides(key_wide, 0.0)
        keys_log = sides(key_wide, minus)
        values_delta = sides(value_wide, minus)
        dk = dk_sum[rows, :]
        dv = dv_sum[rows, :]
        for head in range(2):
            weights = jnp.exp2(dot_nt(keys_log[head], queries_log[head]) * SCORE_EXPONENT)
            if diagonal:
                row = lax.broadcasted_iota(jnp.int32, weights.shape, 0)
                weights = jnp.where(row <= lanes_of(weights.shape), weights, 0.0)
            grad_weights = dot_nt(values_delta[head], grads_delta[head])
            grad_scores = (weights * grad_weights).astype(bf16)
            dv = dv + dot_nn(weights.astype(bf16), grads[head])
            dk = dk + dot_nn(grad_scores, queries[head])
            dq = dq + dot_tn(grad_scores, keys[head])
        dk_sum[rows, :] = dk
        dv_sum[rows, :] = dv
        return dq

    dq = lax.fori_loop(
        0, place, lambda j, c: step(j, c, False), jnp.zeros((tokens, LANES), f32)
    )
    dq = step(place, dq, True)
    dq_ref[...] = (dq * HEAD_SIZE**-0.5).astype(bf16)

    @pl.when(pair_index % 2 == 1)
    def _():
        wide_lane = lanes_of(dk_sum.shape)
        for total, slot, factor in (
            (dk_sum, group, HEAD_SIZE**-0.5),
            (dv_sum, KEY_VALUE_HEADS + group, 1.0),
        ):
            both = (total[...] + pltpu.roll(total[...], HEAD_SIZE, 1)) * factor
            columns = pl.ds(pl.multiple_of(slot // 2 * LANES, LANES), LANES)
            mine = wide_lane // HEAD_SIZE == slot % 2
            dkv_ref[:, columns] = jnp.where(
                mine, both, dkv_ref[:, columns].astype(f32)
            ).astype(bf16)


def attend_backward(place, queries, keys_values, mixed, logs, grad_mixed):
    tokens = queries.shape[0]
    length = keys_values.shape[0]
    pairs = QUERY_COLUMNS // LANES
    own = pl.BlockSpec((tokens, LANES), lambda i, s: (0, i))
    return pl.pallas_call(
        attend_backward_kernel,
        grid_spec=pltpu.PrefetchScalarGridSpec(
            num_scalar_prefetch=1,
            grid=(pairs,),
            in_specs=[
                own,
                pl.BlockSpec((length, LANES), lambda i, s: (0, (i // 2) // 2)),
                pl.BlockSpec((length, LANES), lambda i, s: (0, (KEY_VALUE_HEADS + i // 2) // 2)),
                own,
                own,
                own,
            ],
            out_specs=[
                own,
                pl.BlockSpec((length, 2 * KEY_COLUMNS), lambda i, s: (0, 0)),
            ],
            scratch_shapes=[pltpu.VMEM((length, LANES), f32), pltpu.VMEM((length, LANES), f32)],
        ),
        out_shape=[
            jax.ShapeDtypeStruct((tokens, QUERY_COLUMNS), bf16),
            jax.ShapeDtypeStruct((length, 2 * KEY_COLUMNS), bf16),
        ],
        compiler_params=pltpu.CompilerParams(vmem_limit_bytes=VMEM_LIMIT),
        name="attend_backward",
        cost_estimate=pl.CostEstimate(
            flops=QUERY_HEADS * tokens * length * 2000,
            bytes_accessed=tokens * QUERY_COLUMNS * 12 + length * 2560,
            transcendentals=QUERY_HEADS * tokens * length,
        ),
    )(place, queries, keys_values, keys_values, mixed, logs, grad_mixed)


def swap(values, bit):
    pairs = [(i, i ^ bit) for i in range(lax.axis_size("rows"))]
    return lax.ppermute(values, "rows", pairs)


def bit_of(bit):
    return (lax.axis_index("rows") // bit) % 2


def joined(own, other, side, axis):
    low = jnp.where(side == 0, own, other)
    high = jnp.where(side == 0, other, own)
    return jnp.stack([low, high], axis)


def gather_bit(values, bit, axis):
    return joined(values, swap(values, bit), bit_of(bit), axis)


def part(values, index, axis):
    return lax.dynamic_index_in_dim(values, index, axis, keepdims=False)


def reduce_bit(values, bit, axis):
    side = bit_of(bit)
    other = swap(part(values, 1 - side, axis), bit)
    return (part(values, side, axis).astype(f32) + other.astype(f32)).astype(bf16)


def outer_pairs(step, low, high):
    size = lax.axis_size("rows")
    return [
        (i, i + 4 * step)
        for i in range(size)
        if low <= i // 4 < high and 0 <= i // 4 + step < size // 4
    ]


def gather_outer(values, axis):
    count = lax.axis_size("rows") // 4
    if count == 1:
        return jnp.expand_dims(values, axis)
    if count == 2:
        return gather_bit(values, 4, axis)
    place = lax.axis_index("rows") // 4
    up, down = values, values
    ups, downs = [], []
    for t in range(1, count):
        up = lax.ppermute(up, "rows", outer_pairs(1, t - 1, count))
        down = lax.ppermute(down, "rows", outer_pairs(-1, 0, count - t + 1))
        ups.append(up)
        downs.append(down)
    line = jnp.stack(ups[::-1] + [values] + downs, axis)
    return lax.dynamic_slice_in_dim(line, count - 1 - place, count, axis)


def reduce_outer(values, axis):
    count = lax.axis_size("rows") // 4
    if count == 1:
        return jnp.squeeze(values, axis)
    if count == 2:
        return reduce_bit(values, 4, axis)
    place = lax.axis_index("rows") // 4

    def entry(index):
        return part(values, jnp.clip(index, 0, count - 1), axis)

    up, down = entry(place + count - 1), entry(place - count + 1)
    for t in range(1, count):
        up = lax.ppermute(up, "rows", outer_pairs(1, 0, t)).astype(f32)
        down = lax.ppermute(down, "rows", outer_pairs(-1, count - t, count)).astype(f32)
        if t < count - 1:
            up = (entry(place + count - 1 - t).astype(f32) + up).astype(bf16)
            down = (entry(place - count + 1 + t).astype(f32) + down).astype(bf16)
    return (entry(place).astype(f32) + up + down).astype(bf16)


def gather_seq(values):
    return lax.all_gather(values, "seq", axis=0, tiled=False)


def reduce_seq(values):
    return lax.psum_scatter(values, "seq", scatter_dimension=0, tiled=False)


def split_columns(columns):
    return columns // LANES // 2 * LANES


def gather_all(shard):
    columns = shard.shape[1]
    half = split_columns(columns)
    lines = gather_seq(shard)
    left = gather_bit(gather_outer(lines[..., :half], 0), 2, 1)
    right = gather_outer(gather_bit(lines[..., half:], 2, 0), 0)
    both = jnp.concatenate([left, right], axis=-1)
    return gather_bit(both, 1, 2).reshape(-1, columns)


def reduce_all(values, rows):
    columns = values.shape[1]
    half = split_columns(columns)
    seq = lax.axis_size("seq")
    blocks = values.reshape(-1, 2, 2, seq, rows, columns)
    blocks = reduce_bit(blocks, 1, 2)
    left = reduce_outer(reduce_bit(blocks[..., :half], 2, 1), 0)
    right = reduce_bit(reduce_outer(blocks[..., half:], 0), 2, 0)
    return reduce_seq(jnp.concatenate([left, right], axis=-1))


def gather_group(values):
    other = swap(values, 1)
    across = swap(values, 2)
    far = swap(across, 1)
    return jnp.concatenate([values, other, across, far], axis=0)


def reduce_group(values):
    tokens = values.shape[0] // 4
    parts = values.reshape(2, 2, tokens, values.shape[1])
    across = parts[1, 0] + swap(parts[1, 1].astype(bf16), 1).astype(f32)
    across = swap(across.astype(bf16), 2).astype(f32)
    own = parts[0, 0] + swap(parts[0, 1].astype(bf16), 1).astype(f32)
    return own + across


def mm(left, right):
    return jnp.einsum("ab,bc->ac", left, right, preferred_element_type=f32)


def mm_t(left, right):
    return jnp.einsum("ab,cb->ac", left, right, preferred_element_type=f32)


def t_mm(left, right):
    return jnp.einsum("ab,ac->bc", left, right, preferred_element_type=f32)


def norm_scale(values):
    return lax.rsqrt(jnp.mean(values * values, axis=-1, keepdims=True) + EPSILON)


def norm_backward(values, scale, gain, grad):
    gained = grad * gain
    inner = jnp.mean(values * gained, axis=-1, keepdims=True)
    result = scale * gained - values * (scale * scale * scale) * inner
    return result, jnp.sum(grad * values * scale, axis=0)


def shards(
    tokens_in,
    corpus,
    corpus_weight,
    w_qkv,
    w_out,
    w_gate,
    w_up,
    w_down,
    attn_gain,
    ffn_gain,
    q_gain,
    k_gain,
    upstream,
):
    shard_length, width = tokens_in.shape[1:]
    row_devices = lax.axis_size("rows")
    seq_devices = lax.axis_size("seq")
    outer = row_devices // 4
    d_rows = w_qkv.shape[0]
    f_rows = w_down.shape[0]
    place = lax.axis_index("seq").astype(jnp.int32)
    inputs = tokens_in[0].astype(f32)

    extra = jnp.stack(
        [
            attn_gain,
            ffn_gain,
            jnp.broadcast_to(corpus.astype(bf16), attn_gain.shape),
        ],
        axis=1,
    )
    extra = jnp.pad(extra, ((0, 0), (0, LANES - extra.shape[1])))
    kv_full = gather_all(jnp.concatenate([w_qkv[:, QUERY_COLUMNS:], extra], axis=1))
    wkv, extra_full = kv_full[:, : 2 * KEY_COLUMNS], kv_full[:, 2 * KEY_COLUMNS :]
    rows = dot_nt(jnp.eye(8, LANES, dtype=bf16), extra_full)
    attn_gain_full, ffn_gain_full, corpus_full = rows[0:1], rows[1:2], rows[2]
    query_out_full = gather_all(jnp.concatenate([w_qkv[:, :QUERY_COLUMNS], w_out.T], axis=1))
    wq, wout_t = query_out_full[:, :QUERY_COLUMNS], query_out_full[:, QUERY_COLUMNS:]

    def to_group(weight):
        blocks = weight.reshape(d_rows, outer, 4, seq_devices * f_rows)
        return jnp.moveaxis(blocks, 2, 0).reshape(2, 2, d_rows, outer * seq_devices * f_rows)

    gate_up = jnp.stack([to_group(w_gate), to_group(w_up)], axis=2)
    core, near = bit_of(1), bit_of(2)
    gate_up = joined(part(gate_up, core, 1), swap(part(gate_up, 1 - core, 1), 1), core, 1)
    gate_up = joined(part(gate_up, near, 0), swap(part(gate_up, 1 - near, 0), 2), near, 0)
    hidden_columns = gate_up.shape[-1]

    def gather_hidden(lines):
        full = gather_outer(gather_seq(lines), 0)
        return jnp.moveaxis(full, 1, 3).reshape(width, hidden_columns)

    wgate = gather_hidden(gate_up[:, :, 0])
    wup = gather_hidden(gate_up[:, :, 1])
    wdown = gather_outer(gather_seq(w_down), 0).reshape(hidden_columns, width)

    corpora = jnp.arange(CORPORA, dtype=jnp.int32)
    per_device = corpus_full.reshape(-1, d_rows)[:, 0].astype(jnp.int32)
    counts = (
        jnp.sum((per_device[:, None] == corpora[None, :]).astype(f32), axis=0) * shard_length
    )
    own_corpus = (corpus[0] == corpora).astype(f32)
    weight_row = jnp.sum(own_corpus * corpus_weight.astype(f32))
    count_row = jnp.sum(own_corpus * counts)
    factor = weight_row / DENOM * (jnp.sum(counts) / (CORPORA * count_row))
    grad_full = upstream[0].astype(f32) * factor
    grad_top = grad_full.astype(bf16)
    grad_top4 = gather_group(grad_top)

    position = (place * shard_length + jnp.arange(shard_length, dtype=jnp.int32)).astype(f32)
    half = HEAD_SIZE // 2
    exponent = jnp.arange(half, dtype=f32) * (-2.0 / HEAD_SIZE)
    angles = position[:, None] * jnp.power(ROPE_BASE, exponent)[None, :]
    cosine, sine = jnp.cos(angles), jnp.sin(angles)
    cos_table = jnp.concatenate([cosine] * 4, axis=1)
    sin_table = jnp.concatenate([-sine, sine] * 2, axis=1)
    wide_q = jnp.tile(q_gain.astype(f32), QUERY_HEADS)
    wide_k = jnp.concatenate(
        [jnp.tile(k_gain.astype(f32), KEY_VALUE_HEADS), jnp.ones((KEY_COLUMNS,), f32)]
    )
    wide_q = jnp.broadcast_to(wide_q[None, :], (8, QUERY_COLUMNS))
    wide_k = jnp.broadcast_to(wide_k[None, :], (8, 2 * KEY_COLUMNS))

    in_scale = norm_scale(inputs)
    normed = (inputs * in_scale * attn_gain_full).astype(bf16)
    joint_kv = mm(normed, wkv)
    keys_values = heads_forward(joint_kv, wide_k, cos_table, sin_table, KEY_COLUMNS)
    keys_values = gather_seq(keys_values).reshape(-1, 2 * KEY_COLUMNS)
    joint_q = mm(normed, wq)
    queries = heads_forward(joint_q, wide_q, cos_table, sin_table, QUERY_COLUMNS)
    place_array = place.reshape(1)
    mixed, logs = attend_forward(place_array, queries, keys_values)
    middle = inputs + mm_t(mixed, wout_t)

    ffn_scale = norm_scale(middle)
    normed_ffn = (middle * ffn_scale * ffn_gain_full).astype(bf16)
    normed4 = gather_group(normed_ffn)
    gate = mm(normed4, wgate)
    up = mm(normed4, wup)
    sigmoid = 1.0 / (1.0 + jnp.exp(-gate))
    silu = gate * sigmoid
    hidden = (silu * up).astype(bf16)
    grad_hidden = mm_t(grad_top4, wdown)
    gate_back = (grad_hidden * up * (sigmoid * (1.0 + gate * (1.0 - sigmoid)))).astype(bf16)
    up_back = (grad_hidden * silu).astype(bf16)
    grad_normed_ffn = reduce_group(mm_t(gate_back, wgate) + mm_t(up_back, wup))
    output = (middle + reduce_group(mm(hidden, wdown))).astype(bf16)

    def scatter_hidden(grad):
        blocks = grad.reshape(outer, 2, 2, seq_devices, d_rows, hidden_columns)
        return reduce_seq(jnp.moveaxis(reduce_outer(blocks, 0), 2, 0))

    grad_wdown = t_mm(hidden, grad_top4).astype(bf16)
    grad_wdown = reduce_seq(
        reduce_outer(grad_wdown.reshape(outer, seq_devices, f_rows, width), 0)
    ).astype(f32)
    grad_gate = scatter_hidden(t_mm(normed4, gate_back).astype(bf16))
    grad_up = scatter_hidden(t_mm(normed4, up_back).astype(bf16))
    grads = jnp.stack([grad_gate, grad_up], axis=2)
    grads = joined(part(grads, near, 0), swap(part(grads, 1 - near, 0), 2), near, 0)
    grads = joined(part(grads, core, 1), swap(part(grads, 1 - core, 1), 1), core, 1)

    def from_group(blocks):
        blocks = blocks.astype(f32).reshape(4, d_rows, outer, seq_devices * f_rows)
        return jnp.transpose(blocks, (1, 2, 0, 3)).reshape(d_rows, -1)

    grad_wgate, grad_wup = from_group(grads[:, :, 0]), from_group(grads[:, :, 1])

    grad_middle_part, grad_ffn_gain = norm_backward(
        middle, ffn_scale, ffn_gain_full, grad_normed_ffn
    )
    grad_middle = grad_full + grad_middle_part
    grad_branch = grad_middle.astype(bf16)
    grad_mixed = mm(grad_branch, wout_t).astype(bf16)
    grad_q, grad_kv = attend_backward(place_array, queries, keys_values, mixed, logs, grad_mixed)
    grad_kv = reduce_seq(grad_kv.reshape(seq_devices, shard_length, -1))
    joint_grad_q, gain_q = heads_backward(
        grad_q, joint_q, wide_q, cos_table, sin_table, QUERY_COLUMNS
    )
    grad_query_out = reduce_all(
        jnp.concatenate(
            [t_mm(normed, joint_grad_q).astype(bf16), t_mm(grad_branch, mixed).astype(bf16)],
            axis=1,
        ),
        d_rows,
    ).astype(f32)
    joint_grad_kv, gain_k = heads_backward(
        grad_kv, joint_kv, wide_k, cos_table, sin_table, KEY_COLUMNS
    )
    grad_wkv = reduce_all(t_mm(normed, joint_grad_kv).astype(bf16), d_rows).astype(f32)
    grad_normed = mm_t(joint_grad_q, wq) + mm_t(joint_grad_kv, wkv)
    grad_input_part, grad_attn_gain = norm_backward(
        inputs, in_scale, attn_gain_full, grad_normed
    )
    input_grad = (grad_middle + grad_input_part).astype(bf16)

    small = lax.psum(
        jnp.concatenate(
            [
                grad_attn_gain,
                grad_ffn_gain,
                jnp.sum(gain_q[0].reshape(-1, HEAD_SIZE), axis=0),
                jnp.sum(gain_k[0, :KEY_COLUMNS].reshape(-1, HEAD_SIZE), axis=0),
            ]
        ),
        ("rows", "seq"),
    )
    start = (lax.axis_index("rows") * seq_devices + place) * d_rows
    return (
        output[None],
        input_grad[None],
        jnp.concatenate([grad_query_out[:, :QUERY_COLUMNS], grad_wkv], axis=1),
        grad_query_out[:, QUERY_COLUMNS:].T,
        grad_wgate,
        grad_wup,
        grad_wdown,
        lax.dynamic_slice_in_dim(small[:width], start, d_rows),
        lax.dynamic_slice_in_dim(small[width : 2 * width], start, d_rows),
        small[2 * width : 2 * width + HEAD_SIZE],
        small[2 * width + HEAD_SIZE :],
    )


def solution(mesh):
    return jax.shard_map(
        shards,
        mesh=mesh,
        in_specs=(
            P("rows", "seq", None),
            P("rows"),
            P(),
            P(("rows", "seq"), None),
            P(None, ("rows", "seq")),
            P(("rows", "seq"), None),
            P(("rows", "seq"), None),
            P(("rows", "seq"), None),
            P(("rows", "seq")),
            P(("rows", "seq")),
            P(),
            P(),
            P("rows", "seq", None),
        ),
        out_specs=(
            P("rows", "seq", None),
            P("rows", "seq", None),
            P(("rows", "seq"), None),
            P(None, ("rows", "seq")),
            P(("rows", "seq"), None),
            P(("rows", "seq"), None),
            P(("rows", "seq"), None),
            P(("rows", "seq")),
            P(("rows", "seq")),
            P(),
            P(),
        ),
        check_vma=False,
    )
```

```python
import math
from functools import partial

import jax
import jax.numpy as jnp
from jax import lax
from jax.experimental import pallas as pl
from jax.experimental.pallas import tpu as pltpu
from jax.sharding import PartitionSpec as P

QUERY_HEADS = 20
KEY_VALUE_HEADS = 5
HEAD_SIZE = 64
CORPORA = 8
DENOM = 64
EPSILON = 1e-06
ROPE_BASE = 10000.0
QUERY_COLUMNS = QUERY_HEADS * HEAD_SIZE
KEY_COLUMNS = KEY_VALUE_HEADS * HEAD_SIZE
LANES = 128
SCORE_EXPONENT = 1.4426950408889634 * HEAD_SIZE**-0.5
VMEM_LIMIT = 48 * 1024 * 1024

f32, bf16 = jnp.float32, jnp.bfloat16
LIGHT = pl.CostEstimate(flops=1000, bytes_accessed=1000, transcendentals=0)


def dot_nn(a, b):
    return lax.dot_general(a, b, (((1,), (0,)), ((), ())), preferred_element_type=f32)


def dot_nt(a, b):
    return lax.dot_general(a, b, (((1,), (1,)), ((), ())), preferred_element_type=f32)


def dot_tn(a, b):
    return lax.dot_general(a, b, (((0,), (0,)), ((), ())), preferred_element_type=f32)


def lanes_of(shape):
    return lax.broadcasted_iota(jnp.int32, shape, len(shape) - 1)


def head_sum(values):
    row = lax.broadcasted_iota(jnp.int32, (LANES, LANES), 0) // HEAD_SIZE
    column = lax.broadcasted_iota(jnp.int32, (LANES, LANES), 1) // HEAD_SIZE
    ones = jnp.where(row == column, 1.0, 0.0).astype(bf16)
    high = values.astype(bf16)
    low = (values - high.astype(f32)).astype(bf16)
    return dot_nn(high, ones) + dot_nn(low, ones)


def partner(values):
    first = lanes_of(values.shape) % HEAD_SIZE < HEAD_SIZE // 2
    return jnp.where(
        first,
        pltpu.roll(values, LANES - HEAD_SIZE // 2, 1),
        pltpu.roll(values, HEAD_SIZE // 2, 1),
    )


def heads_forward_kernel(norm_columns, joint_ref, gain_ref, cos_ref, sin_ref, out_ref):
    values = joint_ref[...]
    scale = lax.rsqrt(head_sum(values * values) * (1.0 / HEAD_SIZE) + EPSILON)
    normed = values * scale * gain_ref[0:1, :]
    turned = normed * cos_ref[...] + partner(normed) * sin_ref[...]
    place = pl.program_id(0) * LANES + lanes_of(values.shape)
    out_ref[...] = jnp.where(place < norm_columns, turned, values).astype(bf16)


def heads_forward(joint, gain, cos, sin, norm_columns):
    tokens, columns = joint.shape
    return pl.pallas_call(
        partial(heads_forward_kernel, norm_columns),
        grid=(columns // LANES,),
        in_specs=[
            pl.BlockSpec((tokens, LANES), lambda i: (0, i)),
            pl.BlockSpec((8, LANES), lambda i: (0, i)),
            pl.BlockSpec((tokens, LANES), lambda i: (0, 0)),
            pl.BlockSpec((tokens, LANES), lambda i: (0, 0)),
        ],
        out_specs=pl.BlockSpec((tokens, LANES), lambda i: (0, i)),
        out_shape=jax.ShapeDtypeStruct((tokens, columns), bf16),
        name="heads_forward",
        cost_estimate=LIGHT,
    )(joint, gain, cos, sin)


def heads_backward_kernel(
    norm_columns, grad_ref, joint_ref, gain_ref, cos_ref, sin_ref, out_ref, gain_out_ref
):
    grad = grad_ref[...].astype(f32)
    values = joint_ref[...]
    gain = gain_ref[0:1, :]
    turned = grad * cos_ref[...] - partner(grad) * sin_ref[...]
    scale = lax.rsqrt(head_sum(values * values) * (1.0 / HEAD_SIZE) + EPSILON)
    gained = turned * gain
    inner = head_sum(values * gained) * (1.0 / HEAD_SIZE)
    result = scale * gained - values * (scale * scale * scale) * inner
    place = pl.program_id(0) * LANES + lanes_of(values.shape)
    out_ref[...] = jnp.where(place < norm_columns, result, grad).astype(bf16)
    gain_out_ref[...] = jnp.broadcast_to(
        jnp.sum(turned * values * scale, axis=0, keepdims=True), gain_out_ref.shape
    )


def heads_backward(grad, joint, gain, cos, sin, norm_columns):
    tokens, columns = joint.shape
    return pl.pallas_call(
        partial(heads_backward_kernel, norm_columns),
        grid=(columns // LANES,),
        in_specs=[
            pl.BlockSpec((tokens, LANES), lambda i: (0, i)),
            pl.BlockSpec((tokens, LANES), lambda i: (0, i)),
            pl.BlockSpec((8, LANES), lambda i: (0, i)),
            pl.BlockSpec((tokens, LANES), lambda i: (0, 0)),
            pl.BlockSpec((tokens, LANES), lambda i: (0, 0)),
        ],
        out_specs=[
            pl.BlockSpec((tokens, LANES), lambda i: (0, i)),
            pl.BlockSpec((8, LANES), lambda i: (0, i)),
        ],
        out_shape=[
            jax.ShapeDtypeStruct((tokens, columns), bf16),
            jax.ShapeDtypeStruct((8, columns), f32),
        ],
        name="heads_backward",
        cost_estimate=LIGHT,
    )(grad, joint, gain, cos, sin)


def both_halves(pair, odd):
    wide = pair.astype(f32)
    first = lanes_of(wide.shape) < HEAD_SIZE
    keep = jnp.where(odd == 1, jnp.where(first, 0, 1), jnp.where(first, 1, 0)) == 1
    return jnp.where(keep, wide, pltpu.roll(wide, HEAD_SIZE, 1))


def attend_forward_kernel(place_ref, q_ref, k_ref, v_ref, out_ref, log_ref):
    group = pl.program_id(0) // 2
    place = place_ref[0]
    tokens = q_ref.shape[0]
    first = lanes_of((tokens, LANES)) < HEAD_SIZE
    pair = q_ref[...].astype(f32)
    queries = (jnp.where(first, pair, 0.0).astype(bf16), jnp.where(first, 0.0, pair).astype(bf16))

    def step(j, totals, diagonal):
        rows = pl.ds(pl.multiple_of(j * tokens, tokens), tokens)
        keys = both_halves(k_ref[rows, :], group % 2).astype(bf16)
        values = both_halves(v_ref[rows, :], (KEY_VALUE_HEADS + group) % 2)
        sides = (
            jnp.where(first, values, 1.0).astype(bf16),
            jnp.where(first, 1.0, values).astype(bf16),
        )
        result = []
        for head in range(2):
            weights = jnp.exp2(dot_nt(queries[head], keys) * SCORE_EXPONENT)
            if diagonal:
                row = lax.broadcasted_iota(jnp.int32, weights.shape, 0)
                weights = jnp.where(lanes_of(weights.shape) <= row, weights, 0.0)
            result.append(totals[head] + dot_nn(weights.astype(bf16), sides[head]))
        return tuple(result)

    zero = jnp.zeros((tokens, LANES), f32)
    totals = lax.fori_loop(0, place, lambda j, c: step(j, c, False), (zero, zero))
    totals = step(place, totals, True)
    numerator = jnp.where(first, totals[0], totals[1])
    swapped = jnp.where(first, totals[1], totals[0])
    out_ref[...] = (numerator / pltpu.roll(swapped, HEAD_SIZE, 1)).astype(bf16)
    log_ref[...] = jnp.log2(swapped)


def attend_forward(place, queries, keys_values):
    tokens = queries.shape[0]
    length = keys_values.shape[0]
    pairs = QUERY_COLUMNS // LANES
    return pl.pallas_call(
        attend_forward_kernel,
        grid_spec=pltpu.PrefetchScalarGridSpec(
            num_scalar_prefetch=1,
            grid=(pairs,),
            in_specs=[
                pl.BlockSpec((tokens, LANES), lambda i, s: (0, i)),
                pl.BlockSpec((length, LANES), lambda i, s: (0, (i // 2) // 2)),
                pl.BlockSpec((length, LANES), lambda i, s: (0, (KEY_VALUE_HEADS + i // 2) // 2)),
            ],
            out_specs=[
                pl.BlockSpec((tokens, LANES), lambda i, s: (0, i)),
                pl.BlockSpec((tokens, LANES), lambda i, s: (0, i)),
            ],
        ),
        out_shape=[
            jax.ShapeDtypeStruct((tokens, QUERY_COLUMNS), bf16),
            jax.ShapeDtypeStruct((tokens, QUERY_COLUMNS), f32),
        ],
        compiler_params=pltpu.CompilerParams(vmem_limit_bytes=VMEM_LIMIT),
        name="attend_forward",
        cost_estimate=LIGHT,
    )(place, queries, keys_values, keys_values)


def three_parts(values, lane):
    high = values.astype(bf16).astype(f32)
    rest = values - high
    middle = rest.astype(bf16).astype(f32)
    low = rest - middle
    return jnp.where(
        lane == 0, high, jnp.where(lane == 1, middle, jnp.where(lane == 2, low, 0.0))
    )


def attend_backward_kernel(
    first_group, count, place_ref, q_ref, k_ref, v_ref, out_ref, log_ref, grad_ref, dq_ref, dkv_ref, dk_sum, dv_sum
):
    pair_index = pl.program_id(0)
    local = pair_index // 2
    group = first_group + local
    place = place_ref[0]
    tokens = q_ref.shape[0]
    lane = lanes_of((tokens, LANES))
    first = lane < HEAD_SIZE
    inside = lane % HEAD_SIZE
    pair = q_ref[...].astype(f32)
    grad = grad_ref[...].astype(f32)
    delta = pltpu.roll(head_sum(grad * out_ref[...].astype(f32)), HEAD_SIZE, 1)
    logs = three_parts(log_ref[...] * (1.0 / SCORE_EXPONENT), inside)
    deltas = three_parts(delta, inside)
    minus = jnp.where(inside < 3, -1.0, 0.0)

    def sides(own, other):
        return (
            jnp.where(first, own, other).astype(bf16),
            jnp.where(first, other, own).astype(bf16),
        )

    queries = sides(pair, 0.0)
    grads = sides(grad, 0.0)
    queries_log = sides(pair, logs)
    grads_delta = sides(grad, deltas)

    @pl.when(pair_index % 2 == 0)
    def _():
        dk_sum[...] = jnp.zeros_like(dk_sum)
        dv_sum[...] = jnp.zeros_like(dv_sum)

    def step(j, dq, diagonal):
        rows = pl.ds(pl.multiple_of(j * tokens, tokens), tokens)
        key_wide = both_halves(k_ref[rows, :], group % 2)
        value_wide = both_halves(v_ref[rows, :], (KEY_VALUE_HEADS + group) % 2)
        keys = sides(key_wide, 0.0)
        keys_log = sides(key_wide, minus)
        values_delta = sides(value_wide, minus)
        dk = dk_sum[rows, :]
        dv = dv_sum[rows, :]
        for head in range(2):
            weights = jnp.exp2(dot_nt(keys_log[head], queries_log[head]) * SCORE_EXPONENT)
            if diagonal:
                row = lax.broadcasted_iota(jnp.int32, weights.shape, 0)
                weights = jnp.where(row <= lanes_of(weights.shape), weights, 0.0)
            grad_weights = dot_nt(values_delta[head], grads_delta[head])
            grad_scores = (weights * grad_weights).astype(bf16)
            dv = dv + dot_nn(weights.astype(bf16), grads[head])
            dk = dk + dot_nn(grad_scores, queries[head])
            dq = dq + dot_tn(grad_scores, keys[head])
        dk_sum[rows, :] = dk
        dv_sum[rows, :] = dv
        return dq

    dq = lax.fori_loop(
        0, place, lambda j, c: step(j, c, False), jnp.zeros((tokens, LANES), f32)
    )
    dq = step(place, dq, True)
    dq_ref[...] = (dq * HEAD_SIZE**-0.5).astype(bf16)

    @pl.when(pair_index % 2 == 1)
    def _():
        wide_lane = lanes_of(dk_sum.shape)
        for total, slot, factor in (
            (dk_sum, local, HEAD_SIZE**-0.5),
            (dv_sum, count + local, 1.0),
        ):
            both = (total[...] + pltpu.roll(total[...], HEAD_SIZE, 1)) * factor
            columns = pl.ds(pl.multiple_of(slot // 2 * LANES, LANES), LANES)
            mine = wide_lane // HEAD_SIZE == slot % 2
            dkv_ref[:, columns] = jnp.where(
                mine, both, dkv_ref[:, columns].astype(f32)
            ).astype(bf16)


def attend_backward(first, count, place, queries, keys_values, mixed, logs, grad_mixed):
    tokens = queries.shape[0]
    length = keys_values.shape[0]
    group = QUERY_HEADS // KEY_VALUE_HEADS * HEAD_SIZE
    own = pl.BlockSpec((tokens, LANES), lambda i, s: (0, 2 * first + i))
    keys = pl.BlockSpec((length, LANES), lambda i, s: (0, (first + i // 2) // 2))
    values = pl.BlockSpec(
        (length, LANES), lambda i, s: (0, (KEY_VALUE_HEADS + first + i // 2) // 2)
    )
    columns = 2 * count * HEAD_SIZE
    return pl.pallas_call(
        partial(attend_backward_kernel, first, count),
        grid_spec=pltpu.PrefetchScalarGridSpec(
            num_scalar_prefetch=1,
            grid=(2 * count,),
            in_specs=[own, keys, values, own, own, own],
            out_specs=[
                pl.BlockSpec((tokens, LANES), lambda i, s: (0, i)),
                pl.BlockSpec((length, columns), lambda i, s: (0, 0)),
            ],
            scratch_shapes=[pltpu.VMEM((length, LANES), f32), pltpu.VMEM((length, LANES), f32)],
        ),
        out_shape=[
            jax.ShapeDtypeStruct((tokens, count * group), bf16),
            jax.ShapeDtypeStruct((length, columns), bf16),
        ],
        compiler_params=pltpu.CompilerParams(vmem_limit_bytes=VMEM_LIMIT),
        name="attend_backward",
        cost_estimate=LIGHT,
    )(place, queries, keys_values, keys_values, mixed, logs, grad_mixed)


def hidden_kernel(n0_ref, n1_ref, wg_ref, wu_ref, hidden_ref, gate_ref, up_ref, n_all):
    tokens = n0_ref.shape[0]

    @pl.when(pl.program_id(0) == 0)
    def _():
        n_all[:tokens] = n0_ref[...]
        n_all[tokens:] = n1_ref[...]

    gate = dot_nn(n_all[...], wg_ref[...])
    up = dot_nn(n_all[...], wu_ref[...])
    hidden_ref[...] = (gate / (1.0 + jnp.exp(-gate)) * up).astype(bf16)
    gate_ref[...] = gate.astype(bf16)
    up_ref[...] = up.astype(bf16)


def hidden_pass(normed, wgate, wup):
    tokens, width = normed[0].shape
    columns = wgate.shape[1]
    tile = min(256, columns)
    whole = pl.BlockSpec((tokens, width), lambda i: (0, 0))
    down = pl.BlockSpec((width, tile), lambda i: (0, i))
    out = pl.BlockSpec((2 * tokens, tile), lambda i: (0, i))
    return pl.pallas_call(
        hidden_kernel,
        grid=(pl.cdiv(columns, tile),),
        in_specs=[whole] * 2 + [down] * 2,
        out_specs=[out] * 3,
        out_shape=[jax.ShapeDtypeStruct((2 * tokens, columns), bf16)] * 3,
        scratch_shapes=[pltpu.VMEM((2 * tokens, width), bf16)],
        compiler_params=pltpu.CompilerParams(vmem_limit_bytes=VMEM_LIMIT),
        name="hidden_pass",
        cost_estimate=LIGHT,
    )(*normed, wgate, wup)


def gates_kernel(g0_ref, g1_ref, wd_ref, gate_ref, up_ref, gate_out_ref, up_out_ref, g_all):
    tokens = g0_ref.shape[0]

    @pl.when(pl.program_id(0) == 0)
    def _():
        g_all[:tokens] = g0_ref[...]
        g_all[tokens:] = g1_ref[...]

    grad = dot_nt(g_all[...], wd_ref[...])
    gate = gate_ref[...].astype(f32)
    up = up_ref[...].astype(f32)
    sigmoid = 1.0 / (1.0 + jnp.exp(-gate))
    gate_out_ref[...] = (grad * up * (sigmoid * (1.0 + gate * (1.0 - sigmoid)))).astype(bf16)
    up_out_ref[...] = (grad * (gate * sigmoid)).astype(bf16)


def gates_pass(grad_top, wdown, gate, up):
    tokens, width = grad_top[0].shape
    columns = gate.shape[1]
    tile = min(256, columns)
    whole = pl.BlockSpec((tokens, width), lambda i: (0, 0))
    out = pl.BlockSpec((2 * tokens, tile), lambda i: (0, i))
    return pl.pallas_call(
        gates_kernel,
        grid=(pl.cdiv(columns, tile),),
        in_specs=[whole] * 2 + [pl.BlockSpec((tile, width), lambda i: (i, 0)), out, out],
        out_specs=[out] * 2,
        out_shape=[jax.ShapeDtypeStruct((2 * tokens, columns), bf16)] * 2,
        scratch_shapes=[pltpu.VMEM((2 * tokens, width), bf16)],
        compiler_params=pltpu.CompilerParams(vmem_limit_bytes=VMEM_LIMIT),
        name="gates_pass",
        cost_estimate=LIGHT,
    )(*grad_top, wdown, gate, up)


def back_kernel(count, transposed, *refs):
    own_ref, send_ref = refs[-2:]
    tokens = own_ref.shape[0]
    dot = dot_nt if transposed else dot_nn

    def total(start):
        rows = pl.ds(start, tokens)
        result = dot(refs[0][rows, :], refs[count][...])
        for i in range(1, count):
            result = result + dot(refs[i][rows, :], refs[count + i][...])
        return result

    own_ref[...] = total(0)
    send_ref[...] = total(tokens).astype(bf16)


def back_pass(lefts, weights, transposed):
    tokens, depth = lefts[0].shape
    width = weights[0].shape[0 if transposed else 1]
    count = len(lefts)
    tile = min(512, width)
    if transposed:
        weight_spec = pl.BlockSpec((tile, depth), lambda i: (i, 0))
    else:
        weight_spec = pl.BlockSpec((depth, tile), lambda i: (0, i))
    out = pl.BlockSpec((tokens // 2, tile), lambda i: (0, i))
    return pl.pallas_call(
        partial(back_kernel, count, transposed),
        grid=(width // tile,),
        in_specs=[pl.BlockSpec((tokens, depth), lambda i: (0, 0))] * count
        + [weight_spec] * count,
        out_specs=[out, out],
        out_shape=[
            jax.ShapeDtypeStruct((tokens // 2, width), f32),
            jax.ShapeDtypeStruct((tokens // 2, width), bf16),
        ],
        compiler_params=pltpu.CompilerParams(vmem_limit_bytes=VMEM_LIMIT),
        name="back_pass",
        cost_estimate=LIGHT,
    )(*lefts, *weights)


def weight_kernel(left_count, *refs):
    lefts, rights, out_ref = refs[:left_count], refs[left_count:-1], refs[-1]
    step = min(lefts[0].shape[0], rights[0].shape[0])

    def piece(refs, start):
        index, offset = divmod(start, refs[0].shape[0])
        return refs[index][pl.ds(offset, step), :]

    total = None
    for start in range(0, left_count * lefts[0].shape[0], step):
        term = dot_tn(piece(lefts, start), piece(rights, start))
        total = term if total is None else total + term
    out_ref[...] = total.astype(bf16)


def weight_pass(lefts, rights):
    rows, columns = lefts[0].shape[1], rights[0].shape[1]
    tile = 512 if rows % 512 == 0 else 384 if rows % 384 == 0 else rows
    return pl.pallas_call(
        partial(weight_kernel, len(lefts)),
        grid=(rows // tile,),
        in_specs=[pl.BlockSpec((left.shape[0], tile), lambda i: (0, i)) for left in lefts]
        + [pl.BlockSpec(right.shape, lambda i: (0, 0)) for right in rights],
        out_specs=pl.BlockSpec((tile, columns), lambda i: (i, 0)),
        out_shape=jax.ShapeDtypeStruct((rows, columns), bf16),
        compiler_params=pltpu.CompilerParams(vmem_limit_bytes=VMEM_LIMIT),
        name="weight_pass",
        cost_estimate=LIGHT,
    )(*lefts, *rights)


def placed_kernel(side_ref, own_ref, other_ref, out_ref):
    mine = pl.program_id(0) == side_ref[0]

    @pl.when(mine)
    def _():
        out_ref[0, 0] = own_ref[:, 0]

    @pl.when(jnp.logical_not(mine))
    def _():
        out_ref[0, 0] = other_ref[:, 0]


def placed(own, other, side):
    seq, group, rows, columns = own.shape

    def entry(mine, e, g, s):
        parked = jnp.where(e == 0, 0, group - 1)
        return (0, jnp.where((e == s[0]) == mine, g, parked), 0, 0)

    return pl.pallas_call(
        placed_kernel,
        grid_spec=pltpu.PrefetchScalarGridSpec(
            num_scalar_prefetch=1,
            grid=(2, group),
            in_specs=[
                pl.BlockSpec((seq, 1, rows, columns), partial(entry, True)),
                pl.BlockSpec((seq, 1, rows, columns), partial(entry, False)),
            ],
            out_specs=pl.BlockSpec(
                (1, 1, seq, rows, columns), lambda e, g, s: (e, g, 0, 0, 0)
            ),
        ),
        out_shape=jax.ShapeDtypeStruct((2, group, seq, rows, columns), own.dtype),
        name="placed",
        cost_estimate=LIGHT,
    )(side.astype(jnp.int32).reshape(1), own, other)


def joined_kernel(side_ref, own_ref, other_ref, out_ref):
    mine = pl.program_id(1) == side_ref[0]

    @pl.when(mine)
    def _():
        out_ref[:, 0] = own_ref[...]

    @pl.when(jnp.logical_not(mine))
    def _():
        out_ref[:, 0] = other_ref[...]


def joined(own, other, side, axis):
    shape = own.shape[:axis] + (2,) + own.shape[axis:]
    columns = own.shape[-1]
    lead = math.prod(own.shape[:axis])
    rows = math.prod(own.shape[axis:-1])
    leads, chunks = lead, 1
    while leads % 2 == 0 and leads * rows * columns > 800_000:
        leads //= 2
    while leads == 1 and rows % (32 * chunks) == 0 and rows // chunks * columns > 800_000:
        chunks *= 2
    block = rows // chunks

    def entry(mine, p, e, i, s):
        parked = jnp.where(e == 0, 0, chunks - 1)
        return (p, jnp.where((e == s[0]) == mine, i, parked), 0)

    return pl.pallas_call(
        joined_kernel,
        grid_spec=pltpu.PrefetchScalarGridSpec(
            num_scalar_prefetch=1,
            grid=(lead // leads, 2, chunks),
            in_specs=[
                pl.BlockSpec((leads, block, columns), partial(entry, True)),
                pl.BlockSpec((leads, block, columns), partial(entry, False)),
            ],
            out_specs=pl.BlockSpec((leads, 1, block, columns), lambda p, e, i, s: (p, e, i, 0)),
        ),
        out_shape=jax.ShapeDtypeStruct((lead, 2, rows, columns), own.dtype),
        compiler_params=pltpu.CompilerParams(vmem_limit_bytes=VMEM_LIMIT),
        name="joined",
        cost_estimate=LIGHT,
    )(
        side.astype(jnp.int32).reshape(1),
        own.reshape(lead, rows, columns),
        other.reshape(lead, rows, columns),
    ).reshape(shape)


def swap(values, bit):
    pairs = [(i, i ^ bit) for i in range(lax.axis_size("rows"))]
    return lax.ppermute(values, "rows", pairs)


def bit_of(bit):
    return (lax.axis_index("rows") // bit) % 2


def gather_bit(values, bit, axis):
    return joined(values, swap(values, bit), bit_of(bit), axis)


def part(values, index, axis):
    return lax.dynamic_index_in_dim(values, index, axis, keepdims=False)


def reduce_bit(values, bit, axis):
    return add_bit(values, pass_bit(values, bit, axis), bit, axis)


def outer_pairs(step, low, high):
    size = lax.axis_size("rows")
    return [
        (i, i + 4 * step)
        for i in range(size)
        if low <= i // 4 < high and 0 <= i // 4 + step < size // 4
    ]


def send_outer(values):
    count = lax.axis_size("rows") // 4
    if count == 2:
        return (swap(values, 4),)
    up, down = values, values
    ups, downs = [], []
    for t in range(1, count):
        up = lax.ppermute(up, "rows", outer_pairs(1, t - 1, count))
        down = lax.ppermute(down, "rows", outer_pairs(-1, 0, count - t + 1))
        ups.append(up)
        downs.append(down)
    return tuple(ups[::-1] + downs)


def join_outer(values, received, axis):
    count = lax.axis_size("rows") // 4
    if count == 2:
        return joined(values, received[0], bit_of(4), axis)
    place = lax.axis_index("rows") // 4
    line = jnp.stack([*received[: count - 1], values, *received[count - 1 :]], axis)
    return lax.dynamic_slice_in_dim(line, count - 1 - place, count, axis)


def gather_outer(values, axis):
    return join_outer(values, send_outer(values), axis)


def pass_outer(values, axis):
    count = lax.axis_size("rows") // 4
    place = lax.axis_index("rows") // 4

    def entry(index):
        return part(values, jnp.clip(index, 0, count - 1), axis)

    if count == 1:
        return ()
    if count == 2:
        return (swap(entry(1 - place), 4),)
    up, down = entry(place + count - 1), entry(place - count + 1)
    for t in range(1, count):
        up = lax.ppermute(up, "rows", outer_pairs(1, 0, t))
        down = lax.ppermute(down, "rows", outer_pairs(-1, count - t, count))
        if t < count - 1:
            up = (entry(place + count - 1 - t).astype(f32) + up.astype(f32)).astype(bf16)
            down = (entry(place - count + 1 + t).astype(f32) + down.astype(f32)).astype(bf16)
    return (up, down)


def add_outer(values, received, axis):
    total = part(values, lax.axis_index("rows") // 4, axis).astype(f32)
    for term in received:
        total = total + term.astype(f32)
    return total.astype(bf16)


def reduce_outer(values, axis):
    return add_outer(values, pass_outer(values, axis), axis)


def pass_bit(values, bit, axis):
    return swap(part(values, 1 - bit_of(bit), axis), bit)


def add_bit(values, received, bit, axis):
    own = part(values, bit_of(bit), axis)
    return (own.astype(f32) + received.astype(f32)).astype(bf16)


def gather_seq(values):
    return lax.all_gather(values, "seq", axis=0, tiled=False)


def reduce_seq(values):
    return lax.psum_scatter(values, "seq", scatter_dimension=0, tiled=False)


def sum_all(values):
    for axis in ("rows", "seq"):
        size = lax.axis_size(axis)
        bit = 1
        while bit < size:
            pairs = [(i, i ^ bit) for i in range(size)]
            values = values + lax.ppermute(values, axis, pairs)
            bit *= 2
    return values


def across_group(own, send):
    return (own + swap(send, 1).astype(f32)).astype(bf16)


def stage(*values):
    return lax.optimization_barrier(values)


def mm(left, right):
    return jnp.einsum("ab,bc->ac", left, right, preferred_element_type=f32)


def mm_t(left, right):
    return jnp.einsum("ab,cb->ac", left, right, preferred_element_type=f32)


def t_mm(left, right):
    return jnp.einsum("ab,ac->bc", left, right, preferred_element_type=f32)


def norm_scale(values):
    return lax.rsqrt(jnp.mean(values * values, axis=-1, keepdims=True) + EPSILON)


def norm_backward(values, scale, gain, grad):
    gained = grad * gain
    inner = jnp.mean(values * gained, axis=-1, keepdims=True)
    result = scale * gained - values * (scale * scale * scale) * inner
    return result, jnp.sum(grad * values * scale, axis=0)


def shards(
    tokens_in,
    corpus,
    corpus_weight,
    w_qkv,
    w_out,
    w_gate,
    w_up,
    w_down,
    attn_gain,
    ffn_gain,
    q_gain,
    k_gain,
    upstream,
):
    shard_length, width = tokens_in.shape[1:]
    row_devices = lax.axis_size("rows")
    seq_devices = lax.axis_size("seq")
    outer = row_devices // 4
    d_rows = w_qkv.shape[0]
    f_rows = w_down.shape[0]
    place = lax.axis_index("seq").astype(jnp.int32)
    inputs = tokens_in[0].astype(f32)

    extra = jnp.stack(
        [
            attn_gain,
            ffn_gain,
            jnp.broadcast_to(corpus.astype(bf16), attn_gain.shape),
        ],
        axis=1,
    )
    extra = jnp.pad(extra, ((0, 0), (0, LANES - extra.shape[1])))
    kv_lines = gather_seq(jnp.concatenate([w_qkv[:, QUERY_COLUMNS:], extra], axis=1))
    query_shard = jnp.concatenate([w_qkv[:, :QUERY_COLUMNS], w_out.T], axis=1)
    query_shard, w_gate, w_up = stage(query_shard, w_gate, w_up)
    query_lines = gather_seq(query_shard)

    def to_group(weight):
        blocks = weight.reshape(d_rows, outer, 4, seq_devices, f_rows)
        blocks = jnp.transpose(blocks, (2, 0, 3, 1, 4))
        return blocks.reshape(2, 2, d_rows, outer * seq_devices * f_rows)

    def spread_hidden(lines, received):
        if outer == 2:
            lines = lines.reshape(seq_devices, 4, d_rows, hidden_columns)
            other = received[0].reshape(lines.shape)
            return placed(lines, other, bit_of(4)).reshape(width, hidden_columns)
        full = join_outer(lines, received, 0)
        return jnp.moveaxis(full, 1, 3).reshape(width, hidden_columns)

    gate_up = jnp.stack([to_group(w_gate), to_group(w_up)], axis=2)
    hidden_columns = gate_up.shape[-1]
    core, near = bit_of(1), bit_of(2)
    other, kv_lines, down_other, query_lines = stage(
        swap(part(gate_up, 1 - core, 1), 1), kv_lines, send_outer(w_down), query_lines
    )
    gate_up = joined(part(gate_up, core, 1), other, core, 1)
    down_pair = join_outer(w_down, down_other, 0)
    left, right = kv_lines[..., : 3 * LANES], kv_lines[..., 3 * LANES :]
    other, left_other, right_other = stage(
        swap(part(gate_up, 1 - near, 0), 2), send_outer(left), swap(right, 2)
    )
    gate_up = joined(part(gate_up, near, 0), other, near, 0)
    gate_lines = gather_seq(gate_up[:, :, 0])
    left = join_outer(left, left_other, 0)
    right = joined(right, right_other, near, 0)
    left_other, right_other = stage(swap(left, 2), send_outer(right))
    left = joined(left, left_other, near, 1)
    right = join_outer(right, right_other, 0)
    q_left, q_right = query_lines[..., :QUERY_COLUMNS], query_lines[..., QUERY_COLUMNS:]
    q_left, q_right, left, right = stage(q_left, q_right, left, right)
    q_left_other, q_right_other = send_outer(q_left), swap(q_right, 2)
    left, right = gather_bit(left, 1, 2), gather_bit(right, 1, 2)
    left, right = left.reshape(width, -1), right.reshape(width, -1)
    wkv = jnp.concatenate([left, right[:, : 2 * LANES]], axis=1)
    rows = dot_nt(jnp.eye(8, LANES, dtype=bf16), right[:, 2 * LANES :])
    attn_gain_full, ffn_gain_full, corpus_full = rows[0:1], rows[1:2], rows[2]

    position = (place * shard_length + jnp.arange(shard_length, dtype=jnp.int32)).astype(f32)
    half = HEAD_SIZE // 2
    exponent = jnp.arange(half, dtype=f32) * (-2.0 / HEAD_SIZE)
    angles = position[:, None] * jnp.power(ROPE_BASE, exponent)[None, :]
    cosine, sine = jnp.cos(angles), jnp.sin(angles)
    cos_table = jnp.concatenate([cosine] * 4, axis=1)
    sin_table = jnp.concatenate([-sine, sine] * 2, axis=1)
    wide_q = jnp.tile(q_gain.astype(f32), QUERY_HEADS)
    wide_k = jnp.concatenate(
        [jnp.tile(k_gain.astype(f32), KEY_VALUE_HEADS), jnp.ones((KEY_COLUMNS,), f32)]
    )
    wide_q = jnp.broadcast_to(wide_q[None, :], (8, QUERY_COLUMNS))
    wide_k = jnp.broadcast_to(wide_k[None, :], (8, 2 * KEY_COLUMNS))

    in_scale = norm_scale(inputs)
    normed = (inputs * in_scale * attn_gain_full).astype(bf16)
    joint_kv = mm(normed, wkv)
    own_kv = heads_forward(joint_kv, wide_k, cos_table, sin_table, KEY_COLUMNS)
    own_kv, q_left_other, q_right_other = stage(own_kv, q_left_other, q_right_other)
    keys_values = gather_seq(own_kv).reshape(-1, 2 * KEY_COLUMNS)
    q_left = join_outer(q_left, q_left_other, 0)
    q_right = joined(q_right, q_right_other, near, 0)
    left_other, right_other, gate_lines = stage(
        swap(q_left, 2), send_outer(q_right), gate_lines
    )
    q_left = joined(q_left, left_other, near, 1)
    q_right = join_outer(q_right, right_other, 0)
    gate_other = send_outer(gate_lines)
    wq = gather_bit(q_left, 1, 2).reshape(width, -1)

    corpora = jnp.arange(CORPORA, dtype=jnp.int32)
    per_device = corpus_full.reshape(-1, d_rows)[:, 0].astype(jnp.int32)
    counts = (
        jnp.sum((per_device[:, None] == corpora[None, :]).astype(f32), axis=0) * shard_length
    )
    own_corpus = (corpus[0] == corpora).astype(f32)
    weight_row = jnp.sum(own_corpus * corpus_weight.astype(f32))
    count_row = jnp.sum(own_corpus * counts)
    factor = weight_row / DENOM * (jnp.sum(counts) / (CORPORA * count_row))
    grad_full = upstream[0].astype(f32) * factor
    grad_top, wq = stage(grad_full.astype(bf16), wq)

    joint_q = mm(normed, wq)
    queries = heads_forward(joint_q, wide_q, cos_table, sin_table, QUERY_COLUMNS)
    place_array = place.reshape(1)
    keys_values, queries, up_in, down_in = stage(
        keys_values, queries, gate_up[:, :, 1], down_pair
    )
    up_lines = gather_seq(up_in)
    down_lines = gather_seq(down_in)
    mixed, logs = attend_forward(place_array, queries, keys_values)
    mixed, grad_top1, grad_top2, gate_other, wout_other = stage(
        mixed, swap(grad_top, 1), swap(grad_top, 2), gate_other, swap(q_right, 1)
    )
    wout_t = joined(q_right, wout_other, core, 2).reshape(width, -1)
    middle = inputs + mm_t(mixed, wout_t)

    ffn_scale = norm_scale(middle)
    normed_ffn = (middle * ffn_scale * ffn_gain_full).astype(bf16)
    normed1, up_other, wgate = stage(
        swap(normed_ffn, 1), send_outer(up_lines), spread_hidden(gate_lines, gate_other)
    )
    wup = spread_hidden(up_lines, up_other)
    hidden_near, gate_near, up_near = hidden_pass((normed_ffn, normed1), wgate, wup)
    normed2, hidden_near, grad_top3 = stage(
        swap(normed_ffn, 2), hidden_near, swap(grad_top2, 1)
    )
    normed3 = swap(normed2, 1)
    hidden_far, gate_far, up_far = hidden_pass((normed2, normed3), wgate, wup)
    normed4 = (normed_ffn, normed1, normed2, normed3)
    grad_top4 = (grad_top, grad_top1, grad_top2, grad_top3)
    grad_wdown = weight_pass((hidden_near, hidden_far), grad_top4)
    grad_wdown, wdown = stage(grad_wdown, down_lines.reshape(hidden_columns, width))
    gate_far, up_far = gates_pass((grad_top2, grad_top3), wdown, gate_far, up_far)
    own, send = back_pass((gate_far, up_far), (wgate, wup), True)
    across, wdown = stage(across_group(own, send), wdown)
    gate_near, up_near = gates_pass((grad_top, grad_top1), wdown, gate_near, up_near)
    own, send = back_pass((gate_near, up_near), (wgate, wup), True)

    hidden_shape = (outer, 2, 2, seq_devices, d_rows, hidden_columns)
    down_shape = (seq_devices, outer, f_rows, width)
    grad_wdown = grad_wdown.reshape(down_shape)
    grad_wgate = weight_pass(normed4, (gate_near, gate_far)).reshape(hidden_shape)
    grad_wup = weight_pass(normed4, (up_near, up_far)).reshape(hidden_shape)
    across, own, send, grad_wgate, grad_wup, down_other = stage(
        swap(across, 2),
        own,
        swap(send, 1),
        grad_wgate,
        grad_wup,
        pass_outer(grad_wdown, 1),
    )
    grad_wdown = add_outer(grad_wdown, down_other, 1)
    own = own + send.astype(f32)
    grad_normed_ffn = own + across.astype(f32)
    grad_wdown = reduce_seq(grad_wdown)

    grad_middle_part, grad_ffn_gain = norm_backward(
        middle, ffn_scale, ffn_gain_full, grad_normed_ffn
    )
    grad_middle = grad_full + grad_middle_part
    grad_branch = grad_middle.astype(bf16)
    grad_mixed = mm(grad_branch, wout_t).astype(bf16)
    attend = (place_array, queries, keys_values, mixed, logs)
    grad_q1, grad_kv1 = attend_backward(0, 3, *attend, grad_mixed)
    grad_q1, grad_kv1, gate_other, grad_mixed, grad_wdown = stage(
        grad_q1, grad_kv1, pass_outer(grad_wgate, 0), grad_mixed, grad_wdown
    )
    grad_kv1 = reduce_seq(grad_kv1.reshape(seq_devices, shard_length, -1))
    grad_gate = jnp.moveaxis(add_outer(grad_wgate, gate_other, 0), 2, 0)
    grad_q2, grad_kv2 = attend_backward(3, 2, *attend, grad_mixed)
    shape = (outer, 2, 2, seq_devices, d_rows)
    grad_wout = t_mm(grad_branch, mixed).astype(bf16).reshape(*shape, QUERY_COLUMNS)
    grad_q2, grad_kv2, up_other, hidden_near, hidden_far, grad_kv1, wout_other = stage(
        grad_q2,
        grad_kv2,
        pass_outer(grad_wup, 0),
        hidden_near,
        hidden_far,
        grad_kv1,
        pass_bit(grad_wout, 1, 2),
    )
    grad_kv2 = reduce_seq(grad_kv2.reshape(seq_devices, shard_length, -1))

    grad_up = jnp.moveaxis(add_outer(grad_wup, up_other, 0), 2, 0)
    grad_q = jnp.concatenate([grad_q1, grad_q2], axis=1)
    joint_grad_q, gain_q = heads_backward(
        grad_q, joint_q, wide_q, cos_table, sin_table, QUERY_COLUMNS
    )
    grad_wq = t_mm(normed, joint_grad_q).astype(bf16).reshape(*shape, QUERY_COLUMNS)
    grad_wout = add_bit(grad_wout, wout_other, 1, 2)
    own_far, send_far = back_pass((hidden_far,), (wdown,), False)
    own_near, send_near = back_pass((hidden_near,), (wdown,), False)
    grad_kv2, wq_other, grad_up, grad_gate, own_far, send_far, send_near = stage(
        grad_kv2, pass_bit(grad_wq, 1, 2), grad_up, grad_gate, own_far, send_far, send_near
    )
    gate_up = reduce_seq(jnp.stack([grad_gate, grad_up], axis=3))
    grad_wq = add_bit(grad_wq, wq_other, 1, 2)
    wq_other, wout_other = pass_bit(grad_wq, 2, 1), pass_outer(grad_wout, 0)

    grad_kv1, grad_kv2 = (
        part_.reshape(shard_length, 2, -1) for part_ in (grad_kv1, grad_kv2)
    )
    grad_kv = jnp.concatenate([grad_kv1, grad_kv2], axis=2).reshape(shard_length, -1)
    joint_grad_kv, gain_k = heads_backward(
        grad_kv, joint_kv, wide_k, cos_table, sin_table, KEY_COLUMNS
    )
    grad_wkv = t_mm(normed, joint_grad_kv).astype(bf16)
    grad_normed = mm_t(joint_grad_q, wq) + mm_t(joint_grad_kv, wkv)
    grad_input_part, grad_attn_gain = norm_backward(
        inputs, in_scale, attn_gain_full, grad_normed
    )
    input_grad = (grad_middle + grad_input_part).astype(bf16)

    gain_rows = jnp.stack([grad_attn_gain, grad_ffn_gain]).astype(bf16)
    gain_columns = t_mm(gain_rows, jnp.eye(2, LANES, dtype=bf16)).astype(bf16)
    left = grad_wkv[:, : 3 * LANES].reshape(*shape, -1)
    right = jnp.concatenate([grad_wkv[:, 3 * LANES :], gain_columns], axis=1)
    right = right.reshape(*shape, -1)
    left, right, left_other, right_other, wq_other, wout_other = stage(
        left, right, pass_bit(left, 1, 2), pass_bit(right, 1, 2), wq_other, wout_other
    )
    left = add_bit(left, left_other, 1, 2)
    right = add_bit(right, right_other, 1, 2)
    grad_wq = add_bit(grad_wq, wq_other, 2, 1)
    grad_wout = add_outer(grad_wout, wout_other, 0)
    left_other, right_other, wq_other, wout_other = stage(
        pass_bit(left, 2, 1),
        pass_outer(right, 0),
        pass_outer(grad_wq, 0),
        pass_bit(grad_wout, 2, 0),
    )
    left = add_bit(left, left_other, 2, 1)
    right = add_outer(right, right_other, 0)
    left_other, right_other = stage(pass_outer(left, 0), pass_bit(right, 2, 0))
    sums = reduce_seq(
        jnp.concatenate(
            [
                add_outer(grad_wq, wq_other, 0),
                add_outer(left, left_other, 0),
                add_bit(right, right_other, 2, 0),
                add_bit(grad_wout, wout_other, 2, 0),
            ],
            axis=-1,
        )
    )
    own_near = own_near + swap(send_near, 1).astype(f32)
    across = across_group(own_far, send_far)
    output = (middle + own_near + swap(across, 2).astype(f32)).astype(bf16)
    columns = QUERY_COLUMNS + 2 * KEY_COLUMNS
    long_gains = sums[:, columns : columns + 2].astype(f32)
    head_gains = sum_all(
        jnp.concatenate(
            [
                jnp.sum(gain_q[0].reshape(-1, HEAD_SIZE), axis=0),
                jnp.sum(gain_k[0, :KEY_COLUMNS].reshape(-1, HEAD_SIZE), axis=0),
            ]
        )[None]
    )[0]

    grads = gate_up
    grads = joined(part(grads, near, 0), swap(part(grads, 1 - near, 0), 2), near, 0)
    grads = joined(part(grads, core, 1), swap(part(grads, 1 - core, 1), 1), core, 1)

    def from_group(blocks):
        blocks = blocks.reshape(4, d_rows, seq_devices, outer, f_rows)
        return jnp.transpose(blocks, (1, 3, 0, 2, 4)).reshape(d_rows, -1).astype(f32)

    grad_wgate, grad_wup = from_group(grads[:, :, 0]), from_group(grads[:, :, 1])
    return (
        output[None],
        input_grad[None],
        sums[:, :columns].astype(f32),
        sums[:, columns + LANES :].T.astype(f32),
        grad_wgate,
        grad_wup,
        grad_wdown.astype(f32),
        long_gains[:, 0],
        long_gains[:, 1],
        head_gains[:HEAD_SIZE],
        head_gains[HEAD_SIZE:],
    )


def solution(mesh):
    return jax.shard_map(
        shards,
        mesh=mesh,
        in_specs=(
            P("rows", "seq", None),
            P("rows"),
            P(),
            P(("rows", "seq"), None),
            P(None, ("rows", "seq")),
            P(("rows", "seq"), None),
            P(("rows", "seq"), None),
            P(("rows", "seq"), None),
            P(("rows", "seq")),
            P(("rows", "seq")),
            P(),
            P(),
            P("rows", "seq", None),
        ),
        out_specs=(
            P("rows", "seq", None),
            P("rows", "seq", None),
            P(("rows", "seq"), None),
            P(None, ("rows", "seq")),
            P(("rows", "seq"), None),
            P(("rows", "seq"), None),
            P(("rows", "seq"), None),
            P(("rows", "seq")),
            P(("rows", "seq")),
            P(),
            P(),
        ),
        check_vma=False,
    )
```

```python
import math
from functools import partial

import jax
import jax.numpy as jnp
from jax import lax
from jax.experimental import pallas as pl
from jax.experimental.pallas import tpu as pltpu
from jax.sharding import PartitionSpec as P

QUERY_HEADS = 20
KEY_VALUE_HEADS = 5
HEAD_SIZE = 64
CORPORA = 8
DENOM = 64
EPSILON = 1e-06
ROPE_BASE = 10000.0
QUERY_COLUMNS = QUERY_HEADS * HEAD_SIZE
KEY_COLUMNS = KEY_VALUE_HEADS * HEAD_SIZE
LANES = 128
SCORE_EXPONENT = 1.4426950408889634 * HEAD_SIZE**-0.5
VMEM_LIMIT = 48 * 1024 * 1024

f32, bf16 = jnp.float32, jnp.bfloat16
LIGHT = pl.CostEstimate(flops=1000, bytes_accessed=1000, transcendentals=0)


def dot_nn(a, b):
    return lax.dot_general(a, b, (((1,), (0,)), ((), ())), preferred_element_type=f32)


def dot_nt(a, b):
    return lax.dot_general(a, b, (((1,), (1,)), ((), ())), preferred_element_type=f32)


def dot_tn(a, b):
    return lax.dot_general(a, b, (((0,), (0,)), ((), ())), preferred_element_type=f32)


def lanes_of(shape):
    return lax.broadcasted_iota(jnp.int32, shape, len(shape) - 1)


def head_sum(values):
    row = lax.broadcasted_iota(jnp.int32, (LANES, LANES), 0) // HEAD_SIZE
    column = lax.broadcasted_iota(jnp.int32, (LANES, LANES), 1) // HEAD_SIZE
    ones = jnp.where(row == column, 1.0, 0.0).astype(bf16)
    high = values.astype(bf16)
    low = (values - high.astype(f32)).astype(bf16)
    return dot_nn(high, ones) + dot_nn(low, ones)


def partner(values):
    first = lanes_of(values.shape) % HEAD_SIZE < HEAD_SIZE // 2
    return jnp.where(
        first,
        pltpu.roll(values, LANES - HEAD_SIZE // 2, 1),
        pltpu.roll(values, HEAD_SIZE // 2, 1),
    )


def heads_forward_kernel(norm_columns, joint_ref, gain_ref, cos_ref, sin_ref, out_ref):
    values = joint_ref[...]
    scale = lax.rsqrt(head_sum(values * values) * (1.0 / HEAD_SIZE) + EPSILON)
    normed = values * scale * gain_ref[0:1, :]
    turned = normed * cos_ref[...] + partner(normed) * sin_ref[...]
    place = pl.program_id(0) * LANES + lanes_of(values.shape)
    out_ref[...] = jnp.where(place < norm_columns, turned, values).astype(bf16)


def heads_forward(joint, gain, cos, sin, norm_columns):
    tokens, columns = joint.shape
    return pl.pallas_call(
        partial(heads_forward_kernel, norm_columns),
        grid=(columns // LANES,),
        in_specs=[
            pl.BlockSpec((tokens, LANES), lambda i: (0, i)),
            pl.BlockSpec((8, LANES), lambda i: (0, i)),
            pl.BlockSpec((tokens, LANES), lambda i: (0, 0)),
            pl.BlockSpec((tokens, LANES), lambda i: (0, 0)),
        ],
        out_specs=pl.BlockSpec((tokens, LANES), lambda i: (0, i)),
        out_shape=jax.ShapeDtypeStruct((tokens, columns), bf16),
        name="heads_forward",
        cost_estimate=LIGHT,
    )(joint, gain, cos, sin)


def heads_backward_kernel(
    norm_columns, grad_ref, joint_ref, gain_ref, cos_ref, sin_ref, out_ref, gain_out_ref
):
    grad = grad_ref[...].astype(f32)
    values = joint_ref[...]
    gain = gain_ref[0:1, :]
    turned = grad * cos_ref[...] - partner(grad) * sin_ref[...]
    scale = lax.rsqrt(head_sum(values * values) * (1.0 / HEAD_SIZE) + EPSILON)
    gained = turned * gain
    inner = head_sum(values * gained) * (1.0 / HEAD_SIZE)
    result = scale * gained - values * (scale * scale * scale) * inner
    place = pl.program_id(0) * LANES + lanes_of(values.shape)
    out_ref[...] = jnp.where(place < norm_columns, result, grad).astype(bf16)
    gain_out_ref[...] = jnp.broadcast_to(
        jnp.sum(turned * values * scale, axis=0, keepdims=True), gain_out_ref.shape
    )


def heads_backward(grad, joint, gain, cos, sin, norm_columns):
    tokens, columns = joint.shape
    return pl.pallas_call(
        partial(heads_backward_kernel, norm_columns),
        grid=(columns // LANES,),
        in_specs=[
            pl.BlockSpec((tokens, LANES), lambda i: (0, i)),
            pl.BlockSpec((tokens, LANES), lambda i: (0, i)),
            pl.BlockSpec((8, LANES), lambda i: (0, i)),
            pl.BlockSpec((tokens, LANES), lambda i: (0, 0)),
            pl.BlockSpec((tokens, LANES), lambda i: (0, 0)),
        ],
        out_specs=[
            pl.BlockSpec((tokens, LANES), lambda i: (0, i)),
            pl.BlockSpec((8, LANES), lambda i: (0, i)),
        ],
        out_shape=[
            jax.ShapeDtypeStruct((tokens, columns), bf16),
            jax.ShapeDtypeStruct((8, columns), f32),
        ],
        name="heads_backward",
        cost_estimate=LIGHT,
    )(grad, joint, gain, cos, sin)


def both_halves(pair, odd):
    wide = pair.astype(f32)
    first = lanes_of(wide.shape) < HEAD_SIZE
    keep = jnp.where(odd == 1, jnp.where(first, 0, 1), jnp.where(first, 1, 0)) == 1
    return jnp.where(keep, wide, pltpu.roll(wide, HEAD_SIZE, 1))


def attend_forward_kernel(place_ref, q_ref, k_ref, v_ref, out_ref, log_ref):
    group = pl.program_id(0) // 2
    place = place_ref[0]
    tokens = q_ref.shape[0]
    first = lanes_of((tokens, LANES)) < HEAD_SIZE
    pair = q_ref[...].astype(f32)
    queries = (jnp.where(first, pair, 0.0).astype(bf16), jnp.where(first, 0.0, pair).astype(bf16))

    def step(j, totals, diagonal):
        rows = pl.ds(pl.multiple_of(j * tokens, tokens), tokens)
        keys = both_halves(k_ref[rows, :], group % 2).astype(bf16)
        values = both_halves(v_ref[rows, :], (KEY_VALUE_HEADS + group) % 2)
        sides = (
            jnp.where(first, values, 1.0).astype(bf16),
            jnp.where(first, 1.0, values).astype(bf16),
        )
        result = []
        for head in range(2):
            weights = jnp.exp2(dot_nt(queries[head], keys) * SCORE_EXPONENT)
            if diagonal:
                row = lax.broadcasted_iota(jnp.int32, weights.shape, 0)
                weights = jnp.where(lanes_of(weights.shape) <= row, weights, 0.0)
            result.append(totals[head] + dot_nn(weights.astype(bf16), sides[head]))
        return tuple(result)

    zero = jnp.zeros((tokens, LANES), f32)
    totals = lax.fori_loop(0, place, lambda j, c: step(j, c, False), (zero, zero))
    totals = step(place, totals, True)
    numerator = jnp.where(first, totals[0], totals[1])
    swapped = jnp.where(first, totals[1], totals[0])
    out_ref[...] = (numerator / pltpu.roll(swapped, HEAD_SIZE, 1)).astype(bf16)
    log_ref[...] = jnp.log2(swapped)


def attend_forward(place, queries, keys_values):
    tokens = queries.shape[0]
    length = keys_values.shape[0]
    pairs = QUERY_COLUMNS // LANES
    return pl.pallas_call(
        attend_forward_kernel,
        grid_spec=pltpu.PrefetchScalarGridSpec(
            num_scalar_prefetch=1,
            grid=(pairs,),
            in_specs=[
                pl.BlockSpec((tokens, LANES), lambda i, s: (0, i)),
                pl.BlockSpec((length, LANES), lambda i, s: (0, (i // 2) // 2)),
                pl.BlockSpec((length, LANES), lambda i, s: (0, (KEY_VALUE_HEADS + i // 2) // 2)),
            ],
            out_specs=[
                pl.BlockSpec((tokens, LANES), lambda i, s: (0, i)),
                pl.BlockSpec((tokens, LANES), lambda i, s: (0, i)),
            ],
        ),
        out_shape=[
            jax.ShapeDtypeStruct((tokens, QUERY_COLUMNS), bf16),
            jax.ShapeDtypeStruct((tokens, QUERY_COLUMNS), f32),
        ],
        compiler_params=pltpu.CompilerParams(vmem_limit_bytes=VMEM_LIMIT),
        name="attend_forward",
        cost_estimate=LIGHT,
    )(place, queries, keys_values, keys_values)


def three_parts(values, lane):
    high = values.astype(bf16).astype(f32)
    rest = values - high
    middle = rest.astype(bf16).astype(f32)
    low = rest - middle
    return jnp.where(
        lane == 0, high, jnp.where(lane == 1, middle, jnp.where(lane == 2, low, 0.0))
    )


def attend_backward_kernel(
    first_group, count, place_ref, q_ref, k_ref, v_ref, out_ref, log_ref, grad_ref, dq_ref, dkv_ref, dk_sum, dv_sum
):
    pair_index = pl.program_id(0)
    local = pair_index // 2
    group = first_group + local
    place = place_ref[0]
    tokens = q_ref.shape[0]
    lane = lanes_of((tokens, LANES))
    first = lane < HEAD_SIZE
    inside = lane % HEAD_SIZE
    pair = q_ref[...].astype(f32)
    grad = grad_ref[...].astype(f32)
    delta = pltpu.roll(head_sum(grad * out_ref[...].astype(f32)), HEAD_SIZE, 1)
    logs = three_parts(log_ref[...] * (1.0 / SCORE_EXPONENT), inside)
    deltas = three_parts(delta, inside)
    minus = jnp.where(inside < 3, -1.0, 0.0)

    def sides(own, other):
        return (
            jnp.where(first, own, other).astype(bf16),
            jnp.where(first, other, own).astype(bf16),
        )

    queries = sides(pair, 0.0)
    grads = sides(grad, 0.0)
    queries_log = sides(pair, logs)
    grads_delta = sides(grad, deltas)

    @pl.when(pair_index % 2 == 0)
    def _():
        dk_sum[...] = jnp.zeros_like(dk_sum)
        dv_sum[...] = jnp.zeros_like(dv_sum)

    def step(j, dq, diagonal):
        rows = pl.ds(pl.multiple_of(j * tokens, tokens), tokens)
        key_wide = both_halves(k_ref[rows, :], group % 2)
        value_wide = both_halves(v_ref[rows, :], (KEY_VALUE_HEADS + group) % 2)
        keys = sides(key_wide, 0.0)
        keys_log = sides(key_wide, minus)
        values_delta = sides(value_wide, minus)
        dk = dk_sum[rows, :]
        dv = dv_sum[rows, :]
        for head in range(2):
            weights = jnp.exp2(dot_nt(keys_log[head], queries_log[head]) * SCORE_EXPONENT)
            if diagonal:
                row = lax.broadcasted_iota(jnp.int32, weights.shape, 0)
                weights = jnp.where(row <= lanes_of(weights.shape), weights, 0.0)
            grad_weights = dot_nt(values_delta[head], grads_delta[head])
            grad_scores = (weights * grad_weights).astype(bf16)
            dv = dv + dot_nn(weights.astype(bf16), grads[head])
            dk = dk + dot_nn(grad_scores, queries[head])
            dq = dq + dot_tn(grad_scores, keys[head])
        dk_sum[rows, :] = dk
        dv_sum[rows, :] = dv
        return dq

    dq = lax.fori_loop(
        0, place, lambda j, c: step(j, c, False), jnp.zeros((tokens, LANES), f32)
    )
    dq = step(place, dq, True)
    dq_ref[...] = (dq * HEAD_SIZE**-0.5).astype(bf16)

    @pl.when(pair_index % 2 == 1)
    def _():
        wide_lane = lanes_of(dk_sum.shape)
        for total, slot, factor in (
            (dk_sum, local, HEAD_SIZE**-0.5),
            (dv_sum, count + local, 1.0),
        ):
            both = (total[...] + pltpu.roll(total[...], HEAD_SIZE, 1)) * factor
            columns = pl.ds(pl.multiple_of(slot // 2 * LANES, LANES), LANES)
            mine = wide_lane // HEAD_SIZE == slot % 2
            dkv_ref[:, columns] = jnp.where(
                mine, both, dkv_ref[:, columns].astype(f32)
            ).astype(bf16)


def attend_backward(first, count, place, queries, keys_values, mixed, logs, grad_mixed):
    tokens = queries.shape[0]
    length = keys_values.shape[0]
    group = QUERY_HEADS // KEY_VALUE_HEADS * HEAD_SIZE
    own = pl.BlockSpec((tokens, LANES), lambda i, s: (0, 2 * first + i))
    keys = pl.BlockSpec((length, LANES), lambda i, s: (0, (first + i // 2) // 2))
    values = pl.BlockSpec(
        (length, LANES), lambda i, s: (0, (KEY_VALUE_HEADS + first + i // 2) // 2)
    )
    columns = 2 * count * HEAD_SIZE
    return pl.pallas_call(
        partial(attend_backward_kernel, first, count),
        grid_spec=pltpu.PrefetchScalarGridSpec(
            num_scalar_prefetch=1,
            grid=(2 * count,),
            in_specs=[own, keys, values, own, own, own],
            out_specs=[
                pl.BlockSpec((tokens, LANES), lambda i, s: (0, i)),
                pl.BlockSpec((length, columns), lambda i, s: (0, 0)),
            ],
            scratch_shapes=[pltpu.VMEM((length, LANES), f32), pltpu.VMEM((length, LANES), f32)],
        ),
        out_shape=[
            jax.ShapeDtypeStruct((tokens, count * group), bf16),
            jax.ShapeDtypeStruct((length, columns), bf16),
        ],
        compiler_params=pltpu.CompilerParams(vmem_limit_bytes=VMEM_LIMIT),
        name="attend_backward",
        cost_estimate=LIGHT,
    )(place, queries, keys_values, keys_values, mixed, logs, grad_mixed)


def hidden_kernel(n0_ref, n1_ref, wg_ref, wu_ref, hidden_ref, gate_ref, up_ref, n_all):
    tokens = n0_ref.shape[0]

    @pl.when(pl.program_id(0) == 0)
    def _():
        n_all[:tokens] = n0_ref[...]
        n_all[tokens:] = n1_ref[...]

    gate = dot_nn(n_all[...], wg_ref[...])
    up = dot_nn(n_all[...], wu_ref[...])
    hidden_ref[...] = (gate / (1.0 + jnp.exp(-gate)) * up).astype(bf16)
    gate_ref[...] = gate.astype(bf16)
    up_ref[...] = up.astype(bf16)


def hidden_pass(normed, wgate, wup):
    tokens, width = normed[0].shape
    columns = wgate.shape[1]
    tile = min(256, columns)
    whole = pl.BlockSpec((tokens, width), lambda i: (0, 0))
    down = pl.BlockSpec((width, tile), lambda i: (0, i))
    out = pl.BlockSpec((2 * tokens, tile), lambda i: (0, i))
    return pl.pallas_call(
        hidden_kernel,
        grid=(pl.cdiv(columns, tile),),
        in_specs=[whole] * 2 + [down] * 2,
        out_specs=[out] * 3,
        out_shape=[jax.ShapeDtypeStruct((2 * tokens, columns), bf16)] * 3,
        scratch_shapes=[pltpu.VMEM((2 * tokens, width), bf16)],
        compiler_params=pltpu.CompilerParams(vmem_limit_bytes=VMEM_LIMIT),
        name="hidden_pass",
        cost_estimate=LIGHT,
    )(*normed, wgate, wup)


def gates_kernel(g0_ref, g1_ref, wd_ref, gate_ref, up_ref, gate_out_ref, up_out_ref, g_all):
    tokens = g0_ref.shape[0]

    @pl.when(pl.program_id(0) == 0)
    def _():
        g_all[:tokens] = g0_ref[...]
        g_all[tokens:] = g1_ref[...]

    grad = dot_nt(g_all[...], wd_ref[...])
    gate = gate_ref[...].astype(f32)
    up = up_ref[...].astype(f32)
    sigmoid = 1.0 / (1.0 + jnp.exp(-gate))
    gate_out_ref[...] = (grad * up * (sigmoid * (1.0 + gate * (1.0 - sigmoid)))).astype(bf16)
    up_out_ref[...] = (grad * (gate * sigmoid)).astype(bf16)


def gates_pass(grad_top, wdown, gate, up):
    tokens, width = grad_top[0].shape
    columns = gate.shape[1]
    tile = min(256, columns)
    whole = pl.BlockSpec((tokens, width), lambda i: (0, 0))
    out = pl.BlockSpec((2 * tokens, tile), lambda i: (0, i))
    return pl.pallas_call(
        gates_kernel,
        grid=(pl.cdiv(columns, tile),),
        in_specs=[whole] * 2 + [pl.BlockSpec((tile, width), lambda i: (i, 0)), out, out],
        out_specs=[out] * 2,
        out_shape=[jax.ShapeDtypeStruct((2 * tokens, columns), bf16)] * 2,
        scratch_shapes=[pltpu.VMEM((2 * tokens, width), bf16)],
        compiler_params=pltpu.CompilerParams(vmem_limit_bytes=VMEM_LIMIT),
        name="gates_pass",
        cost_estimate=LIGHT,
    )(*grad_top, wdown, gate, up)


def back_kernel(count, transposed, *refs):
    own_ref, send_ref = refs[-2:]
    tokens = own_ref.shape[0]
    dot = dot_nt if transposed else dot_nn

    def total(start):
        rows = pl.ds(start, tokens)
        result = dot(refs[0][rows, :], refs[count][...])
        for i in range(1, count):
            result = result + dot(refs[i][rows, :], refs[count + i][...])
        return result

    own_ref[...] = total(0)
    send_ref[...] = total(tokens).astype(bf16)


def back_pass(lefts, weights, transposed):
    tokens, depth = lefts[0].shape
    width = weights[0].shape[0 if transposed else 1]
    count = len(lefts)
    tile = min(512, width)
    if transposed:
        weight_spec = pl.BlockSpec((tile, depth), lambda i: (i, 0))
    else:
        weight_spec = pl.BlockSpec((depth, tile), lambda i: (0, i))
    out = pl.BlockSpec((tokens // 2, tile), lambda i: (0, i))
    return pl.pallas_call(
        partial(back_kernel, count, transposed),
        grid=(width // tile,),
        in_specs=[pl.BlockSpec((tokens, depth), lambda i: (0, 0))] * count
        + [weight_spec] * count,
        out_specs=[out, out],
        out_shape=[
            jax.ShapeDtypeStruct((tokens // 2, width), f32),
            jax.ShapeDtypeStruct((tokens // 2, width), bf16),
        ],
        compiler_params=pltpu.CompilerParams(vmem_limit_bytes=VMEM_LIMIT),
        name="back_pass",
        cost_estimate=LIGHT,
    )(*lefts, *weights)


def weight_kernel(left_count, *refs):
    lefts, rights, out_ref = refs[:left_count], refs[left_count:-1], refs[-1]
    step = min(lefts[0].shape[0], rights[0].shape[0])

    def piece(refs, start):
        index, offset = divmod(start, refs[0].shape[0])
        return refs[index][pl.ds(offset, step), :]

    total = None
    for start in range(0, left_count * lefts[0].shape[0], step):
        term = dot_tn(piece(lefts, start), piece(rights, start))
        total = term if total is None else total + term
    out_ref[...] = total.astype(bf16)


def weight_pass(lefts, rights):
    rows, columns = lefts[0].shape[1], rights[0].shape[1]
    tile = 512 if rows % 512 == 0 else 384 if rows % 384 == 0 else rows
    return pl.pallas_call(
        partial(weight_kernel, len(lefts)),
        grid=(rows // tile,),
        in_specs=[pl.BlockSpec((left.shape[0], tile), lambda i: (0, i)) for left in lefts]
        + [pl.BlockSpec(right.shape, lambda i: (0, 0)) for right in rights],
        out_specs=pl.BlockSpec((tile, columns), lambda i: (i, 0)),
        out_shape=jax.ShapeDtypeStruct((rows, columns), bf16),
        compiler_params=pltpu.CompilerParams(vmem_limit_bytes=VMEM_LIMIT),
        name="weight_pass",
        cost_estimate=LIGHT,
    )(*lefts, *rights)


def placed_kernel(side_ref, own_ref, other_ref, out_ref):
    mine = pl.program_id(0) == side_ref[0]

    @pl.when(mine)
    def _():
        out_ref[0, 0] = own_ref[:, 0]

    @pl.when(jnp.logical_not(mine))
    def _():
        out_ref[0, 0] = other_ref[:, 0]


def placed(own, other, side):
    seq, group, rows, columns = own.shape

    def entry(mine, e, g, s):
        parked = jnp.where(e == 0, 0, group - 1)
        return (0, jnp.where((e == s[0]) == mine, g, parked), 0, 0)

    return pl.pallas_call(
        placed_kernel,
        grid_spec=pltpu.PrefetchScalarGridSpec(
            num_scalar_prefetch=1,
            grid=(2, group),
            in_specs=[
                pl.BlockSpec((seq, 1, rows, columns), partial(entry, True)),
                pl.BlockSpec((seq, 1, rows, columns), partial(entry, False)),
            ],
            out_specs=pl.BlockSpec(
                (1, 1, seq, rows, columns), lambda e, g, s: (e, g, 0, 0, 0)
            ),
        ),
        out_shape=jax.ShapeDtypeStruct((2, group, seq, rows, columns), own.dtype),
        name="placed",
        cost_estimate=LIGHT,
    )(side.astype(jnp.int32).reshape(1), own, other)


def joined_kernel(side_ref, own_ref, other_ref, out_ref):
    mine = pl.program_id(1) == side_ref[0]

    @pl.when(mine)
    def _():
        out_ref[:, 0] = own_ref[...]

    @pl.when(jnp.logical_not(mine))
    def _():
        out_ref[:, 0] = other_ref[...]


def joined(own, other, side, axis):
    shape = own.shape[:axis] + (2,) + own.shape[axis:]
    columns = own.shape[-1]
    lead = math.prod(own.shape[:axis])
    rows = math.prod(own.shape[axis:-1])
    leads, chunks = lead, 1
    while leads % 2 == 0 and leads * rows * columns > 800_000:
        leads //= 2
    while leads == 1 and rows % (32 * chunks) == 0 and rows // chunks * columns > 800_000:
        chunks *= 2
    block = rows // chunks

    def entry(mine, p, e, i, s):
        parked = jnp.where(e == 0, 0, chunks - 1)
        return (p, jnp.where((e == s[0]) == mine, i, parked), 0)

    return pl.pallas_call(
        joined_kernel,
        grid_spec=pltpu.PrefetchScalarGridSpec(
            num_scalar_prefetch=1,
            grid=(lead // leads, 2, chunks),
            in_specs=[
                pl.BlockSpec((leads, block, columns), partial(entry, True)),
                pl.BlockSpec((leads, block, columns), partial(entry, False)),
            ],
            out_specs=pl.BlockSpec((leads, 1, block, columns), lambda p, e, i, s: (p, e, i, 0)),
        ),
        out_shape=jax.ShapeDtypeStruct((lead, 2, rows, columns), own.dtype),
        compiler_params=pltpu.CompilerParams(vmem_limit_bytes=VMEM_LIMIT),
        name="joined",
        cost_estimate=LIGHT,
    )(
        side.astype(jnp.int32).reshape(1),
        own.reshape(lead, rows, columns),
        other.reshape(lead, rows, columns),
    ).reshape(shape)


def swap(values, bit):
    pairs = [(i, i ^ bit) for i in range(lax.axis_size("rows"))]
    return lax.ppermute(values, "rows", pairs)


def bit_of(bit):
    return (lax.axis_index("rows") // bit) % 2


def gather_bit(values, bit, axis):
    return joined(values, swap(values, bit), bit_of(bit), axis)


def part(values, index, axis):
    return lax.dynamic_index_in_dim(values, index, axis, keepdims=False)


def reduce_bit(values, bit, axis):
    return add_bit(values, pass_bit(values, bit, axis), bit, axis)


def outer_pairs(step, low, high):
    size = lax.axis_size("rows")
    return [
        (i, i + 4 * step)
        for i in range(size)
        if low <= i // 4 < high and 0 <= i // 4 + step < size // 4
    ]


def send_outer(values):
    count = lax.axis_size("rows") // 4
    if count == 2:
        return (swap(values, 4),)
    up, down = values, values
    ups, downs = [], []
    for t in range(1, count):
        up = lax.ppermute(up, "rows", outer_pairs(1, t - 1, count))
        down = lax.ppermute(down, "rows", outer_pairs(-1, 0, count - t + 1))
        ups.append(up)
        downs.append(down)
    return tuple(ups[::-1] + downs)


def join_outer(values, received, axis):
    count = lax.axis_size("rows") // 4
    if count == 2:
        return joined(values, received[0], bit_of(4), axis)
    place = lax.axis_index("rows") // 4
    line = jnp.stack([*received[: count - 1], values, *received[count - 1 :]], axis)
    return lax.dynamic_slice_in_dim(line, count - 1 - place, count, axis)


def gather_outer(values, axis):
    return join_outer(values, send_outer(values), axis)


def pass_outer(values, axis):
    count = lax.axis_size("rows") // 4
    place = lax.axis_index("rows") // 4

    def entry(index):
        return part(values, jnp.clip(index, 0, count - 1), axis)

    if count == 1:
        return ()
    if count == 2:
        return (swap(entry(1 - place), 4),)
    up, down = entry(place + count - 1), entry(place - count + 1)
    for t in range(1, count):
        up = lax.ppermute(up, "rows", outer_pairs(1, 0, t))
        down = lax.ppermute(down, "rows", outer_pairs(-1, count - t, count))
        if t < count - 1:
            up = (entry(place + count - 1 - t).astype(f32) + up.astype(f32)).astype(bf16)
            down = (entry(place - count + 1 + t).astype(f32) + down.astype(f32)).astype(bf16)
    return (up, down)


def add_outer(values, received, axis):
    total = part(values, lax.axis_index("rows") // 4, axis).astype(f32)
    for term in received:
        total = total + term.astype(f32)
    return total.astype(bf16)


def reduce_outer(values, axis):
    return add_outer(values, pass_outer(values, axis), axis)


def pass_bit(values, bit, axis):
    return swap(part(values, 1 - bit_of(bit), axis), bit)


def add_bit(values, received, bit, axis):
    own = part(values, bit_of(bit), axis)
    return (own.astype(f32) + received.astype(f32)).astype(bf16)


def gather_seq(values):
    return lax.all_gather(values, "seq", axis=0, tiled=False)


def reduce_seq(values):
    return lax.psum_scatter(values, "seq", scatter_dimension=0, tiled=False)


def exchange(values, axis, bit):
    size = lax.axis_size(axis)
    return lax.ppermute(values, axis, [(i, i ^ bit) for i in range(size)])


def across_group(own, send):
    return (own + swap(send, 1).astype(f32)).astype(bf16)


def stage(*values):
    return lax.optimization_barrier(values)


def mm(left, right):
    return jnp.einsum("ab,bc->ac", left, right, preferred_element_type=f32)


def mm_t(left, right):
    return jnp.einsum("ab,cb->ac", left, right, preferred_element_type=f32)


def t_mm(left, right):
    return jnp.einsum("ab,ac->bc", left, right, preferred_element_type=f32)


def norm_scale(values):
    return lax.rsqrt(jnp.mean(values * values, axis=-1, keepdims=True) + EPSILON)


def norm_backward(values, scale, gain, grad):
    gained = grad * gain
    inner = jnp.mean(values * gained, axis=-1, keepdims=True)
    result = scale * gained - values * (scale * scale * scale) * inner
    return result, jnp.sum(grad * values * scale, axis=0)


def shards(
    tokens_in,
    corpus,
    corpus_weight,
    w_qkv,
    w_out,
    w_gate,
    w_up,
    w_down,
    attn_gain,
    ffn_gain,
    q_gain,
    k_gain,
    upstream,
):
    shard_length, width = tokens_in.shape[1:]
    row_devices = lax.axis_size("rows")
    seq_devices = lax.axis_size("seq")
    outer = row_devices // 4
    d_rows = w_qkv.shape[0]
    f_rows = w_down.shape[0]
    place = lax.axis_index("seq").astype(jnp.int32)
    inputs = tokens_in[0].astype(f32)

    extra = jnp.stack(
        [
            attn_gain,
            ffn_gain,
            jnp.broadcast_to(corpus.astype(bf16), attn_gain.shape),
        ],
        axis=1,
    )
    extra = jnp.pad(extra, ((0, 0), (0, LANES - extra.shape[1])))
    kv_shard = jnp.concatenate([w_qkv[:, QUERY_COLUMNS:], extra], axis=1)
    query_shard = jnp.concatenate([w_qkv[:, :QUERY_COLUMNS], w_out.T], axis=1)
    query_shard, w_gate, w_up = stage(query_shard, w_gate, w_up)
    query_lines = gather_seq(query_shard)

    def to_group(weight):
        blocks = weight.reshape(d_rows, outer, 4, seq_devices, f_rows)
        blocks = jnp.transpose(blocks, (2, 0, 3, 1, 4))
        return blocks.reshape(2, 2, d_rows, outer * seq_devices * f_rows)

    def spread_hidden(lines, received):
        if outer == 2:
            lines = lines.reshape(seq_devices, 4, d_rows, hidden_columns)
            other = received[0].reshape(lines.shape)
            return placed(lines, other, bit_of(4)).reshape(width, hidden_columns)
        full = join_outer(lines, received, 0)
        return jnp.moveaxis(full, 1, 3).reshape(width, hidden_columns)

    gate_up = jnp.stack([to_group(w_gate), to_group(w_up)], axis=2)
    hidden_columns = gate_up.shape[-1]
    core, near = bit_of(1), bit_of(2)
    gate_up = joined(
        part(gate_up, core, 1), swap(part(gate_up, 1 - core, 1), 1), core, 1
    )
    gate_up, kv_shard = stage(gate_up, kv_shard)
    other, kv_lines, query_lines = stage(
        swap(part(gate_up, 1 - near, 0), 2), gather_seq(kv_shard), query_lines
    )
    gate_up = joined(part(gate_up, near, 0), other, near, 0)
    gate_lines = gather_seq(gate_up[:, :, 0])
    left, right = kv_lines[..., : 3 * LANES], kv_lines[..., 3 * LANES :]
    left_other, right_other = stage(send_outer(left), swap(right, 2))
    left = join_outer(left, left_other, 0)
    right = joined(right, right_other, near, 0)
    left_other, right_other = stage(swap(left, 2), send_outer(right))
    left = joined(left, left_other, near, 1)
    right = join_outer(right, right_other, 0)
    q_left, q_right = query_lines[..., :QUERY_COLUMNS], query_lines[..., QUERY_COLUMNS:]
    q_left, q_right, left, right = stage(q_left, q_right, left, right)
    q_left_other, q_right_other = send_outer(q_left), swap(q_right, 2)
    left, right = gather_bit(left, 1, 2), gather_bit(right, 1, 2)
    left, right = left.reshape(width, -1), right.reshape(width, -1)
    wkv = jnp.concatenate([left, right[:, : 2 * LANES]], axis=1)
    rows = dot_nt(jnp.eye(8, LANES, dtype=bf16), right[:, 2 * LANES :])
    attn_gain_full, ffn_gain_full, corpus_full = rows[0:1], rows[1:2], rows[2]

    position = (place * shard_length + jnp.arange(shard_length, dtype=jnp.int32)).astype(f32)
    half = HEAD_SIZE // 2
    exponent = jnp.arange(half, dtype=f32) * (-2.0 / HEAD_SIZE)
    angles = position[:, None] * jnp.power(ROPE_BASE, exponent)[None, :]
    cosine, sine = jnp.cos(angles), jnp.sin(angles)
    cos_table = jnp.concatenate([cosine] * 4, axis=1)
    sin_table = jnp.concatenate([-sine, sine] * 2, axis=1)
    wide_q = jnp.tile(q_gain.astype(f32), QUERY_HEADS)
    wide_k = jnp.concatenate(
        [jnp.tile(k_gain.astype(f32), KEY_VALUE_HEADS), jnp.ones((KEY_COLUMNS,), f32)]
    )
    wide_q = jnp.broadcast_to(wide_q[None, :], (8, QUERY_COLUMNS))
    wide_k = jnp.broadcast_to(wide_k[None, :], (8, 2 * KEY_COLUMNS))

    in_scale = norm_scale(inputs)
    normed = (inputs * in_scale * attn_gain_full).astype(bf16)
    joint_kv = mm(normed, wkv)
    own_kv = heads_forward(joint_kv, wide_k, cos_table, sin_table, KEY_COLUMNS)
    own_kv, q_left_other, q_right_other, down_other = stage(
        own_kv, q_left_other, q_right_other, send_outer(w_down)
    )
    down_pair = join_outer(w_down, down_other, 0)
    keys_values = gather_seq(own_kv).reshape(-1, 2 * KEY_COLUMNS)
    q_left = join_outer(q_left, q_left_other, 0)
    q_right = joined(q_right, q_right_other, near, 0)
    left_other, right_other, gate_lines = stage(
        swap(q_left, 2), send_outer(q_right), gate_lines
    )
    q_left = joined(q_left, left_other, near, 1)
    q_right = join_outer(q_right, right_other, 0)
    gate_other = send_outer(gate_lines)
    wq = gather_bit(q_left, 1, 2).reshape(width, -1)

    corpora = jnp.arange(CORPORA, dtype=jnp.int32)
    per_device = corpus_full.reshape(-1, d_rows)[:, 0].astype(jnp.int32)
    counts = (
        jnp.sum((per_device[:, None] == corpora[None, :]).astype(f32), axis=0) * shard_length
    )
    own_corpus = (corpus[0] == corpora).astype(f32)
    weight_row = jnp.sum(own_corpus * corpus_weight.astype(f32))
    count_row = jnp.sum(own_corpus * counts)
    factor = weight_row / DENOM * (jnp.sum(counts) / (CORPORA * count_row))
    grad_full = upstream[0].astype(f32) * factor
    grad_top, wq = stage(grad_full.astype(bf16), wq)

    joint_q = mm(normed, wq)
    queries = heads_forward(joint_q, wide_q, cos_table, sin_table, QUERY_COLUMNS)
    place_array = place.reshape(1)
    keys_values, queries, up_in, down_in = stage(
        keys_values, queries, gate_up[:, :, 1], down_pair
    )
    up_lines = gather_seq(up_in)
    down_lines = gather_seq(down_in)
    mixed, logs = attend_forward(place_array, queries, keys_values)
    mixed, grad_top1, grad_top2, gate_other, wout_other = stage(
        mixed, swap(grad_top, 1), swap(grad_top, 2), gate_other, swap(q_right, 1)
    )
    wout_t = joined(q_right, wout_other, core, 2).reshape(width, -1)
    middle = inputs + mm_t(mixed, wout_t)

    ffn_scale = norm_scale(middle)
    normed_ffn = (middle * ffn_scale * ffn_gain_full).astype(bf16)
    normed1, up_other, wgate = stage(
        swap(normed_ffn, 1), send_outer(up_lines), spread_hidden(gate_lines, gate_other)
    )
    wup = spread_hidden(up_lines, up_other)
    hidden_near, gate_near, up_near = hidden_pass((normed_ffn, normed1), wgate, wup)
    normed2, hidden_near, grad_top3 = stage(
        swap(normed_ffn, 2), hidden_near, swap(grad_top2, 1)
    )
    normed3 = swap(normed2, 1)
    hidden_far, gate_far, up_far = hidden_pass((normed2, normed3), wgate, wup)
    normed4 = (normed_ffn, normed1, normed2, normed3)
    grad_top4 = (grad_top, grad_top1, grad_top2, grad_top3)
    wdown = down_lines.reshape(hidden_columns, width)
    gate_far, up_far = gates_pass((grad_top2, grad_top3), wdown, gate_far, up_far)
    own, send = back_pass((gate_far, up_far), (wgate, wup), True)
    across, wdown, hidden_far = stage(across_group(own, send), wdown, hidden_far)
    grad_wdown = weight_pass((hidden_near, hidden_far), grad_top4)
    grad_wdown, wdown = stage(grad_wdown, wdown)
    gate_near, up_near = gates_pass((grad_top, grad_top1), wdown, gate_near, up_near)
    own, send = back_pass((gate_near, up_near), (wgate, wup), True)

    hidden_shape = (outer, 2, 2, seq_devices, d_rows, hidden_columns)
    down_shape = (seq_devices, outer, f_rows, width)
    grad_wdown = grad_wdown.reshape(down_shape)
    grad_wgate = weight_pass(normed4, (gate_near, gate_far)).reshape(hidden_shape)
    grad_wup = weight_pass(normed4, (up_near, up_far)).reshape(hidden_shape)
    across, own, send, grad_wgate, grad_wup, down_other = stage(
        swap(across, 2),
        own,
        swap(send, 1),
        grad_wgate,
        grad_wup,
        pass_outer(grad_wdown, 1),
    )
    grad_wdown = add_outer(grad_wdown, down_other, 1)
    own = own + send.astype(f32)
    grad_normed_ffn = own + across.astype(f32)
    grad_wdown = reduce_seq(grad_wdown)

    grad_middle_part, grad_ffn_gain = norm_backward(
        middle, ffn_scale, ffn_gain_full, grad_normed_ffn
    )
    grad_middle = grad_full + grad_middle_part
    grad_branch = grad_middle.astype(bf16)
    grad_mixed = mm(grad_branch, wout_t).astype(bf16)
    attend = (place_array, queries, keys_values, mixed, logs)
    grad_q1, grad_kv1 = attend_backward(0, 2, *attend, grad_mixed)
    grad_q1, grad_kv1, gate_other, grad_mixed, grad_wdown, hidden_far = stage(
        grad_q1, grad_kv1, pass_outer(grad_wgate, 0), grad_mixed, grad_wdown, hidden_far
    )
    grad_kv1 = reduce_seq(grad_kv1.reshape(seq_devices, shard_length, -1))
    grad_gate = jnp.moveaxis(add_outer(grad_wgate, gate_other, 0), 2, 0)
    shape = (outer, 2, 2, seq_devices, d_rows)
    own_far, send_far = back_pass((hidden_far,), (wdown,), False)
    grad_wout, far_other, grad_mixed = stage(
        t_mm(grad_branch, mixed).astype(bf16).reshape(*shape, QUERY_COLUMNS),
        swap(send_far, 1),
        grad_mixed,
    )
    across = (own_far + far_other.astype(f32)).astype(bf16)
    across, grad_mixed = stage(across, grad_mixed)
    grad_q2, grad_kv2 = attend_backward(2, 3, *attend, grad_mixed)
    grad_q2, grad_kv2, hidden_near, grad_kv1, wout_other, up_other, across = stage(
        grad_q2,
        grad_kv2,
        hidden_near,
        grad_kv1,
        pass_bit(grad_wout, 1, 2),
        pass_outer(grad_wup, 0),
        swap(across, 2),
    )
    grad_kv2 = reduce_seq(grad_kv2.reshape(seq_devices, shard_length, -1))

    grad_q = jnp.concatenate([grad_q1, grad_q2], axis=1)
    joint_grad_q, gain_q = heads_backward(
        grad_q, joint_q, wide_q, cos_table, sin_table, QUERY_COLUMNS
    )
    grad_wq = t_mm(normed, joint_grad_q).astype(bf16).reshape(*shape, QUERY_COLUMNS)
    grad_wout = add_bit(grad_wout, wout_other, 1, 2)
    own_near, send_near = back_pass((hidden_near,), (wdown,), False)
    grad_up = jnp.moveaxis(add_outer(grad_wup, up_other, 0), 2, 0)
    grad_gate_up = jnp.stack([grad_gate, grad_up], axis=3)
    grad_kv2, wq_other, own_near, near_other, grad_gate_up = stage(
        grad_kv2, pass_bit(grad_wq, 1, 2), own_near, swap(send_near, 1), grad_gate_up
    )
    output = (middle + own_near + near_other.astype(f32) + across.astype(f32)).astype(bf16)
    gate_up = reduce_seq(grad_gate_up)
    grad_wq = add_bit(grad_wq, wq_other, 1, 2)
    wq_other, wout_other = pass_bit(grad_wq, 2, 1), pass_outer(grad_wout, 0)

    grad_kv1, grad_kv2 = (
        part_.reshape(shard_length, 2, -1) for part_ in (grad_kv1, grad_kv2)
    )
    grad_kv = jnp.concatenate([grad_kv1, grad_kv2], axis=2).reshape(shard_length, -1)
    joint_grad_kv, gain_k = heads_backward(
        grad_kv, joint_kv, wide_k, cos_table, sin_table, KEY_COLUMNS
    )
    grad_wkv = t_mm(normed, joint_grad_kv).astype(bf16)
    grad_normed = mm_t(joint_grad_q, wq) + mm_t(joint_grad_kv, wkv)
    grad_input_part, grad_attn_gain = norm_backward(
        inputs, in_scale, attn_gain_full, grad_normed
    )
    input_grad = (grad_middle + grad_input_part).astype(bf16)

    gain_rows = jnp.stack([grad_attn_gain, grad_ffn_gain]).astype(bf16)
    gain_columns = t_mm(gain_rows, jnp.eye(2, LANES, dtype=bf16)).astype(bf16)
    left = grad_wkv[:, : 3 * LANES].reshape(*shape, -1)
    right = jnp.concatenate([grad_wkv[:, 3 * LANES :], gain_columns], axis=1)
    right = right.reshape(*shape, -1)
    head_gains = jnp.concatenate(
        [
            jnp.sum(gain_q[0].reshape(-1, HEAD_SIZE), axis=0),
            jnp.sum(gain_k[0, :KEY_COLUMNS].reshape(-1, HEAD_SIZE), axis=0),
        ]
    )[None]
    left, right, left_other, right_other, wq_other, wout_other, gains_other = stage(
        left,
        right,
        pass_bit(left, 1, 2),
        pass_bit(right, 1, 2),
        wq_other,
        wout_other,
        exchange(head_gains, "rows", 1),
    )
    head_gains = head_gains + gains_other
    left = add_bit(left, left_other, 1, 2)
    right = add_bit(right, right_other, 1, 2)
    grad_wq = add_bit(grad_wq, wq_other, 2, 1)
    grad_wout = add_outer(grad_wout, wout_other, 0)
    left_other, right_other, wq_other, wout_other, gains_other = stage(
        pass_bit(left, 2, 1),
        pass_outer(right, 0),
        pass_outer(grad_wq, 0),
        pass_bit(grad_wout, 2, 0),
        exchange(head_gains, "seq", 1),
    )
    head_gains = head_gains + gains_other
    left = add_bit(left, left_other, 2, 1)
    right = add_outer(right, right_other, 0)
    left_other, right_other, gains_other = stage(
        pass_outer(left, 0), pass_bit(right, 2, 0), exchange(head_gains, "rows", 2)
    )
    head_gains = head_gains + gains_other
    sums = reduce_seq(
        jnp.concatenate(
            [
                add_outer(grad_wq, wq_other, 0),
                add_outer(left, left_other, 0),
                add_bit(right, right_other, 2, 0),
                add_bit(grad_wout, wout_other, 2, 0),
            ],
            axis=-1,
        )
    )
    rest = [("rows", bit) for bit in (4, 8, 16) if bit < row_devices]
    rest += [("seq", bit) for bit in (2, 4, 8) if bit < seq_devices]
    other, gains_other = stage(
        swap(part(gate_up, 1 - near, 0), 2), exchange(head_gains, *rest[0])
    )
    head_gains = head_gains + gains_other
    grads = joined(part(gate_up, near, 0), other, near, 0)
    for axis, bit in rest[1:]:
        head_gains = head_gains + exchange(head_gains, axis, bit)
    head_gains = head_gains[0]
    grads = joined(part(grads, core, 1), swap(part(grads, 1 - core, 1), 1), core, 1)

    def from_group(blocks):
        blocks = blocks.reshape(4, d_rows, seq_devices, outer, f_rows)
        return jnp.transpose(blocks, (1, 3, 0, 2, 4)).reshape(d_rows, -1)

    grad_wgate, grad_wup = stage(from_group(grads[:, :, 0]), from_group(grads[:, :, 1]))
    sums, grad_wgate, grad_wup, grad_wdown, output, input_grad = stage(
        sums, grad_wgate.astype(f32), grad_wup.astype(f32), grad_wdown.astype(f32), output, input_grad
    )
    columns = QUERY_COLUMNS + 2 * KEY_COLUMNS
    long_gains = sums[:, columns : columns + 2].astype(f32)
    return (
        output[None],
        input_grad[None],
        sums[:, :columns].astype(f32),
        sums[:, columns + LANES :].T.astype(f32),
        grad_wgate,
        grad_wup,
        grad_wdown,
        long_gains[:, 0],
        long_gains[:, 1],
        head_gains[:HEAD_SIZE],
        head_gains[HEAD_SIZE:],
    )


def solution(mesh):
    return jax.shard_map(
        shards,
        mesh=mesh,
        in_specs=(
            P("rows", "seq", None),
            P("rows"),
            P(),
            P(("rows", "seq"), None),
            P(None, ("rows", "seq")),
            P(("rows", "seq"), None),
            P(("rows", "seq"), None),
            P(("rows", "seq"), None),
            P(("rows", "seq")),
            P(("rows", "seq")),
            P(),
            P(),
            P("rows", "seq", None),
        ),
        out_specs=(
            P("rows", "seq", None),
            P("rows", "seq", None),
            P(("rows", "seq"), None),
            P(None, ("rows", "seq")),
            P(("rows", "seq"), None),
            P(("rows", "seq"), None),
            P(("rows", "seq"), None),
            P(("rows", "seq")),
            P(("rows", "seq")),
            P(),
            P(),
        ),
        check_vma=False,
    )
```

```python
import math
from functools import partial

import jax
import jax.numpy as jnp
from jax import lax
from jax.experimental import pallas as pl
from jax.experimental.pallas import tpu as pltpu
from jax.sharding import PartitionSpec as P

QUERY_HEADS = 20
KEY_VALUE_HEADS = 5
HEAD_SIZE = 64
CORPORA = 8
DENOM = 64
EPSILON = 1e-06
ROPE_BASE = 10000.0
QUERY_COLUMNS = QUERY_HEADS * HEAD_SIZE
KEY_COLUMNS = KEY_VALUE_HEADS * HEAD_SIZE
LANES = 128
SCORE_EXPONENT = 1.4426950408889634 * HEAD_SIZE**-0.5
VMEM_LIMIT = 48 * 1024 * 1024

f32, bf16 = jnp.float32, jnp.bfloat16
LIGHT = pl.CostEstimate(flops=1000, bytes_accessed=1000, transcendentals=0)


def dot_nn(a, b):
    return lax.dot_general(a, b, (((1,), (0,)), ((), ())), preferred_element_type=f32)


def dot_nt(a, b):
    return lax.dot_general(a, b, (((1,), (1,)), ((), ())), preferred_element_type=f32)


def dot_tn(a, b):
    return lax.dot_general(a, b, (((0,), (0,)), ((), ())), preferred_element_type=f32)


def lanes_of(shape):
    return lax.broadcasted_iota(jnp.int32, shape, len(shape) - 1)


def head_sum(values):
    row = lax.broadcasted_iota(jnp.int32, (LANES, LANES), 0) // HEAD_SIZE
    column = lax.broadcasted_iota(jnp.int32, (LANES, LANES), 1) // HEAD_SIZE
    ones = jnp.where(row == column, 1.0, 0.0).astype(bf16)
    high = values.astype(bf16)
    low = (values - high.astype(f32)).astype(bf16)
    return dot_nn(high, ones) + dot_nn(low, ones)


def partner(values):
    first = lanes_of(values.shape) % HEAD_SIZE < HEAD_SIZE // 2
    return jnp.where(
        first,
        pltpu.roll(values, LANES - HEAD_SIZE // 2, 1),
        pltpu.roll(values, HEAD_SIZE // 2, 1),
    )


def heads_forward_kernel(norm_columns, joint_ref, gain_ref, cos_ref, sin_ref, out_ref):
    values = joint_ref[...]
    scale = lax.rsqrt(head_sum(values * values) * (1.0 / HEAD_SIZE) + EPSILON)
    normed = values * scale * gain_ref[0:1, :]
    turned = normed * cos_ref[...] + partner(normed) * sin_ref[...]
    place = pl.program_id(0) * LANES + lanes_of(values.shape)
    out_ref[...] = jnp.where(place < norm_columns, turned, values).astype(bf16)


def heads_forward(joint, gain, cos, sin, norm_columns):
    tokens, columns = joint.shape
    return pl.pallas_call(
        partial(heads_forward_kernel, norm_columns),
        grid=(columns // LANES,),
        in_specs=[
            pl.BlockSpec((tokens, LANES), lambda i: (0, i)),
            pl.BlockSpec((8, LANES), lambda i: (0, i)),
            pl.BlockSpec((tokens, LANES), lambda i: (0, 0)),
            pl.BlockSpec((tokens, LANES), lambda i: (0, 0)),
        ],
        out_specs=pl.BlockSpec((tokens, LANES), lambda i: (0, i)),
        out_shape=jax.ShapeDtypeStruct((tokens, columns), bf16),
        name="heads_forward",
        cost_estimate=LIGHT,
    )(joint, gain, cos, sin)


def heads_backward_kernel(
    norm_columns, grad_ref, joint_ref, gain_ref, cos_ref, sin_ref, out_ref, gain_out_ref
):
    grad = grad_ref[...].astype(f32)
    values = joint_ref[...]
    gain = gain_ref[0:1, :]
    turned = grad * cos_ref[...] - partner(grad) * sin_ref[...]
    scale = lax.rsqrt(head_sum(values * values) * (1.0 / HEAD_SIZE) + EPSILON)
    gained = turned * gain
    inner = head_sum(values * gained) * (1.0 / HEAD_SIZE)
    result = scale * gained - values * (scale * scale * scale) * inner
    place = pl.program_id(0) * LANES + lanes_of(values.shape)
    out_ref[...] = jnp.where(place < norm_columns, result, grad).astype(bf16)
    gain_out_ref[...] = jnp.broadcast_to(
        jnp.sum(turned * values * scale, axis=0, keepdims=True), gain_out_ref.shape
    )


def heads_backward(grad, joint, gain, cos, sin, norm_columns):
    tokens, columns = joint.shape
    return pl.pallas_call(
        partial(heads_backward_kernel, norm_columns),
        grid=(columns // LANES,),
        in_specs=[
            pl.BlockSpec((tokens, LANES), lambda i: (0, i)),
            pl.BlockSpec((tokens, LANES), lambda i: (0, i)),
            pl.BlockSpec((8, LANES), lambda i: (0, i)),
            pl.BlockSpec((tokens, LANES), lambda i: (0, 0)),
            pl.BlockSpec((tokens, LANES), lambda i: (0, 0)),
        ],
        out_specs=[
            pl.BlockSpec((tokens, LANES), lambda i: (0, i)),
            pl.BlockSpec((8, LANES), lambda i: (0, i)),
        ],
        out_shape=[
            jax.ShapeDtypeStruct((tokens, columns), bf16),
            jax.ShapeDtypeStruct((8, columns), f32),
        ],
        name="heads_backward",
        cost_estimate=LIGHT,
    )(grad, joint, gain, cos, sin)


def both_halves(pair, odd):
    wide = pair.astype(f32)
    first = lanes_of(wide.shape) < HEAD_SIZE
    keep = jnp.where(odd == 1, jnp.where(first, 0, 1), jnp.where(first, 1, 0)) == 1
    return jnp.where(keep, wide, pltpu.roll(wide, HEAD_SIZE, 1))


def attend_forward_kernel(place_ref, q_ref, k_ref, v_ref, out_ref, log_ref):
    group = pl.program_id(0) // 2
    place = place_ref[0]
    tokens = q_ref.shape[0]
    first = lanes_of((tokens, LANES)) < HEAD_SIZE
    pair = q_ref[...].astype(f32)
    queries = (jnp.where(first, pair, 0.0).astype(bf16), jnp.where(first, 0.0, pair).astype(bf16))

    def step(j, totals, diagonal):
        rows = pl.ds(pl.multiple_of(j * tokens, tokens), tokens)
        keys = both_halves(k_ref[rows, :], group % 2).astype(bf16)
        values = both_halves(v_ref[rows, :], (KEY_VALUE_HEADS + group) % 2)
        sides = (
            jnp.where(first, values, 1.0).astype(bf16),
            jnp.where(first, 1.0, values).astype(bf16),
        )
        result = []
        for head in range(2):
            weights = jnp.exp2(dot_nt(queries[head], keys) * SCORE_EXPONENT)
            if diagonal:
                row = lax.broadcasted_iota(jnp.int32, weights.shape, 0)
                weights = jnp.where(lanes_of(weights.shape) <= row, weights, 0.0)
            result.append(totals[head] + dot_nn(weights.astype(bf16), sides[head]))
        return tuple(result)

    zero = jnp.zeros((tokens, LANES), f32)
    totals = lax.fori_loop(0, place, lambda j, c: step(j, c, False), (zero, zero))
    totals = step(place, totals, True)
    numerator = jnp.where(first, totals[0], totals[1])
    swapped = jnp.where(first, totals[1], totals[0])
    out_ref[...] = (numerator / pltpu.roll(swapped, HEAD_SIZE, 1)).astype(bf16)
    log_ref[...] = jnp.log2(swapped)


def attend_forward(place, queries, keys_values):
    tokens = queries.shape[0]
    length = keys_values.shape[0]
    pairs = QUERY_COLUMNS // LANES
    return pl.pallas_call(
        attend_forward_kernel,
        grid_spec=pltpu.PrefetchScalarGridSpec(
            num_scalar_prefetch=1,
            grid=(pairs,),
            in_specs=[
                pl.BlockSpec((tokens, LANES), lambda i, s: (0, i)),
                pl.BlockSpec((length, LANES), lambda i, s: (0, (i // 2) // 2)),
                pl.BlockSpec((length, LANES), lambda i, s: (0, (KEY_VALUE_HEADS + i // 2) // 2)),
            ],
            out_specs=[
                pl.BlockSpec((tokens, LANES), lambda i, s: (0, i)),
                pl.BlockSpec((tokens, LANES), lambda i, s: (0, i)),
            ],
        ),
        out_shape=[
            jax.ShapeDtypeStruct((tokens, QUERY_COLUMNS), bf16),
            jax.ShapeDtypeStruct((tokens, QUERY_COLUMNS), f32),
        ],
        compiler_params=pltpu.CompilerParams(vmem_limit_bytes=VMEM_LIMIT),
        name="attend_forward",
        cost_estimate=LIGHT,
    )(place, queries, keys_values, keys_values)


def three_parts(values, lane):
    high = values.astype(bf16).astype(f32)
    rest = values - high
    middle = rest.astype(bf16).astype(f32)
    low = rest - middle
    return jnp.where(
        lane == 0, high, jnp.where(lane == 1, middle, jnp.where(lane == 2, low, 0.0))
    )


def attend_backward_kernel(
    first_group, count, place_ref, q_ref, k_ref, v_ref, out_ref, log_ref, grad_ref, dq_ref, dkv_ref, dk_sum, dv_sum
):
    pair_index = pl.program_id(0)
    local = pair_index // 2
    group = first_group + local
    place = place_ref[0]
    tokens = q_ref.shape[0]
    lane = lanes_of((tokens, LANES))
    first = lane < HEAD_SIZE
    inside = lane % HEAD_SIZE
    pair = q_ref[...].astype(f32)
    grad = grad_ref[...].astype(f32)
    delta = pltpu.roll(head_sum(grad * out_ref[...].astype(f32)), HEAD_SIZE, 1)
    logs = three_parts(log_ref[...] * (1.0 / SCORE_EXPONENT), inside)
    deltas = three_parts(delta, inside)
    minus = jnp.where(inside < 3, -1.0, 0.0)

    def sides(own, other):
        return (
            jnp.where(first, own, other).astype(bf16),
            jnp.where(first, other, own).astype(bf16),
        )

    queries = sides(pair, 0.0)
    grads = sides(grad, 0.0)
    queries_log = sides(pair, logs)
    grads_delta = sides(grad, deltas)

    @pl.when(pair_index % 2 == 0)
    def _():
        dk_sum[...] = jnp.zeros_like(dk_sum)
        dv_sum[...] = jnp.zeros_like(dv_sum)

    def step(j, dq, diagonal):
        rows = pl.ds(pl.multiple_of(j * tokens, tokens), tokens)
        key_wide = both_halves(k_ref[rows, :], group % 2)
        value_wide = both_halves(v_ref[rows, :], (KEY_VALUE_HEADS + group) % 2)
        keys = sides(key_wide, 0.0)
        keys_log = sides(key_wide, minus)
        values_delta = sides(value_wide, minus)
        dk = dk_sum[rows, :]
        dv = dv_sum[rows, :]
        for head in range(2):
            weights = jnp.exp2(dot_nt(keys_log[head], queries_log[head]) * SCORE_EXPONENT)
            if diagonal:
                row = lax.broadcasted_iota(jnp.int32, weights.shape, 0)
                weights = jnp.where(row <= lanes_of(weights.shape), weights, 0.0)
            grad_weights = dot_nt(values_delta[head], grads_delta[head])
            grad_scores = (weights * grad_weights).astype(bf16)
            dv = dv + dot_nn(weights.astype(bf16), grads[head])
            dk = dk + dot_nn(grad_scores, queries[head])
            dq = dq + dot_tn(grad_scores, keys[head])
        dk_sum[rows, :] = dk
        dv_sum[rows, :] = dv
        return dq

    dq = lax.fori_loop(
        0, place, lambda j, c: step(j, c, False), jnp.zeros((tokens, LANES), f32)
    )
    dq = step(place, dq, True)
    dq_ref[...] = (dq * HEAD_SIZE**-0.5).astype(bf16)

    @pl.when(pair_index % 2 == 1)
    def _():
        wide_lane = lanes_of(dk_sum.shape)
        for total, slot, factor in (
            (dk_sum, local, HEAD_SIZE**-0.5),
            (dv_sum, count + local, 1.0),
        ):
            both = (total[...] + pltpu.roll(total[...], HEAD_SIZE, 1)) * factor
            columns = pl.ds(pl.multiple_of(slot // 2 * LANES, LANES), LANES)
            mine = wide_lane // HEAD_SIZE == slot % 2
            dkv_ref[:, columns] = jnp.where(
                mine, both, dkv_ref[:, columns].astype(f32)
            ).astype(bf16)


def attend_backward(first, count, place, queries, keys_values, mixed, logs, grad_mixed):
    tokens = queries.shape[0]
    length = keys_values.shape[0]
    group = QUERY_HEADS // KEY_VALUE_HEADS * HEAD_SIZE
    own = pl.BlockSpec((tokens, LANES), lambda i, s: (0, 2 * first + i))
    keys = pl.BlockSpec((length, LANES), lambda i, s: (0, (first + i // 2) // 2))
    values = pl.BlockSpec(
        (length, LANES), lambda i, s: (0, (KEY_VALUE_HEADS + first + i // 2) // 2)
    )
    columns = 2 * count * HEAD_SIZE
    return pl.pallas_call(
        partial(attend_backward_kernel, first, count),
        grid_spec=pltpu.PrefetchScalarGridSpec(
            num_scalar_prefetch=1,
            grid=(2 * count,),
            in_specs=[own, keys, values, own, own, own],
            out_specs=[
                pl.BlockSpec((tokens, LANES), lambda i, s: (0, i)),
                pl.BlockSpec((length, columns), lambda i, s: (0, 0)),
            ],
            scratch_shapes=[pltpu.VMEM((length, LANES), f32), pltpu.VMEM((length, LANES), f32)],
        ),
        out_shape=[
            jax.ShapeDtypeStruct((tokens, count * group), bf16),
            jax.ShapeDtypeStruct((length, columns), bf16),
        ],
        compiler_params=pltpu.CompilerParams(vmem_limit_bytes=VMEM_LIMIT),
        name="attend_backward",
        cost_estimate=LIGHT,
    )(place, queries, keys_values, keys_values, mixed, logs, grad_mixed)


def hidden_kernel(n0_ref, n1_ref, wg_ref, wu_ref, hidden_ref, gate_ref, up_ref, n_all):
    tokens = n0_ref.shape[0]

    @pl.when(pl.program_id(0) == 0)
    def _():
        n_all[:tokens] = n0_ref[...]
        n_all[tokens:] = n1_ref[...]

    gate = dot_nn(n_all[...], wg_ref[...])
    up = dot_nn(n_all[...], wu_ref[...])
    hidden_ref[...] = (gate / (1.0 + jnp.exp(-gate)) * up).astype(bf16)
    gate_ref[...] = gate.astype(bf16)
    up_ref[...] = up.astype(bf16)


def hidden_pass(normed, wgate, wup):
    tokens, width = normed[0].shape
    columns = wgate.shape[1]
    tile = min(256, columns)
    whole = pl.BlockSpec((tokens, width), lambda i: (0, 0))
    down = pl.BlockSpec((width, tile), lambda i: (0, i))
    out = pl.BlockSpec((2 * tokens, tile), lambda i: (0, i))
    return pl.pallas_call(
        hidden_kernel,
        grid=(pl.cdiv(columns, tile),),
        in_specs=[whole] * 2 + [down] * 2,
        out_specs=[out] * 3,
        out_shape=[jax.ShapeDtypeStruct((2 * tokens, columns), bf16)] * 3,
        scratch_shapes=[pltpu.VMEM((2 * tokens, width), bf16)],
        compiler_params=pltpu.CompilerParams(vmem_limit_bytes=VMEM_LIMIT),
        name="hidden_pass",
        cost_estimate=LIGHT,
    )(*normed, wgate, wup)


def gates_kernel(g0_ref, g1_ref, wd_ref, gate_ref, up_ref, gate_out_ref, up_out_ref, g_all):
    tokens = g0_ref.shape[0]

    @pl.when(pl.program_id(0) == 0)
    def _():
        g_all[:tokens] = g0_ref[...]
        g_all[tokens:] = g1_ref[...]

    grad = dot_nt(g_all[...], wd_ref[...])
    gate = gate_ref[...].astype(f32)
    up = up_ref[...].astype(f32)
    sigmoid = 1.0 / (1.0 + jnp.exp(-gate))
    gate_out_ref[...] = (grad * up * (sigmoid * (1.0 + gate * (1.0 - sigmoid)))).astype(bf16)
    up_out_ref[...] = (grad * (gate * sigmoid)).astype(bf16)


def gates_pass(grad_top, wdown, gate, up):
    tokens, width = grad_top[0].shape
    columns = gate.shape[1]
    tile = min(256, columns)
    whole = pl.BlockSpec((tokens, width), lambda i: (0, 0))
    out = pl.BlockSpec((2 * tokens, tile), lambda i: (0, i))
    return pl.pallas_call(
        gates_kernel,
        grid=(pl.cdiv(columns, tile),),
        in_specs=[whole] * 2 + [pl.BlockSpec((tile, width), lambda i: (i, 0)), out, out],
        out_specs=[out] * 2,
        out_shape=[jax.ShapeDtypeStruct((2 * tokens, columns), bf16)] * 2,
        scratch_shapes=[pltpu.VMEM((2 * tokens, width), bf16)],
        compiler_params=pltpu.CompilerParams(vmem_limit_bytes=VMEM_LIMIT),
        name="gates_pass",
        cost_estimate=LIGHT,
    )(*grad_top, wdown, gate, up)


def back_kernel(count, transposed, *refs):
    own_ref, send_ref = refs[-2:]
    tokens = own_ref.shape[0]
    dot = dot_nt if transposed else dot_nn

    def total(start):
        rows = pl.ds(start, tokens)
        result = dot(refs[0][rows, :], refs[count][...])
        for i in range(1, count):
            result = result + dot(refs[i][rows, :], refs[count + i][...])
        return result

    own_ref[...] = total(0)
    send_ref[...] = total(tokens).astype(bf16)


def back_pass(lefts, weights, transposed):
    tokens, depth = lefts[0].shape
    width = weights[0].shape[0 if transposed else 1]
    count = len(lefts)
    tile = min(512, width)
    if transposed:
        weight_spec = pl.BlockSpec((tile, depth), lambda i: (i, 0))
    else:
        weight_spec = pl.BlockSpec((depth, tile), lambda i: (0, i))
    out = pl.BlockSpec((tokens // 2, tile), lambda i: (0, i))
    return pl.pallas_call(
        partial(back_kernel, count, transposed),
        grid=(width // tile,),
        in_specs=[pl.BlockSpec((tokens, depth), lambda i: (0, 0))] * count
        + [weight_spec] * count,
        out_specs=[out, out],
        out_shape=[
            jax.ShapeDtypeStruct((tokens // 2, width), f32),
            jax.ShapeDtypeStruct((tokens // 2, width), bf16),
        ],
        compiler_params=pltpu.CompilerParams(vmem_limit_bytes=VMEM_LIMIT),
        name="back_pass",
        cost_estimate=LIGHT,
    )(*lefts, *weights)


def weight_kernel(left_count, *refs):
    lefts, rights, out_ref = refs[:left_count], refs[left_count:-1], refs[-1]
    step = min(lefts[0].shape[0], rights[0].shape[0])

    def piece(refs, start):
        index, offset = divmod(start, refs[0].shape[0])
        return refs[index][pl.ds(offset, step), :]

    total = None
    for start in range(0, left_count * lefts[0].shape[0], step):
        term = dot_tn(piece(lefts, start), piece(rights, start))
        total = term if total is None else total + term
    out_ref[...] = total.astype(bf16)


def weight_pass(lefts, rights):
    rows, columns = lefts[0].shape[1], rights[0].shape[1]
    tile = 512 if rows % 512 == 0 else 384 if rows % 384 == 0 else rows
    return pl.pallas_call(
        partial(weight_kernel, len(lefts)),
        grid=(rows // tile,),
        in_specs=[pl.BlockSpec((left.shape[0], tile), lambda i: (0, i)) for left in lefts]
        + [pl.BlockSpec(right.shape, lambda i: (0, 0)) for right in rights],
        out_specs=pl.BlockSpec((tile, columns), lambda i: (i, 0)),
        out_shape=jax.ShapeDtypeStruct((rows, columns), bf16),
        compiler_params=pltpu.CompilerParams(vmem_limit_bytes=VMEM_LIMIT),
        name="weight_pass",
        cost_estimate=LIGHT,
    )(*lefts, *rights)


def placed_kernel(side_ref, own_ref, other_ref, out_ref):
    mine = pl.program_id(0) == side_ref[0]

    @pl.when(mine)
    def _():
        out_ref[0, 0] = own_ref[:, 0]

    @pl.when(jnp.logical_not(mine))
    def _():
        out_ref[0, 0] = other_ref[:, 0]


def placed(own, other, side):
    seq, group, rows, columns = own.shape

    def entry(mine, e, g, s):
        parked = jnp.where(e == 0, 0, group - 1)
        return (0, jnp.where((e == s[0]) == mine, g, parked), 0, 0)

    return pl.pallas_call(
        placed_kernel,
        grid_spec=pltpu.PrefetchScalarGridSpec(
            num_scalar_prefetch=1,
            grid=(2, group),
            in_specs=[
                pl.BlockSpec((seq, 1, rows, columns), partial(entry, True)),
                pl.BlockSpec((seq, 1, rows, columns), partial(entry, False)),
            ],
            out_specs=pl.BlockSpec(
                (1, 1, seq, rows, columns), lambda e, g, s: (e, g, 0, 0, 0)
            ),
        ),
        out_shape=jax.ShapeDtypeStruct((2, group, seq, rows, columns), own.dtype),
        name="placed",
        cost_estimate=LIGHT,
    )(side.astype(jnp.int32).reshape(1), own, other)


def joined_kernel(side_ref, own_ref, other_ref, out_ref):
    mine = pl.program_id(1) == side_ref[0]

    @pl.when(mine)
    def _():
        out_ref[:, 0] = own_ref[...]

    @pl.when(jnp.logical_not(mine))
    def _():
        out_ref[:, 0] = other_ref[...]


def joined(own, other, side, axis):
    shape = own.shape[:axis] + (2,) + own.shape[axis:]
    columns = own.shape[-1]
    lead = math.prod(own.shape[:axis])
    rows = math.prod(own.shape[axis:-1])
    leads, chunks = lead, 1
    while leads % 2 == 0 and leads * rows * columns > 800_000:
        leads //= 2
    while leads == 1 and rows % (32 * chunks) == 0 and rows // chunks * columns > 800_000:
        chunks *= 2
    block = rows // chunks

    def entry(mine, p, e, i, s):
        parked = jnp.where(e == 0, 0, chunks - 1)
        return (p, jnp.where((e == s[0]) == mine, i, parked), 0)

    return pl.pallas_call(
        joined_kernel,
        grid_spec=pltpu.PrefetchScalarGridSpec(
            num_scalar_prefetch=1,
            grid=(lead // leads, 2, chunks),
            in_specs=[
                pl.BlockSpec((leads, block, columns), partial(entry, True)),
                pl.BlockSpec((leads, block, columns), partial(entry, False)),
            ],
            out_specs=pl.BlockSpec((leads, 1, block, columns), lambda p, e, i, s: (p, e, i, 0)),
        ),
        out_shape=jax.ShapeDtypeStruct((lead, 2, rows, columns), own.dtype),
        compiler_params=pltpu.CompilerParams(vmem_limit_bytes=VMEM_LIMIT),
        name="joined",
        cost_estimate=LIGHT,
    )(
        side.astype(jnp.int32).reshape(1),
        own.reshape(lead, rows, columns),
        other.reshape(lead, rows, columns),
    ).reshape(shape)


def swap(values, bit):
    pairs = [(i, i ^ bit) for i in range(lax.axis_size("rows"))]
    return lax.ppermute(values, "rows", pairs)


def bit_of(bit):
    return (lax.axis_index("rows") // bit) % 2


def gather_bit(values, bit, axis):
    return joined(values, swap(values, bit), bit_of(bit), axis)


def part(values, index, axis):
    return lax.dynamic_index_in_dim(values, index, axis, keepdims=False)


def reduce_bit(values, bit, axis):
    return add_bit(values, pass_bit(values, bit, axis), bit, axis)


def outer_pairs(step, low, high):
    size = lax.axis_size("rows")
    return [
        (i, i + 4 * step)
        for i in range(size)
        if low <= i // 4 < high and 0 <= i // 4 + step < size // 4
    ]


def send_outer(values):
    count = lax.axis_size("rows") // 4
    if count == 2:
        return (swap(values, 4),)
    up, down = values, values
    ups, downs = [], []
    for t in range(1, count):
        up = lax.ppermute(up, "rows", outer_pairs(1, t - 1, count))
        down = lax.ppermute(down, "rows", outer_pairs(-1, 0, count - t + 1))
        ups.append(up)
        downs.append(down)
    return tuple(ups[::-1] + downs)


def join_outer(values, received, axis):
    count = lax.axis_size("rows") // 4
    if count == 2:
        return joined(values, received[0], bit_of(4), axis)
    place = lax.axis_index("rows") // 4
    line = jnp.stack([*received[: count - 1], values, *received[count - 1 :]], axis)
    return lax.dynamic_slice_in_dim(line, count - 1 - place, count, axis)


def gather_outer(values, axis):
    return join_outer(values, send_outer(values), axis)


def pass_outer(values, axis):
    count = lax.axis_size("rows") // 4
    place = lax.axis_index("rows") // 4

    def entry(index):
        return part(values, jnp.clip(index, 0, count - 1), axis)

    if count == 1:
        return ()
    if count == 2:
        return (swap(entry(1 - place), 4),)
    up, down = entry(place + count - 1), entry(place - count + 1)
    for t in range(1, count):
        up = lax.ppermute(up, "rows", outer_pairs(1, 0, t))
        down = lax.ppermute(down, "rows", outer_pairs(-1, count - t, count))
        if t < count - 1:
            up = (entry(place + count - 1 - t).astype(f32) + up.astype(f32)).astype(bf16)
            down = (entry(place - count + 1 + t).astype(f32) + down.astype(f32)).astype(bf16)
    return (up, down)


def add_outer(values, received, axis):
    total = part(values, lax.axis_index("rows") // 4, axis).astype(f32)
    for term in received:
        total = total + term.astype(f32)
    return total.astype(bf16)


def reduce_outer(values, axis):
    return add_outer(values, pass_outer(values, axis), axis)


def pass_bit(values, bit, axis):
    return swap(part(values, 1 - bit_of(bit), axis), bit)


def add_bit(values, received, bit, axis):
    own = part(values, bit_of(bit), axis)
    return (own.astype(f32) + received.astype(f32)).astype(bf16)


def gather_seq(values):
    return lax.all_gather(values, "seq", axis=0, tiled=False)


def reduce_seq(values):
    return lax.psum_scatter(values, "seq", scatter_dimension=0, tiled=False)


def exchange(values, axis, bit):
    size = lax.axis_size(axis)
    return lax.ppermute(values, axis, [(i, i ^ bit) for i in range(size)])


def across_group(own, send):
    return (own + swap(send, 1).astype(f32)).astype(bf16)


def stage(*values):
    return lax.optimization_barrier(values)


def mm(left, right):
    return jnp.einsum("ab,bc->ac", left, right, preferred_element_type=f32)


def mm_t(left, right):
    return jnp.einsum("ab,cb->ac", left, right, preferred_element_type=f32)


def t_mm(left, right):
    return jnp.einsum("ab,ac->bc", left, right, preferred_element_type=f32)


def norm_scale(values):
    return lax.rsqrt(jnp.mean(values * values, axis=-1, keepdims=True) + EPSILON)


def norm_backward(values, scale, gain, grad):
    gained = grad * gain
    inner = jnp.mean(values * gained, axis=-1, keepdims=True)
    result = scale * gained - values * (scale * scale * scale) * inner
    return result, jnp.sum(grad * values * scale, axis=0)


def shards(
    tokens_in,
    corpus,
    corpus_weight,
    w_qkv,
    w_out,
    w_gate,
    w_up,
    w_down,
    attn_gain,
    ffn_gain,
    q_gain,
    k_gain,
    upstream,
):
    shard_length, width = tokens_in.shape[1:]
    row_devices = lax.axis_size("rows")
    seq_devices = lax.axis_size("seq")
    outer = row_devices // 4
    d_rows = w_qkv.shape[0]
    f_rows = w_down.shape[0]
    place = lax.axis_index("seq").astype(jnp.int32)
    inputs = tokens_in[0].astype(f32)

    extra = jnp.stack(
        [
            attn_gain,
            ffn_gain,
            jnp.broadcast_to(corpus.astype(bf16), attn_gain.shape),
        ],
        axis=1,
    )
    extra = jnp.pad(extra, ((0, 0), (0, LANES - extra.shape[1])))
    kv_shard = jnp.concatenate([w_qkv[:, QUERY_COLUMNS:], extra], axis=1)
    query_shard = jnp.concatenate([w_qkv[:, :QUERY_COLUMNS], w_out.T], axis=1)
    query_shard, w_gate, w_up = stage(query_shard, w_gate, w_up)
    query_lines = gather_seq(query_shard)

    def to_group(weight):
        blocks = weight.reshape(d_rows, outer, 4, seq_devices, f_rows)
        blocks = jnp.transpose(blocks, (2, 0, 3, 1, 4))
        return blocks.reshape(2, 2, d_rows, outer * seq_devices * f_rows)

    def spread_hidden(lines, received):
        if outer == 2:
            lines = lines.reshape(seq_devices, 4, d_rows, hidden_columns)
            other = received[0].reshape(lines.shape)
            return placed(lines, other, bit_of(4)).reshape(width, hidden_columns)
        full = join_outer(lines, received, 0)
        return jnp.moveaxis(full, 1, 3).reshape(width, hidden_columns)

    gate_up = jnp.stack([to_group(w_gate), to_group(w_up)], axis=2)
    hidden_columns = gate_up.shape[-1]
    core, near = bit_of(1), bit_of(2)
    gate_up = joined(
        part(gate_up, core, 1), swap(part(gate_up, 1 - core, 1), 1), core, 1
    )
    gate_up, kv_shard = stage(gate_up, kv_shard)
    other, kv_lines, query_lines = stage(
        swap(part(gate_up, 1 - near, 0), 2), gather_seq(kv_shard), query_lines
    )
    gate_up = joined(part(gate_up, near, 0), other, near, 0)
    gate_lines = gather_seq(gate_up[:, :, 0])
    left, right = kv_lines[..., : 3 * LANES], kv_lines[..., 3 * LANES :]
    left_other, right_other = stage(send_outer(left), swap(right, 2))
    left = join_outer(left, left_other, 0)
    right = joined(right, right_other, near, 0)
    left_other, right_other = stage(swap(left, 2), send_outer(right))
    left = joined(left, left_other, near, 1)
    right = join_outer(right, right_other, 0)
    q_left, q_right = query_lines[..., :QUERY_COLUMNS], query_lines[..., QUERY_COLUMNS:]
    q_left, q_right, left, right = stage(q_left, q_right, left, right)
    q_left_other, q_right_other = send_outer(q_left), swap(q_right, 2)
    left, right = gather_bit(left, 1, 2), gather_bit(right, 1, 2)
    left, right = left.reshape(width, -1), right.reshape(width, -1)
    wkv = jnp.concatenate([left, right[:, : 2 * LANES]], axis=1)
    rows = dot_nt(jnp.eye(8, LANES, dtype=bf16), right[:, 2 * LANES :])
    attn_gain_full, ffn_gain_full, corpus_full = rows[0:1], rows[1:2], rows[2]

    position = (place * shard_length + jnp.arange(shard_length, dtype=jnp.int32)).astype(f32)
    half = HEAD_SIZE // 2
    exponent = jnp.arange(half, dtype=f32) * (-2.0 / HEAD_SIZE)
    angles = position[:, None] * jnp.power(ROPE_BASE, exponent)[None, :]
    cosine, sine = jnp.cos(angles), jnp.sin(angles)
    cos_table = jnp.concatenate([cosine] * 4, axis=1)
    sin_table = jnp.concatenate([-sine, sine] * 2, axis=1)
    wide_q = jnp.tile(q_gain.astype(f32), QUERY_HEADS)
    wide_k = jnp.concatenate(
        [jnp.tile(k_gain.astype(f32), KEY_VALUE_HEADS), jnp.ones((KEY_COLUMNS,), f32)]
    )
    wide_q = jnp.broadcast_to(wide_q[None, :], (8, QUERY_COLUMNS))
    wide_k = jnp.broadcast_to(wide_k[None, :], (8, 2 * KEY_COLUMNS))

    in_scale = norm_scale(inputs)
    normed = (inputs * in_scale * attn_gain_full).astype(bf16)
    joint_kv = mm(normed, wkv)
    own_kv = heads_forward(joint_kv, wide_k, cos_table, sin_table, KEY_COLUMNS)
    own_kv, q_left_other, q_right_other, down_other, up_in = stage(
        own_kv, q_left_other, q_right_other, send_outer(w_down), gate_up[:, :, 1]
    )
    up_lines = gather_seq(up_in)
    down_pair = join_outer(w_down, down_other, 0)
    keys_values = gather_seq(own_kv).reshape(-1, 2 * KEY_COLUMNS)
    q_left = join_outer(q_left, q_left_other, 0)
    q_right = joined(q_right, q_right_other, near, 0)
    left_other, right_other, gate_lines = stage(
        swap(q_left, 2), send_outer(q_right), gate_lines
    )
    q_left = joined(q_left, left_other, near, 1)
    q_right = join_outer(q_right, right_other, 0)
    gate_other = send_outer(gate_lines)
    wq = gather_bit(q_left, 1, 2).reshape(width, -1)

    corpora = jnp.arange(CORPORA, dtype=jnp.int32)
    per_device = corpus_full.reshape(-1, d_rows)[:, 0].astype(jnp.int32)
    counts = (
        jnp.sum((per_device[:, None] == corpora[None, :]).astype(f32), axis=0) * shard_length
    )
    own_corpus = (corpus[0] == corpora).astype(f32)
    weight_row = jnp.sum(own_corpus * corpus_weight.astype(f32))
    count_row = jnp.sum(own_corpus * counts)
    factor = weight_row / DENOM * (jnp.sum(counts) / (CORPORA * count_row))
    grad_full = upstream[0].astype(f32) * factor
    grad_top, wq = stage(grad_full.astype(bf16), wq)

    joint_q = mm(normed, wq)
    queries = heads_forward(joint_q, wide_q, cos_table, sin_table, QUERY_COLUMNS)
    place_array = place.reshape(1)
    keys_values, queries, down_in = stage(keys_values, queries, down_pair)
    down_lines = gather_seq(down_in)
    mixed, logs = attend_forward(place_array, queries, keys_values)
    mixed, grad_top1, grad_top2, up_lines, wout_other = stage(
        mixed, swap(grad_top, 1), swap(grad_top, 2), up_lines, swap(q_right, 1)
    )
    wout_t = joined(q_right, wout_other, core, 2).reshape(width, -1)
    middle = inputs + mm_t(mixed, wout_t)

    ffn_scale = norm_scale(middle)
    normed_ffn = (middle * ffn_scale * ffn_gain_full).astype(bf16)
    up_other = send_outer(up_lines)
    normed_ffn, gate_other = stage(normed_ffn, gate_other)
    normed1, normed2, up_other, wgate = stage(
        swap(normed_ffn, 1),
        swap(normed_ffn, 2),
        up_other,
        spread_hidden(gate_lines, gate_other),
    )
    wup = spread_hidden(up_lines, up_other)
    hidden_near, gate_near, up_near = hidden_pass((normed_ffn, normed1), wgate, wup)
    normed3, hidden_near, grad_top3 = stage(
        swap(normed2, 1), hidden_near, swap(grad_top2, 1)
    )
    hidden_far, gate_far, up_far = hidden_pass((normed2, normed3), wgate, wup)
    normed4 = (normed_ffn, normed1, normed2, normed3)
    grad_top4 = (grad_top, grad_top1, grad_top2, grad_top3)
    wdown = down_lines.reshape(hidden_columns, width)
    gate_far, up_far = gates_pass((grad_top2, grad_top3), wdown, gate_far, up_far)
    own, send = back_pass((gate_far, up_far), (wgate, wup), True)
    grad_wdown = weight_pass((hidden_near, hidden_far), grad_top4)
    own, send, grad_wdown, wdown = stage(own, swap(send, 1), grad_wdown, wdown)
    across = (own + send.astype(f32)).astype(bf16)
    across, wdown = stage(across, wdown)
    gate_near, up_near = gates_pass((grad_top, grad_top1), wdown, gate_near, up_near)
    own, send = back_pass((gate_near, up_near), (wgate, wup), True)
    hidden_shape = (outer, 2, 2, seq_devices, d_rows, hidden_columns)
    grad_wdown = grad_wdown.reshape(seq_devices, outer, f_rows, width)
    grad_wgate = weight_pass(normed4, (gate_near, gate_far)).reshape(hidden_shape)
    across, own, send, grad_wgate, up_near = stage(
        swap(across, 2), own, send, grad_wgate, up_near
    )
    grad_wup = weight_pass(normed4, (up_near, up_far)).reshape(hidden_shape)
    send, grad_wup, down_other = stage(swap(send, 1), grad_wup, pass_outer(grad_wdown, 1))
    grad_wdown = add_outer(grad_wdown, down_other, 1)
    own = own + send.astype(f32)
    grad_normed_ffn = own + across.astype(f32)
    grad_wdown = reduce_seq(grad_wdown)

    grad_middle_part, grad_ffn_gain = norm_backward(
        middle, ffn_scale, ffn_gain_full, grad_normed_ffn
    )
    grad_middle = grad_full + grad_middle_part
    grad_branch = grad_middle.astype(bf16)
    grad_mixed = mm(grad_branch, wout_t).astype(bf16)
    attend = (place_array, queries, keys_values, mixed, logs)
    grad_q1, grad_kv1 = attend_backward(0, 2, *attend, grad_mixed)
    grad_q1, grad_kv1, gate_other, grad_mixed, grad_wdown, hidden_far = stage(
        grad_q1, grad_kv1, pass_outer(grad_wgate, 0), grad_mixed, grad_wdown, hidden_far
    )
    grad_kv1 = reduce_seq(grad_kv1.reshape(seq_devices, shard_length, -1))
    grad_gate = reduce_seq(jnp.moveaxis(add_outer(grad_wgate, gate_other, 0), 2, 0))
    shape = (outer, 2, 2, seq_devices, d_rows)
    own_far, send_far = back_pass((hidden_far,), (wdown,), False)
    grad_wout, far_other, grad_mixed = stage(
        t_mm(grad_branch, mixed).astype(bf16).reshape(*shape, QUERY_COLUMNS),
        swap(send_far, 1),
        grad_mixed,
    )
    across = (own_far + far_other.astype(f32)).astype(bf16)
    across, grad_mixed = stage(across, grad_mixed)
    grad_q2, grad_kv2 = attend_backward(2, 3, *attend, grad_mixed)
    grad_q2, grad_kv2, hidden_near, grad_kv1, grad_gate, wout_other, up_other, across = stage(
        grad_q2,
        grad_kv2,
        hidden_near,
        grad_kv1,
        grad_gate,
        pass_bit(grad_wout, 1, 2),
        pass_outer(grad_wup, 0),
        swap(across, 2),
    )
    grad_kv2 = reduce_seq(grad_kv2.reshape(seq_devices, shard_length, -1))

    grad_q = jnp.concatenate([grad_q1, grad_q2], axis=1)
    joint_grad_q, gain_q = heads_backward(
        grad_q, joint_q, wide_q, cos_table, sin_table, QUERY_COLUMNS
    )
    grad_wq = t_mm(normed, joint_grad_q).astype(bf16).reshape(*shape, QUERY_COLUMNS)
    grad_wout = add_bit(grad_wout, wout_other, 1, 2)
    own_near, send_near = back_pass((hidden_near,), (wdown,), False)
    grad_up = jnp.moveaxis(add_outer(grad_wup, up_other, 0), 2, 0)
    wq_other, own_near, near_other, grad_up = stage(
        pass_bit(grad_wq, 1, 2), own_near, swap(send_near, 1), grad_up
    )
    grad_kv2, grad_wq, grad_wout, grad_up = stage(
        grad_kv2, add_bit(grad_wq, wq_other, 1, 2), grad_wout, grad_up
    )
    output = (middle + own_near + near_other.astype(f32) + across.astype(f32)).astype(bf16)
    grad_up = reduce_seq(grad_up)
    wq_other, wout_other = pass_bit(grad_wq, 2, 1), pass_outer(grad_wout, 0)

    grad_kv1, grad_kv2 = (
        part_.reshape(shard_length, 2, -1) for part_ in (grad_kv1, grad_kv2)
    )
    grad_kv = jnp.concatenate([grad_kv1, grad_kv2], axis=2).reshape(shard_length, -1)
    joint_grad_kv, gain_k = heads_backward(
        grad_kv, joint_kv, wide_k, cos_table, sin_table, KEY_COLUMNS
    )
    grad_wkv = t_mm(normed, joint_grad_kv).astype(bf16)
    grad_normed = mm_t(joint_grad_q, wq) + mm_t(joint_grad_kv, wkv)
    grad_input_part, grad_attn_gain = norm_backward(
        inputs, in_scale, attn_gain_full, grad_normed
    )
    input_grad = (grad_middle + grad_input_part).astype(bf16)

    gain_rows = jnp.stack([grad_attn_gain, grad_ffn_gain]).astype(bf16)
    gain_columns = t_mm(gain_rows, jnp.eye(2, LANES, dtype=bf16)).astype(bf16)
    left = grad_wkv[:, : 3 * LANES].reshape(*shape, -1)
    right = jnp.concatenate([grad_wkv[:, 3 * LANES :], gain_columns], axis=1)
    right = right.reshape(*shape, -1)
    head_gains = jnp.concatenate(
        [
            jnp.sum(gain_q[0].reshape(-1, HEAD_SIZE), axis=0),
            jnp.sum(gain_k[0, :KEY_COLUMNS].reshape(-1, HEAD_SIZE), axis=0),
        ]
    )[None]
    left, right, left_other, right_other, wq_other, wout_other, gains_other = stage(
        left,
        right,
        pass_bit(left, 1, 2),
        pass_bit(right, 1, 2),
        wq_other,
        wout_other,
        exchange(head_gains, "rows", 1),
    )
    head_gains = head_gains + gains_other
    left = add_bit(left, left_other, 1, 2)
    right = add_bit(right, right_other, 1, 2)
    grad_wq = add_bit(grad_wq, wq_other, 2, 1)
    grad_wout = add_outer(grad_wout, wout_other, 0)
    left_other, right_other, wq_other, wout_other, gains_other, grad_up = stage(
        pass_bit(left, 2, 1),
        pass_outer(right, 0),
        pass_outer(grad_wq, 0),
        pass_bit(grad_wout, 2, 0),
        exchange(head_gains, "seq", 1),
        grad_up,
    )
    head_gains = head_gains + gains_other
    left = add_bit(left, left_other, 2, 1)
    right = add_outer(right, right_other, 0)
    left_other, right_other, gains_other = stage(
        pass_outer(left, 0), pass_bit(right, 2, 0), exchange(head_gains, "rows", 2)
    )
    head_gains = head_gains + gains_other
    sums = reduce_seq(
        jnp.concatenate(
            [
                add_outer(grad_wq, wq_other, 0),
                add_outer(left, left_other, 0),
                add_bit(right, right_other, 2, 0),
                add_bit(grad_wout, wout_other, 2, 0),
            ],
            axis=-1,
        )
    )
    rest = [("rows", bit) for bit in (4, 8, 16) if bit < row_devices]
    rest += [("seq", bit) for bit in (2, 4, 8) if bit < seq_devices]
    gate_up = jnp.stack([grad_gate, grad_up], axis=2)
    other, gains_other = stage(
        swap(part(gate_up, 1 - near, 0), 2), exchange(head_gains, *rest[0])
    )
    head_gains = head_gains + gains_other
    grads = joined(part(gate_up, near, 0), other, near, 0)
    for axis, bit in rest[1:]:
        head_gains = head_gains + exchange(head_gains, axis, bit)
    head_gains = head_gains[0]
    grads = joined(part(grads, core, 1), swap(part(grads, 1 - core, 1), 1), core, 1)

    def from_group(blocks):
        blocks = blocks.reshape(4, d_rows, seq_devices, outer, f_rows)
        return jnp.transpose(blocks, (1, 3, 0, 2, 4)).reshape(d_rows, -1)

    grad_wgate, grad_wup = stage(from_group(grads[:, :, 0]), from_group(grads[:, :, 1]))
    sums, grad_wgate, grad_wup, grad_wdown, output, input_grad = stage(
        sums, grad_wgate.astype(f32), grad_wup.astype(f32), grad_wdown.astype(f32), output, input_grad
    )
    columns = QUERY_COLUMNS + 2 * KEY_COLUMNS
    long_gains = sums[:, columns : columns + 2].astype(f32)
    return (
        output[None],
        input_grad[None],
        sums[:, :columns].astype(f32),
        sums[:, columns + LANES :].T.astype(f32),
        grad_wgate,
        grad_wup,
        grad_wdown,
        long_gains[:, 0],
        long_gains[:, 1],
        head_gains[:HEAD_SIZE],
        head_gains[HEAD_SIZE:],
    )


def solution(mesh):
    return jax.shard_map(
        shards,
        mesh=mesh,
        in_specs=(
            P("rows", "seq", None),
            P("rows"),
            P(),
            P(("rows", "seq"), None),
            P(None, ("rows", "seq")),
            P(("rows", "seq"), None),
            P(("rows", "seq"), None),
            P(("rows", "seq"), None),
            P(("rows", "seq")),
            P(("rows", "seq")),
            P(),
            P(),
            P("rows", "seq", None),
        ),
        out_specs=(
            P("rows", "seq", None),
            P("rows", "seq", None),
            P(("rows", "seq"), None),
            P(None, ("rows", "seq")),
            P(("rows", "seq"), None),
            P(("rows", "seq"), None),
            P(("rows", "seq"), None),
            P(("rows", "seq")),
            P(("rows", "seq")),
            P(),
            P(),
        ),
        check_vma=False,
    )
```

```python
import math
from functools import partial

import jax
import jax.numpy as jnp
from jax import lax
from jax.experimental import pallas as pl
from jax.experimental.pallas import tpu as pltpu
from jax.sharding import PartitionSpec as P

QUERY_HEADS = 20
KEY_VALUE_HEADS = 5
HEAD_SIZE = 64
CORPORA = 8
DENOM = 64
EPSILON = 1e-06
ROPE_BASE = 10000.0
QUERY_COLUMNS = QUERY_HEADS * HEAD_SIZE
KEY_COLUMNS = KEY_VALUE_HEADS * HEAD_SIZE
LANES = 128
SCORE_EXPONENT = 1.4426950408889634 * HEAD_SIZE**-0.5
SPLIT = 2
VMEM_LIMIT = 48 * 1024 * 1024

f32, bf16 = jnp.float32, jnp.bfloat16
LIGHT = pl.CostEstimate(flops=1000, bytes_accessed=1000, transcendentals=0)


def dot_nn(a, b):
    return lax.dot_general(a, b, (((1,), (0,)), ((), ())), preferred_element_type=f32)


def dot_nt(a, b):
    return lax.dot_general(a, b, (((1,), (1,)), ((), ())), preferred_element_type=f32)


def dot_tn(a, b):
    return lax.dot_general(a, b, (((0,), (0,)), ((), ())), preferred_element_type=f32)


def lanes_of(shape):
    return lax.broadcasted_iota(jnp.int32, shape, len(shape) - 1)


def head_sum(values):
    row = lax.broadcasted_iota(jnp.int32, (LANES, LANES), 0) // HEAD_SIZE
    column = lax.broadcasted_iota(jnp.int32, (LANES, LANES), 1) // HEAD_SIZE
    ones = jnp.where(row == column, 1.0, 0.0).astype(bf16)
    high = values.astype(bf16)
    low = (values - high.astype(f32)).astype(bf16)
    return dot_nn(high, ones) + dot_nn(low, ones)


def partner(values):
    first = lanes_of(values.shape) % HEAD_SIZE < HEAD_SIZE // 2
    return jnp.where(
        first,
        pltpu.roll(values, LANES - HEAD_SIZE // 2, 1),
        pltpu.roll(values, HEAD_SIZE // 2, 1),
    )


def heads_forward_kernel(
    norm_columns, normed_ref, weight_ref, gain_ref, cos_ref, sin_ref, joint_ref, out_ref
):
    joint = dot_nn(normed_ref[...], weight_ref[...])
    joint_ref[...] = joint
    columns = joint.shape[1]
    for start in range(0, columns, LANES):
        chunk = slice(start, start + LANES)
        values = joint[:, chunk]
        scale = lax.rsqrt(head_sum(values * values) * (1.0 / HEAD_SIZE) + EPSILON)
        normed = values * scale * gain_ref[0:1, chunk]
        turned = normed * cos_ref[...] + partner(normed) * sin_ref[...]
        place = pl.program_id(0) * columns + start + lanes_of(values.shape)
        out_ref[:, chunk] = jnp.where(place < norm_columns, turned, values).astype(bf16)


def heads_forward(normed, weight, gain, cos, sin, norm_columns):
    tokens, width = normed.shape
    columns = weight.shape[1]
    tile = 2 * LANES if columns % (2 * LANES) == 0 else LANES
    out = pl.BlockSpec((tokens, tile), lambda i: (0, i))
    table = pl.BlockSpec((tokens, LANES), lambda i: (0, 0))
    return pl.pallas_call(
        partial(heads_forward_kernel, norm_columns),
        grid=(columns // tile,),
        in_specs=[
            pl.BlockSpec((tokens, width), lambda i: (0, 0)),
            pl.BlockSpec((width, tile), lambda i: (0, i)),
            pl.BlockSpec((8, tile), lambda i: (0, i)),
            table,
            table,
        ],
        out_specs=[out, out],
        out_shape=[
            jax.ShapeDtypeStruct((tokens, columns), f32),
            jax.ShapeDtypeStruct((tokens, columns), bf16),
        ],
        compiler_params=pltpu.CompilerParams(vmem_limit_bytes=VMEM_LIMIT),
        name="heads_forward",
        cost_estimate=LIGHT,
    )(normed, weight, gain, cos, sin)


def heads_backward_kernel(
    norm_columns, grad_ref, joint_ref, gain_ref, cos_ref, sin_ref, out_ref, gain_out_ref
):
    grad = grad_ref[...].astype(f32)
    values = joint_ref[...]
    gain = gain_ref[0:1, :]
    turned = grad * cos_ref[...] - partner(grad) * sin_ref[...]
    scale = lax.rsqrt(head_sum(values * values) * (1.0 / HEAD_SIZE) + EPSILON)
    gained = turned * gain
    inner = head_sum(values * gained) * (1.0 / HEAD_SIZE)
    result = scale * gained - values * (scale * scale * scale) * inner
    place = pl.program_id(0) * LANES + lanes_of(values.shape)
    out_ref[...] = jnp.where(place < norm_columns, result, grad).astype(bf16)
    gain_out_ref[...] = jnp.broadcast_to(
        jnp.sum(turned * values * scale, axis=0, keepdims=True), gain_out_ref.shape
    )


def heads_backward(grad, joint, gain, cos, sin, norm_columns):
    tokens, columns = joint.shape
    return pl.pallas_call(
        partial(heads_backward_kernel, norm_columns),
        grid=(columns // LANES,),
        in_specs=[
            pl.BlockSpec((tokens, LANES), lambda i: (0, i)),
            pl.BlockSpec((tokens, LANES), lambda i: (0, i)),
            pl.BlockSpec((8, LANES), lambda i: (0, i)),
            pl.BlockSpec((tokens, LANES), lambda i: (0, 0)),
            pl.BlockSpec((tokens, LANES), lambda i: (0, 0)),
        ],
        out_specs=[
            pl.BlockSpec((tokens, LANES), lambda i: (0, i)),
            pl.BlockSpec((8, LANES), lambda i: (0, i)),
        ],
        out_shape=[
            jax.ShapeDtypeStruct((tokens, columns), bf16),
            jax.ShapeDtypeStruct((8, columns), f32),
        ],
        name="heads_backward",
        cost_estimate=LIGHT,
    )(grad, joint, gain, cos, sin)


def both_halves(pair, odd):
    wide = pair.astype(f32)
    first = lanes_of(wide.shape) < HEAD_SIZE
    keep = jnp.where(odd == 1, jnp.where(first, 0, 1), jnp.where(first, 1, 0)) == 1
    return jnp.where(keep, wide, pltpu.roll(wide, HEAD_SIZE, 1))


def attend_forward_kernel(place_ref, q_ref, k_ref, v_ref, out_ref, log_ref):
    group = pl.program_id(0) // 2
    place = place_ref[0]
    tokens = q_ref.shape[0]
    first = lanes_of((tokens, LANES)) < HEAD_SIZE
    pair = q_ref[...].astype(f32)
    queries = (jnp.where(first, pair, 0.0).astype(bf16), jnp.where(first, 0.0, pair).astype(bf16))

    def step(j, totals, diagonal):
        rows = pl.ds(pl.multiple_of(j * tokens, tokens), tokens)
        keys = both_halves(k_ref[rows, :], group % 2).astype(bf16)
        values = both_halves(v_ref[rows, :], (KEY_VALUE_HEADS + group) % 2)
        sides = (
            jnp.where(first, values, 1.0).astype(bf16),
            jnp.where(first, 1.0, values).astype(bf16),
        )
        result = []
        for head in range(2):
            weights = jnp.exp2(dot_nt(queries[head], keys) * SCORE_EXPONENT)
            if diagonal:
                row = lax.broadcasted_iota(jnp.int32, weights.shape, 0)
                weights = jnp.where(lanes_of(weights.shape) <= row, weights, 0.0)
            result.append(totals[head] + dot_nn(weights.astype(bf16), sides[head]))
        return tuple(result)

    zero = jnp.zeros((tokens, LANES), f32)
    totals = lax.fori_loop(0, place, lambda j, c: step(j, c, False), (zero, zero))
    totals = step(place, totals, True)
    numerator = jnp.where(first, totals[0], totals[1])
    swapped = jnp.where(first, totals[1], totals[0])
    out_ref[...] = (numerator / pltpu.roll(swapped, HEAD_SIZE, 1)).astype(bf16)
    log_ref[...] = jnp.log2(swapped)


def attend_forward(place, queries, keys_values):
    tokens = queries.shape[0]
    length = keys_values.shape[0]
    pairs = QUERY_COLUMNS // LANES
    return pl.pallas_call(
        attend_forward_kernel,
        grid_spec=pltpu.PrefetchScalarGridSpec(
            num_scalar_prefetch=1,
            grid=(pairs,),
            in_specs=[
                pl.BlockSpec((tokens, LANES), lambda i, s: (0, i)),
                pl.BlockSpec((length, LANES), lambda i, s: (0, (i // 2) // 2)),
                pl.BlockSpec((length, LANES), lambda i, s: (0, (KEY_VALUE_HEADS + i // 2) // 2)),
            ],
            out_specs=[
                pl.BlockSpec((tokens, LANES), lambda i, s: (0, i)),
                pl.BlockSpec((tokens, LANES), lambda i, s: (0, i)),
            ],
        ),
        out_shape=[
            jax.ShapeDtypeStruct((tokens, QUERY_COLUMNS), bf16),
            jax.ShapeDtypeStruct((tokens, QUERY_COLUMNS), f32),
        ],
        compiler_params=pltpu.CompilerParams(vmem_limit_bytes=VMEM_LIMIT),
        name="attend_forward",
        cost_estimate=LIGHT,
    )(place, queries, keys_values, keys_values)


def three_parts(values, lane):
    high = values.astype(bf16).astype(f32)
    rest = values - high
    middle = rest.astype(bf16).astype(f32)
    low = rest - middle
    return jnp.where(
        lane == 0, high, jnp.where(lane == 1, middle, jnp.where(lane == 2, low, 0.0))
    )


def attend_backward_kernel(
    first_group, count, place_ref, q_ref, k_ref, v_ref, out_ref, log_ref, grad_ref, dq_ref, dkv_ref, dk_sum, dv_sum
):
    pair_index = pl.program_id(0)
    local = pair_index // 2
    group = first_group + local
    place = place_ref[0]
    tokens = q_ref.shape[0]
    lane = lanes_of((tokens, LANES))
    first = lane < HEAD_SIZE
    inside = lane % HEAD_SIZE
    pair = q_ref[...].astype(f32)
    grad = grad_ref[...].astype(f32)
    delta = pltpu.roll(head_sum(grad * out_ref[...].astype(f32)), HEAD_SIZE, 1)
    logs = three_parts(log_ref[...] * (1.0 / SCORE_EXPONENT), inside)
    deltas = three_parts(delta, inside)
    minus = jnp.where(inside < 3, -1.0, 0.0)

    def sides(own, other):
        return (
            jnp.where(first, own, other).astype(bf16),
            jnp.where(first, other, own).astype(bf16),
        )

    queries = sides(pair, 0.0)
    grads = sides(grad, 0.0)
    def turned(values):
        return jnp.transpose(values.astype(f32)).astype(bf16)

    queries_log = tuple(turned(v) for v in sides(pair, logs))
    grads_delta = tuple(turned(v) for v in sides(grad, deltas))

    @pl.when(pair_index % 2 == 0)
    def _():
        dk_sum[...] = jnp.zeros_like(dk_sum)
        dv_sum[...] = jnp.zeros_like(dv_sum)

    def step(j, dq, diagonal):
        rows = pl.ds(pl.multiple_of(j * tokens, tokens), tokens)
        key_wide = both_halves(k_ref[rows, :], group % 2)
        value_wide = both_halves(v_ref[rows, :], (KEY_VALUE_HEADS + group) % 2)
        keys_turned = jnp.transpose(key_wide)[:HEAD_SIZE].astype(bf16)
        keys_log = sides(key_wide, minus)
        values_delta = sides(value_wide, minus)
        dk = dk_sum[rows, :]
        dv = dv_sum[rows, :]
        parts = list(dq)
        block = tokens // SPLIT
        for sub in range(SPLIT):
            keep = slice(sub * block, (sub + 1) * block)
            dk_part, dv_part = dk[keep], dv[keep]
            start = sub * block if diagonal else 0
            for head in range(2):
                weights = jnp.exp2(
                    dot_nn(keys_log[head][keep], queries_log[head][:, start:]) * SCORE_EXPONENT
                )
                if diagonal:
                    row = lax.broadcasted_iota(jnp.int32, weights.shape, 0)
                    weights = jnp.where(row <= lanes_of(weights.shape), weights, 0.0)
                grad_weights = dot_nn(values_delta[head][keep], grads_delta[head][:, start:])
                grad_scores = (weights * grad_weights).astype(bf16)
                dv_part = dv_part + dot_nn(weights.astype(bf16), grads[head][start:])
                dk_part = dk_part + dot_nn(grad_scores, queries[head][start:])
                term = dot_nn(keys_turned[:, keep], grad_scores)
                if start:
                    term = jnp.concatenate([jnp.zeros((HEAD_SIZE, start), f32), term], axis=1)
                parts[head] = parts[head] + term
            target = pl.ds(pl.multiple_of(j * tokens + sub * block, block), block)
            dk_sum[target, :] = dk_part
            dv_sum[target, :] = dv_part
        return tuple(parts)

    zero = jnp.zeros((HEAD_SIZE, tokens), f32)
    dq = lax.fori_loop(0, place, lambda j, c: step(j, c, False), (zero, zero))
    dq = jnp.transpose(jnp.concatenate(step(place, dq, True), axis=0))
    dq_ref[...] = (dq * HEAD_SIZE**-0.5).astype(bf16)

    @pl.when(pair_index % 2 == 1)
    def _():
        wide_lane = lanes_of(dk_sum.shape)
        for total, slot, factor in (
            (dk_sum, local, HEAD_SIZE**-0.5),
            (dv_sum, count + local, 1.0),
        ):
            both = (total[...] + pltpu.roll(total[...], HEAD_SIZE, 1)) * factor
            columns = pl.ds(pl.multiple_of(slot // 2 * LANES, LANES), LANES)
            mine = wide_lane // HEAD_SIZE == slot % 2
            dkv_ref[:, columns] = jnp.where(
                mine, both, dkv_ref[:, columns].astype(f32)
            ).astype(bf16)


def attend_backward(first, count, place, queries, keys_values, mixed, logs, grad_mixed):
    tokens = queries.shape[0]
    length = keys_values.shape[0]
    group = QUERY_HEADS // KEY_VALUE_HEADS * HEAD_SIZE
    own = pl.BlockSpec((tokens, LANES), lambda i, s: (0, 2 * first + i))
    keys = pl.BlockSpec((length, LANES), lambda i, s: (0, (first + i // 2) // 2))
    values = pl.BlockSpec(
        (length, LANES), lambda i, s: (0, (KEY_VALUE_HEADS + first + i // 2) // 2)
    )
    columns = 2 * count * HEAD_SIZE
    return pl.pallas_call(
        partial(attend_backward_kernel, first, count),
        grid_spec=pltpu.PrefetchScalarGridSpec(
            num_scalar_prefetch=1,
            grid=(2 * count,),
            in_specs=[own, keys, values, own, own, own],
            out_specs=[
                pl.BlockSpec((tokens, LANES), lambda i, s: (0, i)),
                pl.BlockSpec((length, columns), lambda i, s: (0, 0)),
            ],
            scratch_shapes=[pltpu.VMEM((length, LANES), f32), pltpu.VMEM((length, LANES), f32)],
        ),
        out_shape=[
            jax.ShapeDtypeStruct((tokens, count * group), bf16),
            jax.ShapeDtypeStruct((length, columns), bf16),
        ],
        compiler_params=pltpu.CompilerParams(vmem_limit_bytes=VMEM_LIMIT),
        name="attend_backward",
        cost_estimate=LIGHT,
    )(place, queries, keys_values, keys_values, mixed, logs, grad_mixed)


def hidden_kernel(n0_ref, n1_ref, wg_ref, wu_ref, hidden_ref, gate_ref, up_ref, n_all):
    tokens = n0_ref.shape[0]

    @pl.when(pl.program_id(0) == 0)
    def _():
        n_all[:tokens] = n0_ref[...]
        n_all[tokens:] = n1_ref[...]

    gate = dot_nn(n_all[...], wg_ref[...])
    up = dot_nn(n_all[...], wu_ref[...])
    hidden_ref[...] = (gate / (1.0 + jnp.exp(-gate)) * up).astype(bf16)
    gate_ref[...] = gate.astype(bf16)
    up_ref[...] = up.astype(bf16)


def hidden_pass(normed, wgate, wup):
    tokens, width = normed[0].shape
    columns = wgate.shape[1]
    tile = min(256, columns)
    whole = pl.BlockSpec((tokens, width), lambda i: (0, 0))
    down = pl.BlockSpec((width, tile), lambda i: (0, i))
    out = pl.BlockSpec((2 * tokens, tile), lambda i: (0, i))
    return pl.pallas_call(
        hidden_kernel,
        grid=(pl.cdiv(columns, tile),),
        in_specs=[whole] * 2 + [down] * 2,
        out_specs=[out] * 3,
        out_shape=[jax.ShapeDtypeStruct((2 * tokens, columns), bf16)] * 3,
        scratch_shapes=[pltpu.VMEM((2 * tokens, width), bf16)],
        compiler_params=pltpu.CompilerParams(vmem_limit_bytes=VMEM_LIMIT),
        name="hidden_pass",
        cost_estimate=LIGHT,
    )(*normed, wgate, wup)


def gates_kernel(g0_ref, g1_ref, wd_ref, gate_ref, up_ref, gate_out_ref, up_out_ref, g_all):
    tokens = g0_ref.shape[0]

    @pl.when(pl.program_id(0) == 0)
    def _():
        g_all[:tokens] = g0_ref[...]
        g_all[tokens:] = g1_ref[...]

    grad = dot_nt(g_all[...], wd_ref[...])
    gate = gate_ref[...].astype(f32)
    up = up_ref[...].astype(f32)
    sigmoid = 1.0 / (1.0 + jnp.exp(-gate))
    gate_out_ref[...] = (grad * up * (sigmoid * (1.0 + gate * (1.0 - sigmoid)))).astype(bf16)
    up_out_ref[...] = (grad * (gate * sigmoid)).astype(bf16)


def gates_pass(grad_top, wdown, gate, up):
    tokens, width = grad_top[0].shape
    columns = gate.shape[1]
    tile = min(256, columns)
    whole = pl.BlockSpec((tokens, width), lambda i: (0, 0))
    out = pl.BlockSpec((2 * tokens, tile), lambda i: (0, i))
    return pl.pallas_call(
        gates_kernel,
        grid=(pl.cdiv(columns, tile),),
        in_specs=[whole] * 2 + [pl.BlockSpec((tile, width), lambda i: (i, 0)), out, out],
        out_specs=[out] * 2,
        out_shape=[jax.ShapeDtypeStruct((2 * tokens, columns), bf16)] * 2,
        scratch_shapes=[pltpu.VMEM((2 * tokens, width), bf16)],
        compiler_params=pltpu.CompilerParams(vmem_limit_bytes=VMEM_LIMIT),
        name="gates_pass",
        cost_estimate=LIGHT,
    )(*grad_top, wdown, gate, up)


def back_kernel(count, transposed, *refs):
    own_ref, send_ref = refs[-2:]
    tokens = own_ref.shape[0]
    dot = dot_nt if transposed else dot_nn

    def total(start):
        rows = pl.ds(start, tokens)
        result = dot(refs[0][rows, :], refs[count][...])
        for i in range(1, count):
            result = result + dot(refs[i][rows, :], refs[count + i][...])
        return result

    own_ref[...] = total(0)
    send_ref[...] = total(tokens).astype(bf16)


def back_pass(lefts, weights, transposed):
    tokens, depth = lefts[0].shape
    width = weights[0].shape[0 if transposed else 1]
    count = len(lefts)
    tile = min(512, width)
    if transposed:
        weight_spec = pl.BlockSpec((tile, depth), lambda i: (i, 0))
    else:
        weight_spec = pl.BlockSpec((depth, tile), lambda i: (0, i))
    out = pl.BlockSpec((tokens // 2, tile), lambda i: (0, i))
    return pl.pallas_call(
        partial(back_kernel, count, transposed),
        grid=(width // tile,),
        in_specs=[pl.BlockSpec((tokens, depth), lambda i: (0, 0))] * count
        + [weight_spec] * count,
        out_specs=[out, out],
        out_shape=[
            jax.ShapeDtypeStruct((tokens // 2, width), f32),
            jax.ShapeDtypeStruct((tokens // 2, width), bf16),
        ],
        compiler_params=pltpu.CompilerParams(vmem_limit_bytes=VMEM_LIMIT),
        name="back_pass",
        cost_estimate=LIGHT,
    )(*lefts, *weights)


def weight_kernel(left_count, *refs):
    lefts, rights, out_ref = refs[:left_count], refs[left_count:-1], refs[-1]
    step = min(lefts[0].shape[0], rights[0].shape[0])

    def piece(refs, start):
        index, offset = divmod(start, refs[0].shape[0])
        return refs[index][pl.ds(offset, step), :]

    total = None
    for start in range(0, left_count * lefts[0].shape[0], step):
        term = dot_tn(piece(lefts, start), piece(rights, start))
        total = term if total is None else total + term
    out_ref[...] = total.astype(bf16)


def weight_pass(lefts, rights):
    rows, columns = lefts[0].shape[1], rights[0].shape[1]
    tile = 512 if rows % 512 == 0 else 384 if rows % 384 == 0 else rows
    return pl.pallas_call(
        partial(weight_kernel, len(lefts)),
        grid=(rows // tile,),
        in_specs=[pl.BlockSpec((left.shape[0], tile), lambda i: (0, i)) for left in lefts]
        + [pl.BlockSpec(right.shape, lambda i: (0, 0)) for right in rights],
        out_specs=pl.BlockSpec((tile, columns), lambda i: (i, 0)),
        out_shape=jax.ShapeDtypeStruct((rows, columns), bf16),
        compiler_params=pltpu.CompilerParams(vmem_limit_bytes=VMEM_LIMIT),
        name="weight_pass",
        cost_estimate=LIGHT,
    )(*lefts, *rights)


def placed_kernel(side_ref, own_ref, other_ref, out_ref):
    mine = pl.program_id(0) == side_ref[0]

    @pl.when(mine)
    def _():
        out_ref[0, 0] = own_ref[:, 0]

    @pl.when(jnp.logical_not(mine))
    def _():
        out_ref[0, 0] = other_ref[:, 0]


def placed(own, other, side):
    seq, group, rows, columns = own.shape

    def entry(mine, e, g, s):
        parked = jnp.where(e == 0, 0, group - 1)
        return (0, jnp.where((e == s[0]) == mine, g, parked), 0, 0)

    return pl.pallas_call(
        placed_kernel,
        grid_spec=pltpu.PrefetchScalarGridSpec(
            num_scalar_prefetch=1,
            grid=(2, group),
            in_specs=[
                pl.BlockSpec((seq, 1, rows, columns), partial(entry, True)),
                pl.BlockSpec((seq, 1, rows, columns), partial(entry, False)),
            ],
            out_specs=pl.BlockSpec(
                (1, 1, seq, rows, columns), lambda e, g, s: (e, g, 0, 0, 0)
            ),
        ),
        out_shape=jax.ShapeDtypeStruct((2, group, seq, rows, columns), own.dtype),
        name="placed",
        cost_estimate=LIGHT,
    )(side.astype(jnp.int32).reshape(1), own, other)


def joined_kernel(side_ref, own_ref, other_ref, out_ref):
    mine = pl.program_id(1) == side_ref[0]

    @pl.when(mine)
    def _():
        out_ref[:, 0] = own_ref[...]

    @pl.when(jnp.logical_not(mine))
    def _():
        out_ref[:, 0] = other_ref[...]


def joined(own, other, side, axis):
    shape = own.shape[:axis] + (2,) + own.shape[axis:]
    columns = own.shape[-1]
    lead = math.prod(own.shape[:axis])
    rows = math.prod(own.shape[axis:-1])
    leads, chunks = lead, 1
    while leads % 2 == 0 and leads * rows * columns > 800_000:
        leads //= 2
    while leads == 1 and rows % (32 * chunks) == 0 and rows // chunks * columns > 800_000:
        chunks *= 2
    block = rows // chunks

    def entry(mine, p, e, i, s):
        parked = jnp.where(e == 0, 0, chunks - 1)
        return (p, jnp.where((e == s[0]) == mine, i, parked), 0)

    return pl.pallas_call(
        joined_kernel,
        grid_spec=pltpu.PrefetchScalarGridSpec(
            num_scalar_prefetch=1,
            grid=(lead // leads, 2, chunks),
            in_specs=[
                pl.BlockSpec((leads, block, columns), partial(entry, True)),
                pl.BlockSpec((leads, block, columns), partial(entry, False)),
            ],
            out_specs=pl.BlockSpec((leads, 1, block, columns), lambda p, e, i, s: (p, e, i, 0)),
        ),
        out_shape=jax.ShapeDtypeStruct((lead, 2, rows, columns), own.dtype),
        compiler_params=pltpu.CompilerParams(vmem_limit_bytes=VMEM_LIMIT),
        name="joined",
        cost_estimate=LIGHT,
    )(
        side.astype(jnp.int32).reshape(1),
        own.reshape(lead, rows, columns),
        other.reshape(lead, rows, columns),
    ).reshape(shape)


def swap(values, bit):
    pairs = [(i, i ^ bit) for i in range(lax.axis_size("rows"))]
    return lax.ppermute(values, "rows", pairs)


def bit_of(bit):
    return (lax.axis_index("rows") // bit) % 2


def gather_bit(values, bit, axis):
    return joined(values, swap(values, bit), bit_of(bit), axis)


def part(values, index, axis):
    return lax.dynamic_index_in_dim(values, index, axis, keepdims=False)


def reduce_bit(values, bit, axis):
    return add_bit(values, pass_bit(values, bit, axis), bit, axis)


def outer_pairs(step, low, high):
    size = lax.axis_size("rows")
    return [
        (i, i + 4 * step)
        for i in range(size)
        if low <= i // 4 < high and 0 <= i // 4 + step < size // 4
    ]


def send_outer(values):
    count = lax.axis_size("rows") // 4
    if count == 2:
        return (swap(values, 4),)
    up, down = values, values
    ups, downs = [], []
    for t in range(1, count):
        up = lax.ppermute(up, "rows", outer_pairs(1, t - 1, count))
        down = lax.ppermute(down, "rows", outer_pairs(-1, 0, count - t + 1))
        ups.append(up)
        downs.append(down)
    return tuple(ups[::-1] + downs)


def join_outer(values, received, axis):
    count = lax.axis_size("rows") // 4
    if count == 2:
        return joined(values, received[0], bit_of(4), axis)
    place = lax.axis_index("rows") // 4
    line = jnp.stack([*received[: count - 1], values, *received[count - 1 :]], axis)
    return lax.dynamic_slice_in_dim(line, count - 1 - place, count, axis)


def gather_outer(values, axis):
    return join_outer(values, send_outer(values), axis)


def pass_outer(values, axis):
    count = lax.axis_size("rows") // 4
    place = lax.axis_index("rows") // 4

    def entry(index):
        return part(values, jnp.clip(index, 0, count - 1), axis)

    if count == 1:
        return ()
    if count == 2:
        return (swap(entry(1 - place), 4),)
    up, down = entry(place + count - 1), entry(place - count + 1)
    for t in range(1, count):
        up = lax.ppermute(up, "rows", outer_pairs(1, 0, t))
        down = lax.ppermute(down, "rows", outer_pairs(-1, count - t, count))
        if t < count - 1:
            up = (entry(place + count - 1 - t).astype(f32) + up.astype(f32)).astype(bf16)
            down = (entry(place - count + 1 + t).astype(f32) + down.astype(f32)).astype(bf16)
    return (up, down)


def add_outer(values, received, axis):
    total = part(values, lax.axis_index("rows") // 4, axis).astype(f32)
    for term in received:
        total = total + term.astype(f32)
    return total.astype(bf16)


def reduce_outer(values, axis):
    return add_outer(values, pass_outer(values, axis), axis)


def pass_bit(values, bit, axis):
    return swap(part(values, 1 - bit_of(bit), axis), bit)


def add_bit(values, received, bit, axis):
    own = part(values, bit_of(bit), axis)
    return (own.astype(f32) + received.astype(f32)).astype(bf16)


def gather_seq(values):
    return lax.all_gather(values, "seq", axis=0, tiled=False)


def reduce_seq(values):
    return lax.psum_scatter(values, "seq", scatter_dimension=0, tiled=False)


def exchange(values, axis, bit):
    size = lax.axis_size(axis)
    return lax.ppermute(values, axis, [(i, i ^ bit) for i in range(size)])


def across_group(own, send):
    return (own + swap(send, 1).astype(f32)).astype(bf16)


def stage(*values):
    return lax.optimization_barrier(values)


def mm(left, right):
    return jnp.einsum("ab,bc->ac", left, right, preferred_element_type=f32)


def mm_t(left, right):
    return jnp.einsum("ab,cb->ac", left, right, preferred_element_type=f32)


def t_mm(left, right):
    return jnp.einsum("ab,ac->bc", left, right, preferred_element_type=f32)


def norm_scale(values):
    return lax.rsqrt(jnp.mean(values * values, axis=-1, keepdims=True) + EPSILON)


def norm_backward(values, scale, gain, grad):
    gained = grad * gain
    inner = jnp.mean(values * gained, axis=-1, keepdims=True)
    result = scale * gained - values * (scale * scale * scale) * inner
    return result, jnp.sum(grad * values * scale, axis=0)


def shards(
    tokens_in,
    corpus,
    corpus_weight,
    w_qkv,
    w_out,
    w_gate,
    w_up,
    w_down,
    attn_gain,
    ffn_gain,
    q_gain,
    k_gain,
    upstream,
):
    shard_length, width = tokens_in.shape[1:]
    row_devices = lax.axis_size("rows")
    seq_devices = lax.axis_size("seq")
    outer = row_devices // 4
    d_rows = w_qkv.shape[0]
    f_rows = w_down.shape[0]
    place = lax.axis_index("seq").astype(jnp.int32)
    inputs = tokens_in[0].astype(f32)

    extra = jnp.stack(
        [
            attn_gain,
            ffn_gain,
            jnp.broadcast_to(corpus.astype(bf16), attn_gain.shape),
        ],
        axis=1,
    )
    extra = jnp.pad(extra, ((0, 0), (0, LANES - extra.shape[1])))
    kv_shard = jnp.concatenate([w_qkv[:, QUERY_COLUMNS:], extra], axis=1)
    query_shard = jnp.concatenate([w_qkv[:, :QUERY_COLUMNS], w_out.T], axis=1)
    query_shard, w_gate, w_up = stage(query_shard, w_gate, w_up)
    query_lines = gather_seq(query_shard)

    def to_group(weight):
        blocks = weight.reshape(d_rows, outer, 4, seq_devices, f_rows)
        blocks = jnp.transpose(blocks, (2, 0, 3, 1, 4))
        return blocks.reshape(2, 2, d_rows, outer * seq_devices * f_rows)

    def spread_hidden(lines, received):
        if outer == 2:
            lines = lines.reshape(seq_devices, 4, d_rows, hidden_columns)
            other = received[0].reshape(lines.shape)
            return placed(lines, other, bit_of(4)).reshape(width, hidden_columns)
        full = join_outer(lines, received, 0)
        return jnp.moveaxis(full, 1, 3).reshape(width, hidden_columns)

    gate_up = jnp.stack([to_group(w_gate), to_group(w_up)], axis=2)
    hidden_columns = gate_up.shape[-1]
    core, near = bit_of(1), bit_of(2)
    gate_up = joined(
        part(gate_up, core, 1), swap(part(gate_up, 1 - core, 1), 1), core, 1
    )
    gate_up, kv_shard = stage(gate_up, kv_shard)
    other, kv_lines, query_lines = stage(
        swap(part(gate_up, 1 - near, 0), 2), gather_seq(kv_shard), query_lines
    )
    gate_up = joined(part(gate_up, near, 0), other, near, 0)
    gate_lines = gather_seq(gate_up[:, :, 0])
    left, right = kv_lines[..., : 3 * LANES], kv_lines[..., 3 * LANES :]
    left_other, right_other = stage(send_outer(left), swap(right, 2))
    left = join_outer(left, left_other, 0)
    right = joined(right, right_other, near, 0)
    left_other, right_other = stage(swap(left, 2), send_outer(right))
    left = joined(left, left_other, near, 1)
    right = join_outer(right, right_other, 0)
    q_left, q_right = query_lines[..., :QUERY_COLUMNS], query_lines[..., QUERY_COLUMNS:]
    q_left, q_right, left, right = stage(q_left, q_right, left, right)
    q_left_other, q_right_other = send_outer(q_left), swap(q_right, 2)
    left, right = gather_bit(left, 1, 2), gather_bit(right, 1, 2)
    left, right = left.reshape(width, -1), right.reshape(width, -1)
    wkv = jnp.concatenate([left, right[:, : 2 * LANES]], axis=1)
    rows = dot_nt(jnp.eye(8, LANES, dtype=bf16), right[:, 2 * LANES :])
    attn_gain_full, ffn_gain_full, corpus_full = rows[0:1], rows[1:2], rows[2]

    position = (place * shard_length + jnp.arange(shard_length, dtype=jnp.int32)).astype(f32)
    half = HEAD_SIZE // 2
    exponent = jnp.arange(half, dtype=f32) * (-2.0 / HEAD_SIZE)
    angles = position[:, None] * jnp.power(ROPE_BASE, exponent)[None, :]
    cosine, sine = jnp.cos(angles), jnp.sin(angles)
    cos_table = jnp.concatenate([cosine] * 4, axis=1)
    sin_table = jnp.concatenate([-sine, sine] * 2, axis=1)
    wide_q = jnp.tile(q_gain.astype(f32), QUERY_HEADS)
    wide_k = jnp.concatenate(
        [jnp.tile(k_gain.astype(f32), KEY_VALUE_HEADS), jnp.ones((KEY_COLUMNS,), f32)]
    )
    wide_q = jnp.broadcast_to(wide_q[None, :], (8, QUERY_COLUMNS))
    wide_k = jnp.broadcast_to(wide_k[None, :], (8, 2 * KEY_COLUMNS))

    in_scale = norm_scale(inputs)
    normed = (inputs * in_scale * attn_gain_full).astype(bf16)
    joint_kv, own_kv = heads_forward(
        normed, wkv, wide_k, cos_table, sin_table, KEY_COLUMNS
    )
    own_kv, q_left_other, q_right_other, down_other, up_in = stage(
        own_kv, q_left_other, q_right_other, send_outer(w_down), gate_up[:, :, 1]
    )
    up_lines = gather_seq(up_in)
    keys_values = gather_seq(own_kv).reshape(-1, 2 * KEY_COLUMNS)
    q_left = join_outer(q_left, q_left_other, 0)
    q_right = joined(q_right, q_right_other, near, 0)
    left_other, right_other, gate_lines = stage(
        swap(q_left, 2), send_outer(q_right), gate_lines
    )
    q_left = joined(q_left, left_other, near, 1)
    gate_other = send_outer(gate_lines)
    wq = gather_bit(q_left, 1, 2).reshape(width, -1)

    corpora = jnp.arange(CORPORA, dtype=jnp.int32)
    per_device = corpus_full.reshape(-1, d_rows)[:, 0].astype(jnp.int32)
    counts = (
        jnp.sum((per_device[:, None] == corpora[None, :]).astype(f32), axis=0) * shard_length
    )
    own_corpus = (corpus[0] == corpora).astype(f32)
    weight_row = jnp.sum(own_corpus * corpus_weight.astype(f32))
    count_row = jnp.sum(own_corpus * counts)
    factor = weight_row / DENOM * (jnp.sum(counts) / (CORPORA * count_row))
    grad_full = upstream[0].astype(f32) * factor
    grad_top, wq = stage(grad_full.astype(bf16), wq)

    joint_q, queries = heads_forward(
        normed, wq, wide_q, cos_table, sin_table, QUERY_COLUMNS
    )
    queries, q_right, right_other, down_other = stage(queries, q_right, right_other, down_other)
    q_right = join_outer(q_right, right_other, 0)
    down_pair = join_outer(w_down, down_other, 0)
    place_array = place.reshape(1)
    keys_values, queries, down_in = stage(keys_values, queries, down_pair)
    down_lines = gather_seq(down_in)
    mixed, logs = attend_forward(place_array, queries, keys_values)
    mixed, grad_top1, grad_top2, up_lines, wout_other = stage(
        mixed, swap(grad_top, 1), swap(grad_top, 2), up_lines, swap(q_right, 1)
    )
    wout_t = joined(q_right, wout_other, core, 2).reshape(width, -1)
    middle = inputs + mm_t(mixed, wout_t)

    ffn_scale = norm_scale(middle)
    normed_ffn = (middle * ffn_scale * ffn_gain_full).astype(bf16)
    up_other = send_outer(up_lines)
    normed_ffn, gate_other = stage(normed_ffn, gate_other)
    normed1, normed2, up_other, wgate = stage(
        swap(normed_ffn, 1),
        swap(normed_ffn, 2),
        up_other,
        spread_hidden(gate_lines, gate_other),
    )
    wup = spread_hidden(up_lines, up_other)
    hidden_near, gate_near, up_near = hidden_pass((normed_ffn, normed1), wgate, wup)
    normed3, hidden_near, grad_top3 = stage(
        swap(normed2, 1), hidden_near, swap(grad_top2, 1)
    )
    hidden_far, gate_far, up_far = hidden_pass((normed2, normed3), wgate, wup)
    normed4 = (normed_ffn, normed1, normed2, normed3)
    grad_top4 = (grad_top, grad_top1, grad_top2, grad_top3)
    wdown = down_lines.reshape(hidden_columns, width)
    gate_far, up_far = gates_pass((grad_top2, grad_top3), wdown, gate_far, up_far)
    own, send = back_pass((gate_far, up_far), (wgate, wup), True)
    grad_wdown = weight_pass((hidden_near, hidden_far), grad_top4)
    own, send, grad_wdown, wdown = stage(own, swap(send, 1), grad_wdown, wdown)
    across = (own + send.astype(f32)).astype(bf16)
    across, wdown = stage(across, wdown)
    gate_near, up_near = gates_pass((grad_top, grad_top1), wdown, gate_near, up_near)
    own, send = back_pass((gate_near, up_near), (wgate, wup), True)
    hidden_shape = (outer, 2, 2, seq_devices, d_rows, hidden_columns)
    grad_wdown = grad_wdown.reshape(seq_devices, outer, f_rows, width)
    grad_wgate = weight_pass(normed4, (gate_near, gate_far)).reshape(hidden_shape)
    across, own, send, grad_wgate, up_near = stage(
        swap(across, 2), own, send, grad_wgate, up_near
    )
    grad_wup = weight_pass(normed4, (up_near, up_far)).reshape(hidden_shape)
    send, grad_wup, down_other = stage(swap(send, 1), grad_wup, pass_outer(grad_wdown, 1))
    grad_wdown = add_outer(grad_wdown, down_other, 1)
    own = own + send.astype(f32)
    grad_normed_ffn = own + across.astype(f32)
    grad_wdown = reduce_seq(grad_wdown)

    grad_middle_part, grad_ffn_gain = norm_backward(
        middle, ffn_scale, ffn_gain_full, grad_normed_ffn
    )
    grad_middle = grad_full + grad_middle_part
    grad_branch = grad_middle.astype(bf16)
    grad_mixed = mm(grad_branch, wout_t).astype(bf16)
    attend = (place_array, queries, keys_values, mixed, logs)
    grad_q1, grad_kv1 = attend_backward(0, 2, *attend, grad_mixed)
    grad_q1, grad_kv1, gate_other, grad_mixed, grad_wdown, hidden_far = stage(
        grad_q1, grad_kv1, pass_outer(grad_wgate, 0), grad_mixed, grad_wdown, hidden_far
    )
    grad_kv1 = reduce_seq(grad_kv1.reshape(seq_devices, shard_length, -1))
    grad_gate = reduce_seq(jnp.moveaxis(add_outer(grad_wgate, gate_other, 0), 2, 0))
    shape = (outer, 2, 2, seq_devices, d_rows)
    own_far, send_far = back_pass((hidden_far,), (wdown,), False)
    grad_wout, far_other, grad_mixed = stage(
        t_mm(grad_branch, mixed).astype(bf16).reshape(*shape, QUERY_COLUMNS),
        swap(send_far, 1),
        grad_mixed,
    )
    across = (own_far + far_other.astype(f32)).astype(bf16)
    across, grad_mixed = stage(across, grad_mixed)
    grad_q2, grad_kv2 = attend_backward(2, 3, *attend, grad_mixed)
    grad_q2, grad_kv2, hidden_near, grad_kv1, grad_gate, wout_other, up_other, across = stage(
        grad_q2,
        grad_kv2,
        hidden_near,
        grad_kv1,
        grad_gate,
        pass_bit(grad_wout, 1, 2),
        pass_outer(grad_wup, 0),
        swap(across, 2),
    )
    grad_kv2 = reduce_seq(grad_kv2.reshape(seq_devices, shard_length, -1))

    grad_q = jnp.concatenate([grad_q1, grad_q2], axis=1)
    joint_grad_q, gain_q = heads_backward(
        grad_q, joint_q, wide_q, cos_table, sin_table, QUERY_COLUMNS
    )
    grad_wq = t_mm(normed, joint_grad_q).astype(bf16).reshape(*shape, QUERY_COLUMNS)
    grad_wout = add_bit(grad_wout, wout_other, 1, 2)
    own_near, send_near = back_pass((hidden_near,), (wdown,), False)
    grad_up = jnp.moveaxis(add_outer(grad_wup, up_other, 0), 2, 0)
    grad_kv2, joint_grad_q, grad_wq, grad_wout, own_near, send_near, grad_up = stage(
        grad_kv2, joint_grad_q, grad_wq, grad_wout, own_near, send_near, grad_up
    )
    grad_up = reduce_seq(grad_up)


    grad_kv1, grad_kv2 = (
        part_.reshape(shard_length, 2, -1) for part_ in (grad_kv1, grad_kv2)
    )
    grad_kv = jnp.concatenate([grad_kv1, grad_kv2], axis=2).reshape(shard_length, -1)
    joint_grad_kv, gain_k = heads_backward(
        grad_kv, joint_kv, wide_k, cos_table, sin_table, KEY_COLUMNS
    )
    wq_other, near_other, joint_grad_kv = stage(
        pass_bit(grad_wq, 1, 2), swap(send_near, 1), joint_grad_kv
    )
    grad_wkv, grad_wq, grad_wout = stage(
        t_mm(normed, joint_grad_kv).astype(bf16), add_bit(grad_wq, wq_other, 1, 2), grad_wout
    )
    wq_other, wout_other = pass_bit(grad_wq, 2, 1), pass_outer(grad_wout, 0)
    output = (middle + own_near + near_other.astype(f32) + across.astype(f32)).astype(bf16)
    grad_normed = mm_t(joint_grad_q, wq) + mm_t(joint_grad_kv, wkv)
    grad_input_part, grad_attn_gain = norm_backward(
        inputs, in_scale, attn_gain_full, grad_normed
    )
    input_grad = (grad_middle + grad_input_part).astype(bf16)

    gain_rows = jnp.stack([grad_attn_gain, grad_ffn_gain]).astype(bf16)
    gain_columns = t_mm(gain_rows, jnp.eye(2, LANES, dtype=bf16)).astype(bf16)
    left = grad_wkv[:, : 3 * LANES].reshape(*shape, -1)
    right = jnp.concatenate([grad_wkv[:, 3 * LANES :], gain_columns], axis=1)
    right = right.reshape(*shape, -1)
    head_gains = jnp.concatenate(
        [
            jnp.sum(gain_q[0].reshape(-1, HEAD_SIZE), axis=0),
            jnp.sum(gain_k[0, :KEY_COLUMNS].reshape(-1, HEAD_SIZE), axis=0),
        ]
    )[None]
    left, right, left_other, right_other, wq_other, wout_other, gains_other = stage(
        left,
        right,
        pass_bit(left, 1, 2),
        pass_bit(right, 1, 2),
        wq_other,
        wout_other,
        exchange(head_gains, "rows", 1),
    )
    head_gains = head_gains + gains_other
    left = add_bit(left, left_other, 1, 2)
    right = add_bit(right, right_other, 1, 2)
    grad_wq = add_bit(grad_wq, wq_other, 2, 1)
    grad_wout = add_outer(grad_wout, wout_other, 0)
    left_other, right_other, wq_other, wout_other, gains_other, grad_up = stage(
        pass_bit(left, 2, 1),
        pass_outer(right, 0),
        pass_outer(grad_wq, 0),
        pass_bit(grad_wout, 2, 0),
        exchange(head_gains, "seq", 1),
        grad_up,
    )
    head_gains = head_gains + gains_other
    left = add_bit(left, left_other, 2, 1)
    right = add_outer(right, right_other, 0)
    left_other, right_other, gains_other = stage(
        pass_outer(left, 0), pass_bit(right, 2, 0), exchange(head_gains, "rows", 2)
    )
    head_gains = head_gains + gains_other
    sums = reduce_seq(
        jnp.concatenate(
            [
                add_outer(grad_wq, wq_other, 0),
                add_outer(left, left_other, 0),
                add_bit(right, right_other, 2, 0),
                add_bit(grad_wout, wout_other, 2, 0),
            ],
            axis=-1,
        )
    )
    rest = [("rows", bit) for bit in (4, 8, 16) if bit < row_devices]
    rest += [("seq", bit) for bit in (2, 4, 8) if bit < seq_devices]
    gate_up = jnp.stack([grad_gate, grad_up], axis=2)
    other, gains_other = stage(
        swap(part(gate_up, 1 - near, 0), 2), exchange(head_gains, *rest[0])
    )
    head_gains = head_gains + gains_other
    grads = joined(part(gate_up, near, 0), other, near, 0)
    for axis, bit in rest[1:]:
        head_gains = head_gains + exchange(head_gains, axis, bit)
    head_gains = head_gains[0]
    grads = joined(part(grads, core, 1), swap(part(grads, 1 - core, 1), 1), core, 1)

    def from_group(blocks):
        blocks = blocks.reshape(4, d_rows, seq_devices, outer, f_rows)
        return jnp.transpose(blocks, (1, 3, 0, 2, 4)).reshape(d_rows, -1)

    grad_wgate, grad_wup = stage(from_group(grads[:, :, 0]), from_group(grads[:, :, 1]))
    sums, grad_wgate, grad_wup, grad_wdown, output, input_grad = stage(
        sums, grad_wgate.astype(f32), grad_wup.astype(f32), grad_wdown.astype(f32), output, input_grad
    )
    columns = QUERY_COLUMNS + 2 * KEY_COLUMNS
    long_gains = sums[:, columns : columns + 2].astype(f32)
    return (
        output[None],
        input_grad[None],
        sums[:, :columns].astype(f32),
        sums[:, columns + LANES :].T.astype(f32),
        grad_wgate,
        grad_wup,
        grad_wdown,
        long_gains[:, 0],
        long_gains[:, 1],
        head_gains[:HEAD_SIZE],
        head_gains[HEAD_SIZE:],
    )


def solution(mesh):
    return jax.shard_map(
        shards,
        mesh=mesh,
        in_specs=(
            P("rows", "seq", None),
            P("rows"),
            P(),
            P(("rows", "seq"), None),
            P(None, ("rows", "seq")),
            P(("rows", "seq"), None),
            P(("rows", "seq"), None),
            P(("rows", "seq"), None),
            P(("rows", "seq")),
            P(("rows", "seq")),
            P(),
            P(),
            P("rows", "seq", None),
        ),
        out_specs=(
            P("rows", "seq", None),
            P("rows", "seq", None),
            P(("rows", "seq"), None),
            P(None, ("rows", "seq")),
            P(("rows", "seq"), None),
            P(("rows", "seq"), None),
            P(("rows", "seq"), None),
            P(("rows", "seq")),
            P(("rows", "seq")),
            P(),
            P(),
        ),
        check_vma=False,
    )
```

```python
import math
from functools import partial

import jax
import jax.numpy as jnp
from jax import lax
from jax.experimental import pallas as pl
from jax.experimental.pallas import tpu as pltpu
from jax.sharding import PartitionSpec as P

QUERY_HEADS = 20
KEY_VALUE_HEADS = 5
HEAD_SIZE = 64
CORPORA = 8
DENOM = 64
EPSILON = 1e-06
ROPE_BASE = 10000.0
QUERY_COLUMNS = QUERY_HEADS * HEAD_SIZE
KEY_COLUMNS = KEY_VALUE_HEADS * HEAD_SIZE
LANES = 128
SCORE_EXPONENT = 1.4426950408889634 * HEAD_SIZE**-0.5
SPLIT = 2
VMEM_LIMIT = 48 * 1024 * 1024

f32, bf16 = jnp.float32, jnp.bfloat16
LIGHT = pl.CostEstimate(flops=1000, bytes_accessed=1000, transcendentals=0)


def dot_nn(a, b):
    return lax.dot_general(a, b, (((1,), (0,)), ((), ())), preferred_element_type=f32)


def dot_nt(a, b):
    return lax.dot_general(a, b, (((1,), (1,)), ((), ())), preferred_element_type=f32)


def dot_tn(a, b):
    return lax.dot_general(a, b, (((0,), (0,)), ((), ())), preferred_element_type=f32)


def lanes_of(shape):
    return lax.broadcasted_iota(jnp.int32, shape, len(shape) - 1)


def head_sum(values):
    row = lax.broadcasted_iota(jnp.int32, (LANES, LANES), 0) // HEAD_SIZE
    column = lax.broadcasted_iota(jnp.int32, (LANES, LANES), 1) // HEAD_SIZE
    ones = jnp.where(row == column, 1.0, 0.0).astype(bf16)
    high = values.astype(bf16)
    low = (values - high.astype(f32)).astype(bf16)
    return dot_nn(high, ones) + dot_nn(low, ones)


def partner(values):
    first = lanes_of(values.shape) % HEAD_SIZE < HEAD_SIZE // 2
    return jnp.where(
        first,
        pltpu.roll(values, LANES - HEAD_SIZE // 2, 1),
        pltpu.roll(values, HEAD_SIZE // 2, 1),
    )


def heads_forward_kernel(
    norm_columns, normed_ref, weight_ref, gain_ref, cos_ref, sin_ref, joint_ref, out_ref
):
    joint = dot_nn(normed_ref[...], weight_ref[...])
    joint_ref[...] = joint
    columns = joint.shape[1]
    for start in range(0, columns, LANES):
        chunk = slice(start, start + LANES)
        values = joint[:, chunk]
        scale = lax.rsqrt(head_sum(values * values) * (1.0 / HEAD_SIZE) + EPSILON)
        normed = values * scale * gain_ref[0:1, chunk]
        turned = normed * cos_ref[...] + partner(normed) * sin_ref[...]
        place = pl.program_id(0) * columns + start + lanes_of(values.shape)
        out_ref[:, chunk] = jnp.where(place < norm_columns, turned, values).astype(bf16)


def heads_forward(normed, weight, gain, cos, sin, norm_columns):
    tokens, width = normed.shape
    columns = weight.shape[1]
    tile = 2 * LANES if columns % (2 * LANES) == 0 else LANES
    out = pl.BlockSpec((tokens, tile), lambda i: (0, i))
    table = pl.BlockSpec((tokens, LANES), lambda i: (0, 0))
    return pl.pallas_call(
        partial(heads_forward_kernel, norm_columns),
        grid=(columns // tile,),
        in_specs=[
            pl.BlockSpec((tokens, width), lambda i: (0, 0)),
            pl.BlockSpec((width, tile), lambda i: (0, i)),
            pl.BlockSpec((8, tile), lambda i: (0, i)),
            table,
            table,
        ],
        out_specs=[out, out],
        out_shape=[
            jax.ShapeDtypeStruct((tokens, columns), f32),
            jax.ShapeDtypeStruct((tokens, columns), bf16),
        ],
        compiler_params=pltpu.CompilerParams(vmem_limit_bytes=VMEM_LIMIT),
        name="heads_forward",
        cost_estimate=LIGHT,
    )(normed, weight, gain, cos, sin)


def heads_backward_kernel(
    norm_columns, grad_ref, joint_ref, gain_ref, cos_ref, sin_ref, out_ref, gain_out_ref
):
    grad = grad_ref[...].astype(f32)
    values = joint_ref[...]
    gain = gain_ref[0:1, :]
    turned = grad * cos_ref[...] - partner(grad) * sin_ref[...]
    scale = lax.rsqrt(head_sum(values * values) * (1.0 / HEAD_SIZE) + EPSILON)
    gained = turned * gain
    inner = head_sum(values * gained) * (1.0 / HEAD_SIZE)
    result = scale * gained - values * (scale * scale * scale) * inner
    place = pl.program_id(0) * LANES + lanes_of(values.shape)
    out_ref[...] = jnp.where(place < norm_columns, result, grad).astype(bf16)
    gain_out_ref[...] = jnp.broadcast_to(
        jnp.sum(turned * values * scale, axis=0, keepdims=True), gain_out_ref.shape
    )


def heads_backward(grad, joint, gain, cos, sin, norm_columns):
    tokens, columns = joint.shape
    return pl.pallas_call(
        partial(heads_backward_kernel, norm_columns),
        grid=(columns // LANES,),
        in_specs=[
            pl.BlockSpec((tokens, LANES), lambda i: (0, i)),
            pl.BlockSpec((tokens, LANES), lambda i: (0, i)),
            pl.BlockSpec((8, LANES), lambda i: (0, i)),
            pl.BlockSpec((tokens, LANES), lambda i: (0, 0)),
            pl.BlockSpec((tokens, LANES), lambda i: (0, 0)),
        ],
        out_specs=[
            pl.BlockSpec((tokens, LANES), lambda i: (0, i)),
            pl.BlockSpec((8, LANES), lambda i: (0, i)),
        ],
        out_shape=[
            jax.ShapeDtypeStruct((tokens, columns), bf16),
            jax.ShapeDtypeStruct((8, columns), f32),
        ],
        name="heads_backward",
        cost_estimate=LIGHT,
    )(grad, joint, gain, cos, sin)


def both_halves(pair, odd):
    wide = pair.astype(f32)
    first = lanes_of(wide.shape) < HEAD_SIZE
    keep = jnp.where(odd == 1, jnp.where(first, 0, 1), jnp.where(first, 1, 0)) == 1
    return jnp.where(keep, wide, pltpu.roll(wide, HEAD_SIZE, 1))


def attend_forward_kernel(place_ref, q_ref, k_ref, v_ref, out_ref, log_ref):
    group = pl.program_id(0) // 2
    place = place_ref[0]
    tokens = q_ref.shape[0]
    first = lanes_of((tokens, LANES)) < HEAD_SIZE
    pair = q_ref[...].astype(f32)
    queries = (jnp.where(first, pair, 0.0).astype(bf16), jnp.where(first, 0.0, pair).astype(bf16))

    def step(j, totals, diagonal):
        rows = pl.ds(pl.multiple_of(j * tokens, tokens), tokens)
        keys = both_halves(k_ref[rows, :], group % 2).astype(bf16)
        values = both_halves(v_ref[rows, :], (KEY_VALUE_HEADS + group) % 2)
        sides = (
            jnp.where(first, values, 1.0).astype(bf16),
            jnp.where(first, 1.0, values).astype(bf16),
        )
        result = []
        for head in range(2):
            weights = jnp.exp2(dot_nt(queries[head], keys) * SCORE_EXPONENT)
            if diagonal:
                row = lax.broadcasted_iota(jnp.int32, weights.shape, 0)
                weights = jnp.where(lanes_of(weights.shape) <= row, weights, 0.0)
            result.append(totals[head] + dot_nn(weights.astype(bf16), sides[head]))
        return tuple(result)

    zero = jnp.zeros((tokens, LANES), f32)
    totals = lax.fori_loop(0, place, lambda j, c: step(j, c, False), (zero, zero))
    totals = step(place, totals, True)
    numerator = jnp.where(first, totals[0], totals[1])
    swapped = jnp.where(first, totals[1], totals[0])
    out_ref[...] = (numerator / pltpu.roll(swapped, HEAD_SIZE, 1)).astype(bf16)
    log_ref[...] = jnp.log2(swapped)


def attend_forward(place, queries, keys_values):
    tokens = queries.shape[0]
    length = keys_values.shape[0]
    pairs = QUERY_COLUMNS // LANES
    return pl.pallas_call(
        attend_forward_kernel,
        grid_spec=pltpu.PrefetchScalarGridSpec(
            num_scalar_prefetch=1,
            grid=(pairs,),
            in_specs=[
                pl.BlockSpec((tokens, LANES), lambda i, s: (0, i)),
                pl.BlockSpec((length, LANES), lambda i, s: (0, (i // 2) // 2)),
                pl.BlockSpec((length, LANES), lambda i, s: (0, (KEY_VALUE_HEADS + i // 2) // 2)),
            ],
            out_specs=[
                pl.BlockSpec((tokens, LANES), lambda i, s: (0, i)),
                pl.BlockSpec((tokens, LANES), lambda i, s: (0, i)),
            ],
        ),
        out_shape=[
            jax.ShapeDtypeStruct((tokens, QUERY_COLUMNS), bf16),
            jax.ShapeDtypeStruct((tokens, QUERY_COLUMNS), f32),
        ],
        compiler_params=pltpu.CompilerParams(vmem_limit_bytes=VMEM_LIMIT),
        name="attend_forward",
        cost_estimate=LIGHT,
    )(place, queries, keys_values, keys_values)


def three_parts(values, lane):
    high = values.astype(bf16).astype(f32)
    rest = values - high
    middle = rest.astype(bf16).astype(f32)
    low = rest - middle
    return jnp.where(
        lane == 0, high, jnp.where(lane == 1, middle, jnp.where(lane == 2, low, 0.0))
    )


def attend_backward_kernel(
    first_group, count, place_ref, q_ref, k_ref, v_ref, out_ref, log_ref, grad_ref, dq_ref, dkv_ref, dk_sum, dv_sum
):
    pair_index = pl.program_id(0)
    local = pair_index // 2
    group = first_group + local
    place = place_ref[0]
    tokens = q_ref.shape[0]
    lane = lanes_of((tokens, LANES))
    first = lane < HEAD_SIZE
    inside = lane % HEAD_SIZE
    pair = q_ref[...].astype(f32)
    grad = grad_ref[...].astype(f32)
    delta = pltpu.roll(head_sum(grad * out_ref[...].astype(f32)), HEAD_SIZE, 1)
    logs = three_parts(log_ref[...] * (1.0 / SCORE_EXPONENT), inside)
    deltas = three_parts(delta, inside)
    minus = jnp.where(inside < 3, -1.0, 0.0)

    def sides(own, other):
        return (
            jnp.where(first, own, other).astype(bf16),
            jnp.where(first, other, own).astype(bf16),
        )

    queries = sides(pair, 0.0)
    grads = sides(grad, 0.0)
    def turned(values):
        return jnp.transpose(values.astype(f32)).astype(bf16)

    queries_log = tuple(turned(v) for v in sides(pair, logs))
    grads_delta = tuple(turned(v) for v in sides(grad, deltas))

    @pl.when(pair_index % 2 == 0)
    def _():
        dk_sum[...] = jnp.zeros_like(dk_sum)
        dv_sum[...] = jnp.zeros_like(dv_sum)

    def step(j, dq, diagonal):
        rows = pl.ds(pl.multiple_of(j * tokens, tokens), tokens)
        key_wide = both_halves(k_ref[rows, :], group % 2)
        value_wide = both_halves(v_ref[rows, :], (KEY_VALUE_HEADS + group) % 2)
        keys_turned = jnp.transpose(key_wide)[:HEAD_SIZE].astype(bf16)
        keys_log = sides(key_wide, minus)
        values_delta = sides(value_wide, minus)
        dk = dk_sum[rows, :]
        dv = dv_sum[rows, :]
        parts = list(dq)
        block = tokens // SPLIT
        for sub in range(SPLIT):
            keep = slice(sub * block, (sub + 1) * block)
            dk_part, dv_part = dk[keep], dv[keep]
            start = sub * block if diagonal else 0
            for head in range(2):
                weights = jnp.exp2(
                    dot_nn(keys_log[head][keep], queries_log[head][:, start:]) * SCORE_EXPONENT
                )
                if diagonal:
                    row = lax.broadcasted_iota(jnp.int32, weights.shape, 0)
                    weights = jnp.where(row <= lanes_of(weights.shape), weights, 0.0)
                grad_weights = dot_nn(values_delta[head][keep], grads_delta[head][:, start:])
                grad_scores = (weights * grad_weights).astype(bf16)
                dv_part = dv_part + dot_nn(weights.astype(bf16), grads[head][start:])
                dk_part = dk_part + dot_nn(grad_scores, queries[head][start:])
                term = dot_nn(keys_turned[:, keep], grad_scores)
                if start:
                    term = jnp.concatenate([jnp.zeros((HEAD_SIZE, start), f32), term], axis=1)
                parts[head] = parts[head] + term
            target = pl.ds(pl.multiple_of(j * tokens + sub * block, block), block)
            dk_sum[target, :] = dk_part
            dv_sum[target, :] = dv_part
        return tuple(parts)

    zero = jnp.zeros((HEAD_SIZE, tokens), f32)
    dq = lax.fori_loop(0, place, lambda j, c: step(j, c, False), (zero, zero))
    dq = jnp.transpose(jnp.concatenate(step(place, dq, True), axis=0))
    dq_ref[...] = (dq * HEAD_SIZE**-0.5).astype(bf16)

    @pl.when(pair_index % 2 == 1)
    def _():
        wide_lane = lanes_of(dk_sum.shape)
        for total, slot, factor in (
            (dk_sum, local, HEAD_SIZE**-0.5),
            (dv_sum, count + local, 1.0),
        ):
            both = (total[...] + pltpu.roll(total[...], HEAD_SIZE, 1)) * factor
            columns = pl.ds(pl.multiple_of(slot // 2 * LANES, LANES), LANES)
            mine = wide_lane // HEAD_SIZE == slot % 2
            dkv_ref[:, columns] = jnp.where(
                mine, both, dkv_ref[:, columns].astype(f32)
            ).astype(bf16)


def attend_backward(first, count, place, queries, keys_values, mixed, logs, grad_mixed):
    tokens = queries.shape[0]
    length = keys_values.shape[0]
    group = QUERY_HEADS // KEY_VALUE_HEADS * HEAD_SIZE
    own = pl.BlockSpec((tokens, LANES), lambda i, s: (0, 2 * first + i))
    keys = pl.BlockSpec((length, LANES), lambda i, s: (0, (first + i // 2) // 2))
    values = pl.BlockSpec(
        (length, LANES), lambda i, s: (0, (KEY_VALUE_HEADS + first + i // 2) // 2)
    )
    columns = 2 * count * HEAD_SIZE
    return pl.pallas_call(
        partial(attend_backward_kernel, first, count),
        grid_spec=pltpu.PrefetchScalarGridSpec(
            num_scalar_prefetch=1,
            grid=(2 * count,),
            in_specs=[own, keys, values, own, own, own],
            out_specs=[
                pl.BlockSpec((tokens, LANES), lambda i, s: (0, i)),
                pl.BlockSpec((length, columns), lambda i, s: (0, 0)),
            ],
            scratch_shapes=[pltpu.VMEM((length, LANES), f32), pltpu.VMEM((length, LANES), f32)],
        ),
        out_shape=[
            jax.ShapeDtypeStruct((tokens, count * group), bf16),
            jax.ShapeDtypeStruct((length, columns), bf16),
        ],
        compiler_params=pltpu.CompilerParams(vmem_limit_bytes=VMEM_LIMIT),
        name="attend_backward",
        cost_estimate=LIGHT,
    )(place, queries, keys_values, keys_values, mixed, logs, grad_mixed)


def hidden_kernel(n0_ref, n1_ref, wg_ref, wu_ref, hidden_ref, gate_ref, up_ref, n_all):
    tokens = n0_ref.shape[0]

    @pl.when(pl.program_id(0) == 0)
    def _():
        n_all[:tokens] = n0_ref[...]
        n_all[tokens:] = n1_ref[...]

    gate = dot_nn(n_all[...], wg_ref[...])
    up = dot_nn(n_all[...], wu_ref[...])
    hidden_ref[...] = (gate / (1.0 + jnp.exp(-gate)) * up).astype(bf16)
    gate_ref[...] = gate.astype(bf16)
    up_ref[...] = up.astype(bf16)


def hidden_pass(normed, wgate, wup):
    tokens, width = normed[0].shape
    columns = wgate.shape[1]
    tile = min(256, columns)
    whole = pl.BlockSpec((tokens, width), lambda i: (0, 0))
    down = pl.BlockSpec((width, tile), lambda i: (0, i))
    out = pl.BlockSpec((2 * tokens, tile), lambda i: (0, i))
    return pl.pallas_call(
        hidden_kernel,
        grid=(pl.cdiv(columns, tile),),
        in_specs=[whole] * 2 + [down] * 2,
        out_specs=[out] * 3,
        out_shape=[jax.ShapeDtypeStruct((2 * tokens, columns), bf16)] * 3,
        scratch_shapes=[pltpu.VMEM((2 * tokens, width), bf16)],
        compiler_params=pltpu.CompilerParams(vmem_limit_bytes=VMEM_LIMIT),
        name="hidden_pass",
        cost_estimate=LIGHT,
    )(*normed, wgate, wup)


def gates_kernel(g0_ref, g1_ref, wd_ref, gate_ref, up_ref, gate_out_ref, up_out_ref, g_all):
    tokens = g0_ref.shape[0]

    @pl.when(pl.program_id(0) == 0)
    def _():
        g_all[:tokens] = g0_ref[...]
        g_all[tokens:] = g1_ref[...]

    grad = dot_nt(g_all[...], wd_ref[...])
    gate = gate_ref[...].astype(f32)
    up = up_ref[...].astype(f32)
    sigmoid = 1.0 / (1.0 + jnp.exp(-gate))
    gate_out_ref[...] = (grad * up * (sigmoid * (1.0 + gate * (1.0 - sigmoid)))).astype(bf16)
    up_out_ref[...] = (grad * (gate * sigmoid)).astype(bf16)


def gates_pass(grad_top, wdown, gate, up):
    tokens, width = grad_top[0].shape
    columns = gate.shape[1]
    tile = min(256, columns)
    whole = pl.BlockSpec((tokens, width), lambda i: (0, 0))
    out = pl.BlockSpec((2 * tokens, tile), lambda i: (0, i))
    return pl.pallas_call(
        gates_kernel,
        grid=(pl.cdiv(columns, tile),),
        in_specs=[whole] * 2 + [pl.BlockSpec((tile, width), lambda i: (i, 0)), out, out],
        out_specs=[out] * 2,
        out_shape=[jax.ShapeDtypeStruct((2 * tokens, columns), bf16)] * 2,
        scratch_shapes=[pltpu.VMEM((2 * tokens, width), bf16)],
        compiler_params=pltpu.CompilerParams(vmem_limit_bytes=VMEM_LIMIT),
        name="gates_pass",
        cost_estimate=LIGHT,
    )(*grad_top, wdown, gate, up)


def back_kernel(count, transposed, *refs):
    own_ref, send_ref = refs[-2:]
    tokens = own_ref.shape[0]
    dot = dot_nt if transposed else dot_nn

    def total(start):
        rows = pl.ds(start, tokens)
        result = dot(refs[0][rows, :], refs[count][...])
        for i in range(1, count):
            result = result + dot(refs[i][rows, :], refs[count + i][...])
        return result

    own_ref[...] = total(0)
    send_ref[...] = total(tokens).astype(bf16)


def back_pass(lefts, weights, transposed):
    tokens, depth = lefts[0].shape
    width = weights[0].shape[0 if transposed else 1]
    count = len(lefts)
    tile = min(512, width)
    if transposed:
        weight_spec = pl.BlockSpec((tile, depth), lambda i: (i, 0))
    else:
        weight_spec = pl.BlockSpec((depth, tile), lambda i: (0, i))
    out = pl.BlockSpec((tokens // 2, tile), lambda i: (0, i))
    return pl.pallas_call(
        partial(back_kernel, count, transposed),
        grid=(width // tile,),
        in_specs=[pl.BlockSpec((tokens, depth), lambda i: (0, 0))] * count
        + [weight_spec] * count,
        out_specs=[out, out],
        out_shape=[
            jax.ShapeDtypeStruct((tokens // 2, width), f32),
            jax.ShapeDtypeStruct((tokens // 2, width), bf16),
        ],
        compiler_params=pltpu.CompilerParams(vmem_limit_bytes=VMEM_LIMIT),
        name="back_pass",
        cost_estimate=LIGHT,
    )(*lefts, *weights)


def weight_kernel(left_count, *refs):
    lefts, rights, out_ref = refs[:left_count], refs[left_count:-1], refs[-1]
    step = min(lefts[0].shape[0], rights[0].shape[0])

    def piece(refs, start):
        index, offset = divmod(start, refs[0].shape[0])
        return refs[index][pl.ds(offset, step), :]

    total = None
    for start in range(0, left_count * lefts[0].shape[0], step):
        term = dot_tn(piece(lefts, start), piece(rights, start))
        total = term if total is None else total + term
    out_ref[...] = total.astype(bf16)


def weight_pass(lefts, rights):
    rows, columns = lefts[0].shape[1], rights[0].shape[1]
    tile = 512 if rows % 512 == 0 else 384 if rows % 384 == 0 else rows
    return pl.pallas_call(
        partial(weight_kernel, len(lefts)),
        grid=(rows // tile,),
        in_specs=[pl.BlockSpec((left.shape[0], tile), lambda i: (0, i)) for left in lefts]
        + [pl.BlockSpec(right.shape, lambda i: (0, 0)) for right in rights],
        out_specs=pl.BlockSpec((tile, columns), lambda i: (i, 0)),
        out_shape=jax.ShapeDtypeStruct((rows, columns), bf16),
        compiler_params=pltpu.CompilerParams(vmem_limit_bytes=VMEM_LIMIT),
        name="weight_pass",
        cost_estimate=LIGHT,
    )(*lefts, *rights)


def placed_kernel(side_ref, own_ref, other_ref, out_ref):
    mine = pl.program_id(0) == side_ref[0]

    @pl.when(mine)
    def _():
        out_ref[0, 0] = own_ref[:, 0]

    @pl.when(jnp.logical_not(mine))
    def _():
        out_ref[0, 0] = other_ref[:, 0]


def placed(own, other, side):
    seq, group, rows, columns = own.shape

    def entry(mine, e, g, s):
        parked = jnp.where(e == 0, 0, group - 1)
        return (0, jnp.where((e == s[0]) == mine, g, parked), 0, 0)

    return pl.pallas_call(
        placed_kernel,
        grid_spec=pltpu.PrefetchScalarGridSpec(
            num_scalar_prefetch=1,
            grid=(2, group),
            in_specs=[
                pl.BlockSpec((seq, 1, rows, columns), partial(entry, True)),
                pl.BlockSpec((seq, 1, rows, columns), partial(entry, False)),
            ],
            out_specs=pl.BlockSpec(
                (1, 1, seq, rows, columns), lambda e, g, s: (e, g, 0, 0, 0)
            ),
        ),
        out_shape=jax.ShapeDtypeStruct((2, group, seq, rows, columns), own.dtype),
        name="placed",
        cost_estimate=LIGHT,
    )(side.astype(jnp.int32).reshape(1), own, other)


def joined_kernel(side_ref, own_ref, other_ref, out_ref):
    mine = pl.program_id(1) == side_ref[0]

    @pl.when(mine)
    def _():
        out_ref[:, 0] = own_ref[...]

    @pl.when(jnp.logical_not(mine))
    def _():
        out_ref[:, 0] = other_ref[...]


def joined(own, other, side, axis):
    shape = own.shape[:axis] + (2,) + own.shape[axis:]
    columns = own.shape[-1]
    lead = math.prod(own.shape[:axis])
    rows = math.prod(own.shape[axis:-1])
    leads, chunks = lead, 1
    while leads % 2 == 0 and leads * rows * columns > 800_000:
        leads //= 2
    while leads == 1 and rows % (32 * chunks) == 0 and rows // chunks * columns > 800_000:
        chunks *= 2
    block = rows // chunks

    def entry(mine, p, e, i, s):
        parked = jnp.where(e == 0, 0, chunks - 1)
        return (p, jnp.where((e == s[0]) == mine, i, parked), 0)

    return pl.pallas_call(
        joined_kernel,
        grid_spec=pltpu.PrefetchScalarGridSpec(
            num_scalar_prefetch=1,
            grid=(lead // leads, 2, chunks),
            in_specs=[
                pl.BlockSpec((leads, block, columns), partial(entry, True)),
                pl.BlockSpec((leads, block, columns), partial(entry, False)),
            ],
            out_specs=pl.BlockSpec((leads, 1, block, columns), lambda p, e, i, s: (p, e, i, 0)),
        ),
        out_shape=jax.ShapeDtypeStruct((lead, 2, rows, columns), own.dtype),
        compiler_params=pltpu.CompilerParams(vmem_limit_bytes=VMEM_LIMIT),
        name="joined",
        cost_estimate=LIGHT,
    )(
        side.astype(jnp.int32).reshape(1),
        own.reshape(lead, rows, columns),
        other.reshape(lead, rows, columns),
    ).reshape(shape)


def swap(values, bit):
    pairs = [(i, i ^ bit) for i in range(lax.axis_size("rows"))]
    return lax.ppermute(values, "rows", pairs)


def bit_of(bit):
    return (lax.axis_index("rows") // bit) % 2


def gather_bit(values, bit, axis):
    return joined(values, swap(values, bit), bit_of(bit), axis)


def part(values, index, axis):
    return lax.dynamic_index_in_dim(values, index, axis, keepdims=False)


def reduce_bit(values, bit, axis):
    return add_bit(values, pass_bit(values, bit, axis), bit, axis)


def outer_pairs(step, low, high):
    size = lax.axis_size("rows")
    return [
        (i, i + 4 * step)
        for i in range(size)
        if low <= i // 4 < high and 0 <= i // 4 + step < size // 4
    ]


def send_outer(values):
    count = lax.axis_size("rows") // 4
    if count == 2:
        return (swap(values, 4),)
    up, down = values, values
    ups, downs = [], []
    for t in range(1, count):
        up = lax.ppermute(up, "rows", outer_pairs(1, t - 1, count))
        down = lax.ppermute(down, "rows", outer_pairs(-1, 0, count - t + 1))
        ups.append(up)
        downs.append(down)
    return tuple(ups[::-1] + downs)


def join_outer(values, received, axis):
    count = lax.axis_size("rows") // 4
    if count == 2:
        return joined(values, received[0], bit_of(4), axis)
    place = lax.axis_index("rows") // 4
    line = jnp.stack([*received[: count - 1], values, *received[count - 1 :]], axis)
    return lax.dynamic_slice_in_dim(line, count - 1 - place, count, axis)


def gather_outer(values, axis):
    return join_outer(values, send_outer(values), axis)


def pass_outer(values, axis):
    count = lax.axis_size("rows") // 4
    place = lax.axis_index("rows") // 4

    def entry(index):
        return part(values, jnp.clip(index, 0, count - 1), axis)

    if count == 1:
        return ()
    if count == 2:
        return (swap(entry(1 - place), 4),)
    up, down = entry(place + count - 1), entry(place - count + 1)
    for t in range(1, count):
        up = lax.ppermute(up, "rows", outer_pairs(1, 0, t))
        down = lax.ppermute(down, "rows", outer_pairs(-1, count - t, count))
        if t < count - 1:
            up = (entry(place + count - 1 - t).astype(f32) + up.astype(f32)).astype(bf16)
            down = (entry(place - count + 1 + t).astype(f32) + down.astype(f32)).astype(bf16)
    return (up, down)


def add_outer(values, received, axis):
    total = part(values, lax.axis_index("rows") // 4, axis).astype(f32)
    for term in received:
        total = total + term.astype(f32)
    return total.astype(bf16)


def reduce_outer(values, axis):
    return add_outer(values, pass_outer(values, axis), axis)


def pass_bit(values, bit, axis):
    return swap(part(values, 1 - bit_of(bit), axis), bit)


def add_bit(values, received, bit, axis):
    own = part(values, bit_of(bit), axis)
    return (own.astype(f32) + received.astype(f32)).astype(bf16)


def gather_seq(values):
    return lax.all_gather(values, "seq", axis=0, tiled=False)


def reduce_seq(values):
    return lax.psum_scatter(values, "seq", scatter_dimension=0, tiled=False)


def exchange(values, axis, bit):
    size = lax.axis_size(axis)
    return lax.ppermute(values, axis, [(i, i ^ bit) for i in range(size)])


def across_group(own, send):
    return (own + swap(send, 1).astype(f32)).astype(bf16)


def stage(*values):
    return lax.optimization_barrier(values)


def mm(left, right):
    return jnp.einsum("ab,bc->ac", left, right, preferred_element_type=f32)


def mm_t(left, right):
    return jnp.einsum("ab,cb->ac", left, right, preferred_element_type=f32)


def t_mm(left, right):
    return jnp.einsum("ab,ac->bc", left, right, preferred_element_type=f32)


def norm_scale(values):
    return lax.rsqrt(jnp.mean(values * values, axis=-1, keepdims=True) + EPSILON)


def norm_backward(values, scale, gain, grad):
    gained = grad * gain
    inner = jnp.mean(values * gained, axis=-1, keepdims=True)
    result = scale * gained - values * (scale * scale * scale) * inner
    return result, jnp.sum(grad * values * scale, axis=0)


def shards(
    tokens_in,
    corpus,
    corpus_weight,
    w_qkv,
    w_out,
    w_gate,
    w_up,
    w_down,
    attn_gain,
    ffn_gain,
    q_gain,
    k_gain,
    upstream,
):
    shard_length, width = tokens_in.shape[1:]
    row_devices = lax.axis_size("rows")
    seq_devices = lax.axis_size("seq")
    outer = row_devices // 4
    d_rows = w_qkv.shape[0]
    f_rows = w_down.shape[0]
    place = lax.axis_index("seq").astype(jnp.int32)
    inputs = tokens_in[0].astype(f32)

    extra = jnp.stack(
        [
            attn_gain,
            ffn_gain,
            jnp.broadcast_to(corpus.astype(bf16), attn_gain.shape),
        ],
        axis=1,
    )
    extra = jnp.pad(extra, ((0, 0), (0, LANES - extra.shape[1])))
    kv_shard = jnp.concatenate([w_qkv[:, QUERY_COLUMNS:], extra], axis=1)
    query_shard = jnp.concatenate([w_qkv[:, :QUERY_COLUMNS], w_out.T], axis=1)
    query_shard, w_gate, w_up = stage(query_shard, w_gate, w_up)
    query_lines = gather_seq(query_shard)

    def to_group(weight):
        blocks = weight.reshape(d_rows, outer, 4, seq_devices, f_rows)
        blocks = jnp.transpose(blocks, (2, 0, 3, 1, 4))
        return blocks.reshape(2, 2, d_rows, outer * seq_devices * f_rows)

    def spread_hidden(lines, received):
        if outer == 2:
            lines = lines.reshape(seq_devices, 4, d_rows, hidden_columns)
            other = received[0].reshape(lines.shape)
            return placed(lines, other, bit_of(4)).reshape(width, hidden_columns)
        full = join_outer(lines, received, 0)
        return jnp.moveaxis(full, 1, 3).reshape(width, hidden_columns)

    gate_up = jnp.stack([to_group(w_gate), to_group(w_up)], axis=2)
    hidden_columns = gate_up.shape[-1]
    core, near = bit_of(1), bit_of(2)
    gate_up = joined(
        part(gate_up, core, 1), swap(part(gate_up, 1 - core, 1), 1), core, 1
    )
    gate_up, kv_shard = stage(gate_up, kv_shard)
    other, kv_lines, query_lines = stage(
        swap(part(gate_up, 1 - near, 0), 2), gather_seq(kv_shard), query_lines
    )
    gate_up = joined(part(gate_up, near, 0), other, near, 0)
    gate_lines = gather_seq(gate_up[:, :, 0])
    left, right = kv_lines[..., : 3 * LANES], kv_lines[..., 3 * LANES :]
    left_other, right_other = stage(send_outer(left), swap(right, 2))
    left = join_outer(left, left_other, 0)
    right = joined(right, right_other, near, 0)
    left_other, right_other = stage(swap(left, 2), send_outer(right))
    left = joined(left, left_other, near, 1)
    right = join_outer(right, right_other, 0)
    q_left, q_right = query_lines[..., :QUERY_COLUMNS], query_lines[..., QUERY_COLUMNS:]
    q_left, q_right, left, right = stage(q_left, q_right, left, right)
    q_left_other, q_right_other = send_outer(q_left), swap(q_right, 2)
    left, right = gather_bit(left, 1, 2), gather_bit(right, 1, 2)
    left, right = left.reshape(width, -1), right.reshape(width, -1)
    wkv = jnp.concatenate([left, right[:, : 2 * LANES]], axis=1)
    rows = dot_nt(jnp.eye(8, LANES, dtype=bf16), right[:, 2 * LANES :])
    attn_gain_full, ffn_gain_full, corpus_full = rows[0:1], rows[1:2], rows[2]

    position = (place * shard_length + jnp.arange(shard_length, dtype=jnp.int32)).astype(f32)
    half = HEAD_SIZE // 2
    exponent = jnp.arange(half, dtype=f32) * (-2.0 / HEAD_SIZE)
    angles = position[:, None] * jnp.power(ROPE_BASE, exponent)[None, :]
    cosine, sine = jnp.cos(angles), jnp.sin(angles)
    cos_table = jnp.concatenate([cosine] * 4, axis=1)
    sin_table = jnp.concatenate([-sine, sine] * 2, axis=1)
    wide_q = jnp.tile(q_gain.astype(f32), QUERY_HEADS)
    wide_k = jnp.concatenate(
        [jnp.tile(k_gain.astype(f32), KEY_VALUE_HEADS), jnp.ones((KEY_COLUMNS,), f32)]
    )
    wide_q = jnp.broadcast_to(wide_q[None, :], (8, QUERY_COLUMNS))
    wide_k = jnp.broadcast_to(wide_k[None, :], (8, 2 * KEY_COLUMNS))

    in_scale = norm_scale(inputs)
    normed = (inputs * in_scale * attn_gain_full).astype(bf16)
    joint_kv, own_kv = heads_forward(
        normed, wkv, wide_k, cos_table, sin_table, KEY_COLUMNS
    )
    own_kv, q_left_other, q_right_other, down_other, up_in = stage(
        own_kv, q_left_other, q_right_other, send_outer(w_down), gate_up[:, :, 1]
    )
    up_lines = gather_seq(up_in)
    keys_values = gather_seq(own_kv).reshape(-1, 2 * KEY_COLUMNS)
    q_left = join_outer(q_left, q_left_other, 0)
    q_right = joined(q_right, q_right_other, near, 0)
    left_other, right_other, gate_lines = stage(
        swap(q_left, 2), send_outer(q_right), gate_lines
    )
    q_left = joined(q_left, left_other, near, 1)
    gate_other = send_outer(gate_lines)
    wq = gather_bit(q_left, 1, 2).reshape(width, -1)

    corpora = jnp.arange(CORPORA, dtype=jnp.int32)
    per_device = corpus_full.reshape(-1, d_rows)[:, 0].astype(jnp.int32)
    counts = (
        jnp.sum((per_device[:, None] == corpora[None, :]).astype(f32), axis=0) * shard_length
    )
    own_corpus = (corpus[0] == corpora).astype(f32)
    weight_row = jnp.sum(own_corpus * corpus_weight.astype(f32))
    count_row = jnp.sum(own_corpus * counts)
    factor = weight_row / DENOM * (jnp.sum(counts) / (CORPORA * count_row))
    grad_full = upstream[0].astype(f32) * factor
    grad_top, wq = stage(grad_full.astype(bf16), wq)

    joint_q, queries = heads_forward(
        normed, wq, wide_q, cos_table, sin_table, QUERY_COLUMNS
    )
    queries, q_right, right_other, down_other = stage(queries, q_right, right_other, down_other)
    q_right = join_outer(q_right, right_other, 0)
    place_array = place.reshape(1)
    keys_values, queries = stage(keys_values, queries)
    mixed, logs = attend_forward(place_array, queries, keys_values)
    mixed, grad_top1, grad_top2, up_lines, wout_other, down_other = stage(
        mixed, swap(grad_top, 1), swap(grad_top, 2), up_lines, swap(q_right, 1), down_other
    )
    down_lines = gather_seq(join_outer(w_down, down_other, 0))
    wout_t = joined(q_right, wout_other, core, 2).reshape(width, -1)
    middle = inputs + mm_t(mixed, wout_t)

    ffn_scale = norm_scale(middle)
    normed_ffn = (middle * ffn_scale * ffn_gain_full).astype(bf16)
    up_other = send_outer(up_lines)
    normed_ffn, gate_other = stage(normed_ffn, gate_other)
    normed1, normed2, up_other, wgate = stage(
        swap(normed_ffn, 1),
        swap(normed_ffn, 2),
        up_other,
        spread_hidden(gate_lines, gate_other),
    )
    wup = spread_hidden(up_lines, up_other)
    hidden_near, gate_near, up_near = hidden_pass((normed_ffn, normed1), wgate, wup)
    normed3, hidden_near, grad_top3 = stage(
        swap(normed2, 1), hidden_near, swap(grad_top2, 1)
    )
    hidden_far, gate_far, up_far = hidden_pass((normed2, normed3), wgate, wup)
    normed4 = (normed_ffn, normed1, normed2, normed3)
    grad_top4 = (grad_top, grad_top1, grad_top2, grad_top3)
    wdown = down_lines.reshape(hidden_columns, width)
    gate_far, up_far = gates_pass((grad_top2, grad_top3), wdown, gate_far, up_far)
    own, send = back_pass((gate_far, up_far), (wgate, wup), True)
    grad_wdown = weight_pass((hidden_near, hidden_far), grad_top4)
    own, send, grad_wdown, wdown = stage(own, swap(send, 1), grad_wdown, wdown)
    across = (own + send.astype(f32)).astype(bf16)
    across, wdown = stage(across, wdown)
    gate_near, up_near = gates_pass((grad_top, grad_top1), wdown, gate_near, up_near)
    own, send = back_pass((gate_near, up_near), (wgate, wup), True)
    hidden_shape = (outer, 2, 2, seq_devices, d_rows, hidden_columns)
    grad_wdown = grad_wdown.reshape(seq_devices, outer, f_rows, width)
    grad_wgate = weight_pass(normed4, (gate_near, gate_far)).reshape(hidden_shape)
    across, own, send, grad_wgate, up_near = stage(
        swap(across, 2), own, send, grad_wgate, up_near
    )
    grad_wup = weight_pass(normed4, (up_near, up_far)).reshape(hidden_shape)
    send, grad_wup, down_other = stage(swap(send, 1), grad_wup, pass_outer(grad_wdown, 1))
    grad_wdown = add_outer(grad_wdown, down_other, 1)
    own = own + send.astype(f32)
    grad_normed_ffn = own + across.astype(f32)
    grad_wdown = reduce_seq(grad_wdown)

    grad_middle_part, grad_ffn_gain = norm_backward(
        middle, ffn_scale, ffn_gain_full, grad_normed_ffn
    )
    grad_middle = grad_full + grad_middle_part
    grad_branch = grad_middle.astype(bf16)
    grad_mixed = mm(grad_branch, wout_t).astype(bf16)
    attend = (place_array, queries, keys_values, mixed, logs)
    grad_q1, grad_kv1 = attend_backward(0, 2, *attend, grad_mixed)
    gate_other = pass_outer(grad_wgate, 0)
    grad_q1, grad_kv1, grad_mixed, grad_wdown, hidden_far = stage(
        grad_q1, grad_kv1, grad_mixed, grad_wdown, hidden_far
    )
    grad_kv1 = reduce_seq(grad_kv1.reshape(seq_devices, shard_length, -1))
    shape = (outer, 2, 2, seq_devices, d_rows)
    own_far, send_far = back_pass((hidden_far,), (wdown,), False)
    grad_wout, far_other, gate_other, grad_mixed = stage(
        t_mm(grad_branch, mixed).astype(bf16).reshape(*shape, QUERY_COLUMNS),
        swap(send_far, 1),
        gate_other,
        grad_mixed,
    )
    grad_gate = reduce_seq(jnp.moveaxis(add_outer(grad_wgate, gate_other, 0), 2, 0))
    across = (own_far + far_other.astype(f32)).astype(bf16)
    across, grad_mixed = stage(across, grad_mixed)
    grad_q2, grad_kv2 = attend_backward(2, 3, *attend, grad_mixed)
    grad_q2, grad_kv2, hidden_near, grad_kv1, grad_gate, wout_other, up_other, across = stage(
        grad_q2,
        grad_kv2,
        hidden_near,
        grad_kv1,
        grad_gate,
        pass_bit(grad_wout, 1, 2),
        pass_outer(grad_wup, 0),
        swap(across, 2),
    )
    grad_kv2 = reduce_seq(grad_kv2.reshape(seq_devices, shard_length, -1))

    grad_q = jnp.concatenate([grad_q1, grad_q2], axis=1)
    joint_grad_q, gain_q = heads_backward(
        grad_q, joint_q, wide_q, cos_table, sin_table, QUERY_COLUMNS
    )
    grad_wq = t_mm(normed, joint_grad_q).astype(bf16).reshape(*shape, QUERY_COLUMNS)
    grad_wout = add_bit(grad_wout, wout_other, 1, 2)
    own_near, send_near = back_pass((hidden_near,), (wdown,), False)
    grad_up = jnp.moveaxis(add_outer(grad_wup, up_other, 0), 2, 0)
    grad_kv2, joint_grad_q, grad_wq, grad_wout, own_near, send_near, grad_up = stage(
        grad_kv2, joint_grad_q, grad_wq, grad_wout, own_near, send_near, grad_up
    )
    grad_up = reduce_seq(grad_up)


    grad_kv1, grad_kv2 = (
        part_.reshape(shard_length, 2, -1) for part_ in (grad_kv1, grad_kv2)
    )
    grad_kv = jnp.concatenate([grad_kv1, grad_kv2], axis=2).reshape(shard_length, -1)
    joint_grad_kv, gain_k = heads_backward(
        grad_kv, joint_kv, wide_k, cos_table, sin_table, KEY_COLUMNS
    )
    wq_other, near_other, joint_grad_kv = stage(
        pass_bit(grad_wq, 1, 2), swap(send_near, 1), joint_grad_kv
    )
    grad_wq = add_bit(grad_wq, wq_other, 1, 2)
    wq_other, wout_other = pass_bit(grad_wq, 2, 1), pass_outer(grad_wout, 0)
    output = (middle + own_near + near_other.astype(f32) + across.astype(f32)).astype(bf16)
    grad_wkv = t_mm(normed, joint_grad_kv).astype(bf16)
    grad_normed = mm_t(joint_grad_q, wq) + mm_t(joint_grad_kv, wkv)
    grad_input_part, grad_attn_gain = norm_backward(
        inputs, in_scale, attn_gain_full, grad_normed
    )
    input_grad = (grad_middle + grad_input_part).astype(bf16)

    gain_rows = jnp.stack([grad_attn_gain, grad_ffn_gain]).astype(bf16)
    gain_columns = t_mm(gain_rows, jnp.eye(2, LANES, dtype=bf16)).astype(bf16)
    grad_wkv, gain_columns, wq_other, wout_other = stage(
        grad_wkv, gain_columns, wq_other, wout_other
    )
    grad_wq = add_bit(grad_wq, wq_other, 2, 1)
    grad_wout = add_outer(grad_wout, wout_other, 0)
    wq_other, wout_other = pass_outer(grad_wq, 0), pass_bit(grad_wout, 2, 0)
    left = grad_wkv[:, : 3 * LANES].reshape(*shape, -1)
    right = jnp.concatenate([grad_wkv[:, 3 * LANES :], gain_columns], axis=1)
    right = right.reshape(*shape, -1)
    head_gains = jnp.concatenate(
        [
            jnp.sum(gain_q[0].reshape(-1, HEAD_SIZE), axis=0),
            jnp.sum(gain_k[0, :KEY_COLUMNS].reshape(-1, HEAD_SIZE), axis=0),
        ]
    )[None]
    left, right, left_other, right_other, gains_other = stage(
        left,
        right,
        pass_bit(left, 1, 2),
        pass_bit(right, 1, 2),
        exchange(head_gains, "rows", 1),
    )
    head_gains = head_gains + gains_other
    left = add_bit(left, left_other, 1, 2)
    right = add_bit(right, right_other, 1, 2)
    left_other, right_other, wq_other, wout_other, gains_other, grad_up = stage(
        pass_bit(left, 2, 1),
        pass_outer(right, 0),
        wq_other,
        wout_other,
        exchange(head_gains, "seq", 1),
        grad_up,
    )
    head_gains = head_gains + gains_other
    left = add_bit(left, left_other, 2, 1)
    right = add_outer(right, right_other, 0)
    left_other, right_other, gains_other = stage(
        pass_outer(left, 0), pass_bit(right, 2, 0), exchange(head_gains, "rows", 2)
    )
    head_gains = head_gains + gains_other
    sums = reduce_seq(
        jnp.concatenate(
            [
                add_outer(grad_wq, wq_other, 0),
                add_outer(left, left_other, 0),
                add_bit(right, right_other, 2, 0),
                add_bit(grad_wout, wout_other, 2, 0),
            ],
            axis=-1,
        )
    )
    rest = [("rows", bit) for bit in (4, 8, 16) if bit < row_devices]
    rest += [("seq", bit) for bit in (2, 4, 8) if bit < seq_devices]
    gate_up = jnp.stack([grad_gate, grad_up], axis=2)
    other, gains_other = stage(
        swap(part(gate_up, 1 - near, 0), 2), exchange(head_gains, *rest[0])
    )
    head_gains = head_gains + gains_other
    grads = joined(part(gate_up, near, 0), other, near, 0)
    for axis, bit in rest[1:]:
        head_gains = head_gains + exchange(head_gains, axis, bit)
    head_gains = head_gains[0]
    grads = joined(part(grads, core, 1), swap(part(grads, 1 - core, 1), 1), core, 1)

    def from_group(blocks):
        blocks = blocks.reshape(4, d_rows, seq_devices, outer, f_rows)
        return jnp.transpose(blocks, (1, 3, 0, 2, 4)).reshape(d_rows, -1)

    grad_wgate, grad_wup = stage(from_group(grads[:, :, 0]), from_group(grads[:, :, 1]))
    sums, grad_wgate, grad_wup, grad_wdown, output, input_grad = stage(
        sums, grad_wgate.astype(f32), grad_wup.astype(f32), grad_wdown.astype(f32), output, input_grad
    )
    columns = QUERY_COLUMNS + 2 * KEY_COLUMNS
    long_gains = sums[:, columns : columns + 2].astype(f32)
    return (
        output[None],
        input_grad[None],
        sums[:, :columns].astype(f32),
        sums[:, columns + LANES :].T.astype(f32),
        grad_wgate,
        grad_wup,
        grad_wdown,
        long_gains[:, 0],
        long_gains[:, 1],
        head_gains[:HEAD_SIZE],
        head_gains[HEAD_SIZE:],
    )


def solution(mesh):
    return jax.shard_map(
        shards,
        mesh=mesh,
        in_specs=(
            P("rows", "seq", None),
            P("rows"),
            P(),
            P(("rows", "seq"), None),
            P(None, ("rows", "seq")),
            P(("rows", "seq"), None),
            P(("rows", "seq"), None),
            P(("rows", "seq"), None),
            P(("rows", "seq")),
            P(("rows", "seq")),
            P(),
            P(),
            P("rows", "seq", None),
        ),
        out_specs=(
            P("rows", "seq", None),
            P("rows", "seq", None),
            P(("rows", "seq"), None),
            P(None, ("rows", "seq")),
            P(("rows", "seq"), None),
            P(("rows", "seq"), None),
            P(("rows", "seq"), None),
            P(("rows", "seq")),
            P(("rows", "seq")),
            P(),
            P(),
        ),
        check_vma=False,
    )
```

```python
import math
from functools import partial

import jax
import jax.numpy as jnp
from jax import lax
from jax.experimental import pallas as pl
from jax.experimental.pallas import tpu as pltpu
from jax.sharding import PartitionSpec as P

QUERY_HEADS = 20
KEY_VALUE_HEADS = 5
HEAD_SIZE = 64
CORPORA = 8
DENOM = 64
EPSILON = 1e-06
ROPE_BASE = 10000.0
QUERY_COLUMNS = QUERY_HEADS * HEAD_SIZE
KEY_COLUMNS = KEY_VALUE_HEADS * HEAD_SIZE
LANES = 128
SCORE_EXPONENT = 1.4426950408889634 * HEAD_SIZE**-0.5
SPLIT = 2
VMEM_LIMIT = 48 * 1024 * 1024

f32, bf16 = jnp.float32, jnp.bfloat16
LIGHT = pl.CostEstimate(flops=1000, bytes_accessed=1000, transcendentals=0)


def dot_nn(a, b):
    return lax.dot_general(a, b, (((1,), (0,)), ((), ())), preferred_element_type=f32)


def dot_nt(a, b):
    return lax.dot_general(a, b, (((1,), (1,)), ((), ())), preferred_element_type=f32)


def dot_tn(a, b):
    return lax.dot_general(a, b, (((0,), (0,)), ((), ())), preferred_element_type=f32)


def lanes_of(shape):
    return lax.broadcasted_iota(jnp.int32, shape, len(shape) - 1)


def head_sum(values):
    row = lax.broadcasted_iota(jnp.int32, (LANES, LANES), 0) // HEAD_SIZE
    column = lax.broadcasted_iota(jnp.int32, (LANES, LANES), 1) // HEAD_SIZE
    ones = jnp.where(row == column, 1.0, 0.0).astype(bf16)
    high = values.astype(bf16)
    low = (values - high.astype(f32)).astype(bf16)
    return dot_nn(high, ones) + dot_nn(low, ones)


def partner(values):
    first = lanes_of(values.shape) % HEAD_SIZE < HEAD_SIZE // 2
    return jnp.where(
        first,
        pltpu.roll(values, LANES - HEAD_SIZE // 2, 1),
        pltpu.roll(values, HEAD_SIZE // 2, 1),
    )


def heads_forward_kernel(
    norm_columns, normed_ref, weight_ref, gain_ref, cos_ref, sin_ref, joint_ref, out_ref
):
    joint = dot_nn(normed_ref[...], weight_ref[...])
    joint_ref[...] = joint
    columns = joint.shape[1]
    for start in range(0, columns, LANES):
        chunk = slice(start, start + LANES)
        values = joint[:, chunk]
        scale = lax.rsqrt(head_sum(values * values) * (1.0 / HEAD_SIZE) + EPSILON)
        normed = values * scale * gain_ref[0:1, chunk]
        turned = normed * cos_ref[...] + partner(normed) * sin_ref[...]
        place = pl.program_id(0) * columns + start + lanes_of(values.shape)
        out_ref[:, chunk] = jnp.where(place < norm_columns, turned, values).astype(bf16)


def heads_forward(normed, weight, gain, cos, sin, norm_columns):
    tokens, width = normed.shape
    columns = weight.shape[1]
    tile = 2 * LANES if columns % (2 * LANES) == 0 else LANES
    out = pl.BlockSpec((tokens, tile), lambda i: (0, i))
    table = pl.BlockSpec((tokens, LANES), lambda i: (0, 0))
    return pl.pallas_call(
        partial(heads_forward_kernel, norm_columns),
        grid=(columns // tile,),
        in_specs=[
            pl.BlockSpec((tokens, width), lambda i: (0, 0)),
            pl.BlockSpec((width, tile), lambda i: (0, i)),
            pl.BlockSpec((8, tile), lambda i: (0, i)),
            table,
            table,
        ],
        out_specs=[out, out],
        out_shape=[
            jax.ShapeDtypeStruct((tokens, columns), f32),
            jax.ShapeDtypeStruct((tokens, columns), bf16),
        ],
        compiler_params=pltpu.CompilerParams(vmem_limit_bytes=VMEM_LIMIT),
        name="heads_forward",
        cost_estimate=LIGHT,
    )(normed, weight, gain, cos, sin)


def heads_backward_kernel(
    norm_columns, grad_ref, joint_ref, gain_ref, cos_ref, sin_ref, out_ref, gain_out_ref
):
    grad = grad_ref[...].astype(f32)
    values = joint_ref[...]
    gain = gain_ref[0:1, :]
    turned = grad * cos_ref[...] - partner(grad) * sin_ref[...]
    scale = lax.rsqrt(head_sum(values * values) * (1.0 / HEAD_SIZE) + EPSILON)
    gained = turned * gain
    inner = head_sum(values * gained) * (1.0 / HEAD_SIZE)
    result = scale * gained - values * (scale * scale * scale) * inner
    place = pl.program_id(0) * LANES + lanes_of(values.shape)
    out_ref[...] = jnp.where(place < norm_columns, result, grad).astype(bf16)
    gain_out_ref[...] = jnp.broadcast_to(
        jnp.sum(turned * values * scale, axis=0, keepdims=True), gain_out_ref.shape
    )


def heads_backward(grad, joint, gain, cos, sin, norm_columns):
    tokens, columns = joint.shape
    return pl.pallas_call(
        partial(heads_backward_kernel, norm_columns),
        grid=(columns // LANES,),
        in_specs=[
            pl.BlockSpec((tokens, LANES), lambda i: (0, i)),
            pl.BlockSpec((tokens, LANES), lambda i: (0, i)),
            pl.BlockSpec((8, LANES), lambda i: (0, i)),
            pl.BlockSpec((tokens, LANES), lambda i: (0, 0)),
            pl.BlockSpec((tokens, LANES), lambda i: (0, 0)),
        ],
        out_specs=[
            pl.BlockSpec((tokens, LANES), lambda i: (0, i)),
            pl.BlockSpec((8, LANES), lambda i: (0, i)),
        ],
        out_shape=[
            jax.ShapeDtypeStruct((tokens, columns), bf16),
            jax.ShapeDtypeStruct((8, columns), f32),
        ],
        name="heads_backward",
        cost_estimate=LIGHT,
    )(grad, joint, gain, cos, sin)


def both_halves(pair, odd):
    wide = pair.astype(f32)
    first = lanes_of(wide.shape) < HEAD_SIZE
    keep = jnp.where(odd == 1, jnp.where(first, 0, 1), jnp.where(first, 1, 0)) == 1
    return jnp.where(keep, wide, pltpu.roll(wide, HEAD_SIZE, 1))


def attend_forward_kernel(place_ref, q_ref, k_ref, v_ref, out_ref, log_ref):
    group = pl.program_id(0) // 2
    place = place_ref[0]
    tokens = q_ref.shape[0]
    first = lanes_of((tokens, LANES)) < HEAD_SIZE
    pair = q_ref[...].astype(f32)
    queries = (jnp.where(first, pair, 0.0).astype(bf16), jnp.where(first, 0.0, pair).astype(bf16))

    def step(j, totals, diagonal):
        rows = pl.ds(pl.multiple_of(j * tokens, tokens), tokens)
        keys = both_halves(k_ref[rows, :], group % 2).astype(bf16)
        values = both_halves(v_ref[rows, :], (KEY_VALUE_HEADS + group) % 2)
        sides = (
            jnp.where(first, values, 1.0).astype(bf16),
            jnp.where(first, 1.0, values).astype(bf16),
        )
        result = []
        for head in range(2):
            weights = jnp.exp2(dot_nt(queries[head], keys) * SCORE_EXPONENT)
            if diagonal:
                row = lax.broadcasted_iota(jnp.int32, weights.shape, 0)
                weights = jnp.where(lanes_of(weights.shape) <= row, weights, 0.0)
            result.append(totals[head] + dot_nn(weights.astype(bf16), sides[head]))
        return tuple(result)

    zero = jnp.zeros((tokens, LANES), f32)
    totals = lax.fori_loop(0, place, lambda j, c: step(j, c, False), (zero, zero))
    totals = step(place, totals, True)
    numerator = jnp.where(first, totals[0], totals[1])
    swapped = jnp.where(first, totals[1], totals[0])
    out_ref[...] = (numerator / pltpu.roll(swapped, HEAD_SIZE, 1)).astype(bf16)
    log_ref[...] = jnp.log2(swapped)


def attend_forward(place, queries, keys_values):
    tokens = queries.shape[0]
    length = keys_values.shape[0]
    pairs = QUERY_COLUMNS // LANES
    return pl.pallas_call(
        attend_forward_kernel,
        grid_spec=pltpu.PrefetchScalarGridSpec(
            num_scalar_prefetch=1,
            grid=(pairs,),
            in_specs=[
                pl.BlockSpec((tokens, LANES), lambda i, s: (0, i)),
                pl.BlockSpec((length, LANES), lambda i, s: (0, (i // 2) // 2)),
                pl.BlockSpec((length, LANES), lambda i, s: (0, (KEY_VALUE_HEADS + i // 2) // 2)),
            ],
            out_specs=[
                pl.BlockSpec((tokens, LANES), lambda i, s: (0, i)),
                pl.BlockSpec((tokens, LANES), lambda i, s: (0, i)),
            ],
        ),
        out_shape=[
            jax.ShapeDtypeStruct((tokens, QUERY_COLUMNS), bf16),
            jax.ShapeDtypeStruct((tokens, QUERY_COLUMNS), f32),
        ],
        compiler_params=pltpu.CompilerParams(vmem_limit_bytes=VMEM_LIMIT),
        name="attend_forward",
        cost_estimate=LIGHT,
    )(place, queries, keys_values, keys_values)


def three_parts(values, lane):
    high = values.astype(bf16).astype(f32)
    rest = values - high
    middle = rest.astype(bf16).astype(f32)
    low = rest - middle
    return jnp.where(
        lane == 0, high, jnp.where(lane == 1, middle, jnp.where(lane == 2, low, 0.0))
    )


def attend_backward_kernel(
    first_group, count, place_ref, q_ref, k_ref, v_ref, out_ref, log_ref, grad_ref, dq_ref, dkv_ref, dk_sum, dv_sum
):
    pair_index = pl.program_id(0)
    local = pair_index // 2
    group = first_group + local
    place = place_ref[0]
    tokens = q_ref.shape[0]
    lane = lanes_of((tokens, LANES))
    first = lane < HEAD_SIZE
    inside = lane % HEAD_SIZE
    pair = q_ref[...].astype(f32)
    grad = grad_ref[...].astype(f32)
    delta = pltpu.roll(head_sum(grad * out_ref[...].astype(f32)), HEAD_SIZE, 1)
    logs = three_parts(log_ref[...] * (1.0 / SCORE_EXPONENT), inside)
    deltas = three_parts(delta, inside)
    minus = jnp.where(inside < 3, -1.0, 0.0)

    def sides(own, other):
        return (
            jnp.where(first, own, other).astype(bf16),
            jnp.where(first, other, own).astype(bf16),
        )

    queries = sides(pair, 0.0)
    grads = sides(grad, 0.0)
    def turned(values):
        return jnp.transpose(values.astype(f32)).astype(bf16)

    queries_log = tuple(turned(v) for v in sides(pair, logs))
    grads_delta = tuple(turned(v) for v in sides(grad, deltas))

    @pl.when(pair_index % 2 == 0)
    def _():
        dk_sum[...] = jnp.zeros_like(dk_sum)
        dv_sum[...] = jnp.zeros_like(dv_sum)

    def step(j, dq, diagonal):
        rows = pl.ds(pl.multiple_of(j * tokens, tokens), tokens)
        key_wide = both_halves(k_ref[rows, :], group % 2)
        value_wide = both_halves(v_ref[rows, :], (KEY_VALUE_HEADS + group) % 2)
        keys_turned = jnp.transpose(key_wide)[:HEAD_SIZE].astype(bf16)
        keys_log = sides(key_wide, minus)
        values_delta = sides(value_wide, minus)
        dk = dk_sum[rows, :]
        dv = dv_sum[rows, :]
        parts = list(dq)
        block = tokens // SPLIT
        for sub in range(SPLIT):
            keep = slice(sub * block, (sub + 1) * block)
            dk_part, dv_part = dk[keep], dv[keep]
            start = sub * block if diagonal else 0
            for head in range(2):
                weights = jnp.exp2(
                    dot_nn(keys_log[head][keep], queries_log[head][:, start:]) * SCORE_EXPONENT
                )
                if diagonal:
                    row = lax.broadcasted_iota(jnp.int32, weights.shape, 0)
                    weights = jnp.where(row <= lanes_of(weights.shape), weights, 0.0)
                grad_weights = dot_nn(values_delta[head][keep], grads_delta[head][:, start:])
                grad_scores = (weights * grad_weights).astype(bf16)
                dv_part = dv_part + dot_nn(weights.astype(bf16), grads[head][start:])
                dk_part = dk_part + dot_nn(grad_scores, queries[head][start:])
                term = dot_nn(keys_turned[:, keep], grad_scores)
                if start:
                    term = jnp.concatenate([jnp.zeros((HEAD_SIZE, start), f32), term], axis=1)
                parts[head] = parts[head] + term
            target = pl.ds(pl.multiple_of(j * tokens + sub * block, block), block)
            dk_sum[target, :] = dk_part
            dv_sum[target, :] = dv_part
        return tuple(parts)

    zero = jnp.zeros((HEAD_SIZE, tokens), f32)
    dq = lax.fori_loop(0, place, lambda j, c: step(j, c, False), (zero, zero))
    dq = jnp.transpose(jnp.concatenate(step(place, dq, True), axis=0))
    dq_ref[...] = (dq * HEAD_SIZE**-0.5).astype(bf16)

    @pl.when(pair_index % 2 == 1)
    def _():
        wide_lane = lanes_of(dk_sum.shape)
        for total, slot, factor in (
            (dk_sum, local, HEAD_SIZE**-0.5),
            (dv_sum, count + local, 1.0),
        ):
            both = (total[...] + pltpu.roll(total[...], HEAD_SIZE, 1)) * factor
            columns = pl.ds(pl.multiple_of(slot // 2 * LANES, LANES), LANES)
            mine = wide_lane // HEAD_SIZE == slot % 2
            dkv_ref[:, columns] = jnp.where(
                mine, both, dkv_ref[:, columns].astype(f32)
            ).astype(bf16)


def attend_backward(first, count, place, queries, keys_values, mixed, logs, grad_mixed):
    tokens = queries.shape[0]
    length = keys_values.shape[0]
    group = QUERY_HEADS // KEY_VALUE_HEADS * HEAD_SIZE
    own = pl.BlockSpec((tokens, LANES), lambda i, s: (0, 2 * first + i))
    keys = pl.BlockSpec((length, LANES), lambda i, s: (0, (first + i // 2) // 2))
    values = pl.BlockSpec(
        (length, LANES), lambda i, s: (0, (KEY_VALUE_HEADS + first + i // 2) // 2)
    )
    columns = 2 * count * HEAD_SIZE
    return pl.pallas_call(
        partial(attend_backward_kernel, first, count),
        grid_spec=pltpu.PrefetchScalarGridSpec(
            num_scalar_prefetch=1,
            grid=(2 * count,),
            in_specs=[own, keys, values, own, own, own],
            out_specs=[
                pl.BlockSpec((tokens, LANES), lambda i, s: (0, i)),
                pl.BlockSpec((length, columns), lambda i, s: (0, 0)),
            ],
            scratch_shapes=[pltpu.VMEM((length, LANES), f32), pltpu.VMEM((length, LANES), f32)],
        ),
        out_shape=[
            jax.ShapeDtypeStruct((tokens, count * group), bf16),
            jax.ShapeDtypeStruct((length, columns), bf16),
        ],
        compiler_params=pltpu.CompilerParams(vmem_limit_bytes=VMEM_LIMIT),
        name="attend_backward",
        cost_estimate=LIGHT,
    )(place, queries, keys_values, keys_values, mixed, logs, grad_mixed)


def hidden_kernel(n0_ref, n1_ref, wg_ref, wu_ref, hidden_ref, gate_ref, up_ref, n_all):
    tokens = n0_ref.shape[0]

    @pl.when(pl.program_id(0) == 0)
    def _():
        n_all[:tokens] = n0_ref[...]
        n_all[tokens:] = n1_ref[...]

    gate = dot_nn(n_all[...], wg_ref[...])
    up = dot_nn(n_all[...], wu_ref[...])
    hidden_ref[...] = (gate / (1.0 + jnp.exp(-gate)) * up).astype(bf16)
    gate_ref[...] = gate.astype(bf16)
    up_ref[...] = up.astype(bf16)


def hidden_pass(normed, wgate, wup):
    tokens, width = normed[0].shape
    columns = wgate.shape[1]
    tile = min(256, columns)
    whole = pl.BlockSpec((tokens, width), lambda i: (0, 0))
    down = pl.BlockSpec((width, tile), lambda i: (0, i))
    out = pl.BlockSpec((2 * tokens, tile), lambda i: (0, i))
    return pl.pallas_call(
        hidden_kernel,
        grid=(pl.cdiv(columns, tile),),
        in_specs=[whole] * 2 + [down] * 2,
        out_specs=[out] * 3,
        out_shape=[jax.ShapeDtypeStruct((2 * tokens, columns), bf16)] * 3,
        scratch_shapes=[pltpu.VMEM((2 * tokens, width), bf16)],
        compiler_params=pltpu.CompilerParams(vmem_limit_bytes=VMEM_LIMIT),
        name="hidden_pass",
        cost_estimate=LIGHT,
    )(*normed, wgate, wup)


def gates_kernel(g0_ref, g1_ref, wd_ref, gate_ref, up_ref, gate_out_ref, up_out_ref, g_all):
    tokens = g0_ref.shape[0]

    @pl.when(pl.program_id(0) == 0)
    def _():
        g_all[:tokens] = g0_ref[...]
        g_all[tokens:] = g1_ref[...]

    grad = dot_nt(g_all[...], wd_ref[...])
    gate = gate_ref[...].astype(f32)
    up = up_ref[...].astype(f32)
    sigmoid = 1.0 / (1.0 + jnp.exp(-gate))
    gate_out_ref[...] = (grad * up * (sigmoid * (1.0 + gate * (1.0 - sigmoid)))).astype(bf16)
    up_out_ref[...] = (grad * (gate * sigmoid)).astype(bf16)


def gates_pass(grad_top, wdown, gate, up):
    tokens, width = grad_top[0].shape
    columns = gate.shape[1]
    tile = min(256, columns)
    whole = pl.BlockSpec((tokens, width), lambda i: (0, 0))
    out = pl.BlockSpec((2 * tokens, tile), lambda i: (0, i))
    return pl.pallas_call(
        gates_kernel,
        grid=(pl.cdiv(columns, tile),),
        in_specs=[whole] * 2 + [pl.BlockSpec((tile, width), lambda i: (i, 0)), out, out],
        out_specs=[out] * 2,
        out_shape=[jax.ShapeDtypeStruct((2 * tokens, columns), bf16)] * 2,
        scratch_shapes=[pltpu.VMEM((2 * tokens, width), bf16)],
        compiler_params=pltpu.CompilerParams(vmem_limit_bytes=VMEM_LIMIT),
        name="gates_pass",
        cost_estimate=LIGHT,
    )(*grad_top, wdown, gate, up)


def back_kernel(count, transposed, *refs):
    own_ref, send_ref = refs[-2:]
    tokens = own_ref.shape[0]
    dot = dot_nt if transposed else dot_nn

    def total(start):
        rows = pl.ds(start, tokens)
        result = dot(refs[0][rows, :], refs[count][...])
        for i in range(1, count):
            result = result + dot(refs[i][rows, :], refs[count + i][...])
        return result

    own_ref[...] = total(0)
    send_ref[...] = total(tokens).astype(bf16)


def back_pass(lefts, weights, transposed):
    tokens, depth = lefts[0].shape
    width = weights[0].shape[0 if transposed else 1]
    count = len(lefts)
    tile = min(512, width)
    if transposed:
        weight_spec = pl.BlockSpec((tile, depth), lambda i: (i, 0))
    else:
        weight_spec = pl.BlockSpec((depth, tile), lambda i: (0, i))
    out = pl.BlockSpec((tokens // 2, tile), lambda i: (0, i))
    return pl.pallas_call(
        partial(back_kernel, count, transposed),
        grid=(width // tile,),
        in_specs=[pl.BlockSpec((tokens, depth), lambda i: (0, 0))] * count
        + [weight_spec] * count,
        out_specs=[out, out],
        out_shape=[
            jax.ShapeDtypeStruct((tokens // 2, width), f32),
            jax.ShapeDtypeStruct((tokens // 2, width), bf16),
        ],
        compiler_params=pltpu.CompilerParams(vmem_limit_bytes=VMEM_LIMIT),
        name="back_pass",
        cost_estimate=LIGHT,
    )(*lefts, *weights)


def weight_kernel(left_count, *refs):
    lefts, rights, out_ref = refs[:left_count], refs[left_count:-1], refs[-1]
    step = min(lefts[0].shape[0], rights[0].shape[0])

    def piece(refs, start):
        index, offset = divmod(start, refs[0].shape[0])
        return refs[index][pl.ds(offset, step), :]

    total = None
    for start in range(0, left_count * lefts[0].shape[0], step):
        term = dot_tn(piece(lefts, start), piece(rights, start))
        total = term if total is None else total + term
    out_ref[...] = total.astype(bf16)


def weight_pass(lefts, rights):
    rows, columns = lefts[0].shape[1], rights[0].shape[1]
    tile = 512 if rows % 512 == 0 else 384 if rows % 384 == 0 else rows
    return pl.pallas_call(
        partial(weight_kernel, len(lefts)),
        grid=(rows // tile,),
        in_specs=[pl.BlockSpec((left.shape[0], tile), lambda i: (0, i)) for left in lefts]
        + [pl.BlockSpec(right.shape, lambda i: (0, 0)) for right in rights],
        out_specs=pl.BlockSpec((tile, columns), lambda i: (i, 0)),
        out_shape=jax.ShapeDtypeStruct((rows, columns), bf16),
        compiler_params=pltpu.CompilerParams(vmem_limit_bytes=VMEM_LIMIT),
        name="weight_pass",
        cost_estimate=LIGHT,
    )(*lefts, *rights)


def placed_kernel(side_ref, own_ref, other_ref, out_ref):
    mine = pl.program_id(0) == side_ref[0]

    @pl.when(mine)
    def _():
        out_ref[0, 0] = own_ref[:, 0]

    @pl.when(jnp.logical_not(mine))
    def _():
        out_ref[0, 0] = other_ref[:, 0]


def placed(own, other, side):
    seq, group, rows, columns = own.shape

    def entry(mine, e, g, s):
        parked = jnp.where(e == 0, 0, group - 1)
        return (0, jnp.where((e == s[0]) == mine, g, parked), 0, 0)

    return pl.pallas_call(
        placed_kernel,
        grid_spec=pltpu.PrefetchScalarGridSpec(
            num_scalar_prefetch=1,
            grid=(2, group),
            in_specs=[
                pl.BlockSpec((seq, 1, rows, columns), partial(entry, True)),
                pl.BlockSpec((seq, 1, rows, columns), partial(entry, False)),
            ],
            out_specs=pl.BlockSpec(
                (1, 1, seq, rows, columns), lambda e, g, s: (e, g, 0, 0, 0)
            ),
        ),
        out_shape=jax.ShapeDtypeStruct((2, group, seq, rows, columns), own.dtype),
        name="placed",
        cost_estimate=LIGHT,
    )(side.astype(jnp.int32).reshape(1), own, other)


def joined_kernel(side_ref, own_ref, other_ref, out_ref):
    mine = pl.program_id(1) == side_ref[0]

    @pl.when(mine)
    def _():
        out_ref[:, 0] = own_ref[...]

    @pl.when(jnp.logical_not(mine))
    def _():
        out_ref[:, 0] = other_ref[...]


def joined(own, other, side, axis):
    shape = own.shape[:axis] + (2,) + own.shape[axis:]
    columns = own.shape[-1]
    lead = math.prod(own.shape[:axis])
    rows = math.prod(own.shape[axis:-1])
    leads, chunks = lead, 1
    while leads % 2 == 0 and leads * rows * columns > 800_000:
        leads //= 2
    while leads == 1 and rows % (32 * chunks) == 0 and rows // chunks * columns > 800_000:
        chunks *= 2
    block = rows // chunks

    def entry(mine, p, e, i, s):
        parked = jnp.where(e == 0, 0, chunks - 1)
        return (p, jnp.where((e == s[0]) == mine, i, parked), 0)

    return pl.pallas_call(
        joined_kernel,
        grid_spec=pltpu.PrefetchScalarGridSpec(
            num_scalar_prefetch=1,
            grid=(lead // leads, 2, chunks),
            in_specs=[
                pl.BlockSpec((leads, block, columns), partial(entry, True)),
                pl.BlockSpec((leads, block, columns), partial(entry, False)),
            ],
            out_specs=pl.BlockSpec((leads, 1, block, columns), lambda p, e, i, s: (p, e, i, 0)),
        ),
        out_shape=jax.ShapeDtypeStruct((lead, 2, rows, columns), own.dtype),
        compiler_params=pltpu.CompilerParams(vmem_limit_bytes=VMEM_LIMIT),
        name="joined",
        cost_estimate=LIGHT,
    )(
        side.astype(jnp.int32).reshape(1),
        own.reshape(lead, rows, columns),
        other.reshape(lead, rows, columns),
    ).reshape(shape)


def swap(values, bit):
    pairs = [(i, i ^ bit) for i in range(lax.axis_size("rows"))]
    return lax.ppermute(values, "rows", pairs)


def bit_of(bit):
    return (lax.axis_index("rows") // bit) % 2


def gather_bit(values, bit, axis):
    return joined(values, swap(values, bit), bit_of(bit), axis)


def part(values, index, axis):
    return lax.dynamic_index_in_dim(values, index, axis, keepdims=False)


def reduce_bit(values, bit, axis):
    return add_bit(values, pass_bit(values, bit, axis), bit, axis)


def outer_pairs(step, low, high):
    size = lax.axis_size("rows")
    return [
        (i, i + 4 * step)
        for i in range(size)
        if low <= i // 4 < high and 0 <= i // 4 + step < size // 4
    ]


def send_outer(values):
    count = lax.axis_size("rows") // 4
    if count == 2:
        return (swap(values, 4),)
    up, down = values, values
    ups, downs = [], []
    for t in range(1, count):
        up = lax.ppermute(up, "rows", outer_pairs(1, t - 1, count))
        down = lax.ppermute(down, "rows", outer_pairs(-1, 0, count - t + 1))
        ups.append(up)
        downs.append(down)
    return tuple(ups[::-1] + downs)


def join_outer(values, received, axis):
    count = lax.axis_size("rows") // 4
    if count == 2:
        return joined(values, received[0], bit_of(4), axis)
    place = lax.axis_index("rows") // 4
    line = jnp.stack([*received[: count - 1], values, *received[count - 1 :]], axis)
    return lax.dynamic_slice_in_dim(line, count - 1 - place, count, axis)


def gather_outer(values, axis):
    return join_outer(values, send_outer(values), axis)


def pass_outer(values, axis):
    count = lax.axis_size("rows") // 4
    place = lax.axis_index("rows") // 4

    def entry(index):
        return part(values, jnp.clip(index, 0, count - 1), axis)

    if count == 1:
        return ()
    if count == 2:
        return (swap(entry(1 - place), 4),)
    up, down = entry(place + count - 1), entry(place - count + 1)
    for t in range(1, count):
        up = lax.ppermute(up, "rows", outer_pairs(1, 0, t))
        down = lax.ppermute(down, "rows", outer_pairs(-1, count - t, count))
        if t < count - 1:
            up = (entry(place + count - 1 - t).astype(f32) + up.astype(f32)).astype(bf16)
            down = (entry(place - count + 1 + t).astype(f32) + down.astype(f32)).astype(bf16)
    return (up, down)


def add_outer(values, received, axis):
    total = part(values, lax.axis_index("rows") // 4, axis).astype(f32)
    for term in received:
        total = total + term.astype(f32)
    return total.astype(bf16)


def reduce_outer(values, axis):
    return add_outer(values, pass_outer(values, axis), axis)


def pass_bit(values, bit, axis):
    return swap(part(values, 1 - bit_of(bit), axis), bit)


def add_bit(values, received, bit, axis):
    own = part(values, bit_of(bit), axis)
    return (own.astype(f32) + received.astype(f32)).astype(bf16)


def gather_seq(values):
    return lax.all_gather(values, "seq", axis=0, tiled=False)


def reduce_seq(values):
    return lax.psum_scatter(values, "seq", scatter_dimension=0, tiled=False)


def exchange(values, axis, bit):
    size = lax.axis_size(axis)
    return lax.ppermute(values, axis, [(i, i ^ bit) for i in range(size)])


def across_group(own, send):
    return (own + swap(send, 1).astype(f32)).astype(bf16)


def stage(*values):
    return lax.optimization_barrier(values)


def mm(left, right):
    return jnp.einsum("ab,bc->ac", left, right, preferred_element_type=f32)


def mm_t(left, right):
    return jnp.einsum("ab,cb->ac", left, right, preferred_element_type=f32)


def t_mm(left, right):
    return jnp.einsum("ab,ac->bc", left, right, preferred_element_type=f32)


def norm_scale(values):
    return lax.rsqrt(jnp.mean(values * values, axis=-1, keepdims=True) + EPSILON)


def norm_backward(values, scale, gain, grad):
    gained = grad * gain
    inner = jnp.mean(values * gained, axis=-1, keepdims=True)
    result = scale * gained - values * (scale * scale * scale) * inner
    return result, jnp.sum(grad * values * scale, axis=0)


def shards(
    tokens_in,
    corpus,
    corpus_weight,
    w_qkv,
    w_out,
    w_gate,
    w_up,
    w_down,
    attn_gain,
    ffn_gain,
    q_gain,
    k_gain,
    upstream,
):
    shard_length, width = tokens_in.shape[1:]
    row_devices = lax.axis_size("rows")
    seq_devices = lax.axis_size("seq")
    outer = row_devices // 4
    d_rows = w_qkv.shape[0]
    f_rows = w_down.shape[0]
    place = lax.axis_index("seq").astype(jnp.int32)
    inputs = tokens_in[0].astype(f32)

    extra = jnp.stack(
        [
            attn_gain,
            ffn_gain,
            jnp.broadcast_to(corpus.astype(bf16), attn_gain.shape),
        ],
        axis=1,
    )
    extra = jnp.pad(extra, ((0, 0), (0, LANES - extra.shape[1])))
    kv_shard = jnp.concatenate([w_qkv[:, QUERY_COLUMNS:], extra], axis=1)
    query_shard = jnp.concatenate([w_qkv[:, :QUERY_COLUMNS], w_out.T], axis=1)
    query_shard, w_gate, w_up = stage(query_shard, w_gate, w_up)
    query_lines = gather_seq(query_shard)

    def to_group(weight):
        blocks = weight.reshape(d_rows, outer, 4, seq_devices, f_rows)
        blocks = jnp.transpose(blocks, (2, 0, 3, 1, 4))
        return blocks.reshape(2, 2, d_rows, outer * seq_devices * f_rows)

    def spread_hidden(lines, received):
        if outer == 2:
            lines = lines.reshape(seq_devices, 4, d_rows, hidden_columns)
            other = received[0].reshape(lines.shape)
            return placed(lines, other, bit_of(4)).reshape(width, hidden_columns)
        full = join_outer(lines, received, 0)
        return jnp.moveaxis(full, 1, 3).reshape(width, hidden_columns)

    gate_up = jnp.stack([to_group(w_gate), to_group(w_up)], axis=2)
    hidden_columns = gate_up.shape[-1]
    core, near = bit_of(1), bit_of(2)
    gate_up = joined(
        part(gate_up, core, 1), swap(part(gate_up, 1 - core, 1), 1), core, 1
    )
    gate_up, kv_shard = stage(gate_up, kv_shard)
    other, kv_lines, query_lines = stage(
        swap(part(gate_up, 1 - near, 0), 2), gather_seq(kv_shard), query_lines
    )
    gate_up = joined(part(gate_up, near, 0), other, near, 0)
    gate_lines = gather_seq(gate_up[:, :, 0])
    left, right = kv_lines[..., : 3 * LANES], kv_lines[..., 3 * LANES :]
    left_other, right_other = stage(send_outer(left), swap(right, 2))
    left = join_outer(left, left_other, 0)
    right = joined(right, right_other, near, 0)
    left_other, right_other = stage(swap(left, 2), send_outer(right))
    left = joined(left, left_other, near, 1)
    right = join_outer(right, right_other, 0)
    q_left, q_right = query_lines[..., :QUERY_COLUMNS], query_lines[..., QUERY_COLUMNS:]
    q_left, q_right, left, right = stage(q_left, q_right, left, right)
    q_left_other, q_right_other = send_outer(q_left), swap(q_right, 2)
    left, right = gather_bit(left, 1, 2), gather_bit(right, 1, 2)
    left, right = left.reshape(width, -1), right.reshape(width, -1)
    wkv = jnp.concatenate([left, right[:, : 2 * LANES]], axis=1)
    rows = dot_nt(jnp.eye(8, LANES, dtype=bf16), right[:, 2 * LANES :])
    attn_gain_full, ffn_gain_full, corpus_full = rows[0:1], rows[1:2], rows[2]

    position = (place * shard_length + jnp.arange(shard_length, dtype=jnp.int32)).astype(f32)
    half = HEAD_SIZE // 2
    exponent = jnp.arange(half, dtype=f32) * (-2.0 / HEAD_SIZE)
    angles = position[:, None] * jnp.power(ROPE_BASE, exponent)[None, :]
    cosine, sine = jnp.cos(angles), jnp.sin(angles)
    cos_table = jnp.concatenate([cosine] * 4, axis=1)
    sin_table = jnp.concatenate([-sine, sine] * 2, axis=1)
    wide_q = jnp.tile(q_gain.astype(f32), QUERY_HEADS)
    wide_k = jnp.concatenate(
        [jnp.tile(k_gain.astype(f32), KEY_VALUE_HEADS), jnp.ones((KEY_COLUMNS,), f32)]
    )
    wide_q = jnp.broadcast_to(wide_q[None, :], (8, QUERY_COLUMNS))
    wide_k = jnp.broadcast_to(wide_k[None, :], (8, 2 * KEY_COLUMNS))

    in_scale = norm_scale(inputs)
    normed = (inputs * in_scale * attn_gain_full).astype(bf16)
    joint_kv, own_kv = heads_forward(
        normed, wkv, wide_k, cos_table, sin_table, KEY_COLUMNS
    )
    own_kv, q_left_other, q_right_other, down_other, up_in = stage(
        own_kv, q_left_other, q_right_other, send_outer(w_down), gate_up[:, :, 1]
    )
    up_lines = gather_seq(up_in)
    keys_values = gather_seq(own_kv).reshape(-1, 2 * KEY_COLUMNS)
    q_left = join_outer(q_left, q_left_other, 0)
    q_right = joined(q_right, q_right_other, near, 0)
    left_other, right_other, gate_lines = stage(
        swap(q_left, 2), send_outer(q_right), gate_lines
    )
    q_left = joined(q_left, left_other, near, 1)
    gate_other = send_outer(gate_lines)
    wq = gather_bit(q_left, 1, 2).reshape(width, -1)

    corpora = jnp.arange(CORPORA, dtype=jnp.int32)
    per_device = corpus_full.reshape(-1, d_rows)[:, 0].astype(jnp.int32)
    counts = (
        jnp.sum((per_device[:, None] == corpora[None, :]).astype(f32), axis=0) * shard_length
    )
    own_corpus = (corpus[0] == corpora).astype(f32)
    weight_row = jnp.sum(own_corpus * corpus_weight.astype(f32))
    count_row = jnp.sum(own_corpus * counts)
    factor = weight_row / DENOM * (jnp.sum(counts) / (CORPORA * count_row))
    grad_full = upstream[0].astype(f32) * factor
    grad_top, wq = stage(grad_full.astype(bf16), wq)

    joint_q, queries = heads_forward(
        normed, wq, wide_q, cos_table, sin_table, QUERY_COLUMNS
    )
    queries, q_right, right_other, down_other = stage(queries, q_right, right_other, down_other)
    q_right = join_outer(q_right, right_other, 0)
    down_pair = join_outer(w_down, down_other, 0)
    place_array = place.reshape(1)
    keys_values, queries, down_in = stage(keys_values, queries, down_pair)
    down_lines = gather_seq(down_in)
    mixed, logs = attend_forward(place_array, queries, keys_values)
    mixed, grad_top1, grad_top2, up_lines, wout_other = stage(
        mixed, swap(grad_top, 1), swap(grad_top, 2), up_lines, swap(q_right, 1)
    )
    wout_t = joined(q_right, wout_other, core, 2).reshape(width, -1)
    middle = inputs + mm_t(mixed, wout_t)

    ffn_scale = norm_scale(middle)
    normed_ffn = (middle * ffn_scale * ffn_gain_full).astype(bf16)
    up_other = send_outer(up_lines)
    normed_ffn, gate_other = stage(normed_ffn, gate_other)
    normed1, normed2, up_other, wgate = stage(
        swap(normed_ffn, 1),
        swap(normed_ffn, 2),
        up_other,
        spread_hidden(gate_lines, gate_other),
    )
    wup = spread_hidden(up_lines, up_other)
    hidden_near, gate_near, up_near = hidden_pass((normed_ffn, normed1), wgate, wup)
    normed3, hidden_near, grad_top3 = stage(
        swap(normed2, 1), hidden_near, swap(grad_top2, 1)
    )
    hidden_far, gate_far, up_far = hidden_pass((normed2, normed3), wgate, wup)
    normed4 = (normed_ffn, normed1, normed2, normed3)
    grad_top4 = (grad_top, grad_top1, grad_top2, grad_top3)
    wdown = down_lines.reshape(hidden_columns, width)
    gate_far, up_far = gates_pass((grad_top2, grad_top3), wdown, gate_far, up_far)
    own, send = back_pass((gate_far, up_far), (wgate, wup), True)
    grad_wdown = weight_pass((hidden_near, hidden_far), grad_top4)
    own, send, grad_wdown, wdown = stage(own, swap(send, 1), grad_wdown, wdown)
    across = (own + send.astype(f32)).astype(bf16)
    across, wdown = stage(across, wdown)
    gate_near, up_near = gates_pass((grad_top, grad_top1), wdown, gate_near, up_near)
    own, send = back_pass((gate_near, up_near), (wgate, wup), True)
    hidden_shape = (outer, 2, 2, seq_devices, d_rows, hidden_columns)
    grad_wdown = grad_wdown.reshape(seq_devices, outer, f_rows, width)
    grad_wgate = weight_pass(normed4, (gate_near, gate_far)).reshape(hidden_shape)
    across, own, send, grad_wgate, up_near = stage(
        swap(across, 2), own, send, grad_wgate, up_near
    )
    grad_wup = weight_pass(normed4, (up_near, up_far)).reshape(hidden_shape)
    send, grad_wup, down_other = stage(swap(send, 1), grad_wup, pass_outer(grad_wdown, 1))
    grad_wdown = add_outer(grad_wdown, down_other, 1)
    own = own + send.astype(f32)
    grad_normed_ffn = own + across.astype(f32)
    grad_wdown = reduce_seq(grad_wdown)

    grad_middle_part, grad_ffn_gain = norm_backward(
        middle, ffn_scale, ffn_gain_full, grad_normed_ffn
    )
    grad_middle = grad_full + grad_middle_part
    grad_branch = grad_middle.astype(bf16)
    grad_mixed = mm(grad_branch, wout_t).astype(bf16)
    attend = (place_array, queries, keys_values, mixed, logs)
    grad_q1, grad_kv1 = attend_backward(0, 2, *attend, grad_mixed)
    gate_other = pass_outer(grad_wgate, 0)
    grad_q1, grad_kv1, grad_mixed, grad_wdown, hidden_far = stage(
        grad_q1, grad_kv1, grad_mixed, grad_wdown, hidden_far
    )
    grad_kv1 = reduce_seq(grad_kv1.reshape(seq_devices, shard_length, -1))
    shape = (outer, 2, 2, seq_devices, d_rows)
    own_far, send_far = back_pass((hidden_far,), (wdown,), False)
    grad_wout, far_other, gate_other, grad_mixed = stage(
        t_mm(grad_branch, mixed).astype(bf16).reshape(*shape, QUERY_COLUMNS),
        swap(send_far, 1),
        gate_other,
        grad_mixed,
    )
    grad_gate = reduce_seq(jnp.moveaxis(add_outer(grad_wgate, gate_other, 0), 2, 0))
    across = (own_far + far_other.astype(f32)).astype(bf16)
    across, grad_mixed = stage(across, grad_mixed)
    grad_q2, grad_kv2 = attend_backward(2, 3, *attend, grad_mixed)
    grad_q2, grad_kv2, hidden_near, grad_kv1, grad_gate, wout_other, up_other, across = stage(
        grad_q2,
        grad_kv2,
        hidden_near,
        grad_kv1,
        grad_gate,
        pass_bit(grad_wout, 1, 2),
        pass_outer(grad_wup, 0),
        swap(across, 2),
    )
    grad_kv2 = reduce_seq(grad_kv2.reshape(seq_devices, shard_length, -1))

    grad_q = jnp.concatenate([grad_q1, grad_q2], axis=1)
    joint_grad_q, gain_q = heads_backward(
        grad_q, joint_q, wide_q, cos_table, sin_table, QUERY_COLUMNS
    )
    grad_wq = t_mm(normed, joint_grad_q).astype(bf16).reshape(*shape, QUERY_COLUMNS)
    grad_wout = add_bit(grad_wout, wout_other, 1, 2)
    grad_up = jnp.moveaxis(add_outer(grad_wup, up_other, 0), 2, 0)
    grad_kv2, joint_grad_q, grad_wq, grad_wout, grad_up = stage(
        grad_kv2, joint_grad_q, grad_wq, grad_wout, grad_up
    )
    grad_up = reduce_seq(grad_up)
    own_near, send_near = back_pass((hidden_near,), (wdown,), False)
    wq_other, grad_kv2, own_near, send_near = stage(
        pass_bit(grad_wq, 1, 2), grad_kv2, own_near, send_near
    )
    grad_wq, grad_kv2 = stage(add_bit(grad_wq, wq_other, 1, 2), grad_kv2)
    wq_other, wout_other = pass_bit(grad_wq, 2, 1), pass_outer(grad_wout, 0)


    grad_kv1, grad_kv2 = (
        part_.reshape(shard_length, 2, -1) for part_ in (grad_kv1, grad_kv2)
    )
    grad_kv = jnp.concatenate([grad_kv1, grad_kv2], axis=2).reshape(shard_length, -1)
    joint_grad_kv, gain_k = heads_backward(
        grad_kv, joint_kv, wide_k, cos_table, sin_table, KEY_COLUMNS
    )
    grad_wkv = t_mm(normed, joint_grad_kv).astype(bf16)
    grad_normed = mm_t(joint_grad_q, wq) + mm_t(joint_grad_kv, wkv)
    grad_input_part, grad_attn_gain = norm_backward(
        inputs, in_scale, attn_gain_full, grad_normed
    )
    input_grad = (grad_middle + grad_input_part).astype(bf16)

    gain_rows = jnp.stack([grad_attn_gain, grad_ffn_gain]).astype(bf16)
    gain_columns = t_mm(gain_rows, jnp.eye(2, LANES, dtype=bf16)).astype(bf16)
    grad_wkv, gain_columns, wq_other, wout_other, near_other = stage(
        grad_wkv, gain_columns, wq_other, wout_other, swap(send_near, 1)
    )
    output = (middle + own_near + near_other.astype(f32) + across.astype(f32)).astype(bf16)
    grad_wq = add_bit(grad_wq, wq_other, 2, 1)
    grad_wout = add_outer(grad_wout, wout_other, 0)
    wq_other, wout_other = pass_outer(grad_wq, 0), pass_bit(grad_wout, 2, 0)
    left = grad_wkv[:, : 3 * LANES].reshape(*shape, -1)
    right = jnp.concatenate([grad_wkv[:, 3 * LANES :], gain_columns], axis=1)
    right = right.reshape(*shape, -1)
    head_gains = jnp.concatenate(
        [
            jnp.sum(gain_q[0].reshape(-1, HEAD_SIZE), axis=0),
            jnp.sum(gain_k[0, :KEY_COLUMNS].reshape(-1, HEAD_SIZE), axis=0),
        ]
    )[None]
    left, right, left_other, right_other, gains_other = stage(
        left,
        right,
        pass_bit(left, 1, 2),
        pass_bit(right, 1, 2),
        exchange(head_gains, "rows", 1),
    )
    head_gains = head_gains + gains_other
    left = add_bit(left, left_other, 1, 2)
    right = add_bit(right, right_other, 1, 2)
    left_other, right_other, wq_other, wout_other, gains_other, grad_up = stage(
        pass_bit(left, 2, 1),
        pass_outer(right, 0),
        wq_other,
        wout_other,
        exchange(head_gains, "seq", 1),
        grad_up,
    )
    head_gains = head_gains + gains_other
    left = add_bit(left, left_other, 2, 1)
    right = add_outer(right, right_other, 0)
    left_other, right_other, gains_other = stage(
        pass_outer(left, 0), pass_bit(right, 2, 0), exchange(head_gains, "rows", 2)
    )
    head_gains = head_gains + gains_other
    sums = reduce_seq(
        jnp.concatenate(
            [
                add_outer(grad_wq, wq_other, 0),
                add_outer(left, left_other, 0),
                add_bit(right, right_other, 2, 0),
                add_bit(grad_wout, wout_other, 2, 0),
            ],
            axis=-1,
        )
    )
    rest = [("rows", bit) for bit in (4, 8, 16) if bit < row_devices]
    rest += [("seq", bit) for bit in (2, 4, 8) if bit < seq_devices]
    gate_up = jnp.stack([grad_gate, grad_up], axis=2)
    other, gains_other = stage(
        swap(part(gate_up, 1 - near, 0), 2), exchange(head_gains, *rest[0])
    )
    head_gains = head_gains + gains_other
    grads = joined(part(gate_up, near, 0), other, near, 0)
    for axis, bit in rest[1:]:
        head_gains = head_gains + exchange(head_gains, axis, bit)
    head_gains = head_gains[0]
    grads = joined(part(grads, core, 1), swap(part(grads, 1 - core, 1), 1), core, 1)

    def from_group(blocks):
        blocks = blocks.reshape(4, d_rows, seq_devices, outer, f_rows)
        return jnp.transpose(blocks, (1, 3, 0, 2, 4)).reshape(d_rows, -1)

    grad_wgate, grad_wup = stage(from_group(grads[:, :, 0]), from_group(grads[:, :, 1]))
    sums, grad_wgate, grad_wup, grad_wdown, output, input_grad = stage(
        sums, grad_wgate.astype(f32), grad_wup.astype(f32), grad_wdown.astype(f32), output, input_grad
    )
    columns = QUERY_COLUMNS + 2 * KEY_COLUMNS
    long_gains = sums[:, columns : columns + 2].astype(f32)
    return (
        output[None],
        input_grad[None],
        sums[:, :columns].astype(f32),
        sums[:, columns + LANES :].T.astype(f32),
        grad_wgate,
        grad_wup,
        grad_wdown,
        long_gains[:, 0],
        long_gains[:, 1],
        head_gains[:HEAD_SIZE],
        head_gains[HEAD_SIZE:],
    )


def solution(mesh):
    return jax.shard_map(
        shards,
        mesh=mesh,
        in_specs=(
            P("rows", "seq", None),
            P("rows"),
            P(),
            P(("rows", "seq"), None),
            P(None, ("rows", "seq")),
            P(("rows", "seq"), None),
            P(("rows", "seq"), None),
            P(("rows", "seq"), None),
            P(("rows", "seq")),
            P(("rows", "seq")),
            P(),
            P(),
            P("rows", "seq", None),
        ),
        out_specs=(
            P("rows", "seq", None),
            P("rows", "seq", None),
            P(("rows", "seq"), None),
            P(None, ("rows", "seq")),
            P(("rows", "seq"), None),
            P(("rows", "seq"), None),
            P(("rows", "seq"), None),
            P(("rows", "seq")),
            P(("rows", "seq")),
            P(),
            P(),
        ),
        check_vma=False,
    )
```

```python
import math
from functools import partial

import jax
import jax.numpy as jnp
from jax import lax
from jax.experimental import pallas as pl
from jax.experimental.pallas import tpu as pltpu
from jax.sharding import PartitionSpec as P

QUERY_HEADS = 20
KEY_VALUE_HEADS = 5
HEAD_SIZE = 64
CORPORA = 8
DENOM = 64
EPSILON = 1e-06
ROPE_BASE = 10000.0
QUERY_COLUMNS = QUERY_HEADS * HEAD_SIZE
KEY_COLUMNS = KEY_VALUE_HEADS * HEAD_SIZE
LANES = 128
SCORE_EXPONENT = 1.4426950408889634 * HEAD_SIZE**-0.5
SPLIT = 2
VMEM_LIMIT = 48 * 1024 * 1024

f32, bf16 = jnp.float32, jnp.bfloat16
LIGHT = pl.CostEstimate(flops=1000, bytes_accessed=1000, transcendentals=0)


def dot_nn(a, b):
    return lax.dot_general(a, b, (((1,), (0,)), ((), ())), preferred_element_type=f32)


def dot_nt(a, b):
    return lax.dot_general(a, b, (((1,), (1,)), ((), ())), preferred_element_type=f32)


def dot_tn(a, b):
    return lax.dot_general(a, b, (((0,), (0,)), ((), ())), preferred_element_type=f32)


def lanes_of(shape):
    return lax.broadcasted_iota(jnp.int32, shape, len(shape) - 1)


def head_sum(values):
    row = lax.broadcasted_iota(jnp.int32, (LANES, LANES), 0) // HEAD_SIZE
    column = lax.broadcasted_iota(jnp.int32, (LANES, LANES), 1) // HEAD_SIZE
    ones = jnp.where(row == column, 1.0, 0.0).astype(bf16)
    high = values.astype(bf16)
    low = (values - high.astype(f32)).astype(bf16)
    return dot_nn(high, ones) + dot_nn(low, ones)


def partner(values):
    first = lanes_of(values.shape) % HEAD_SIZE < HEAD_SIZE // 2
    return jnp.where(
        first,
        pltpu.roll(values, LANES - HEAD_SIZE // 2, 1),
        pltpu.roll(values, HEAD_SIZE // 2, 1),
    )


def heads_forward_kernel(
    norm_columns, normed_ref, weight_ref, gain_ref, cos_ref, sin_ref, joint_ref, out_ref
):
    joint = dot_nn(normed_ref[...], weight_ref[...])
    joint_ref[...] = joint
    columns = joint.shape[1]
    for start in range(0, columns, LANES):
        chunk = slice(start, start + LANES)
        values = joint[:, chunk]
        scale = lax.rsqrt(head_sum(values * values) * (1.0 / HEAD_SIZE) + EPSILON)
        normed = values * scale * gain_ref[0:1, chunk]
        turned = normed * cos_ref[...] + partner(normed) * sin_ref[...]
        place = pl.program_id(0) * columns + start + lanes_of(values.shape)
        out_ref[:, chunk] = jnp.where(place < norm_columns, turned, values).astype(bf16)


def heads_forward(normed, weight, gain, cos, sin, norm_columns):
    tokens, width = normed.shape
    columns = weight.shape[1]
    tile = 2 * LANES if columns % (2 * LANES) == 0 else LANES
    out = pl.BlockSpec((tokens, tile), lambda i: (0, i))
    table = pl.BlockSpec((tokens, LANES), lambda i: (0, 0))
    return pl.pallas_call(
        partial(heads_forward_kernel, norm_columns),
        grid=(columns // tile,),
        in_specs=[
            pl.BlockSpec((tokens, width), lambda i: (0, 0)),
            pl.BlockSpec((width, tile), lambda i: (0, i)),
            pl.BlockSpec((8, tile), lambda i: (0, i)),
            table,
            table,
        ],
        out_specs=[out, out],
        out_shape=[
            jax.ShapeDtypeStruct((tokens, columns), f32),
            jax.ShapeDtypeStruct((tokens, columns), bf16),
        ],
        compiler_params=pltpu.CompilerParams(vmem_limit_bytes=VMEM_LIMIT),
        name="heads_forward",
        cost_estimate=LIGHT,
    )(normed, weight, gain, cos, sin)


def project_kernel(side_ref, mixed_ref, own_ref, other_ref, inputs_ref, out_ref):
    mine = pl.program_id(0) % 2 == side_ref[0]

    @pl.when(mine)
    def _():
        out_ref[...] = inputs_ref[...].astype(f32) + dot_nt(mixed_ref[...], own_ref[0])

    @pl.when(jnp.logical_not(mine))
    def _():
        out_ref[...] = inputs_ref[...].astype(f32) + dot_nt(mixed_ref[...], other_ref[0])


def project(mixed, own, other, inputs, side):
    tokens, depth = mixed.shape
    count, block, _ = own.shape
    weight = pl.BlockSpec((1, block, depth), lambda i, s: (i // 2, 0, 0))
    out = pl.BlockSpec((tokens, block), lambda i, s: (0, i))
    return pl.pallas_call(
        project_kernel,
        grid_spec=pltpu.PrefetchScalarGridSpec(
            num_scalar_prefetch=1,
            grid=(2 * count,),
            in_specs=[pl.BlockSpec((tokens, depth), lambda i, s: (0, 0)), weight, weight, out],
            out_specs=out,
        ),
        out_shape=jax.ShapeDtypeStruct((tokens, 2 * count * block), f32),
        compiler_params=pltpu.CompilerParams(vmem_limit_bytes=VMEM_LIMIT),
        name="project",
        cost_estimate=LIGHT,
    )(side.astype(jnp.int32).reshape(1), mixed, own, other, inputs)


def heads_backward_kernel(
    norm_columns, grad_ref, joint_ref, gain_ref, cos_ref, sin_ref, out_ref, gain_out_ref
):
    grad = grad_ref[...].astype(f32)
    values = joint_ref[...]
    gain = gain_ref[0:1, :]
    turned = grad * cos_ref[...] - partner(grad) * sin_ref[...]
    scale = lax.rsqrt(head_sum(values * values) * (1.0 / HEAD_SIZE) + EPSILON)
    gained = turned * gain
    inner = head_sum(values * gained) * (1.0 / HEAD_SIZE)
    result = scale * gained - values * (scale * scale * scale) * inner
    place = pl.program_id(0) * LANES + lanes_of(values.shape)
    out_ref[...] = jnp.where(place < norm_columns, result, grad).astype(bf16)
    gain_out_ref[...] = jnp.broadcast_to(
        jnp.sum(turned * values * scale, axis=0, keepdims=True), gain_out_ref.shape
    )


def heads_backward(grad, joint, gain, cos, sin, norm_columns):
    tokens, columns = joint.shape
    return pl.pallas_call(
        partial(heads_backward_kernel, norm_columns),
        grid=(columns // LANES,),
        in_specs=[
            pl.BlockSpec((tokens, LANES), lambda i: (0, i)),
            pl.BlockSpec((tokens, LANES), lambda i: (0, i)),
            pl.BlockSpec((8, LANES), lambda i: (0, i)),
            pl.BlockSpec((tokens, LANES), lambda i: (0, 0)),
            pl.BlockSpec((tokens, LANES), lambda i: (0, 0)),
        ],
        out_specs=[
            pl.BlockSpec((tokens, LANES), lambda i: (0, i)),
            pl.BlockSpec((8, LANES), lambda i: (0, i)),
        ],
        out_shape=[
            jax.ShapeDtypeStruct((tokens, columns), bf16),
            jax.ShapeDtypeStruct((8, columns), f32),
        ],
        name="heads_backward",
        cost_estimate=LIGHT,
    )(grad, joint, gain, cos, sin)


def both_halves(pair, odd):
    wide = pair.astype(f32)
    first = lanes_of(wide.shape) < HEAD_SIZE
    keep = jnp.where(odd == 1, jnp.where(first, 0, 1), jnp.where(first, 1, 0)) == 1
    return jnp.where(keep, wide, pltpu.roll(wide, HEAD_SIZE, 1))


def attend_forward_kernel(place_ref, q_ref, k_ref, v_ref, out_ref, log_ref):
    group = pl.program_id(0) // 2
    place = place_ref[0]
    tokens = q_ref.shape[0]
    first = lanes_of((tokens, LANES)) < HEAD_SIZE
    pair = q_ref[...].astype(f32)
    queries = (jnp.where(first, pair, 0.0).astype(bf16), jnp.where(first, 0.0, pair).astype(bf16))

    def step(j, totals, diagonal):
        rows = pl.ds(pl.multiple_of(j * tokens, tokens), tokens)
        keys = both_halves(k_ref[rows, :], group % 2).astype(bf16)
        values = both_halves(v_ref[rows, :], (KEY_VALUE_HEADS + group) % 2)
        sides = (
            jnp.where(first, values, 1.0).astype(bf16),
            jnp.where(first, 1.0, values).astype(bf16),
        )
        result = []
        for head in range(2):
            weights = jnp.exp2(dot_nt(queries[head], keys) * SCORE_EXPONENT)
            if diagonal:
                row = lax.broadcasted_iota(jnp.int32, weights.shape, 0)
                weights = jnp.where(lanes_of(weights.shape) <= row, weights, 0.0)
            result.append(totals[head] + dot_nn(weights.astype(bf16), sides[head]))
        return tuple(result)

    zero = jnp.zeros((tokens, LANES), f32)
    totals = lax.fori_loop(0, place, lambda j, c: step(j, c, False), (zero, zero))
    totals = step(place, totals, True)
    numerator = jnp.where(first, totals[0], totals[1])
    swapped = jnp.where(first, totals[1], totals[0])
    out_ref[...] = (numerator / pltpu.roll(swapped, HEAD_SIZE, 1)).astype(bf16)
    log_ref[...] = jnp.log2(swapped)


def attend_forward(place, queries, keys_values):
    tokens = queries.shape[0]
    length = keys_values.shape[0]
    pairs = QUERY_COLUMNS // LANES
    return pl.pallas_call(
        attend_forward_kernel,
        grid_spec=pltpu.PrefetchScalarGridSpec(
            num_scalar_prefetch=1,
            grid=(pairs,),
            in_specs=[
                pl.BlockSpec((tokens, LANES), lambda i, s: (0, i)),
                pl.BlockSpec((length, LANES), lambda i, s: (0, (i // 2) // 2)),
                pl.BlockSpec((length, LANES), lambda i, s: (0, (KEY_VALUE_HEADS + i // 2) // 2)),
            ],
            out_specs=[
                pl.BlockSpec((tokens, LANES), lambda i, s: (0, i)),
                pl.BlockSpec((tokens, LANES), lambda i, s: (0, i)),
            ],
        ),
        out_shape=[
            jax.ShapeDtypeStruct((tokens, QUERY_COLUMNS), bf16),
            jax.ShapeDtypeStruct((tokens, QUERY_COLUMNS), f32),
        ],
        compiler_params=pltpu.CompilerParams(vmem_limit_bytes=VMEM_LIMIT),
        name="attend_forward",
        cost_estimate=LIGHT,
    )(place, queries, keys_values, keys_values)


def three_parts(values, lane):
    high = values.astype(bf16).astype(f32)
    rest = values - high
    middle = rest.astype(bf16).astype(f32)
    low = rest - middle
    return jnp.where(
        lane == 0, high, jnp.where(lane == 1, middle, jnp.where(lane == 2, low, 0.0))
    )


def attend_backward_kernel(
    first_group, count, place_ref, q_ref, k_ref, v_ref, out_ref, log_ref, grad_ref, dq_ref, dkv_ref, dk_sum, dv_sum
):
    pair_index = pl.program_id(0)
    local = pair_index // 2
    group = first_group + local
    place = place_ref[0]
    tokens = q_ref.shape[0]
    lane = lanes_of((tokens, LANES))
    first = lane < HEAD_SIZE
    inside = lane % HEAD_SIZE
    pair = q_ref[...].astype(f32)
    grad = grad_ref[...].astype(f32)
    delta = pltpu.roll(head_sum(grad * out_ref[...].astype(f32)), HEAD_SIZE, 1)
    logs = three_parts(log_ref[...] * (1.0 / SCORE_EXPONENT), inside)
    deltas = three_parts(delta, inside)
    minus = jnp.where(inside < 3, -1.0, 0.0)

    def sides(own, other):
        return (
            jnp.where(first, own, other).astype(bf16),
            jnp.where(first, other, own).astype(bf16),
        )

    queries = sides(pair, 0.0)
    grads = sides(grad, 0.0)
    def turned(values):
        return jnp.transpose(values.astype(f32)).astype(bf16)

    queries_log = tuple(turned(v) for v in sides(pair, logs))
    grads_delta = tuple(turned(v) for v in sides(grad, deltas))

    @pl.when(pair_index % 2 == 0)
    def _():
        dk_sum[...] = jnp.zeros_like(dk_sum)
        dv_sum[...] = jnp.zeros_like(dv_sum)

    def step(j, dq, diagonal):
        rows = pl.ds(pl.multiple_of(j * tokens, tokens), tokens)
        key_wide = both_halves(k_ref[rows, :], group % 2)
        value_wide = both_halves(v_ref[rows, :], (KEY_VALUE_HEADS + group) % 2)
        keys_turned = jnp.transpose(key_wide)[:HEAD_SIZE].astype(bf16)
        keys_log = sides(key_wide, minus)
        values_delta = sides(value_wide, minus)
        dk = dk_sum[rows, :]
        dv = dv_sum[rows, :]
        parts = list(dq)
        block = tokens // SPLIT
        for sub in range(SPLIT):
            keep = slice(sub * block, (sub + 1) * block)
            dk_part, dv_part = dk[keep], dv[keep]
            start = sub * block if diagonal else 0
            for head in range(2):
                weights = jnp.exp2(
                    dot_nn(keys_log[head][keep], queries_log[head][:, start:]) * SCORE_EXPONENT
                )
                if diagonal:
                    row = lax.broadcasted_iota(jnp.int32, weights.shape, 0)
                    weights = jnp.where(row <= lanes_of(weights.shape), weights, 0.0)
                grad_weights = dot_nn(values_delta[head][keep], grads_delta[head][:, start:])
                grad_scores = (weights * grad_weights).astype(bf16)
                dv_part = dv_part + dot_nn(weights.astype(bf16), grads[head][start:])
                dk_part = dk_part + dot_nn(grad_scores, queries[head][start:])
                term = dot_nn(keys_turned[:, keep], grad_scores)
                if start:
                    term = jnp.concatenate([jnp.zeros((HEAD_SIZE, start), f32), term], axis=1)
                parts[head] = parts[head] + term
            target = pl.ds(pl.multiple_of(j * tokens + sub * block, block), block)
            dk_sum[target, :] = dk_part
            dv_sum[target, :] = dv_part
        return tuple(parts)

    zero = jnp.zeros((HEAD_SIZE, tokens), f32)
    dq = lax.fori_loop(0, place, lambda j, c: step(j, c, False), (zero, zero))
    dq = jnp.transpose(jnp.concatenate(step(place, dq, True), axis=0))
    dq_ref[...] = (dq * HEAD_SIZE**-0.5).astype(bf16)

    @pl.when(pair_index % 2 == 1)
    def _():
        wide_lane = lanes_of(dk_sum.shape)
        for total, slot, factor in (
            (dk_sum, local, HEAD_SIZE**-0.5),
            (dv_sum, count + local, 1.0),
        ):
            both = (total[...] + pltpu.roll(total[...], HEAD_SIZE, 1)) * factor
            columns = pl.ds(pl.multiple_of(slot // 2 * LANES, LANES), LANES)
            mine = wide_lane // HEAD_SIZE == slot % 2
            dkv_ref[:, columns] = jnp.where(
                mine, both, dkv_ref[:, columns].astype(f32)
            ).astype(bf16)


def attend_backward(first, count, place, queries, keys_values, mixed, logs, grad_mixed):
    tokens = queries.shape[0]
    length = keys_values.shape[0]
    group = QUERY_HEADS // KEY_VALUE_HEADS * HEAD_SIZE
    own = pl.BlockSpec((tokens, LANES), lambda i, s: (0, 2 * first + i))
    keys = pl.BlockSpec((length, LANES), lambda i, s: (0, (first + i // 2) // 2))
    values = pl.BlockSpec(
        (length, LANES), lambda i, s: (0, (KEY_VALUE_HEADS + first + i // 2) // 2)
    )
    columns = 2 * count * HEAD_SIZE
    return pl.pallas_call(
        partial(attend_backward_kernel, first, count),
        grid_spec=pltpu.PrefetchScalarGridSpec(
            num_scalar_prefetch=1,
            grid=(2 * count,),
            in_specs=[own, keys, values, own, own, own],
            out_specs=[
                pl.BlockSpec((tokens, LANES), lambda i, s: (0, i)),
                pl.BlockSpec((length, columns), lambda i, s: (0, 0)),
            ],
            scratch_shapes=[pltpu.VMEM((length, LANES), f32), pltpu.VMEM((length, LANES), f32)],
        ),
        out_shape=[
            jax.ShapeDtypeStruct((tokens, count * group), bf16),
            jax.ShapeDtypeStruct((length, columns), bf16),
        ],
        compiler_params=pltpu.CompilerParams(vmem_limit_bytes=VMEM_LIMIT),
        name="attend_backward",
        cost_estimate=LIGHT,
    )(place, queries, keys_values, keys_values, mixed, logs, grad_mixed)


def hidden_kernel(n0_ref, n1_ref, wg_ref, wu_ref, hidden_ref, gate_ref, up_ref, n_all):
    tokens = n0_ref.shape[0]

    @pl.when(pl.program_id(0) == 0)
    def _():
        n_all[:tokens] = n0_ref[...]
        n_all[tokens:] = n1_ref[...]

    gate = dot_nn(n_all[...], wg_ref[...])
    up = dot_nn(n_all[...], wu_ref[...])
    hidden_ref[...] = (gate / (1.0 + jnp.exp(-gate)) * up).astype(bf16)
    gate_ref[...] = gate.astype(bf16)
    up_ref[...] = up.astype(bf16)


def hidden_pass(normed, wgate, wup):
    tokens, width = normed[0].shape
    columns = wgate.shape[1]
    tile = min(256, columns)
    whole = pl.BlockSpec((tokens, width), lambda i: (0, 0))
    down = pl.BlockSpec((width, tile), lambda i: (0, i))
    out = pl.BlockSpec((2 * tokens, tile), lambda i: (0, i))
    return pl.pallas_call(
        hidden_kernel,
        grid=(pl.cdiv(columns, tile),),
        in_specs=[whole] * 2 + [down] * 2,
        out_specs=[out] * 3,
        out_shape=[jax.ShapeDtypeStruct((2 * tokens, columns), bf16)] * 3,
        scratch_shapes=[pltpu.VMEM((2 * tokens, width), bf16)],
        compiler_params=pltpu.CompilerParams(vmem_limit_bytes=VMEM_LIMIT),
        name="hidden_pass",
        cost_estimate=LIGHT,
    )(*normed, wgate, wup)


def gates_kernel(g0_ref, g1_ref, wd_ref, gate_ref, up_ref, gate_out_ref, up_out_ref, g_all):
    tokens = g0_ref.shape[0]

    @pl.when(pl.program_id(0) == 0)
    def _():
        g_all[:tokens] = g0_ref[...]
        g_all[tokens:] = g1_ref[...]

    grad = dot_nt(g_all[...], wd_ref[...])
    gate = gate_ref[...].astype(f32)
    up = up_ref[...].astype(f32)
    sigmoid = 1.0 / (1.0 + jnp.exp(-gate))
    gate_out_ref[...] = (grad * up * (sigmoid * (1.0 + gate * (1.0 - sigmoid)))).astype(bf16)
    up_out_ref[...] = (grad * (gate * sigmoid)).astype(bf16)


def gates_pass(grad_top, wdown, gate, up):
    tokens, width = grad_top[0].shape
    columns = gate.shape[1]
    tile = min(256, columns)
    whole = pl.BlockSpec((tokens, width), lambda i: (0, 0))
    out = pl.BlockSpec((2 * tokens, tile), lambda i: (0, i))
    return pl.pallas_call(
        gates_kernel,
        grid=(pl.cdiv(columns, tile),),
        in_specs=[whole] * 2 + [pl.BlockSpec((tile, width), lambda i: (i, 0)), out, out],
        out_specs=[out] * 2,
        out_shape=[jax.ShapeDtypeStruct((2 * tokens, columns), bf16)] * 2,
        scratch_shapes=[pltpu.VMEM((2 * tokens, width), bf16)],
        compiler_params=pltpu.CompilerParams(vmem_limit_bytes=VMEM_LIMIT),
        name="gates_pass",
        cost_estimate=LIGHT,
    )(*grad_top, wdown, gate, up)


def back_kernel(count, transposed, *refs):
    own_ref, send_ref = refs[-2:]
    tokens = own_ref.shape[0]
    dot = dot_nt if transposed else dot_nn

    def total(start):
        rows = pl.ds(start, tokens)
        result = dot(refs[0][rows, :], refs[count][...])
        for i in range(1, count):
            result = result + dot(refs[i][rows, :], refs[count + i][...])
        return result

    own_ref[...] = total(0)
    send_ref[...] = total(tokens).astype(bf16)


def back_pass(lefts, weights, transposed):
    tokens, depth = lefts[0].shape
    width = weights[0].shape[0 if transposed else 1]
    count = len(lefts)
    tile = min(512, width)
    if transposed:
        weight_spec = pl.BlockSpec((tile, depth), lambda i: (i, 0))
    else:
        weight_spec = pl.BlockSpec((depth, tile), lambda i: (0, i))
    out = pl.BlockSpec((tokens // 2, tile), lambda i: (0, i))
    return pl.pallas_call(
        partial(back_kernel, count, transposed),
        grid=(width // tile,),
        in_specs=[pl.BlockSpec((tokens, depth), lambda i: (0, 0))] * count
        + [weight_spec] * count,
        out_specs=[out, out],
        out_shape=[
            jax.ShapeDtypeStruct((tokens // 2, width), f32),
            jax.ShapeDtypeStruct((tokens // 2, width), bf16),
        ],
        compiler_params=pltpu.CompilerParams(vmem_limit_bytes=VMEM_LIMIT),
        name="back_pass",
        cost_estimate=LIGHT,
    )(*lefts, *weights)


def weight_kernel(left_count, *refs):
    lefts, rights, out_ref = refs[:left_count], refs[left_count:-1], refs[-1]
    step = min(lefts[0].shape[0], rights[0].shape[0])

    def piece(refs, start):
        index, offset = divmod(start, refs[0].shape[0])
        return refs[index][pl.ds(offset, step), :]

    total = None
    for start in range(0, left_count * lefts[0].shape[0], step):
        term = dot_tn(piece(lefts, start), piece(rights, start))
        total = term if total is None else total + term
    out_ref[...] = total.astype(bf16)


def weight_pass(lefts, rights):
    rows, columns = lefts[0].shape[1], rights[0].shape[1]
    tile = 512 if rows % 512 == 0 else 384 if rows % 384 == 0 else rows
    return pl.pallas_call(
        partial(weight_kernel, len(lefts)),
        grid=(rows // tile,),
        in_specs=[pl.BlockSpec((left.shape[0], tile), lambda i: (0, i)) for left in lefts]
        + [pl.BlockSpec(right.shape, lambda i: (0, 0)) for right in rights],
        out_specs=pl.BlockSpec((tile, columns), lambda i: (i, 0)),
        out_shape=jax.ShapeDtypeStruct((rows, columns), bf16),
        compiler_params=pltpu.CompilerParams(vmem_limit_bytes=VMEM_LIMIT),
        name="weight_pass",
        cost_estimate=LIGHT,
    )(*lefts, *rights)


def placed_kernel(side_ref, own_ref, other_ref, out_ref):
    mine = pl.program_id(0) == side_ref[0]

    @pl.when(mine)
    def _():
        out_ref[0, 0] = own_ref[:, 0]

    @pl.when(jnp.logical_not(mine))
    def _():
        out_ref[0, 0] = other_ref[:, 0]


def placed(own, other, side):
    seq, group, rows, columns = own.shape

    def entry(mine, e, g, s):
        parked = jnp.where(e == 0, 0, group - 1)
        return (0, jnp.where((e == s[0]) == mine, g, parked), 0, 0)

    return pl.pallas_call(
        placed_kernel,
        grid_spec=pltpu.PrefetchScalarGridSpec(
            num_scalar_prefetch=1,
            grid=(2, group),
            in_specs=[
                pl.BlockSpec((seq, 1, rows, columns), partial(entry, True)),
                pl.BlockSpec((seq, 1, rows, columns), partial(entry, False)),
            ],
            out_specs=pl.BlockSpec(
                (1, 1, seq, rows, columns), lambda e, g, s: (e, g, 0, 0, 0)
            ),
        ),
        out_shape=jax.ShapeDtypeStruct((2, group, seq, rows, columns), own.dtype),
        name="placed",
        cost_estimate=LIGHT,
    )(side.astype(jnp.int32).reshape(1), own, other)


def joined_kernel(side_ref, own_ref, other_ref, out_ref):
    mine = pl.program_id(1) == side_ref[0]

    @pl.when(mine)
    def _():
        out_ref[:, 0] = own_ref[...]

    @pl.when(jnp.logical_not(mine))
    def _():
        out_ref[:, 0] = other_ref[...]


def joined(own, other, side, axis):
    shape = own.shape[:axis] + (2,) + own.shape[axis:]
    columns = own.shape[-1]
    lead = math.prod(own.shape[:axis])
    rows = math.prod(own.shape[axis:-1])
    leads, chunks = lead, 1
    while leads % 2 == 0 and leads * rows * columns > 800_000:
        leads //= 2
    while leads == 1 and rows % (32 * chunks) == 0 and rows // chunks * columns > 800_000:
        chunks *= 2
    block = rows // chunks

    def entry(mine, p, e, i, s):
        parked = jnp.where(e == 0, 0, chunks - 1)
        return (p, jnp.where((e == s[0]) == mine, i, parked), 0)

    return pl.pallas_call(
        joined_kernel,
        grid_spec=pltpu.PrefetchScalarGridSpec(
            num_scalar_prefetch=1,
            grid=(lead // leads, 2, chunks),
            in_specs=[
                pl.BlockSpec((leads, block, columns), partial(entry, True)),
                pl.BlockSpec((leads, block, columns), partial(entry, False)),
            ],
            out_specs=pl.BlockSpec((leads, 1, block, columns), lambda p, e, i, s: (p, e, i, 0)),
        ),
        out_shape=jax.ShapeDtypeStruct((lead, 2, rows, columns), own.dtype),
        compiler_params=pltpu.CompilerParams(vmem_limit_bytes=VMEM_LIMIT),
        name="joined",
        cost_estimate=LIGHT,
    )(
        side.astype(jnp.int32).reshape(1),
        own.reshape(lead, rows, columns),
        other.reshape(lead, rows, columns),
    ).reshape(shape)


def swap(values, bit):
    pairs = [(i, i ^ bit) for i in range(lax.axis_size("rows"))]
    return lax.ppermute(values, "rows", pairs)


def bit_of(bit):
    return (lax.axis_index("rows") // bit) % 2


def gather_bit(values, bit, axis):
    return joined(values, swap(values, bit), bit_of(bit), axis)


def part(values, index, axis):
    return lax.dynamic_index_in_dim(values, index, axis, keepdims=False)


def reduce_bit(values, bit, axis):
    return add_bit(values, pass_bit(values, bit, axis), bit, axis)


def outer_pairs(step, low, high):
    size = lax.axis_size("rows")
    return [
        (i, i + 4 * step)
        for i in range(size)
        if low <= i // 4 < high and 0 <= i // 4 + step < size // 4
    ]


def send_outer(values):
    count = lax.axis_size("rows") // 4
    if count == 2:
        return (swap(values, 4),)
    up, down = values, values
    ups, downs = [], []
    for t in range(1, count):
        up = lax.ppermute(up, "rows", outer_pairs(1, t - 1, count))
        down = lax.ppermute(down, "rows", outer_pairs(-1, 0, count - t + 1))
        ups.append(up)
        downs.append(down)
    return tuple(ups[::-1] + downs)


def join_outer(values, received, axis):
    count = lax.axis_size("rows") // 4
    if count == 2:
        return joined(values, received[0], bit_of(4), axis)
    place = lax.axis_index("rows") // 4
    line = jnp.stack([*received[: count - 1], values, *received[count - 1 :]], axis)
    return lax.dynamic_slice_in_dim(line, count - 1 - place, count, axis)


def gather_outer(values, axis):
    return join_outer(values, send_outer(values), axis)


def pass_outer(values, axis):
    count = lax.axis_size("rows") // 4
    place = lax.axis_index("rows") // 4

    def entry(index):
        return part(values, jnp.clip(index, 0, count - 1), axis)

    if count == 1:
        return ()
    if count == 2:
        return (swap(entry(1 - place), 4),)
    up, down = entry(place + count - 1), entry(place - count + 1)
    for t in range(1, count):
        up = lax.ppermute(up, "rows", outer_pairs(1, 0, t))
        down = lax.ppermute(down, "rows", outer_pairs(-1, count - t, count))
        if t < count - 1:
            up = (entry(place + count - 1 - t).astype(f32) + up.astype(f32)).astype(bf16)
            down = (entry(place - count + 1 + t).astype(f32) + down.astype(f32)).astype(bf16)
    return (up, down)


def add_outer(values, received, axis):
    total = part(values, lax.axis_index("rows") // 4, axis).astype(f32)
    for term in received:
        total = total + term.astype(f32)
    return total.astype(bf16)


def reduce_outer(values, axis):
    return add_outer(values, pass_outer(values, axis), axis)


def pass_bit(values, bit, axis):
    return swap(part(values, 1 - bit_of(bit), axis), bit)


def add_bit(values, received, bit, axis):
    own = part(values, bit_of(bit), axis)
    return (own.astype(f32) + received.astype(f32)).astype(bf16)


def gather_seq(values):
    return lax.all_gather(values, "seq", axis=0, tiled=False)


def reduce_seq(values):
    return lax.psum_scatter(values, "seq", scatter_dimension=0, tiled=False)


def exchange(values, axis, bit):
    size = lax.axis_size(axis)
    return lax.ppermute(values, axis, [(i, i ^ bit) for i in range(size)])


def across_group(own, send):
    return (own + swap(send, 1).astype(f32)).astype(bf16)


def stage(*values):
    return lax.optimization_barrier(values)


def mm(left, right):
    return jnp.einsum("ab,bc->ac", left, right, preferred_element_type=f32)


def mm_t(left, right):
    return jnp.einsum("ab,cb->ac", left, right, preferred_element_type=f32)


def t_mm(left, right):
    return jnp.einsum("ab,ac->bc", left, right, preferred_element_type=f32)


def norm_scale(values):
    return lax.rsqrt(jnp.mean(values * values, axis=-1, keepdims=True) + EPSILON)


def norm_backward(values, scale, gain, grad):
    gained = grad * gain
    inner = jnp.mean(values * gained, axis=-1, keepdims=True)
    result = scale * gained - values * (scale * scale * scale) * inner
    return result, jnp.sum(grad * values * scale, axis=0)


def shards(
    tokens_in,
    corpus,
    corpus_weight,
    w_qkv,
    w_out,
    w_gate,
    w_up,
    w_down,
    attn_gain,
    ffn_gain,
    q_gain,
    k_gain,
    upstream,
):
    shard_length, width = tokens_in.shape[1:]
    row_devices = lax.axis_size("rows")
    seq_devices = lax.axis_size("seq")
    outer = row_devices // 4
    d_rows = w_qkv.shape[0]
    f_rows = w_down.shape[0]
    place = lax.axis_index("seq").astype(jnp.int32)
    inputs = tokens_in[0].astype(f32)

    extra = jnp.stack(
        [
            attn_gain,
            ffn_gain,
            jnp.broadcast_to(corpus.astype(bf16), attn_gain.shape),
        ],
        axis=1,
    )
    extra = jnp.pad(extra, ((0, 0), (0, LANES - extra.shape[1])))
    kv_shard = jnp.concatenate([w_qkv[:, QUERY_COLUMNS:], extra], axis=1)
    query_shard = jnp.concatenate([w_qkv[:, :QUERY_COLUMNS], w_out.T], axis=1)
    query_shard, w_gate, w_up = stage(query_shard, w_gate, w_up)
    query_lines = gather_seq(query_shard)

    def to_group(weight):
        blocks = weight.reshape(d_rows, outer, 4, seq_devices, f_rows)
        blocks = jnp.transpose(blocks, (2, 0, 3, 1, 4))
        return blocks.reshape(2, 2, d_rows, outer * seq_devices * f_rows)

    def spread_hidden(lines, received):
        if outer == 2:
            lines = lines.reshape(seq_devices, 4, d_rows, hidden_columns)
            other = received[0].reshape(lines.shape)
            return placed(lines, other, bit_of(4)).reshape(width, hidden_columns)
        full = join_outer(lines, received, 0)
        return jnp.moveaxis(full, 1, 3).reshape(width, hidden_columns)

    gate_up = jnp.stack([to_group(w_gate), to_group(w_up)], axis=2)
    hidden_columns = gate_up.shape[-1]
    core, near = bit_of(1), bit_of(2)
    gate_up = joined(
        part(gate_up, core, 1), swap(part(gate_up, 1 - core, 1), 1), core, 1
    )
    gate_up, kv_shard = stage(gate_up, kv_shard)
    other, kv_lines, query_lines = stage(
        swap(part(gate_up, 1 - near, 0), 2), gather_seq(kv_shard), query_lines
    )
    gate_up = joined(part(gate_up, near, 0), other, near, 0)
    gate_lines = gather_seq(gate_up[:, :, 0])
    left, right = kv_lines[..., : 3 * LANES], kv_lines[..., 3 * LANES :]
    left_other, right_other = stage(send_outer(left), swap(right, 2))
    left = join_outer(left, left_other, 0)
    right = joined(right, right_other, near, 0)
    left_other, right_other = stage(swap(left, 2), send_outer(right))
    left = joined(left, left_other, near, 1)
    right = join_outer(right, right_other, 0)
    q_left, q_right = query_lines[..., :QUERY_COLUMNS], query_lines[..., QUERY_COLUMNS:]
    q_left, q_right, left, right = stage(q_left, q_right, left, right)
    q_left_other, q_right_other = send_outer(q_left), swap(q_right, 2)
    left, right = gather_bit(left, 1, 2), gather_bit(right, 1, 2)
    left, right = left.reshape(width, -1), right.reshape(width, -1)
    wkv = jnp.concatenate([left, right[:, : 2 * LANES]], axis=1)
    rows = dot_nt(jnp.eye(8, LANES, dtype=bf16), right[:, 2 * LANES :])
    attn_gain_full, ffn_gain_full, corpus_full = rows[0:1], rows[1:2], rows[2]

    position = (place * shard_length + jnp.arange(shard_length, dtype=jnp.int32)).astype(f32)
    half = HEAD_SIZE // 2
    exponent = jnp.arange(half, dtype=f32) * (-2.0 / HEAD_SIZE)
    angles = position[:, None] * jnp.power(ROPE_BASE, exponent)[None, :]
    cosine, sine = jnp.cos(angles), jnp.sin(angles)
    cos_table = jnp.concatenate([cosine] * 4, axis=1)
    sin_table = jnp.concatenate([-sine, sine] * 2, axis=1)
    wide_q = jnp.tile(q_gain.astype(f32), QUERY_HEADS)
    wide_k = jnp.concatenate(
        [jnp.tile(k_gain.astype(f32), KEY_VALUE_HEADS), jnp.ones((KEY_COLUMNS,), f32)]
    )
    wide_q = jnp.broadcast_to(wide_q[None, :], (8, QUERY_COLUMNS))
    wide_k = jnp.broadcast_to(wide_k[None, :], (8, 2 * KEY_COLUMNS))

    in_scale = norm_scale(inputs)
    normed = (inputs * in_scale * attn_gain_full).astype(bf16)
    joint_kv, own_kv = heads_forward(
        normed, wkv, wide_k, cos_table, sin_table, KEY_COLUMNS
    )
    own_kv, q_left_other, q_right_other, down_other, up_in = stage(
        own_kv, q_left_other, q_right_other, send_outer(w_down), gate_up[:, :, 1]
    )
    up_lines = gather_seq(up_in)
    keys_values = gather_seq(own_kv).reshape(-1, 2 * KEY_COLUMNS)
    q_left = join_outer(q_left, q_left_other, 0)
    q_right = joined(q_right, q_right_other, near, 0)
    left_other, right_other, gate_lines = stage(
        swap(q_left, 2), send_outer(q_right), gate_lines
    )
    q_left = joined(q_left, left_other, near, 1)
    gate_other = send_outer(gate_lines)
    wq = gather_bit(q_left, 1, 2).reshape(width, -1)

    corpora = jnp.arange(CORPORA, dtype=jnp.int32)
    per_device = corpus_full.reshape(-1, d_rows)[:, 0].astype(jnp.int32)
    counts = (
        jnp.sum((per_device[:, None] == corpora[None, :]).astype(f32), axis=0) * shard_length
    )
    own_corpus = (corpus[0] == corpora).astype(f32)
    weight_row = jnp.sum(own_corpus * corpus_weight.astype(f32))
    count_row = jnp.sum(own_corpus * counts)
    factor = weight_row / DENOM * (jnp.sum(counts) / (CORPORA * count_row))
    grad_full = upstream[0].astype(f32) * factor
    grad_top, wq = stage(grad_full.astype(bf16), wq)

    joint_q, queries = heads_forward(
        normed, wq, wide_q, cos_table, sin_table, QUERY_COLUMNS
    )
    queries, q_right, right_other, down_other = stage(queries, q_right, right_other, down_other)
    q_right = join_outer(q_right, right_other, 0)
    down_pair = join_outer(w_down, down_other, 0)
    place_array = place.reshape(1)
    keys_values, queries, down_in = stage(keys_values, queries, down_pair)
    down_lines = gather_seq(down_in)
    mixed, logs = attend_forward(place_array, queries, keys_values)
    mixed, grad_top1, grad_top2, up_lines, wout_other = stage(
        mixed, swap(grad_top, 1), swap(grad_top, 2), up_lines, swap(q_right, 1)
    )
    half_rows = (2 * outer, seq_devices * d_rows, QUERY_COLUMNS)
    middle = project(
        mixed, q_right.reshape(half_rows), wout_other.reshape(half_rows), tokens_in[0], core
    )

    ffn_scale = norm_scale(middle)
    normed_ffn = (middle * ffn_scale * ffn_gain_full).astype(bf16)
    up_other = send_outer(up_lines)
    normed_ffn, gate_other, q_right, wout_other = stage(
        normed_ffn, gate_other, q_right, wout_other
    )
    wout_t = joined(q_right, wout_other, core, 2).reshape(width, -1)
    normed1, normed2, up_other, wgate = stage(
        swap(normed_ffn, 1),
        swap(normed_ffn, 2),
        up_other,
        spread_hidden(gate_lines, gate_other),
    )
    wup = spread_hidden(up_lines, up_other)
    hidden_near, gate_near, up_near = hidden_pass((normed_ffn, normed1), wgate, wup)
    normed3, hidden_near, grad_top3 = stage(
        swap(normed2, 1), hidden_near, swap(grad_top2, 1)
    )
    hidden_far, gate_far, up_far = hidden_pass((normed2, normed3), wgate, wup)
    normed4 = (normed_ffn, normed1, normed2, normed3)
    grad_top4 = (grad_top, grad_top1, grad_top2, grad_top3)
    wdown = down_lines.reshape(hidden_columns, width)
    gate_far, up_far = gates_pass((grad_top2, grad_top3), wdown, gate_far, up_far)
    own, send = back_pass((gate_far, up_far), (wgate, wup), True)
    grad_wdown = weight_pass((hidden_near, hidden_far), grad_top4)
    own, send, grad_wdown, wdown = stage(own, swap(send, 1), grad_wdown, wdown)
    across = (own + send.astype(f32)).astype(bf16)
    across, wdown = stage(across, wdown)
    gate_near, up_near = gates_pass((grad_top, grad_top1), wdown, gate_near, up_near)
    own, send = back_pass((gate_near, up_near), (wgate, wup), True)
    hidden_shape = (outer, 2, 2, seq_devices, d_rows, hidden_columns)
    grad_wdown = grad_wdown.reshape(seq_devices, outer, f_rows, width)
    grad_wgate = weight_pass(normed4, (gate_near, gate_far)).reshape(hidden_shape)
    across, own, send, grad_wgate, up_near = stage(
        swap(across, 2), own, send, grad_wgate, up_near
    )
    grad_wup = weight_pass(normed4, (up_near, up_far)).reshape(hidden_shape)
    send, grad_wup, down_other = stage(swap(send, 1), grad_wup, pass_outer(grad_wdown, 1))
    grad_wdown = add_outer(grad_wdown, down_other, 1)
    own = own + send.astype(f32)
    grad_normed_ffn = own + across.astype(f32)
    grad_wdown = reduce_seq(grad_wdown)

    grad_middle_part, grad_ffn_gain = norm_backward(
        middle, ffn_scale, ffn_gain_full, grad_normed_ffn
    )
    grad_middle = grad_full + grad_middle_part
    grad_branch = grad_middle.astype(bf16)
    grad_mixed = mm(grad_branch, wout_t).astype(bf16)
    attend = (place_array, queries, keys_values, mixed, logs)
    grad_q1, grad_kv1 = attend_backward(0, 2, *attend, grad_mixed)
    gate_other = pass_outer(grad_wgate, 0)
    grad_q1, grad_kv1, grad_mixed, grad_wdown, hidden_far = stage(
        grad_q1, grad_kv1, grad_mixed, grad_wdown, hidden_far
    )
    grad_kv1 = reduce_seq(grad_kv1.reshape(seq_devices, shard_length, -1))
    shape = (outer, 2, 2, seq_devices, d_rows)
    own_far, send_far = back_pass((hidden_far,), (wdown,), False)
    grad_wout, far_other, gate_other, grad_mixed = stage(
        t_mm(grad_branch, mixed).astype(bf16).reshape(*shape, QUERY_COLUMNS),
        swap(send_far, 1),
        gate_other,
        grad_mixed,
    )
    grad_gate = reduce_seq(jnp.moveaxis(add_outer(grad_wgate, gate_other, 0), 2, 0))
    across = (own_far + far_other.astype(f32)).astype(bf16)
    across, grad_mixed = stage(across, grad_mixed)
    grad_q2, grad_kv2 = attend_backward(2, 3, *attend, grad_mixed)
    grad_q2, grad_kv2, hidden_near, grad_kv1, grad_gate, wout_other, up_other, across = stage(
        grad_q2,
        grad_kv2,
        hidden_near,
        grad_kv1,
        grad_gate,
        pass_bit(grad_wout, 1, 2),
        pass_outer(grad_wup, 0),
        swap(across, 2),
    )
    grad_kv2 = reduce_seq(grad_kv2.reshape(seq_devices, shard_length, -1))

    grad_q = jnp.concatenate([grad_q1, grad_q2], axis=1)
    joint_grad_q, gain_q = heads_backward(
        grad_q, joint_q, wide_q, cos_table, sin_table, QUERY_COLUMNS
    )
    grad_wq = t_mm(normed, joint_grad_q).astype(bf16).reshape(*shape, QUERY_COLUMNS)
    grad_wout = add_bit(grad_wout, wout_other, 1, 2)
    grad_up = jnp.moveaxis(add_outer(grad_wup, up_other, 0), 2, 0)
    grad_kv2, grad_normed, grad_wq, grad_wout, grad_up = stage(
        grad_kv2, mm_t(joint_grad_q, wq), grad_wq, grad_wout, grad_up
    )
    grad_up = reduce_seq(grad_up)
    grad_wq, grad_kv2 = stage(reduce_bit(grad_wq, 1, 2), grad_kv2)
    wq_other, wout_other = pass_bit(grad_wq, 2, 1), pass_outer(grad_wout, 0)


    grad_kv1, grad_kv2 = (
        part_.reshape(shard_length, 2, -1) for part_ in (grad_kv1, grad_kv2)
    )
    grad_kv = jnp.concatenate([grad_kv1, grad_kv2], axis=2).reshape(shard_length, -1)
    joint_grad_kv, gain_k = heads_backward(
        grad_kv, joint_kv, wide_k, cos_table, sin_table, KEY_COLUMNS
    )
    grad_wkv = t_mm(normed, joint_grad_kv).astype(bf16)
    grad_normed = grad_normed + mm_t(joint_grad_kv, wkv)
    grad_input_part, grad_attn_gain = norm_backward(
        inputs, in_scale, attn_gain_full, grad_normed
    )
    input_grad = (grad_middle + grad_input_part).astype(bf16)

    gain_rows = jnp.stack([grad_attn_gain, grad_ffn_gain]).astype(bf16)
    gain_columns = t_mm(gain_rows, jnp.eye(2, LANES, dtype=bf16)).astype(bf16)
    grad_wkv, gain_columns, wq_other, wout_other, hidden_near = stage(
        grad_wkv, gain_columns, wq_other, wout_other, hidden_near
    )
    own_near, send_near = back_pass((hidden_near,), (wdown,), False)
    grad_wq = add_bit(grad_wq, wq_other, 2, 1)
    grad_wout = add_outer(grad_wout, wout_other, 0)
    wq_other, wout_other = pass_outer(grad_wq, 0), pass_bit(grad_wout, 2, 0)
    left = grad_wkv[:, : 3 * LANES].reshape(*shape, -1)
    right = jnp.concatenate([grad_wkv[:, 3 * LANES :], gain_columns], axis=1)
    right = right.reshape(*shape, -1)
    head_gains = jnp.concatenate(
        [
            jnp.sum(gain_q[0].reshape(-1, HEAD_SIZE), axis=0),
            jnp.sum(gain_k[0, :KEY_COLUMNS].reshape(-1, HEAD_SIZE), axis=0),
        ]
    )[None]
    left, right, left_other, right_other, gains_other = stage(
        left,
        right,
        pass_bit(left, 1, 2),
        pass_bit(right, 1, 2),
        exchange(head_gains, "rows", 1),
    )
    head_gains = head_gains + gains_other
    left = add_bit(left, left_other, 1, 2)
    right = add_bit(right, right_other, 1, 2)
    left_other, right_other, wq_other, wout_other, gains_other, grad_up = stage(
        pass_bit(left, 2, 1),
        pass_outer(right, 0),
        wq_other,
        wout_other,
        exchange(head_gains, "seq", 1),
        grad_up,
    )
    head_gains = head_gains + gains_other
    left = add_bit(left, left_other, 2, 1)
    right = add_outer(right, right_other, 0)
    left_other, right_other, gains_other, near_other = stage(
        pass_outer(left, 0),
        pass_bit(right, 2, 0),
        exchange(head_gains, "rows", 2),
        swap(send_near, 1),
    )
    output = (middle + own_near + near_other.astype(f32) + across.astype(f32)).astype(bf16)
    head_gains = head_gains + gains_other
    sums = reduce_seq(
        jnp.concatenate(
            [
                add_outer(grad_wq, wq_other, 0),
                add_outer(left, left_other, 0),
                add_bit(right, right_other, 2, 0),
                add_bit(grad_wout, wout_other, 2, 0),
            ],
            axis=-1,
        )
    )
    rest = [("rows", bit) for bit in (4, 8, 16) if bit < row_devices]
    rest += [("seq", bit) for bit in (2, 4, 8) if bit < seq_devices]
    gate_up = jnp.stack([grad_gate, grad_up], axis=2)
    other, gains_other = stage(
        swap(part(gate_up, 1 - near, 0), 2), exchange(head_gains, *rest[0])
    )
    head_gains = head_gains + gains_other
    grads = joined(part(gate_up, near, 0), other, near, 0)
    for axis, bit in rest[1:]:
        head_gains = head_gains + exchange(head_gains, axis, bit)
    head_gains = head_gains[0]
    grads = joined(part(grads, core, 1), swap(part(grads, 1 - core, 1), 1), core, 1)

    def from_group(blocks):
        blocks = blocks.reshape(4, d_rows, seq_devices, outer, f_rows)
        return jnp.transpose(blocks, (1, 3, 0, 2, 4)).reshape(d_rows, -1)

    grad_wgate, grad_wup = stage(from_group(grads[:, :, 0]), from_group(grads[:, :, 1]))
    sums, grad_wgate, grad_wup, grad_wdown, output, input_grad = stage(
        sums, grad_wgate.astype(f32), grad_wup.astype(f32), grad_wdown.astype(f32), output, input_grad
    )
    columns = QUERY_COLUMNS + 2 * KEY_COLUMNS
    long_gains = sums[:, columns : columns + 2].astype(f32)
    return (
        output[None],
        input_grad[None],
        sums[:, :columns].astype(f32),
        sums[:, columns + LANES :].T.astype(f32),
        grad_wgate,
        grad_wup,
        grad_wdown,
        long_gains[:, 0],
        long_gains[:, 1],
        head_gains[:HEAD_SIZE],
        head_gains[HEAD_SIZE:],
    )


def solution(mesh):
    return jax.shard_map(
        shards,
        mesh=mesh,
        in_specs=(
            P("rows", "seq", None),
            P("rows"),
            P(),
            P(("rows", "seq"), None),
            P(None, ("rows", "seq")),
            P(("rows", "seq"), None),
            P(("rows", "seq"), None),
            P(("rows", "seq"), None),
            P(("rows", "seq")),
            P(("rows", "seq")),
            P(),
            P(),
            P("rows", "seq", None),
        ),
        out_specs=(
            P("rows", "seq", None),
            P("rows", "seq", None),
            P(("rows", "seq"), None),
            P(None, ("rows", "seq")),
            P(("rows", "seq"), None),
            P(("rows", "seq"), None),
            P(("rows", "seq"), None),
            P(("rows", "seq")),
            P(("rows", "seq")),
            P(),
            P(),
        ),
        check_vma=False,
    )
```

```python
import math
from functools import partial

import jax
import jax.numpy as jnp
from jax import lax
from jax.experimental import pallas as pl
from jax.experimental.pallas import tpu as pltpu
from jax.sharding import PartitionSpec as P

QUERY_HEADS = 20
KEY_VALUE_HEADS = 5
HEAD_SIZE = 64
CORPORA = 8
DENOM = 64
EPSILON = 1e-06
ROPE_BASE = 10000.0
QUERY_COLUMNS = QUERY_HEADS * HEAD_SIZE
KEY_COLUMNS = KEY_VALUE_HEADS * HEAD_SIZE
LANES = 128
SCORE_EXPONENT = 1.4426950408889634 * HEAD_SIZE**-0.5
SPLIT = 2
VMEM_LIMIT = 48 * 1024 * 1024

f32, bf16 = jnp.float32, jnp.bfloat16
LIGHT = pl.CostEstimate(flops=1000, bytes_accessed=1000, transcendentals=0)


def dot_nn(a, b):
    return lax.dot_general(a, b, (((1,), (0,)), ((), ())), preferred_element_type=f32)


def dot_nt(a, b):
    return lax.dot_general(a, b, (((1,), (1,)), ((), ())), preferred_element_type=f32)


def dot_tn(a, b):
    return lax.dot_general(a, b, (((0,), (0,)), ((), ())), preferred_element_type=f32)


def lanes_of(shape):
    return lax.broadcasted_iota(jnp.int32, shape, len(shape) - 1)


def head_sum(values):
    row = lax.broadcasted_iota(jnp.int32, (LANES, LANES), 0) // HEAD_SIZE
    column = lax.broadcasted_iota(jnp.int32, (LANES, LANES), 1) // HEAD_SIZE
    ones = jnp.where(row == column, 1.0, 0.0).astype(bf16)
    high = values.astype(bf16)
    low = (values - high.astype(f32)).astype(bf16)
    return dot_nn(high, ones) + dot_nn(low, ones)


def partner(values):
    first = lanes_of(values.shape) % HEAD_SIZE < HEAD_SIZE // 2
    return jnp.where(
        first,
        pltpu.roll(values, LANES - HEAD_SIZE // 2, 1),
        pltpu.roll(values, HEAD_SIZE // 2, 1),
    )


def heads_of(joint, norm_columns, gain_ref, cos_ref, sin_ref, out_ref):
    columns = joint.shape[1]
    for start in range(0, columns, LANES):
        chunk = slice(start, start + LANES)
        values = joint[:, chunk]
        scale = lax.rsqrt(head_sum(values * values) * (1.0 / HEAD_SIZE) + EPSILON)
        normed = values * scale * gain_ref[0:1, chunk]
        turned = normed * cos_ref[...] + partner(normed) * sin_ref[...]
        place = pl.program_id(0) * columns + start + lanes_of(values.shape)
        out_ref[:, chunk] = jnp.where(place < norm_columns, turned, values).astype(bf16)


def heads_forward_kernel(
    norm_columns, normed_ref, weight_ref, gain_ref, cos_ref, sin_ref, joint_ref, out_ref
):
    joint = dot_nn(normed_ref[...], weight_ref[...])
    joint_ref[...] = joint
    heads_of(joint, norm_columns, gain_ref, cos_ref, sin_ref, out_ref)


def heads_halves_kernel(
    side_ref, normed_ref, own_ref, other_ref, gain_ref, cos_ref, sin_ref, joint_ref, out_ref
):
    count, block, _ = own_ref.shape
    joint = None
    for index in range(count):
        for weight_ref, side in ((own_ref, side_ref[0]), (other_ref, 1 - side_ref[0])):
            rows = pl.ds(pl.multiple_of((2 * index + side) * block, block), block)
            term = dot_nn(normed_ref[:, rows], weight_ref[index])
            joint = term if joint is None else joint + term
    joint_ref[...] = joint
    heads_of(joint, QUERY_COLUMNS, gain_ref, cos_ref, sin_ref, out_ref)


def heads_forward_halves(normed, own, other, side, gain, cos, sin):
    tokens, width = normed.shape
    count, block, columns = own.shape
    tile = 2 * LANES
    out = pl.BlockSpec((tokens, tile), lambda i, s: (0, i))
    table = pl.BlockSpec((tokens, LANES), lambda i, s: (0, 0))
    weight = pl.BlockSpec((count, block, tile), lambda i, s: (0, 0, i))
    return pl.pallas_call(
        heads_halves_kernel,
        grid_spec=pltpu.PrefetchScalarGridSpec(
            num_scalar_prefetch=1,
            grid=(columns // tile,),
            in_specs=[
                pl.BlockSpec((tokens, width), lambda i, s: (0, 0)),
                weight,
                weight,
                pl.BlockSpec((8, tile), lambda i, s: (0, i)),
                table,
                table,
            ],
            out_specs=[out, out],
        ),
        out_shape=[
            jax.ShapeDtypeStruct((tokens, columns), f32),
            jax.ShapeDtypeStruct((tokens, columns), bf16),
        ],
        compiler_params=pltpu.CompilerParams(vmem_limit_bytes=VMEM_LIMIT),
        name="heads_forward_halves",
        cost_estimate=LIGHT,
    )(side.astype(jnp.int32).reshape(1), normed, own, other, gain, cos, sin)


def heads_forward(normed, weight, gain, cos, sin, norm_columns):
    tokens, width = normed.shape
    columns = weight.shape[1]
    tile = 2 * LANES if columns % (2 * LANES) == 0 else LANES
    out = pl.BlockSpec((tokens, tile), lambda i: (0, i))
    table = pl.BlockSpec((tokens, LANES), lambda i: (0, 0))
    return pl.pallas_call(
        partial(heads_forward_kernel, norm_columns),
        grid=(columns // tile,),
        in_specs=[
            pl.BlockSpec((tokens, width), lambda i: (0, 0)),
            pl.BlockSpec((width, tile), lambda i: (0, i)),
            pl.BlockSpec((8, tile), lambda i: (0, i)),
            table,
            table,
        ],
        out_specs=[out, out],
        out_shape=[
            jax.ShapeDtypeStruct((tokens, columns), f32),
            jax.ShapeDtypeStruct((tokens, columns), bf16),
        ],
        compiler_params=pltpu.CompilerParams(vmem_limit_bytes=VMEM_LIMIT),
        name="heads_forward",
        cost_estimate=LIGHT,
    )(normed, weight, gain, cos, sin)


def project_kernel(side_ref, mixed_ref, own_ref, other_ref, inputs_ref, out_ref):
    block = own_ref.shape[1]
    for weight_ref, side in ((own_ref, side_ref[0]), (other_ref, 1 - side_ref[0])):
        columns = pl.ds(pl.multiple_of(side * block, block), block)
        out_ref[:, columns] = inputs_ref[:, columns].astype(f32) + dot_nt(
            mixed_ref[...], weight_ref[0]
        )


def project(mixed, own, other, inputs, side):
    tokens, depth = mixed.shape
    count, block, _ = own.shape
    weight = pl.BlockSpec((1, block, depth), lambda i, s: (i, 0, 0))
    out = pl.BlockSpec((tokens, 2 * block), lambda i, s: (0, i))
    return pl.pallas_call(
        project_kernel,
        grid_spec=pltpu.PrefetchScalarGridSpec(
            num_scalar_prefetch=1,
            grid=(count,),
            in_specs=[pl.BlockSpec((tokens, depth), lambda i, s: (0, 0)), weight, weight, out],
            out_specs=out,
        ),
        out_shape=jax.ShapeDtypeStruct((tokens, 2 * count * block), f32),
        compiler_params=pltpu.CompilerParams(vmem_limit_bytes=VMEM_LIMIT),
        name="project",
        cost_estimate=LIGHT,
    )(side.astype(jnp.int32).reshape(1), mixed, own, other, inputs)


def heads_backward_kernel(
    norm_columns, grad_ref, joint_ref, gain_ref, cos_ref, sin_ref, out_ref, gain_out_ref
):
    grad = grad_ref[...].astype(f32)
    values = joint_ref[...]
    gain = gain_ref[0:1, :]
    turned = grad * cos_ref[...] - partner(grad) * sin_ref[...]
    scale = lax.rsqrt(head_sum(values * values) * (1.0 / HEAD_SIZE) + EPSILON)
    gained = turned * gain
    inner = head_sum(values * gained) * (1.0 / HEAD_SIZE)
    result = scale * gained - values * (scale * scale * scale) * inner
    place = pl.program_id(0) * LANES + lanes_of(values.shape)
    out_ref[...] = jnp.where(place < norm_columns, result, grad).astype(bf16)
    gain_out_ref[...] = jnp.broadcast_to(
        jnp.sum(turned * values * scale, axis=0, keepdims=True), gain_out_ref.shape
    )


def heads_backward(grad, joint, gain, cos, sin, norm_columns):
    tokens, columns = joint.shape
    return pl.pallas_call(
        partial(heads_backward_kernel, norm_columns),
        grid=(columns // LANES,),
        in_specs=[
            pl.BlockSpec((tokens, LANES), lambda i: (0, i)),
            pl.BlockSpec((tokens, LANES), lambda i: (0, i)),
            pl.BlockSpec((8, LANES), lambda i: (0, i)),
            pl.BlockSpec((tokens, LANES), lambda i: (0, 0)),
            pl.BlockSpec((tokens, LANES), lambda i: (0, 0)),
        ],
        out_specs=[
            pl.BlockSpec((tokens, LANES), lambda i: (0, i)),
            pl.BlockSpec((8, LANES), lambda i: (0, i)),
        ],
        out_shape=[
            jax.ShapeDtypeStruct((tokens, columns), bf16),
            jax.ShapeDtypeStruct((8, columns), f32),
        ],
        name="heads_backward",
        cost_estimate=LIGHT,
    )(grad, joint, gain, cos, sin)


def both_halves(pair, odd):
    wide = pair.astype(f32)
    first = lanes_of(wide.shape) < HEAD_SIZE
    keep = jnp.where(odd == 1, jnp.where(first, 0, 1), jnp.where(first, 1, 0)) == 1
    return jnp.where(keep, wide, pltpu.roll(wide, HEAD_SIZE, 1))


def attend_forward_kernel(place_ref, q_ref, k_ref, v_ref, out_ref, log_ref):
    group = pl.program_id(0) // 2
    place = place_ref[0]
    tokens = q_ref.shape[0]
    first = lanes_of((tokens, LANES)) < HEAD_SIZE
    pair = q_ref[...].astype(f32)
    queries = (jnp.where(first, pair, 0.0).astype(bf16), jnp.where(first, 0.0, pair).astype(bf16))

    def step(j, totals, diagonal):
        rows = pl.ds(pl.multiple_of(j * tokens, tokens), tokens)
        keys = both_halves(k_ref[rows, :], group % 2).astype(bf16)
        values = both_halves(v_ref[rows, :], (KEY_VALUE_HEADS + group) % 2)
        sides = (
            jnp.where(first, values, 1.0).astype(bf16),
            jnp.where(first, 1.0, values).astype(bf16),
        )
        result = []
        for head in range(2):
            weights = jnp.exp2(dot_nt(queries[head], keys) * SCORE_EXPONENT)
            if diagonal:
                row = lax.broadcasted_iota(jnp.int32, weights.shape, 0)
                weights = jnp.where(lanes_of(weights.shape) <= row, weights, 0.0)
            result.append(totals[head] + dot_nn(weights.astype(bf16), sides[head]))
        return tuple(result)

    zero = jnp.zeros((tokens, LANES), f32)
    totals = lax.fori_loop(0, place, lambda j, c: step(j, c, False), (zero, zero))
    totals = step(place, totals, True)
    numerator = jnp.where(first, totals[0], totals[1])
    swapped = jnp.where(first, totals[1], totals[0])
    out_ref[...] = (numerator / pltpu.roll(swapped, HEAD_SIZE, 1)).astype(bf16)
    log_ref[...] = jnp.log2(swapped)


def attend_forward(place, queries, keys_values):
    tokens = queries.shape[0]
    length = keys_values.shape[0]
    pairs = QUERY_COLUMNS // LANES
    return pl.pallas_call(
        attend_forward_kernel,
        grid_spec=pltpu.PrefetchScalarGridSpec(
            num_scalar_prefetch=1,
            grid=(pairs,),
            in_specs=[
                pl.BlockSpec((tokens, LANES), lambda i, s: (0, i)),
                pl.BlockSpec((length, LANES), lambda i, s: (0, (i // 2) // 2)),
                pl.BlockSpec((length, LANES), lambda i, s: (0, (KEY_VALUE_HEADS + i // 2) // 2)),
            ],
            out_specs=[
                pl.BlockSpec((tokens, LANES), lambda i, s: (0, i)),
                pl.BlockSpec((tokens, LANES), lambda i, s: (0, i)),
            ],
        ),
        out_shape=[
            jax.ShapeDtypeStruct((tokens, QUERY_COLUMNS), bf16),
            jax.ShapeDtypeStruct((tokens, QUERY_COLUMNS), f32),
        ],
        compiler_params=pltpu.CompilerParams(vmem_limit_bytes=VMEM_LIMIT),
        name="attend_forward",
        cost_estimate=LIGHT,
    )(place, queries, keys_values, keys_values)


def three_parts(values, lane):
    high = values.astype(bf16).astype(f32)
    rest = values - high
    middle = rest.astype(bf16).astype(f32)
    low = rest - middle
    return jnp.where(
        lane == 0, high, jnp.where(lane == 1, middle, jnp.where(lane == 2, low, 0.0))
    )


def attend_backward_kernel(
    first_group, count, place_ref, q_ref, k_ref, v_ref, out_ref, log_ref, grad_ref, dq_ref, dkv_ref, dk_sum, dv_sum
):
    pair_index = pl.program_id(0)
    local = pair_index // 2
    group = first_group + local
    place = place_ref[0]
    tokens = q_ref.shape[0]
    lane = lanes_of((tokens, LANES))
    first = lane < HEAD_SIZE
    inside = lane % HEAD_SIZE
    pair = q_ref[...].astype(f32)
    grad = grad_ref[...].astype(f32)
    delta = pltpu.roll(head_sum(grad * out_ref[...].astype(f32)), HEAD_SIZE, 1)
    logs = three_parts(log_ref[...] * (1.0 / SCORE_EXPONENT), inside)
    deltas = three_parts(delta, inside)
    minus = jnp.where(inside < 3, -1.0, 0.0)

    def sides(own, other):
        return (
            jnp.where(first, own, other).astype(bf16),
            jnp.where(first, other, own).astype(bf16),
        )

    queries = sides(pair, 0.0)
    grads = sides(grad, 0.0)
    def turned(values):
        return jnp.transpose(values.astype(f32)).astype(bf16)

    queries_log = tuple(turned(v) for v in sides(pair, logs))
    grads_delta = tuple(turned(v) for v in sides(grad, deltas))

    @pl.when(pair_index % 2 == 0)
    def _():
        dk_sum[...] = jnp.zeros_like(dk_sum)
        dv_sum[...] = jnp.zeros_like(dv_sum)

    def step(j, dq, diagonal):
        rows = pl.ds(pl.multiple_of(j * tokens, tokens), tokens)
        key_wide = both_halves(k_ref[rows, :], group % 2)
        value_wide = both_halves(v_ref[rows, :], (KEY_VALUE_HEADS + group) % 2)
        keys_turned = jnp.transpose(key_wide)[:HEAD_SIZE].astype(bf16)
        keys_log = sides(key_wide, minus)
        values_delta = sides(value_wide, minus)
        dk = dk_sum[rows, :]
        dv = dv_sum[rows, :]
        parts = list(dq)
        block = tokens // SPLIT
        for sub in range(SPLIT):
            keep = slice(sub * block, (sub + 1) * block)
            dk_part, dv_part = dk[keep], dv[keep]
            start = sub * block if diagonal else 0
            for head in range(2):
                weights = jnp.exp2(
                    dot_nn(keys_log[head][keep], queries_log[head][:, start:]) * SCORE_EXPONENT
                )
                if diagonal:
                    row = lax.broadcasted_iota(jnp.int32, weights.shape, 0)
                    weights = jnp.where(row <= lanes_of(weights.shape), weights, 0.0)
                grad_weights = dot_nn(values_delta[head][keep], grads_delta[head][:, start:])
                grad_scores = (weights * grad_weights).astype(bf16)
                dv_part = dv_part + dot_nn(weights.astype(bf16), grads[head][start:])
                dk_part = dk_part + dot_nn(grad_scores, queries[head][start:])
                term = dot_nn(keys_turned[:, keep], grad_scores)
                if start:
                    term = jnp.concatenate([jnp.zeros((HEAD_SIZE, start), f32), term], axis=1)
                parts[head] = parts[head] + term
            target = pl.ds(pl.multiple_of(j * tokens + sub * block, block), block)
            dk_sum[target, :] = dk_part
            dv_sum[target, :] = dv_part
        return tuple(parts)

    zero = jnp.zeros((HEAD_SIZE, tokens), f32)
    dq = lax.fori_loop(0, place, lambda j, c: step(j, c, False), (zero, zero))
    dq = jnp.transpose(jnp.concatenate(step(place, dq, True), axis=0))
    dq_ref[...] = (dq * HEAD_SIZE**-0.5).astype(bf16)

    @pl.when(pair_index % 2 == 1)
    def _():
        wide_lane = lanes_of(dk_sum.shape)
        for total, slot, factor in (
            (dk_sum, local, HEAD_SIZE**-0.5),
            (dv_sum, count + local, 1.0),
        ):
            both = (total[...] + pltpu.roll(total[...], HEAD_SIZE, 1)) * factor
            columns = pl.ds(pl.multiple_of(slot // 2 * LANES, LANES), LANES)
            mine = wide_lane // HEAD_SIZE == slot % 2
            dkv_ref[:, columns] = jnp.where(
                mine, both, dkv_ref[:, columns].astype(f32)
            ).astype(bf16)


def attend_backward(first, count, place, queries, keys_values, mixed, logs, grad_mixed):
    tokens = queries.shape[0]
    length = keys_values.shape[0]
    group = QUERY_HEADS // KEY_VALUE_HEADS * HEAD_SIZE
    own = pl.BlockSpec((tokens, LANES), lambda i, s: (0, 2 * first + i))
    keys = pl.BlockSpec((length, LANES), lambda i, s: (0, (first + i // 2) // 2))
    values = pl.BlockSpec(
        (length, LANES), lambda i, s: (0, (KEY_VALUE_HEADS + first + i // 2) // 2)
    )
    columns = 2 * count * HEAD_SIZE
    return pl.pallas_call(
        partial(attend_backward_kernel, first, count),
        grid_spec=pltpu.PrefetchScalarGridSpec(
            num_scalar_prefetch=1,
            grid=(2 * count,),
            in_specs=[own, keys, values, own, own, own],
            out_specs=[
                pl.BlockSpec((tokens, LANES), lambda i, s: (0, i)),
                pl.BlockSpec((length, columns), lambda i, s: (0, 0)),
            ],
            scratch_shapes=[pltpu.VMEM((length, LANES), f32), pltpu.VMEM((length, LANES), f32)],
        ),
        out_shape=[
            jax.ShapeDtypeStruct((tokens, count * group), bf16),
            jax.ShapeDtypeStruct((length, columns), bf16),
        ],
        compiler_params=pltpu.CompilerParams(vmem_limit_bytes=VMEM_LIMIT),
        name="attend_backward",
        cost_estimate=LIGHT,
    )(place, queries, keys_values, keys_values, mixed, logs, grad_mixed)


def hidden_kernel(n0_ref, n1_ref, wg_ref, wu_ref, hidden_ref, gate_ref, up_ref, n_all):
    tokens = n0_ref.shape[0]

    @pl.when(pl.program_id(0) == 0)
    def _():
        n_all[:tokens] = n0_ref[...]
        n_all[tokens:] = n1_ref[...]

    gate = dot_nn(n_all[...], wg_ref[...])
    up = dot_nn(n_all[...], wu_ref[...])
    hidden_ref[...] = (gate / (1.0 + jnp.exp(-gate)) * up).astype(bf16)
    gate_ref[...] = gate.astype(bf16)
    up_ref[...] = up.astype(bf16)


def hidden_pass(normed, wgate, wup):
    tokens, width = normed[0].shape
    columns = wgate.shape[1]
    tile = min(256, columns)
    whole = pl.BlockSpec((tokens, width), lambda i: (0, 0))
    down = pl.BlockSpec((width, tile), lambda i: (0, i))
    out = pl.BlockSpec((2 * tokens, tile), lambda i: (0, i))
    return pl.pallas_call(
        hidden_kernel,
        grid=(pl.cdiv(columns, tile),),
        in_specs=[whole] * 2 + [down] * 2,
        out_specs=[out] * 3,
        out_shape=[jax.ShapeDtypeStruct((2 * tokens, columns), bf16)] * 3,
        scratch_shapes=[pltpu.VMEM((2 * tokens, width), bf16)],
        compiler_params=pltpu.CompilerParams(vmem_limit_bytes=VMEM_LIMIT),
        name="hidden_pass",
        cost_estimate=LIGHT,
    )(*normed, wgate, wup)


def gates_kernel(g0_ref, g1_ref, wd_ref, gate_ref, up_ref, gate_out_ref, up_out_ref, g_all):
    tokens = g0_ref.shape[0]

    @pl.when(pl.program_id(0) == 0)
    def _():
        g_all[:tokens] = g0_ref[...]
        g_all[tokens:] = g1_ref[...]

    grad = dot_nt(g_all[...], wd_ref[...])
    gate = gate_ref[...].astype(f32)
    up = up_ref[...].astype(f32)
    sigmoid = 1.0 / (1.0 + jnp.exp(-gate))
    gate_out_ref[...] = (grad * up * (sigmoid * (1.0 + gate * (1.0 - sigmoid)))).astype(bf16)
    up_out_ref[...] = (grad * (gate * sigmoid)).astype(bf16)


def gates_pass(grad_top, wdown, gate, up):
    tokens, width = grad_top[0].shape
    columns = gate.shape[1]
    tile = min(256, columns)
    whole = pl.BlockSpec((tokens, width), lambda i: (0, 0))
    out = pl.BlockSpec((2 * tokens, tile), lambda i: (0, i))
    return pl.pallas_call(
        gates_kernel,
        grid=(pl.cdiv(columns, tile),),
        in_specs=[whole] * 2 + [pl.BlockSpec((tile, width), lambda i: (i, 0)), out, out],
        out_specs=[out] * 2,
        out_shape=[jax.ShapeDtypeStruct((2 * tokens, columns), bf16)] * 2,
        scratch_shapes=[pltpu.VMEM((2 * tokens, width), bf16)],
        compiler_params=pltpu.CompilerParams(vmem_limit_bytes=VMEM_LIMIT),
        name="gates_pass",
        cost_estimate=LIGHT,
    )(*grad_top, wdown, gate, up)


def back_kernel(count, transposed, *refs):
    own_ref, send_ref = refs[-2:]
    tokens = own_ref.shape[0]
    dot = dot_nt if transposed else dot_nn

    def total(start):
        rows = pl.ds(start, tokens)
        result = dot(refs[0][rows, :], refs[count][...])
        for i in range(1, count):
            result = result + dot(refs[i][rows, :], refs[count + i][...])
        return result

    own_ref[...] = total(0)
    send_ref[...] = total(tokens).astype(bf16)


def back_pass(lefts, weights, transposed):
    tokens, depth = lefts[0].shape
    width = weights[0].shape[0 if transposed else 1]
    count = len(lefts)
    tile = min(512, width)
    if transposed:
        weight_spec = pl.BlockSpec((tile, depth), lambda i: (i, 0))
    else:
        weight_spec = pl.BlockSpec((depth, tile), lambda i: (0, i))
    out = pl.BlockSpec((tokens // 2, tile), lambda i: (0, i))
    return pl.pallas_call(
        partial(back_kernel, count, transposed),
        grid=(width // tile,),
        in_specs=[pl.BlockSpec((tokens, depth), lambda i: (0, 0))] * count
        + [weight_spec] * count,
        out_specs=[out, out],
        out_shape=[
            jax.ShapeDtypeStruct((tokens // 2, width), f32),
            jax.ShapeDtypeStruct((tokens // 2, width), bf16),
        ],
        compiler_params=pltpu.CompilerParams(vmem_limit_bytes=VMEM_LIMIT),
        name="back_pass",
        cost_estimate=LIGHT,
    )(*lefts, *weights)


def weight_kernel(left_count, *refs):
    lefts, rights, out_ref = refs[:left_count], refs[left_count:-1], refs[-1]
    step = min(lefts[0].shape[0], rights[0].shape[0])

    def piece(refs, start):
        index, offset = divmod(start, refs[0].shape[0])
        return refs[index][pl.ds(offset, step), :]

    total = None
    for start in range(0, left_count * lefts[0].shape[0], step):
        term = dot_tn(piece(lefts, start), piece(rights, start))
        total = term if total is None else total + term
    out_ref[...] = total.astype(bf16)


def weight_pass(lefts, rights):
    rows, columns = lefts[0].shape[1], rights[0].shape[1]
    tile = 512 if rows % 512 == 0 else 384 if rows % 384 == 0 else rows
    return pl.pallas_call(
        partial(weight_kernel, len(lefts)),
        grid=(rows // tile,),
        in_specs=[pl.BlockSpec((left.shape[0], tile), lambda i: (0, i)) for left in lefts]
        + [pl.BlockSpec(right.shape, lambda i: (0, 0)) for right in rights],
        out_specs=pl.BlockSpec((tile, columns), lambda i: (i, 0)),
        out_shape=jax.ShapeDtypeStruct((rows, columns), bf16),
        compiler_params=pltpu.CompilerParams(vmem_limit_bytes=VMEM_LIMIT),
        name="weight_pass",
        cost_estimate=LIGHT,
    )(*lefts, *rights)


def placed_kernel(side_ref, own_ref, other_ref, out_ref):
    mine = pl.program_id(0) == side_ref[0]

    @pl.when(mine)
    def _():
        for g in range(out_ref.shape[1]):
            out_ref[0, g] = own_ref[:, g]

    @pl.when(jnp.logical_not(mine))
    def _():
        for g in range(out_ref.shape[1]):
            out_ref[0, g] = other_ref[:, g]


def placed(own, other, side):
    seq, group, rows, columns = own.shape

    def entry(mine, e, g, s):
        parked = jnp.where(e == 0, 0, group // 2 - 1)
        return (0, jnp.where((e == s[0]) == mine, g, parked), 0, 0)

    return pl.pallas_call(
        placed_kernel,
        grid_spec=pltpu.PrefetchScalarGridSpec(
            num_scalar_prefetch=1,
            grid=(2, group // 2),
            in_specs=[
                pl.BlockSpec((seq, 2, rows, columns), partial(entry, True)),
                pl.BlockSpec((seq, 2, rows, columns), partial(entry, False)),
            ],
            out_specs=pl.BlockSpec(
                (1, 2, seq, rows, columns), lambda e, g, s: (e, g, 0, 0, 0)
            ),
        ),
        out_shape=jax.ShapeDtypeStruct((2, group, seq, rows, columns), own.dtype),
        compiler_params=pltpu.CompilerParams(vmem_limit_bytes=VMEM_LIMIT),
        name="placed",
        cost_estimate=LIGHT,
    )(side.astype(jnp.int32).reshape(1), own, other)


def joined_kernel(side_ref, own_ref, other_ref, out_ref):
    mine = pl.program_id(1) == side_ref[0]

    @pl.when(mine)
    def _():
        out_ref[:, 0] = own_ref[...]

    @pl.when(jnp.logical_not(mine))
    def _():
        out_ref[:, 0] = other_ref[...]


def joined(own, other, side, axis):
    shape = own.shape[:axis] + (2,) + own.shape[axis:]
    columns = own.shape[-1]
    lead = math.prod(own.shape[:axis])
    rows = math.prod(own.shape[axis:-1])
    leads, chunks = lead, 1
    while leads % 2 == 0 and leads * rows * columns > 800_000:
        leads //= 2
    while leads == 1 and rows % (32 * chunks) == 0 and rows // chunks * columns > 800_000:
        chunks *= 2
    block = rows // chunks

    def entry(mine, p, e, i, s):
        parked = jnp.where(e == 0, 0, chunks - 1)
        return (p, jnp.where((e == s[0]) == mine, i, parked), 0)

    return pl.pallas_call(
        joined_kernel,
        grid_spec=pltpu.PrefetchScalarGridSpec(
            num_scalar_prefetch=1,
            grid=(lead // leads, 2, chunks),
            in_specs=[
                pl.BlockSpec((leads, block, columns), partial(entry, True)),
                pl.BlockSpec((leads, block, columns), partial(entry, False)),
            ],
            out_specs=pl.BlockSpec((leads, 1, block, columns), lambda p, e, i, s: (p, e, i, 0)),
        ),
        out_shape=jax.ShapeDtypeStruct((lead, 2, rows, columns), own.dtype),
        compiler_params=pltpu.CompilerParams(vmem_limit_bytes=VMEM_LIMIT),
        name="joined",
        cost_estimate=LIGHT,
    )(
        side.astype(jnp.int32).reshape(1),
        own.reshape(lead, rows, columns),
        other.reshape(lead, rows, columns),
    ).reshape(shape)


def swap(values, bit):
    pairs = [(i, i ^ bit) for i in range(lax.axis_size("rows"))]
    return lax.ppermute(values, "rows", pairs)


def bit_of(bit):
    return (lax.axis_index("rows") // bit) % 2


def gather_bit(values, bit, axis):
    return joined(values, swap(values, bit), bit_of(bit), axis)


def part(values, index, axis):
    return lax.dynamic_index_in_dim(values, index, axis, keepdims=False)


def reduce_bit(values, bit, axis):
    return add_bit(values, pass_bit(values, bit, axis), bit, axis)


def outer_pairs(step, low, high):
    size = lax.axis_size("rows")
    return [
        (i, i + 4 * step)
        for i in range(size)
        if low <= i // 4 < high and 0 <= i // 4 + step < size // 4
    ]


def send_outer(values):
    count = lax.axis_size("rows") // 4
    if count == 2:
        return (swap(values, 4),)
    up, down = values, values
    ups, downs = [], []
    for t in range(1, count):
        up = lax.ppermute(up, "rows", outer_pairs(1, t - 1, count))
        down = lax.ppermute(down, "rows", outer_pairs(-1, 0, count - t + 1))
        ups.append(up)
        downs.append(down)
    return tuple(ups[::-1] + downs)


def join_outer(values, received, axis):
    count = lax.axis_size("rows") // 4
    if count == 2:
        return joined(values, received[0], bit_of(4), axis)
    place = lax.axis_index("rows") // 4
    line = jnp.stack([*received[: count - 1], values, *received[count - 1 :]], axis)
    return lax.dynamic_slice_in_dim(line, count - 1 - place, count, axis)


def gather_outer(values, axis):
    return join_outer(values, send_outer(values), axis)


def pass_outer(values, axis):
    count = lax.axis_size("rows") // 4
    place = lax.axis_index("rows") // 4

    def entry(index):
        return part(values, jnp.clip(index, 0, count - 1), axis)

    if count == 1:
        return ()
    if count == 2:
        return (swap(entry(1 - place), 4),)
    up, down = entry(place + count - 1), entry(place - count + 1)
    for t in range(1, count):
        up = lax.ppermute(up, "rows", outer_pairs(1, 0, t))
        down = lax.ppermute(down, "rows", outer_pairs(-1, count - t, count))
        if t < count - 1:
            up = (entry(place + count - 1 - t).astype(f32) + up.astype(f32)).astype(bf16)
            down = (entry(place - count + 1 + t).astype(f32) + down.astype(f32)).astype(bf16)
    return (up, down)


def add_outer(values, received, axis):
    total = part(values, lax.axis_index("rows") // 4, axis).astype(f32)
    for term in received:
        total = total + term.astype(f32)
    return total.astype(bf16)


def reduce_outer(values, axis):
    return add_outer(values, pass_outer(values, axis), axis)


def pass_bit(values, bit, axis):
    return swap(part(values, 1 - bit_of(bit), axis), bit)


def add_bit(values, received, bit, axis):
    own = part(values, bit_of(bit), axis)
    return (own.astype(f32) + received.astype(f32)).astype(bf16)


def gather_seq(values):
    return lax.all_gather(values, "seq", axis=0, tiled=False)


def reduce_seq(values):
    return lax.psum_scatter(values, "seq", scatter_dimension=0, tiled=False)


def exchange(values, axis, bit):
    size = lax.axis_size(axis)
    return lax.ppermute(values, axis, [(i, i ^ bit) for i in range(size)])


def across_group(own, send):
    return (own + swap(send, 1).astype(f32)).astype(bf16)


def stage(*values):
    return lax.optimization_barrier(values)


def mm(left, right):
    return jnp.einsum("ab,bc->ac", left, right, preferred_element_type=f32)


def mm_t(left, right):
    return jnp.einsum("ab,cb->ac", left, right, preferred_element_type=f32)


def t_mm(left, right):
    return jnp.einsum("ab,ac->bc", left, right, preferred_element_type=f32)


def norm_scale(values):
    return lax.rsqrt(jnp.mean(values * values, axis=-1, keepdims=True) + EPSILON)


def norm_backward(values, scale, gain, grad):
    gained = grad * gain
    inner = jnp.mean(values * gained, axis=-1, keepdims=True)
    result = scale * gained - values * (scale * scale * scale) * inner
    return result, jnp.sum(grad * values * scale, axis=0)


def shards(
    tokens_in,
    corpus,
    corpus_weight,
    w_qkv,
    w_out,
    w_gate,
    w_up,
    w_down,
    attn_gain,
    ffn_gain,
    q_gain,
    k_gain,
    upstream,
):
    shard_length, width = tokens_in.shape[1:]
    row_devices = lax.axis_size("rows")
    seq_devices = lax.axis_size("seq")
    outer = row_devices // 4
    d_rows = w_qkv.shape[0]
    f_rows = w_down.shape[0]
    place = lax.axis_index("seq").astype(jnp.int32)
    inputs = tokens_in[0].astype(f32)

    extra = jnp.stack(
        [
            attn_gain,
            ffn_gain,
            jnp.broadcast_to(corpus.astype(bf16), attn_gain.shape),
        ],
        axis=1,
    )
    extra = jnp.pad(extra, ((0, 0), (0, LANES - extra.shape[1])))
    kv_shard = jnp.concatenate([w_qkv[:, QUERY_COLUMNS:], extra], axis=1)
    query_shard = jnp.concatenate([w_qkv[:, :QUERY_COLUMNS], w_out.T], axis=1)
    query_shard, w_gate, w_up = stage(query_shard, w_gate, w_up)
    query_lines = gather_seq(query_shard)

    def to_group(weight):
        blocks = weight.reshape(d_rows, outer, 4, seq_devices, f_rows)
        blocks = jnp.transpose(blocks, (2, 0, 3, 1, 4))
        return blocks.reshape(2, 2, d_rows, outer * seq_devices * f_rows)

    def spread_hidden(lines, received):
        if outer == 2:
            lines = lines.reshape(seq_devices, 4, d_rows, hidden_columns)
            other = received[0].reshape(lines.shape)
            return placed(lines, other, bit_of(4)).reshape(width, hidden_columns)
        full = join_outer(lines, received, 0)
        return jnp.moveaxis(full, 1, 3).reshape(width, hidden_columns)

    gate_up = jnp.stack([to_group(w_gate), to_group(w_up)], axis=2)
    hidden_columns = gate_up.shape[-1]
    core, near = bit_of(1), bit_of(2)
    gate_up = joined(
        part(gate_up, core, 1), swap(part(gate_up, 1 - core, 1), 1), core, 1
    )
    gate_up, kv_shard = stage(gate_up, kv_shard)
    other, kv_lines, query_lines = stage(
        swap(part(gate_up, 1 - near, 0), 2), gather_seq(kv_shard), query_lines
    )
    gate_up = joined(part(gate_up, near, 0), other, near, 0)
    gate_lines = gather_seq(gate_up[:, :, 0])
    left, right = kv_lines[..., : 3 * LANES], kv_lines[..., 3 * LANES :]
    left_other, right_other = stage(send_outer(left), swap(right, 2))
    left = join_outer(left, left_other, 0)
    right = joined(right, right_other, near, 0)
    left_other, right_other = stage(swap(left, 2), send_outer(right))
    left = joined(left, left_other, near, 1)
    right = join_outer(right, right_other, 0)
    q_left, q_right = query_lines[..., :QUERY_COLUMNS], query_lines[..., QUERY_COLUMNS:]
    q_left, q_right, left, right = stage(q_left, q_right, left, right)
    q_left_other, q_right_other = send_outer(q_left), swap(q_right, 2)
    left, right = gather_bit(left, 1, 2), gather_bit(right, 1, 2)
    left, right = left.reshape(width, -1), right.reshape(width, -1)
    wkv = jnp.concatenate([left, right[:, : 2 * LANES]], axis=1)
    rows = dot_nt(jnp.eye(8, LANES, dtype=bf16), right[:, 2 * LANES :])
    attn_gain_full, ffn_gain_full, corpus_full = rows[0:1], rows[1:2], rows[2]

    position = (place * shard_length + jnp.arange(shard_length, dtype=jnp.int32)).astype(f32)
    half = HEAD_SIZE // 2
    exponent = jnp.arange(half, dtype=f32) * (-2.0 / HEAD_SIZE)
    angles = position[:, None] * jnp.power(ROPE_BASE, exponent)[None, :]
    cosine, sine = jnp.cos(angles), jnp.sin(angles)
    cos_table = jnp.concatenate([cosine] * 4, axis=1)
    sin_table = jnp.concatenate([-sine, sine] * 2, axis=1)
    wide_q = jnp.tile(q_gain.astype(f32), QUERY_HEADS)
    wide_k = jnp.concatenate(
        [jnp.tile(k_gain.astype(f32), KEY_VALUE_HEADS), jnp.ones((KEY_COLUMNS,), f32)]
    )
    wide_q = jnp.broadcast_to(wide_q[None, :], (8, QUERY_COLUMNS))
    wide_k = jnp.broadcast_to(wide_k[None, :], (8, 2 * KEY_COLUMNS))

    in_scale = norm_scale(inputs)
    normed = (inputs * in_scale * attn_gain_full).astype(bf16)
    joint_kv, own_kv = heads_forward(
        normed, wkv, wide_k, cos_table, sin_table, KEY_COLUMNS
    )
    own_kv, q_left_other, q_right_other, up_in = stage(
        own_kv, q_left_other, q_right_other, gate_up[:, :, 1]
    )
    up_lines = gather_seq(up_in)
    keys_values = gather_seq(own_kv).reshape(-1, 2 * KEY_COLUMNS)
    q_left = join_outer(q_left, q_left_other, 0)
    q_right = joined(q_right, q_right_other, near, 0)
    left_other, right_other, gate_lines, w_down = stage(
        swap(q_left, 2), send_outer(q_right), gate_lines, w_down
    )
    q_left = joined(q_left, left_other, near, 1)
    gate_other = send_outer(gate_lines)
    down_other = send_outer(w_down)
    half_rows = (2 * outer, seq_devices * d_rows, QUERY_COLUMNS)
    q_left_other = swap(q_left, 1)

    corpora = jnp.arange(CORPORA, dtype=jnp.int32)
    per_device = corpus_full.reshape(-1, d_rows)[:, 0].astype(jnp.int32)
    counts = (
        jnp.sum((per_device[:, None] == corpora[None, :]).astype(f32), axis=0) * shard_length
    )
    own_corpus = (corpus[0] == corpora).astype(f32)
    weight_row = jnp.sum(own_corpus * corpus_weight.astype(f32))
    count_row = jnp.sum(own_corpus * counts)
    factor = weight_row / DENOM * (jnp.sum(counts) / (CORPORA * count_row))
    grad_full = upstream[0].astype(f32) * factor
    grad_top, q_left, q_left_other = stage(grad_full.astype(bf16), q_left, q_left_other)

    q_halves = (q_left.reshape(half_rows), q_left_other.reshape(half_rows))
    joint_q, queries = heads_forward_halves(
        normed, *q_halves, core, wide_q, cos_table, sin_table
    )
    queries, q_right, right_other, down_other = stage(queries, q_right, right_other, down_other)
    q_right = join_outer(q_right, right_other, 0)
    down_pair = join_outer(w_down, down_other, 0)
    place_array = place.reshape(1)
    keys_values, queries, down_in = stage(keys_values, queries, down_pair)
    down_lines = gather_seq(down_in)
    mixed, logs = attend_forward(place_array, queries, keys_values)
    mixed, grad_top1, grad_top2, up_lines, wout_other = stage(
        mixed, swap(grad_top, 1), swap(grad_top, 2), up_lines, swap(q_right, 1)
    )
    middle = project(
        mixed, q_right.reshape(half_rows), wout_other.reshape(half_rows), tokens_in[0], core
    )

    ffn_scale = norm_scale(middle)
    normed_ffn = (middle * ffn_scale * ffn_gain_full).astype(bf16)
    up_other = send_outer(up_lines)
    normed_ffn, gate_other, q_right, wout_other, q_left, q_left_other = stage(
        normed_ffn, gate_other, q_right, wout_other, q_left, q_left_other
    )
    wq = joined(q_left, q_left_other, core, 2).reshape(width, -1)
    wout_t = joined(q_right, wout_other, core, 2).reshape(width, -1)
    normed1, normed2, up_other, wgate = stage(
        swap(normed_ffn, 1),
        swap(normed_ffn, 2),
        up_other,
        spread_hidden(gate_lines, gate_other),
    )
    wup = spread_hidden(up_lines, up_other)
    hidden_near, gate_near, up_near = hidden_pass((normed_ffn, normed1), wgate, wup)
    normed3, hidden_near, grad_top3 = stage(
        swap(normed2, 1), hidden_near, swap(grad_top2, 1)
    )
    hidden_far, gate_far, up_far = hidden_pass((normed2, normed3), wgate, wup)
    normed4 = (normed_ffn, normed1, normed2, normed3)
    grad_top4 = (grad_top, grad_top1, grad_top2, grad_top3)
    wdown = down_lines.reshape(hidden_columns, width)
    gate_far, up_far = gates_pass((grad_top2, grad_top3), wdown, gate_far, up_far)
    own, send = back_pass((gate_far, up_far), (wgate, wup), True)
    grad_wdown = weight_pass((hidden_near, hidden_far), grad_top4)
    own, send, grad_wdown, wdown = stage(own, swap(send, 1), grad_wdown, wdown)
    across = (own + send.astype(f32)).astype(bf16)
    across, wdown = stage(across, wdown)
    gate_near, up_near = gates_pass((grad_top, grad_top1), wdown, gate_near, up_near)
    own, send = back_pass((gate_near, up_near), (wgate, wup), True)
    hidden_shape = (outer, 2, 2, seq_devices, d_rows, hidden_columns)
    grad_wdown = grad_wdown.reshape(seq_devices, outer, f_rows, width)
    grad_wgate = weight_pass(normed4, (gate_near, gate_far)).reshape(hidden_shape)
    across, own, send, grad_wgate, up_near = stage(
        swap(across, 2), own, send, grad_wgate, up_near
    )
    grad_wup = weight_pass(normed4, (up_near, up_far)).reshape(hidden_shape)
    send, grad_wup, down_other = stage(swap(send, 1), grad_wup, pass_outer(grad_wdown, 1))
    grad_wdown = add_outer(grad_wdown, down_other, 1)
    own = own + send.astype(f32)
    grad_normed_ffn = own + across.astype(f32)
    grad_wdown = reduce_seq(grad_wdown)

    grad_middle_part, grad_ffn_gain = norm_backward(
        middle, ffn_scale, ffn_gain_full, grad_normed_ffn
    )
    grad_middle = grad_full + grad_middle_part
    grad_branch = grad_middle.astype(bf16)
    grad_mixed = mm(grad_branch, wout_t).astype(bf16)
    attend = (place_array, queries, keys_values, mixed, logs)
    grad_q1, grad_kv1 = attend_backward(0, 2, *attend, grad_mixed)
    gate_other = pass_outer(grad_wgate, 0)
    grad_q1, grad_kv1, grad_mixed, grad_wdown, hidden_far = stage(
        grad_q1, grad_kv1, grad_mixed, grad_wdown, hidden_far
    )
    grad_kv1 = reduce_seq(grad_kv1.reshape(seq_devices, shard_length, -1))
    shape = (outer, 2, 2, seq_devices, d_rows)
    own_far, send_far = back_pass((hidden_far,), (wdown,), False)
    grad_wout, far_other, gate_other, grad_mixed = stage(
        t_mm(grad_branch, mixed).astype(bf16).reshape(*shape, QUERY_COLUMNS),
        swap(send_far, 1),
        gate_other,
        grad_mixed,
    )
    grad_gate = reduce_seq(jnp.moveaxis(add_outer(grad_wgate, gate_other, 0), 2, 0))
    across = (own_far + far_other.astype(f32)).astype(bf16)
    across, grad_mixed = stage(across, grad_mixed)
    grad_q2, grad_kv2 = attend_backward(2, 3, *attend, grad_mixed)
    grad_q2, grad_kv2, hidden_near, grad_kv1, grad_gate, wout_other, up_other, across = stage(
        grad_q2,
        grad_kv2,
        hidden_near,
        grad_kv1,
        grad_gate,
        pass_bit(grad_wout, 1, 2),
        pass_outer(grad_wup, 0),
        swap(across, 2),
    )
    grad_kv2 = reduce_seq(grad_kv2.reshape(seq_devices, shard_length, -1))

    grad_q = jnp.concatenate([grad_q1, grad_q2], axis=1)
    joint_grad_q, gain_q = heads_backward(
        grad_q, joint_q, wide_q, cos_table, sin_table, QUERY_COLUMNS
    )
    grad_wq = t_mm(normed, joint_grad_q).astype(bf16).reshape(*shape, QUERY_COLUMNS)
    grad_wout = add_bit(grad_wout, wout_other, 1, 2)
    grad_up = jnp.moveaxis(add_outer(grad_wup, up_other, 0), 2, 0)
    grad_kv2, grad_normed, grad_wq, grad_wout, grad_up = stage(
        grad_kv2, mm_t(joint_grad_q, wq), grad_wq, grad_wout, grad_up
    )
    grad_up = reduce_seq(grad_up)
    grad_wq, grad_kv2 = stage(reduce_bit(grad_wq, 1, 2), grad_kv2)
    wq_other, wout_other = pass_bit(grad_wq, 2, 1), pass_outer(grad_wout, 0)


    grad_kv1, grad_kv2 = (
        part_.reshape(shard_length, 2, -1) for part_ in (grad_kv1, grad_kv2)
    )
    grad_kv = jnp.concatenate([grad_kv1, grad_kv2], axis=2).reshape(shard_length, -1)
    joint_grad_kv, gain_k = heads_backward(
        grad_kv, joint_kv, wide_k, cos_table, sin_table, KEY_COLUMNS
    )
    grad_wkv = t_mm(normed, joint_grad_kv).astype(bf16)
    grad_normed = grad_normed + mm_t(joint_grad_kv, wkv)
    grad_input_part, grad_attn_gain = norm_backward(
        inputs, in_scale, attn_gain_full, grad_normed
    )
    input_grad = (grad_middle + grad_input_part).astype(bf16)

    gain_rows = jnp.stack([grad_attn_gain, grad_ffn_gain]).astype(bf16)
    gain_columns = t_mm(gain_rows, jnp.eye(2, LANES, dtype=bf16)).astype(bf16)
    grad_wkv, gain_columns, wq_other, wout_other, hidden_near = stage(
        grad_wkv, gain_columns, wq_other, wout_other, hidden_near
    )
    own_near, send_near = back_pass((hidden_near,), (wdown,), False)
    grad_wq = add_bit(grad_wq, wq_other, 2, 1)
    grad_wout = add_outer(grad_wout, wout_other, 0)
    wq_other, wout_other = pass_outer(grad_wq, 0), pass_bit(grad_wout, 2, 0)
    left = grad_wkv[:, : 3 * LANES].reshape(*shape, -1)
    right = jnp.concatenate([grad_wkv[:, 3 * LANES :], gain_columns], axis=1)
    right = right.reshape(*shape, -1)
    head_gains = jnp.concatenate(
        [
            jnp.sum(gain_q[0].reshape(-1, HEAD_SIZE), axis=0),
            jnp.sum(gain_k[0, :KEY_COLUMNS].reshape(-1, HEAD_SIZE), axis=0),
        ]
    )[None]
    left, right, left_other, right_other, gains_other = stage(
        left,
        right,
        pass_bit(left, 1, 2),
        pass_bit(right, 1, 2),
        exchange(head_gains, "rows", 1),
    )
    head_gains = head_gains + gains_other
    left = add_bit(left, left_other, 1, 2)
    right = add_bit(right, right_other, 1, 2)
    left_other, right_other, wq_other, wout_other, gains_other, grad_up = stage(
        pass_bit(left, 2, 1),
        pass_outer(right, 0),
        wq_other,
        wout_other,
        exchange(head_gains, "seq", 1),
        grad_up,
    )
    head_gains = head_gains + gains_other
    left = add_bit(left, left_other, 2, 1)
    right = add_outer(right, right_other, 0)
    left_other, right_other, gains_other, near_other = stage(
        pass_outer(left, 0),
        pass_bit(right, 2, 0),
        exchange(head_gains, "rows", 2),
        swap(send_near, 1),
    )
    output = (middle + own_near + near_other.astype(f32) + across.astype(f32)).astype(bf16)
    head_gains = head_gains + gains_other
    sums = reduce_seq(
        jnp.concatenate(
            [
                add_outer(grad_wq, wq_other, 0),
                add_outer(left, left_other, 0),
                add_bit(right, right_other, 2, 0),
                add_bit(grad_wout, wout_other, 2, 0),
            ],
            axis=-1,
        )
    )
    rest = [("rows", bit) for bit in (4, 8, 16) if bit < row_devices]
    rest += [("seq", bit) for bit in (2, 4, 8) if bit < seq_devices]
    gate_up = jnp.stack([grad_gate, grad_up], axis=2)
    other, gains_other = stage(
        swap(part(gate_up, 1 - near, 0), 2), exchange(head_gains, *rest[0])
    )
    head_gains = head_gains + gains_other
    grads = joined(part(gate_up, near, 0), other, near, 0)
    for axis, bit in rest[1:]:
        head_gains = head_gains + exchange(head_gains, axis, bit)
    head_gains = head_gains[0]
    grads = joined(part(grads, core, 1), swap(part(grads, 1 - core, 1), 1), core, 1)

    def from_group(blocks):
        blocks = blocks.reshape(4, d_rows, seq_devices, outer, f_rows)
        return jnp.transpose(blocks, (1, 3, 0, 2, 4)).reshape(d_rows, -1)

    grad_wgate, grad_wup = stage(from_group(grads[:, :, 0]), from_group(grads[:, :, 1]))
    sums, grad_wgate, grad_wup, grad_wdown, output, input_grad = stage(
        sums, grad_wgate.astype(f32), grad_wup.astype(f32), grad_wdown.astype(f32), output, input_grad
    )
    columns = QUERY_COLUMNS + 2 * KEY_COLUMNS
    long_gains = sums[:, columns : columns + 2].astype(f32)
    return (
        output[None],
        input_grad[None],
        sums[:, :columns].astype(f32),
        sums[:, columns + LANES :].T.astype(f32),
        grad_wgate,
        grad_wup,
        grad_wdown,
        long_gains[:, 0],
        long_gains[:, 1],
        head_gains[:HEAD_SIZE],
        head_gains[HEAD_SIZE:],
    )


def solution(mesh):
    return jax.shard_map(
        shards,
        mesh=mesh,
        in_specs=(
            P("rows", "seq", None),
            P("rows"),
            P(),
            P(("rows", "seq"), None),
            P(None, ("rows", "seq")),
            P(("rows", "seq"), None),
            P(("rows", "seq"), None),
            P(("rows", "seq"), None),
            P(("rows", "seq")),
            P(("rows", "seq")),
            P(),
            P(),
            P("rows", "seq", None),
        ),
        out_specs=(
            P("rows", "seq", None),
            P("rows", "seq", None),
            P(("rows", "seq"), None),
            P(None, ("rows", "seq")),
            P(("rows", "seq"), None),
            P(("rows", "seq"), None),
            P(("rows", "seq"), None),
            P(("rows", "seq")),
            P(("rows", "seq")),
            P(),
            P(),
        ),
        check_vma=False,
    )
```

```python
import math
from functools import partial

import jax
import jax.numpy as jnp
from jax import lax
from jax.experimental import pallas as pl
from jax.experimental.pallas import tpu as pltpu
from jax.sharding import PartitionSpec as P

QUERY_HEADS = 20
KEY_VALUE_HEADS = 5
HEAD_SIZE = 64
CORPORA = 8
DENOM = 64
EPSILON = 1e-06
ROPE_BASE = 10000.0
QUERY_COLUMNS = QUERY_HEADS * HEAD_SIZE
KEY_COLUMNS = KEY_VALUE_HEADS * HEAD_SIZE
LANES = 128
SCORE_EXPONENT = 1.4426950408889634 * HEAD_SIZE**-0.5
SPLIT = 2
VMEM_LIMIT = 48 * 1024 * 1024

f32, bf16 = jnp.float32, jnp.bfloat16
LIGHT = pl.CostEstimate(flops=1000, bytes_accessed=1000, transcendentals=0)


def dot_nn(a, b):
    return lax.dot_general(a, b, (((1,), (0,)), ((), ())), preferred_element_type=f32)


def dot_nt(a, b):
    return lax.dot_general(a, b, (((1,), (1,)), ((), ())), preferred_element_type=f32)


def dot_tn(a, b):
    return lax.dot_general(a, b, (((0,), (0,)), ((), ())), preferred_element_type=f32)


def lanes_of(shape):
    return lax.broadcasted_iota(jnp.int32, shape, len(shape) - 1)


def head_sum(values):
    row = lax.broadcasted_iota(jnp.int32, (LANES, LANES), 0) // HEAD_SIZE
    column = lax.broadcasted_iota(jnp.int32, (LANES, LANES), 1) // HEAD_SIZE
    ones = jnp.where(row == column, 1.0, 0.0).astype(bf16)
    high = values.astype(bf16)
    low = (values - high.astype(f32)).astype(bf16)
    return dot_nn(high, ones) + dot_nn(low, ones)


def partner(values):
    first = lanes_of(values.shape) % HEAD_SIZE < HEAD_SIZE // 2
    return jnp.where(
        first,
        pltpu.roll(values, LANES - HEAD_SIZE // 2, 1),
        pltpu.roll(values, HEAD_SIZE // 2, 1),
    )


def heads_of(joint, norm_columns, gain_ref, cos_ref, sin_ref, out_ref):
    columns = joint.shape[1]
    for start in range(0, columns, LANES):
        chunk = slice(start, start + LANES)
        values = joint[:, chunk]
        scale = lax.rsqrt(head_sum(values * values) * (1.0 / HEAD_SIZE) + EPSILON)
        normed = values * scale * gain_ref[0:1, chunk]
        turned = normed * cos_ref[...] + partner(normed) * sin_ref[...]
        place = pl.program_id(0) * columns + start + lanes_of(values.shape)
        out_ref[:, chunk] = jnp.where(place < norm_columns, turned, values).astype(bf16)


def heads_forward_kernel(
    norm_columns, normed_ref, weight_ref, gain_ref, cos_ref, sin_ref, joint_ref, out_ref
):
    joint = dot_nn(normed_ref[...], weight_ref[...])
    joint_ref[...] = joint
    heads_of(joint, norm_columns, gain_ref, cos_ref, sin_ref, out_ref)


def heads_halves_kernel(
    side_ref, normed_ref, own_ref, other_ref, gain_ref, cos_ref, sin_ref, joint_ref, out_ref
):
    count, block, _ = own_ref.shape
    joint = None
    for index in range(count):
        for weight_ref, side in ((own_ref, side_ref[0]), (other_ref, 1 - side_ref[0])):
            rows = pl.ds(pl.multiple_of((2 * index + side) * block, block), block)
            term = dot_nn(normed_ref[:, rows], weight_ref[index])
            joint = term if joint is None else joint + term
    joint_ref[...] = joint
    heads_of(joint, QUERY_COLUMNS, gain_ref, cos_ref, sin_ref, out_ref)


def heads_forward_halves(normed, own, other, side, gain, cos, sin):
    tokens, width = normed.shape
    count, block, columns = own.shape
    tile = 2 * LANES
    out = pl.BlockSpec((tokens, tile), lambda i, s: (0, i))
    table = pl.BlockSpec((tokens, LANES), lambda i, s: (0, 0))
    weight = pl.BlockSpec((count, block, tile), lambda i, s: (0, 0, i))
    return pl.pallas_call(
        heads_halves_kernel,
        grid_spec=pltpu.PrefetchScalarGridSpec(
            num_scalar_prefetch=1,
            grid=(columns // tile,),
            in_specs=[
                pl.BlockSpec((tokens, width), lambda i, s: (0, 0)),
                weight,
                weight,
                pl.BlockSpec((8, tile), lambda i, s: (0, i)),
                table,
                table,
            ],
            out_specs=[out, out],
        ),
        out_shape=[
            jax.ShapeDtypeStruct((tokens, columns), f32),
            jax.ShapeDtypeStruct((tokens, columns), bf16),
        ],
        compiler_params=pltpu.CompilerParams(vmem_limit_bytes=VMEM_LIMIT),
        name="heads_forward_halves",
        cost_estimate=LIGHT,
    )(side.astype(jnp.int32).reshape(1), normed, own, other, gain, cos, sin)


def heads_forward(normed, weight, gain, cos, sin, norm_columns):
    tokens, width = normed.shape
    columns = weight.shape[1]
    tile = 2 * LANES if columns % (2 * LANES) == 0 else LANES
    out = pl.BlockSpec((tokens, tile), lambda i: (0, i))
    table = pl.BlockSpec((tokens, LANES), lambda i: (0, 0))
    return pl.pallas_call(
        partial(heads_forward_kernel, norm_columns),
        grid=(columns // tile,),
        in_specs=[
            pl.BlockSpec((tokens, width), lambda i: (0, 0)),
            pl.BlockSpec((width, tile), lambda i: (0, i)),
            pl.BlockSpec((8, tile), lambda i: (0, i)),
            table,
            table,
        ],
        out_specs=[out, out],
        out_shape=[
            jax.ShapeDtypeStruct((tokens, columns), f32),
            jax.ShapeDtypeStruct((tokens, columns), bf16),
        ],
        compiler_params=pltpu.CompilerParams(vmem_limit_bytes=VMEM_LIMIT),
        name="heads_forward",
        cost_estimate=LIGHT,
    )(normed, weight, gain, cos, sin)


def project_kernel(side_ref, mixed_ref, own_ref, other_ref, inputs_ref, out_ref):
    block = own_ref.shape[1]
    for weight_ref, side in ((own_ref, side_ref[0]), (other_ref, 1 - side_ref[0])):
        columns = pl.ds(pl.multiple_of(side * block, block), block)
        out_ref[:, columns] = inputs_ref[:, columns].astype(f32) + dot_nt(
            mixed_ref[...], weight_ref[0]
        )


def project(mixed, own, other, inputs, side):
    tokens, depth = mixed.shape
    count, block, _ = own.shape
    weight = pl.BlockSpec((1, block, depth), lambda i, s: (i, 0, 0))
    out = pl.BlockSpec((tokens, 2 * block), lambda i, s: (0, i))
    return pl.pallas_call(
        project_kernel,
        grid_spec=pltpu.PrefetchScalarGridSpec(
            num_scalar_prefetch=1,
            grid=(count,),
            in_specs=[pl.BlockSpec((tokens, depth), lambda i, s: (0, 0)), weight, weight, out],
            out_specs=out,
        ),
        out_shape=jax.ShapeDtypeStruct((tokens, 2 * count * block), f32),
        compiler_params=pltpu.CompilerParams(vmem_limit_bytes=VMEM_LIMIT),
        name="project",
        cost_estimate=LIGHT,
    )(side.astype(jnp.int32).reshape(1), mixed, own, other, inputs)


def heads_backward_kernel(
    norm_columns, grad_ref, joint_ref, gain_ref, cos_ref, sin_ref, out_ref, gain_out_ref
):
    grad = grad_ref[...].astype(f32)
    values = joint_ref[...]
    gain = gain_ref[0:1, :]
    turned = grad * cos_ref[...] - partner(grad) * sin_ref[...]
    scale = lax.rsqrt(head_sum(values * values) * (1.0 / HEAD_SIZE) + EPSILON)
    gained = turned * gain
    inner = head_sum(values * gained) * (1.0 / HEAD_SIZE)
    result = scale * gained - values * (scale * scale * scale) * inner
    place = pl.program_id(0) * LANES + lanes_of(values.shape)
    out_ref[...] = jnp.where(place < norm_columns, result, grad).astype(bf16)
    gain_out_ref[...] = jnp.broadcast_to(
        jnp.sum(turned * values * scale, axis=0, keepdims=True), gain_out_ref.shape
    )


def heads_backward(grad, joint, gain, cos, sin, norm_columns):
    tokens, columns = joint.shape
    return pl.pallas_call(
        partial(heads_backward_kernel, norm_columns),
        grid=(columns // LANES,),
        in_specs=[
            pl.BlockSpec((tokens, LANES), lambda i: (0, i)),
            pl.BlockSpec((tokens, LANES), lambda i: (0, i)),
            pl.BlockSpec((8, LANES), lambda i: (0, i)),
            pl.BlockSpec((tokens, LANES), lambda i: (0, 0)),
            pl.BlockSpec((tokens, LANES), lambda i: (0, 0)),
        ],
        out_specs=[
            pl.BlockSpec((tokens, LANES), lambda i: (0, i)),
            pl.BlockSpec((8, LANES), lambda i: (0, i)),
        ],
        out_shape=[
            jax.ShapeDtypeStruct((tokens, columns), bf16),
            jax.ShapeDtypeStruct((8, columns), f32),
        ],
        name="heads_backward",
        cost_estimate=LIGHT,
    )(grad, joint, gain, cos, sin)


def both_halves(pair, odd):
    wide = pair.astype(f32)
    first = lanes_of(wide.shape) < HEAD_SIZE
    keep = jnp.where(odd == 1, jnp.where(first, 0, 1), jnp.where(first, 1, 0)) == 1
    return jnp.where(keep, wide, pltpu.roll(wide, HEAD_SIZE, 1))


def attend_forward_kernel(place_ref, q_ref, k_ref, v_ref, out_ref, log_ref):
    group = pl.program_id(0) // 2
    place = place_ref[0]
    tokens = q_ref.shape[0]
    first = lanes_of((tokens, LANES)) < HEAD_SIZE
    pair = q_ref[...].astype(f32)
    queries = (jnp.where(first, pair, 0.0).astype(bf16), jnp.where(first, 0.0, pair).astype(bf16))

    def step(j, totals, diagonal):
        rows = pl.ds(pl.multiple_of(j * tokens, tokens), tokens)
        keys = both_halves(k_ref[rows, :], group % 2).astype(bf16)
        values = both_halves(v_ref[rows, :], (KEY_VALUE_HEADS + group) % 2)
        sides = (
            jnp.where(first, values, 1.0).astype(bf16),
            jnp.where(first, 1.0, values).astype(bf16),
        )
        result = []
        for head in range(2):
            weights = jnp.exp2(dot_nt(queries[head], keys) * SCORE_EXPONENT)
            if diagonal:
                row = lax.broadcasted_iota(jnp.int32, weights.shape, 0)
                weights = jnp.where(lanes_of(weights.shape) <= row, weights, 0.0)
            result.append(totals[head] + dot_nn(weights.astype(bf16), sides[head]))
        return tuple(result)

    zero = jnp.zeros((tokens, LANES), f32)
    totals = lax.fori_loop(0, place, lambda j, c: step(j, c, False), (zero, zero))
    totals = step(place, totals, True)
    numerator = jnp.where(first, totals[0], totals[1])
    swapped = jnp.where(first, totals[1], totals[0])
    out_ref[...] = (numerator / pltpu.roll(swapped, HEAD_SIZE, 1)).astype(bf16)
    log_ref[...] = jnp.log2(swapped)


def attend_forward(place, queries, keys_values):
    tokens = queries.shape[0]
    length = keys_values.shape[0]
    pairs = QUERY_COLUMNS // LANES
    return pl.pallas_call(
        attend_forward_kernel,
        grid_spec=pltpu.PrefetchScalarGridSpec(
            num_scalar_prefetch=1,
            grid=(pairs,),
            in_specs=[
                pl.BlockSpec((tokens, LANES), lambda i, s: (0, i)),
                pl.BlockSpec((length, LANES), lambda i, s: (0, (i // 2) // 2)),
                pl.BlockSpec((length, LANES), lambda i, s: (0, (KEY_VALUE_HEADS + i // 2) // 2)),
            ],
            out_specs=[
                pl.BlockSpec((tokens, LANES), lambda i, s: (0, i)),
                pl.BlockSpec((tokens, LANES), lambda i, s: (0, i)),
            ],
        ),
        out_shape=[
            jax.ShapeDtypeStruct((tokens, QUERY_COLUMNS), bf16),
            jax.ShapeDtypeStruct((tokens, QUERY_COLUMNS), f32),
        ],
        compiler_params=pltpu.CompilerParams(vmem_limit_bytes=VMEM_LIMIT),
        name="attend_forward",
        cost_estimate=LIGHT,
    )(place, queries, keys_values, keys_values)


def three_parts(values, lane):
    high = values.astype(bf16).astype(f32)
    rest = values - high
    middle = rest.astype(bf16).astype(f32)
    low = rest - middle
    return jnp.where(
        lane == 0, high, jnp.where(lane == 1, middle, jnp.where(lane == 2, low, 0.0))
    )


def attend_backward_kernel(
    first_group, count, place_ref, q_ref, k_ref, v_ref, out_ref, log_ref, grad_ref, dq_ref, dkv_ref, dk_sum, dv_sum
):
    pair_index = pl.program_id(0)
    local = pair_index // 2
    group = first_group + local
    place = place_ref[0]
    tokens = q_ref.shape[0]
    lane = lanes_of((tokens, LANES))
    first = lane < HEAD_SIZE
    inside = lane % HEAD_SIZE
    pair = q_ref[...].astype(f32)
    grad = grad_ref[...].astype(f32)
    delta = pltpu.roll(head_sum(grad * out_ref[...].astype(f32)), HEAD_SIZE, 1)
    logs = three_parts(log_ref[...] * (1.0 / SCORE_EXPONENT), inside)
    deltas = three_parts(delta, inside)
    minus = jnp.where(inside < 3, -1.0, 0.0)

    def sides(own, other):
        return (
            jnp.where(first, own, other).astype(bf16),
            jnp.where(first, other, own).astype(bf16),
        )

    queries = sides(pair, 0.0)
    grads = sides(grad, 0.0)
    def turned(values):
        return jnp.transpose(values.astype(f32)).astype(bf16)

    queries_log = tuple(turned(v) for v in sides(pair, logs))
    grads_delta = tuple(turned(v) for v in sides(grad, deltas))

    @pl.when(pair_index % 2 == 0)
    def _():
        dk_sum[...] = jnp.zeros_like(dk_sum)
        dv_sum[...] = jnp.zeros_like(dv_sum)

    def step(j, dq, diagonal):
        rows = pl.ds(pl.multiple_of(j * tokens, tokens), tokens)
        key_wide = both_halves(k_ref[rows, :], group % 2)
        value_wide = both_halves(v_ref[rows, :], (KEY_VALUE_HEADS + group) % 2)
        keys_turned = jnp.transpose(key_wide)[:HEAD_SIZE].astype(bf16)
        keys_log = sides(key_wide, minus)
        values_delta = sides(value_wide, minus)
        dk = dk_sum[rows, :]
        dv = dv_sum[rows, :]
        parts = list(dq)
        block = tokens // SPLIT
        for sub in range(SPLIT):
            keep = slice(sub * block, (sub + 1) * block)
            dk_part, dv_part = dk[keep], dv[keep]
            start = sub * block if diagonal else 0
            for head in range(2):
                weights = jnp.exp2(
                    dot_nn(keys_log[head][keep], queries_log[head][:, start:]) * SCORE_EXPONENT
                )
                if diagonal:
                    row = lax.broadcasted_iota(jnp.int32, weights.shape, 0)
                    weights = jnp.where(row <= lanes_of(weights.shape), weights, 0.0)
                grad_weights = dot_nn(values_delta[head][keep], grads_delta[head][:, start:])
                grad_scores = (weights * grad_weights).astype(bf16)
                dv_part = dv_part + dot_nn(weights.astype(bf16), grads[head][start:])
                dk_part = dk_part + dot_nn(grad_scores, queries[head][start:])
                term = dot_nn(keys_turned[:, keep], grad_scores)
                if start:
                    term = jnp.concatenate([jnp.zeros((HEAD_SIZE, start), f32), term], axis=1)
                parts[head] = parts[head] + term
            target = pl.ds(pl.multiple_of(j * tokens + sub * block, block), block)
            dk_sum[target, :] = dk_part
            dv_sum[target, :] = dv_part
        return tuple(parts)

    zero = jnp.zeros((HEAD_SIZE, tokens), f32)
    dq = lax.fori_loop(0, place, lambda j, c: step(j, c, False), (zero, zero))
    dq = jnp.transpose(jnp.concatenate(step(place, dq, True), axis=0))
    dq_ref[...] = (dq * HEAD_SIZE**-0.5).astype(bf16)

    @pl.when(pair_index % 2 == 1)
    def _():
        wide_lane = lanes_of(dk_sum.shape)
        for total, slot, factor in (
            (dk_sum, local, HEAD_SIZE**-0.5),
            (dv_sum, count + local, 1.0),
        ):
            both = (total[...] + pltpu.roll(total[...], HEAD_SIZE, 1)) * factor
            columns = pl.ds(pl.multiple_of(slot // 2 * LANES, LANES), LANES)
            mine = wide_lane // HEAD_SIZE == slot % 2
            dkv_ref[:, columns] = jnp.where(
                mine, both, dkv_ref[:, columns].astype(f32)
            ).astype(bf16)


def attend_backward(first, count, place, queries, keys_values, mixed, logs, grad_mixed):
    tokens = queries.shape[0]
    length = keys_values.shape[0]
    group = QUERY_HEADS // KEY_VALUE_HEADS * HEAD_SIZE
    own = pl.BlockSpec((tokens, LANES), lambda i, s: (0, 2 * first + i))
    keys = pl.BlockSpec((length, LANES), lambda i, s: (0, (first + i // 2) // 2))
    values = pl.BlockSpec(
        (length, LANES), lambda i, s: (0, (KEY_VALUE_HEADS + first + i // 2) // 2)
    )
    columns = 2 * count * HEAD_SIZE
    return pl.pallas_call(
        partial(attend_backward_kernel, first, count),
        grid_spec=pltpu.PrefetchScalarGridSpec(
            num_scalar_prefetch=1,
            grid=(2 * count,),
            in_specs=[own, keys, values, own, own, own],
            out_specs=[
                pl.BlockSpec((tokens, LANES), lambda i, s: (0, i)),
                pl.BlockSpec((length, columns), lambda i, s: (0, 0)),
            ],
            scratch_shapes=[pltpu.VMEM((length, LANES), f32), pltpu.VMEM((length, LANES), f32)],
        ),
        out_shape=[
            jax.ShapeDtypeStruct((tokens, count * group), bf16),
            jax.ShapeDtypeStruct((length, columns), bf16),
        ],
        compiler_params=pltpu.CompilerParams(vmem_limit_bytes=VMEM_LIMIT),
        name="attend_backward",
        cost_estimate=LIGHT,
    )(place, queries, keys_values, keys_values, mixed, logs, grad_mixed)


def hidden_kernel(n0_ref, n1_ref, wg_ref, wu_ref, hidden_ref, gate_ref, up_ref, n_all):
    tokens = n0_ref.shape[0]

    @pl.when(pl.program_id(0) == 0)
    def _():
        n_all[:tokens] = n0_ref[...]
        n_all[tokens:] = n1_ref[...]

    gate = dot_nn(n_all[...], wg_ref[...])
    up = dot_nn(n_all[...], wu_ref[...])
    hidden_ref[...] = (gate / (1.0 + jnp.exp(-gate)) * up).astype(bf16)
    gate_ref[...] = gate.astype(bf16)
    up_ref[...] = up.astype(bf16)


def hidden_pass(normed, wgate, wup):
    tokens, width = normed[0].shape
    columns = wgate.shape[1]
    tile = min(256, columns)
    whole = pl.BlockSpec((tokens, width), lambda i: (0, 0))
    down = pl.BlockSpec((width, tile), lambda i: (0, i))
    out = pl.BlockSpec((2 * tokens, tile), lambda i: (0, i))
    return pl.pallas_call(
        hidden_kernel,
        grid=(pl.cdiv(columns, tile),),
        in_specs=[whole] * 2 + [down] * 2,
        out_specs=[out] * 3,
        out_shape=[jax.ShapeDtypeStruct((2 * tokens, columns), bf16)] * 3,
        scratch_shapes=[pltpu.VMEM((2 * tokens, width), bf16)],
        compiler_params=pltpu.CompilerParams(vmem_limit_bytes=VMEM_LIMIT),
        name="hidden_pass",
        cost_estimate=LIGHT,
    )(*normed, wgate, wup)


def gate_kernel(n0_ref, n1_ref, wg_ref, gate_ref):
    tokens = n0_ref.shape[0]
    gate_ref[:tokens] = dot_nn(n0_ref[...], wg_ref[...]).astype(bf16)
    gate_ref[tokens:] = dot_nn(n1_ref[...], wg_ref[...]).astype(bf16)


def gate_pass(normed, wgate):
    tokens, width = normed[0].shape
    columns = wgate.shape[1]
    tile = min(256, columns)
    whole = pl.BlockSpec((tokens, width), lambda i: (0, 0))
    return pl.pallas_call(
        gate_kernel,
        grid=(pl.cdiv(columns, tile),),
        in_specs=[whole] * 2 + [pl.BlockSpec((width, tile), lambda i: (0, i))],
        out_specs=pl.BlockSpec((2 * tokens, tile), lambda i: (0, i)),
        out_shape=jax.ShapeDtypeStruct((2 * tokens, columns), bf16),
        compiler_params=pltpu.CompilerParams(vmem_limit_bytes=VMEM_LIMIT),
        name="gate_pass",
        cost_estimate=LIGHT,
    )(*normed, wgate)


def up_kernel(n0_ref, n1_ref, wu_ref, gate_ref, hidden_ref, up_ref):
    tokens = n0_ref.shape[0]
    for n_ref, rows in ((n0_ref, slice(0, tokens)), (n1_ref, slice(tokens, 2 * tokens))):
        up = dot_nn(n_ref[...], wu_ref[...])
        gate = gate_ref[rows].astype(f32)
        hidden_ref[rows] = (gate / (1.0 + jnp.exp(-gate)) * up).astype(bf16)
        up_ref[rows] = up.astype(bf16)


def up_pass(normed, wup, gate):
    tokens, width = normed[0].shape
    columns = wup.shape[1]
    tile = min(256, columns)
    whole = pl.BlockSpec((tokens, width), lambda i: (0, 0))
    out = pl.BlockSpec((2 * tokens, tile), lambda i: (0, i))
    return pl.pallas_call(
        up_kernel,
        grid=(pl.cdiv(columns, tile),),
        in_specs=[whole] * 2 + [pl.BlockSpec((width, tile), lambda i: (0, i)), out],
        out_specs=[out] * 2,
        out_shape=[jax.ShapeDtypeStruct((2 * tokens, columns), bf16)] * 2,
        compiler_params=pltpu.CompilerParams(vmem_limit_bytes=VMEM_LIMIT),
        name="up_pass",
        cost_estimate=LIGHT,
    )(*normed, wup, gate)


def gates_kernel(g0_ref, g1_ref, wd_ref, gate_ref, up_ref, gate_out_ref, up_out_ref, g_all):
    tokens = g0_ref.shape[0]

    @pl.when(pl.program_id(0) == 0)
    def _():
        g_all[:tokens] = g0_ref[...]
        g_all[tokens:] = g1_ref[...]

    grad = dot_nt(g_all[...], wd_ref[...])
    gate = gate_ref[...].astype(f32)
    up = up_ref[...].astype(f32)
    sigmoid = 1.0 / (1.0 + jnp.exp(-gate))
    gate_out_ref[...] = (grad * up * (sigmoid * (1.0 + gate * (1.0 - sigmoid)))).astype(bf16)
    up_out_ref[...] = (grad * (gate * sigmoid)).astype(bf16)


def gates_pass(grad_top, wdown, gate, up):
    tokens, width = grad_top[0].shape
    columns = gate.shape[1]
    tile = min(256, columns)
    whole = pl.BlockSpec((tokens, width), lambda i: (0, 0))
    out = pl.BlockSpec((2 * tokens, tile), lambda i: (0, i))
    return pl.pallas_call(
        gates_kernel,
        grid=(pl.cdiv(columns, tile),),
        in_specs=[whole] * 2 + [pl.BlockSpec((tile, width), lambda i: (i, 0)), out, out],
        out_specs=[out] * 2,
        out_shape=[jax.ShapeDtypeStruct((2 * tokens, columns), bf16)] * 2,
        scratch_shapes=[pltpu.VMEM((2 * tokens, width), bf16)],
        compiler_params=pltpu.CompilerParams(vmem_limit_bytes=VMEM_LIMIT),
        name="gates_pass",
        cost_estimate=LIGHT,
    )(*grad_top, wdown, gate, up)


def back_kernel(count, transposed, *refs):
    own_ref, send_ref = refs[-2:]
    tokens = own_ref.shape[0]
    dot = dot_nt if transposed else dot_nn

    def total(start):
        rows = pl.ds(start, tokens)
        result = dot(refs[0][rows, :], refs[count][...])
        for i in range(1, count):
            result = result + dot(refs[i][rows, :], refs[count + i][...])
        return result

    own_ref[...] = total(0)
    send_ref[...] = total(tokens).astype(bf16)


def back_pass(lefts, weights, transposed):
    tokens, depth = lefts[0].shape
    width = weights[0].shape[0 if transposed else 1]
    count = len(lefts)
    tile = min(512, width)
    if transposed:
        weight_spec = pl.BlockSpec((tile, depth), lambda i: (i, 0))
    else:
        weight_spec = pl.BlockSpec((depth, tile), lambda i: (0, i))
    out = pl.BlockSpec((tokens // 2, tile), lambda i: (0, i))
    return pl.pallas_call(
        partial(back_kernel, count, transposed),
        grid=(width // tile,),
        in_specs=[pl.BlockSpec((tokens, depth), lambda i: (0, 0))] * count
        + [weight_spec] * count,
        out_specs=[out, out],
        out_shape=[
            jax.ShapeDtypeStruct((tokens // 2, width), f32),
            jax.ShapeDtypeStruct((tokens // 2, width), bf16),
        ],
        compiler_params=pltpu.CompilerParams(vmem_limit_bytes=VMEM_LIMIT),
        name="back_pass",
        cost_estimate=LIGHT,
    )(*lefts, *weights)


def weight_kernel(left_count, *refs):
    lefts, rights, out_ref = refs[:left_count], refs[left_count:-1], refs[-1]
    step = min(lefts[0].shape[0], rights[0].shape[0])

    def piece(refs, start):
        index, offset = divmod(start, refs[0].shape[0])
        return refs[index][pl.ds(offset, step), :]

    total = None
    for start in range(0, left_count * lefts[0].shape[0], step):
        term = dot_tn(piece(lefts, start), piece(rights, start))
        total = term if total is None else total + term
    out_ref[...] = total.astype(bf16)


def weight_pass(lefts, rights):
    rows, columns = lefts[0].shape[1], rights[0].shape[1]
    tile = 512 if rows % 512 == 0 else 384 if rows % 384 == 0 else rows
    return pl.pallas_call(
        partial(weight_kernel, len(lefts)),
        grid=(rows // tile,),
        in_specs=[pl.BlockSpec((left.shape[0], tile), lambda i: (0, i)) for left in lefts]
        + [pl.BlockSpec(right.shape, lambda i: (0, 0)) for right in rights],
        out_specs=pl.BlockSpec((tile, columns), lambda i: (i, 0)),
        out_shape=jax.ShapeDtypeStruct((rows, columns), bf16),
        compiler_params=pltpu.CompilerParams(vmem_limit_bytes=VMEM_LIMIT),
        name="weight_pass",
        cost_estimate=LIGHT,
    )(*lefts, *rights)


def placed_kernel(side_ref, own_ref, other_ref, out_ref):
    mine = pl.program_id(0) == side_ref[0]

    @pl.when(mine)
    def _():
        for g in range(out_ref.shape[1]):
            out_ref[0, g] = own_ref[:, g]

    @pl.when(jnp.logical_not(mine))
    def _():
        for g in range(out_ref.shape[1]):
            out_ref[0, g] = other_ref[:, g]


def placed(own, other, side):
    seq, group, rows, columns = own.shape

    def entry(mine, e, g, s):
        parked = jnp.where(e == 0, 0, group // 2 - 1)
        return (0, jnp.where((e == s[0]) == mine, g, parked), 0, 0)

    return pl.pallas_call(
        placed_kernel,
        grid_spec=pltpu.PrefetchScalarGridSpec(
            num_scalar_prefetch=1,
            grid=(2, group // 2),
            in_specs=[
                pl.BlockSpec((seq, 2, rows, columns), partial(entry, True)),
                pl.BlockSpec((seq, 2, rows, columns), partial(entry, False)),
            ],
            out_specs=pl.BlockSpec(
                (1, 2, seq, rows, columns), lambda e, g, s: (e, g, 0, 0, 0)
            ),
        ),
        out_shape=jax.ShapeDtypeStruct((2, group, seq, rows, columns), own.dtype),
        compiler_params=pltpu.CompilerParams(vmem_limit_bytes=VMEM_LIMIT),
        name="placed",
        cost_estimate=LIGHT,
    )(side.astype(jnp.int32).reshape(1), own, other)


def joined_kernel(side_ref, own_ref, other_ref, out_ref):
    mine = pl.program_id(1) == side_ref[0]

    @pl.when(mine)
    def _():
        out_ref[:, 0] = own_ref[...]

    @pl.when(jnp.logical_not(mine))
    def _():
        out_ref[:, 0] = other_ref[...]


def joined(own, other, side, axis):
    shape = own.shape[:axis] + (2,) + own.shape[axis:]
    columns = own.shape[-1]
    lead = math.prod(own.shape[:axis])
    rows = math.prod(own.shape[axis:-1])
    leads, chunks = lead, 1
    while leads % 2 == 0 and leads * rows * columns > 800_000:
        leads //= 2
    while leads == 1 and rows % (32 * chunks) == 0 and rows // chunks * columns > 800_000:
        chunks *= 2
    block = rows // chunks

    def entry(mine, p, e, i, s):
        parked = jnp.where(e == 0, 0, chunks - 1)
        return (p, jnp.where((e == s[0]) == mine, i, parked), 0)

    return pl.pallas_call(
        joined_kernel,
        grid_spec=pltpu.PrefetchScalarGridSpec(
            num_scalar_prefetch=1,
            grid=(lead // leads, 2, chunks),
            in_specs=[
                pl.BlockSpec((leads, block, columns), partial(entry, True)),
                pl.BlockSpec((leads, block, columns), partial(entry, False)),
            ],
            out_specs=pl.BlockSpec((leads, 1, block, columns), lambda p, e, i, s: (p, e, i, 0)),
        ),
        out_shape=jax.ShapeDtypeStruct((lead, 2, rows, columns), own.dtype),
        compiler_params=pltpu.CompilerParams(vmem_limit_bytes=VMEM_LIMIT),
        name="joined",
        cost_estimate=LIGHT,
    )(
        side.astype(jnp.int32).reshape(1),
        own.reshape(lead, rows, columns),
        other.reshape(lead, rows, columns),
    ).reshape(shape)


def swap(values, bit):
    pairs = [(i, i ^ bit) for i in range(lax.axis_size("rows"))]
    return lax.ppermute(values, "rows", pairs)


def bit_of(bit):
    return (lax.axis_index("rows") // bit) % 2


def gather_bit(values, bit, axis):
    return joined(values, swap(values, bit), bit_of(bit), axis)


def part(values, index, axis):
    return lax.dynamic_index_in_dim(values, index, axis, keepdims=False)


def reduce_bit(values, bit, axis):
    return add_bit(values, pass_bit(values, bit, axis), bit, axis)


def outer_pairs(step, low, high):
    size = lax.axis_size("rows")
    return [
        (i, i + 4 * step)
        for i in range(size)
        if low <= i // 4 < high and 0 <= i // 4 + step < size // 4
    ]


def send_outer(values):
    count = lax.axis_size("rows") // 4
    if count == 2:
        return (swap(values, 4),)
    up, down = values, values
    ups, downs = [], []
    for t in range(1, count):
        up = lax.ppermute(up, "rows", outer_pairs(1, t - 1, count))
        down = lax.ppermute(down, "rows", outer_pairs(-1, 0, count - t + 1))
        ups.append(up)
        downs.append(down)
    return tuple(ups[::-1] + downs)


def join_outer(values, received, axis):
    count = lax.axis_size("rows") // 4
    if count == 2:
        return joined(values, received[0], bit_of(4), axis)
    place = lax.axis_index("rows") // 4
    line = jnp.stack([*received[: count - 1], values, *received[count - 1 :]], axis)
    return lax.dynamic_slice_in_dim(line, count - 1 - place, count, axis)


def gather_outer(values, axis):
    return join_outer(values, send_outer(values), axis)


def pass_outer(values, axis):
    count = lax.axis_size("rows") // 4
    place = lax.axis_index("rows") // 4

    def entry(index):
        return part(values, jnp.clip(index, 0, count - 1), axis)

    if count == 1:
        return ()
    if count == 2:
        return (swap(entry(1 - place), 4),)
    up, down = entry(place + count - 1), entry(place - count + 1)
    for t in range(1, count):
        up = lax.ppermute(up, "rows", outer_pairs(1, 0, t))
        down = lax.ppermute(down, "rows", outer_pairs(-1, count - t, count))
        if t < count - 1:
            up = (entry(place + count - 1 - t).astype(f32) + up.astype(f32)).astype(bf16)
            down = (entry(place - count + 1 + t).astype(f32) + down.astype(f32)).astype(bf16)
    return (up, down)


def add_outer(values, received, axis):
    total = part(values, lax.axis_index("rows") // 4, axis).astype(f32)
    for term in received:
        total = total + term.astype(f32)
    return total.astype(bf16)


def reduce_outer(values, axis):
    return add_outer(values, pass_outer(values, axis), axis)


def pass_bit(values, bit, axis):
    return swap(part(values, 1 - bit_of(bit), axis), bit)


def add_bit(values, received, bit, axis):
    own = part(values, bit_of(bit), axis)
    return (own.astype(f32) + received.astype(f32)).astype(bf16)


def gather_seq(values):
    return lax.all_gather(values, "seq", axis=0, tiled=False)


def reduce_seq(values):
    return lax.psum_scatter(values, "seq", scatter_dimension=0, tiled=False)


def exchange(values, axis, bit):
    size = lax.axis_size(axis)
    return lax.ppermute(values, axis, [(i, i ^ bit) for i in range(size)])


def across_group(own, send):
    return (own + swap(send, 1).astype(f32)).astype(bf16)


def stage(*values):
    return lax.optimization_barrier(values)


def mm(left, right):
    return jnp.einsum("ab,bc->ac", left, right, preferred_element_type=f32)


def mm_t(left, right):
    return jnp.einsum("ab,cb->ac", left, right, preferred_element_type=f32)


def t_mm(left, right):
    return jnp.einsum("ab,ac->bc", left, right, preferred_element_type=f32)


def norm_scale(values):
    return lax.rsqrt(jnp.mean(values * values, axis=-1, keepdims=True) + EPSILON)


def norm_backward(values, scale, gain, grad):
    gained = grad * gain
    inner = jnp.mean(values * gained, axis=-1, keepdims=True)
    result = scale * gained - values * (scale * scale * scale) * inner
    return result, jnp.sum(grad * values * scale, axis=0)


def shards(
    tokens_in,
    corpus,
    corpus_weight,
    w_qkv,
    w_out,
    w_gate,
    w_up,
    w_down,
    attn_gain,
    ffn_gain,
    q_gain,
    k_gain,
    upstream,
):
    shard_length, width = tokens_in.shape[1:]
    row_devices = lax.axis_size("rows")
    seq_devices = lax.axis_size("seq")
    outer = row_devices // 4
    d_rows = w_qkv.shape[0]
    f_rows = w_down.shape[0]
    place = lax.axis_index("seq").astype(jnp.int32)
    inputs = tokens_in[0].astype(f32)

    extra = jnp.stack(
        [
            attn_gain,
            ffn_gain,
            jnp.broadcast_to(corpus.astype(bf16), attn_gain.shape),
        ],
        axis=1,
    )
    extra = jnp.pad(extra, ((0, 0), (0, LANES - extra.shape[1])))
    kv_shard = jnp.concatenate([w_qkv[:, QUERY_COLUMNS:], extra], axis=1)
    query_shard = jnp.concatenate([w_qkv[:, :QUERY_COLUMNS], w_out.T], axis=1)
    query_shard, w_gate, w_up = stage(query_shard, w_gate, w_up)
    query_lines = gather_seq(query_shard)

    def to_group(weight):
        blocks = weight.reshape(d_rows, outer, 4, seq_devices, f_rows)
        blocks = jnp.transpose(blocks, (2, 0, 3, 1, 4))
        return blocks.reshape(2, 2, d_rows, outer * seq_devices * f_rows)

    def spread_hidden(lines, received):
        if outer == 2:
            lines = lines.reshape(seq_devices, 4, d_rows, hidden_columns)
            other = received[0].reshape(lines.shape)
            return placed(lines, other, bit_of(4)).reshape(width, hidden_columns)
        full = join_outer(lines, received, 0)
        return jnp.moveaxis(full, 1, 3).reshape(width, hidden_columns)

    gate_up = jnp.stack([to_group(w_gate), to_group(w_up)], axis=2)
    hidden_columns = gate_up.shape[-1]
    core, near = bit_of(1), bit_of(2)
    gate_up = joined(
        part(gate_up, core, 1), swap(part(gate_up, 1 - core, 1), 1), core, 1
    )
    gate_up, kv_shard = stage(gate_up, kv_shard)
    other, kv_lines, query_lines = stage(
        swap(part(gate_up, 1 - near, 0), 2), gather_seq(kv_shard), query_lines
    )
    gate_up = joined(part(gate_up, near, 0), other, near, 0)
    gate_lines = gather_seq(gate_up[:, :, 0])
    left, right = kv_lines[..., : 3 * LANES], kv_lines[..., 3 * LANES :]
    left_other, right_other = stage(send_outer(left), swap(right, 2))
    left = join_outer(left, left_other, 0)
    right = joined(right, right_other, near, 0)
    left_other, right_other = stage(swap(left, 2), send_outer(right))
    left = joined(left, left_other, near, 1)
    right = join_outer(right, right_other, 0)
    q_left, q_right = query_lines[..., :QUERY_COLUMNS], query_lines[..., QUERY_COLUMNS:]
    q_left, q_right, left, right = stage(q_left, q_right, left, right)
    q_left_other, q_right_other = send_outer(q_left), swap(q_right, 2)
    left, right = gather_bit(left, 1, 2), gather_bit(right, 1, 2)
    left, right = left.reshape(width, -1), right.reshape(width, -1)
    wkv = jnp.concatenate([left, right[:, : 2 * LANES]], axis=1)
    rows = dot_nt(jnp.eye(8, LANES, dtype=bf16), right[:, 2 * LANES :])
    attn_gain_full, ffn_gain_full, corpus_full = rows[0:1], rows[1:2], rows[2]

    position = (place * shard_length + jnp.arange(shard_length, dtype=jnp.int32)).astype(f32)
    half = HEAD_SIZE // 2
    exponent = jnp.arange(half, dtype=f32) * (-2.0 / HEAD_SIZE)
    angles = position[:, None] * jnp.power(ROPE_BASE, exponent)[None, :]
    cosine, sine = jnp.cos(angles), jnp.sin(angles)
    cos_table = jnp.concatenate([cosine] * 4, axis=1)
    sin_table = jnp.concatenate([-sine, sine] * 2, axis=1)
    wide_q = jnp.tile(q_gain.astype(f32), QUERY_HEADS)
    wide_k = jnp.concatenate(
        [jnp.tile(k_gain.astype(f32), KEY_VALUE_HEADS), jnp.ones((KEY_COLUMNS,), f32)]
    )
    wide_q = jnp.broadcast_to(wide_q[None, :], (8, QUERY_COLUMNS))
    wide_k = jnp.broadcast_to(wide_k[None, :], (8, 2 * KEY_COLUMNS))

    in_scale = norm_scale(inputs)
    normed = (inputs * in_scale * attn_gain_full).astype(bf16)
    joint_kv, own_kv = heads_forward(
        normed, wkv, wide_k, cos_table, sin_table, KEY_COLUMNS
    )
    own_kv, q_left_other, q_right_other, up_in = stage(
        own_kv, q_left_other, q_right_other, gate_up[:, :, 1]
    )
    up_lines = gather_seq(up_in)
    keys_values = gather_seq(own_kv).reshape(-1, 2 * KEY_COLUMNS)
    q_left = join_outer(q_left, q_left_other, 0)
    q_right = joined(q_right, q_right_other, near, 0)
    left_other, right_other, gate_lines, w_down = stage(
        swap(q_left, 2), send_outer(q_right), gate_lines, w_down
    )
    q_left = joined(q_left, left_other, near, 1)
    gate_other = send_outer(gate_lines)
    down_other = send_outer(w_down)
    half_rows = (2 * outer, seq_devices * d_rows, QUERY_COLUMNS)
    q_left_other = swap(q_left, 1)

    corpora = jnp.arange(CORPORA, dtype=jnp.int32)
    per_device = corpus_full.reshape(-1, d_rows)[:, 0].astype(jnp.int32)
    counts = (
        jnp.sum((per_device[:, None] == corpora[None, :]).astype(f32), axis=0) * shard_length
    )
    own_corpus = (corpus[0] == corpora).astype(f32)
    weight_row = jnp.sum(own_corpus * corpus_weight.astype(f32))
    count_row = jnp.sum(own_corpus * counts)
    factor = weight_row / DENOM * (jnp.sum(counts) / (CORPORA * count_row))
    grad_full = upstream[0].astype(f32) * factor
    grad_top, q_left, q_left_other = stage(grad_full.astype(bf16), q_left, q_left_other)

    q_halves = (q_left.reshape(half_rows), q_left_other.reshape(half_rows))
    joint_q, queries = heads_forward_halves(
        normed, *q_halves, core, wide_q, cos_table, sin_table
    )
    queries, q_right, right_other, down_other = stage(queries, q_right, right_other, down_other)
    q_right = join_outer(q_right, right_other, 0)
    down_pair = join_outer(w_down, down_other, 0)
    place_array = place.reshape(1)
    keys_values, queries, down_in = stage(keys_values, queries, down_pair)
    down_lines = gather_seq(down_in)
    mixed, logs = attend_forward(place_array, queries, keys_values)
    mixed, grad_top1, grad_top2, up_lines, wout_other = stage(
        mixed, swap(grad_top, 1), swap(grad_top, 2), up_lines, swap(q_right, 1)
    )
    middle = project(
        mixed, q_right.reshape(half_rows), wout_other.reshape(half_rows), tokens_in[0], core
    )

    ffn_scale = norm_scale(middle)
    normed_ffn = (middle * ffn_scale * ffn_gain_full).astype(bf16)
    up_other = send_outer(up_lines)
    normed_ffn, gate_other, q_right, wout_other, q_left, q_left_other = stage(
        normed_ffn, gate_other, q_right, wout_other, q_left, q_left_other
    )
    normed1 = swap(normed_ffn, 1)
    wgate = spread_hidden(gate_lines, gate_other)
    gate_near, normed2, up_other, wout_t, wq = stage(
        gate_pass((normed_ffn, normed1), wgate),
        swap(normed_ffn, 2),
        up_other,
        joined(q_right, wout_other, core, 2),
        joined(q_left, q_left_other, core, 2),
    )
    wout_t, wq = wout_t.reshape(width, -1), wq.reshape(width, -1)
    wup = spread_hidden(up_lines, up_other)
    hidden_near, up_near = up_pass((normed_ffn, normed1), wup, gate_near)
    normed3, hidden_near, grad_top3 = stage(
        swap(normed2, 1), hidden_near, swap(grad_top2, 1)
    )
    hidden_far, gate_far, up_far = hidden_pass((normed2, normed3), wgate, wup)
    normed4 = (normed_ffn, normed1, normed2, normed3)
    grad_top4 = (grad_top, grad_top1, grad_top2, grad_top3)
    wdown = down_lines.reshape(hidden_columns, width)
    gate_far, up_far = gates_pass((grad_top2, grad_top3), wdown, gate_far, up_far)
    own, send = back_pass((gate_far, up_far), (wgate, wup), True)
    grad_wdown = weight_pass((hidden_near, hidden_far), grad_top4)
    own, send, grad_wdown, wdown = stage(own, swap(send, 1), grad_wdown, wdown)
    across = (own + send.astype(f32)).astype(bf16)
    across, wdown = stage(across, wdown)
    gate_near, up_near = gates_pass((grad_top, grad_top1), wdown, gate_near, up_near)
    own, send = back_pass((gate_near, up_near), (wgate, wup), True)
    hidden_shape = (outer, 2, 2, seq_devices, d_rows, hidden_columns)
    grad_wdown = grad_wdown.reshape(seq_devices, outer, f_rows, width)
    grad_wgate = weight_pass(normed4, (gate_near, gate_far)).reshape(hidden_shape)
    across, own, send, grad_wgate, up_near = stage(
        swap(across, 2), own, send, grad_wgate, up_near
    )
    grad_wup = weight_pass(normed4, (up_near, up_far)).reshape(hidden_shape)
    send, grad_wup, down_other = stage(swap(send, 1), grad_wup, pass_outer(grad_wdown, 1))
    grad_wdown = add_outer(grad_wdown, down_other, 1)
    own = own + send.astype(f32)
    grad_normed_ffn = own + across.astype(f32)
    grad_wdown = reduce_seq(grad_wdown)

    grad_middle_part, grad_ffn_gain = norm_backward(
        middle, ffn_scale, ffn_gain_full, grad_normed_ffn
    )
    grad_middle = grad_full + grad_middle_part
    grad_branch = grad_middle.astype(bf16)
    grad_mixed = mm(grad_branch, wout_t).astype(bf16)
    attend = (place_array, queries, keys_values, mixed, logs)
    grad_q1, grad_kv1 = attend_backward(0, 2, *attend, grad_mixed)
    gate_other = pass_outer(grad_wgate, 0)
    grad_q1, grad_kv1, grad_mixed, grad_wdown, hidden_far = stage(
        grad_q1, grad_kv1, grad_mixed, grad_wdown, hidden_far
    )
    grad_kv1 = reduce_seq(grad_kv1.reshape(seq_devices, shard_length, -1))
    shape = (outer, 2, 2, seq_devices, d_rows)
    own_far, send_far = back_pass((hidden_far,), (wdown,), False)
    grad_wout, far_other, gate_other, grad_mixed = stage(
        t_mm(grad_branch, mixed).astype(bf16).reshape(*shape, QUERY_COLUMNS),
        swap(send_far, 1),
        gate_other,
        grad_mixed,
    )
    grad_gate = reduce_seq(jnp.moveaxis(add_outer(grad_wgate, gate_other, 0), 2, 0))
    across = (own_far + far_other.astype(f32)).astype(bf16)
    across, grad_mixed = stage(across, grad_mixed)
    grad_q2, grad_kv2 = attend_backward(2, 3, *attend, grad_mixed)
    grad_q2, grad_kv2, hidden_near, grad_kv1, grad_gate, wout_other, up_other, across = stage(
        grad_q2,
        grad_kv2,
        hidden_near,
        grad_kv1,
        grad_gate,
        pass_bit(grad_wout, 1, 2),
        pass_outer(grad_wup, 0),
        swap(across, 2),
    )
    grad_kv2 = reduce_seq(grad_kv2.reshape(seq_devices, shard_length, -1))

    grad_q = jnp.concatenate([grad_q1, grad_q2], axis=1)
    joint_grad_q, gain_q = heads_backward(
        grad_q, joint_q, wide_q, cos_table, sin_table, QUERY_COLUMNS
    )
    grad_wq = t_mm(normed, joint_grad_q).astype(bf16).reshape(*shape, QUERY_COLUMNS)
    grad_wout = add_bit(grad_wout, wout_other, 1, 2)
    grad_up = jnp.moveaxis(add_outer(grad_wup, up_other, 0), 2, 0)
    grad_kv2, grad_normed, grad_wq, grad_wout, grad_up, wq_other = stage(
        grad_kv2,
        mm_t(joint_grad_q, wq),
        grad_wq,
        grad_wout,
        grad_up,
        pass_bit(grad_wq, 1, 2),
    )
    grad_up = reduce_seq(grad_up)
    grad_wq, grad_kv2 = stage(add_bit(grad_wq, wq_other, 1, 2), grad_kv2)
    wq_other, wout_other = pass_bit(grad_wq, 2, 1), pass_outer(grad_wout, 0)


    grad_kv1, grad_kv2 = (
        part_.reshape(shard_length, 2, -1) for part_ in (grad_kv1, grad_kv2)
    )
    grad_kv = jnp.concatenate([grad_kv1, grad_kv2], axis=2).reshape(shard_length, -1)
    joint_grad_kv, gain_k = heads_backward(
        grad_kv, joint_kv, wide_k, cos_table, sin_table, KEY_COLUMNS
    )
    grad_wkv = t_mm(normed, joint_grad_kv).astype(bf16)
    grad_normed = grad_normed + mm_t(joint_grad_kv, wkv)
    grad_input_part, grad_attn_gain = norm_backward(
        inputs, in_scale, attn_gain_full, grad_normed
    )
    input_grad = (grad_middle + grad_input_part).astype(bf16)

    gain_rows = jnp.stack([grad_attn_gain, grad_ffn_gain]).astype(bf16)
    gain_columns = t_mm(gain_rows, jnp.eye(2, LANES, dtype=bf16)).astype(bf16)
    grad_wkv, gain_columns, wq_other, wout_other, hidden_near = stage(
        grad_wkv, gain_columns, wq_other, wout_other, hidden_near
    )
    own_near, send_near = back_pass((hidden_near,), (wdown,), False)
    grad_wq = add_bit(grad_wq, wq_other, 2, 1)
    grad_wout = add_outer(grad_wout, wout_other, 0)
    wq_other, wout_other = pass_outer(grad_wq, 0), pass_bit(grad_wout, 2, 0)
    left = grad_wkv[:, : 3 * LANES].reshape(*shape, -1)
    right = jnp.concatenate([grad_wkv[:, 3 * LANES :], gain_columns], axis=1)
    right = right.reshape(*shape, -1)
    head_gains = jnp.concatenate(
        [
            jnp.sum(gain_q[0].reshape(-1, HEAD_SIZE), axis=0),
            jnp.sum(gain_k[0, :KEY_COLUMNS].reshape(-1, HEAD_SIZE), axis=0),
        ]
    )[None]
    left, right, left_other, right_other, gains_other = stage(
        left,
        right,
        pass_bit(left, 1, 2),
        pass_bit(right, 1, 2),
        exchange(head_gains, "rows", 1),
    )
    head_gains = head_gains + gains_other
    left = add_bit(left, left_other, 1, 2)
    right = add_bit(right, right_other, 1, 2)
    left_other, right_other, wq_other, wout_other, gains_other, grad_up = stage(
        pass_bit(left, 2, 1),
        pass_outer(right, 0),
        wq_other,
        wout_other,
        exchange(head_gains, "seq", 1),
        grad_up,
    )
    head_gains = head_gains + gains_other
    left = add_bit(left, left_other, 2, 1)
    right = add_outer(right, right_other, 0)
    left_other, right_other, gains_other, near_other = stage(
        pass_outer(left, 0),
        pass_bit(right, 2, 0),
        exchange(head_gains, "rows", 2),
        swap(send_near, 1),
    )
    output = (middle + own_near + near_other.astype(f32) + across.astype(f32)).astype(bf16)
    head_gains = head_gains + gains_other
    sums = reduce_seq(
        jnp.concatenate(
            [
                add_outer(grad_wq, wq_other, 0),
                add_outer(left, left_other, 0),
                add_bit(right, right_other, 2, 0),
                add_bit(grad_wout, wout_other, 2, 0),
            ],
            axis=-1,
        )
    )
    rest = [("rows", bit) for bit in (4, 8, 16) if bit < row_devices]
    rest += [("seq", bit) for bit in (2, 4, 8) if bit < seq_devices]
    gate_up = jnp.stack([grad_gate, grad_up], axis=2)
    other, gains_other = stage(
        swap(part(gate_up, 1 - near, 0), 2), exchange(head_gains, *rest[0])
    )
    head_gains = head_gains + gains_other
    grads = joined(part(gate_up, near, 0), other, near, 0)
    for axis, bit in rest[1:]:
        head_gains = head_gains + exchange(head_gains, axis, bit)
    head_gains = head_gains[0]
    grads = joined(part(grads, core, 1), swap(part(grads, 1 - core, 1), 1), core, 1)

    def from_group(blocks):
        blocks = blocks.reshape(4, d_rows, seq_devices, outer, f_rows)
        return jnp.transpose(blocks, (1, 3, 0, 2, 4)).reshape(d_rows, -1)

    grad_wgate, grad_wup = stage(from_group(grads[:, :, 0]), from_group(grads[:, :, 1]))
    sums, grad_wgate, grad_wup, grad_wdown, output, input_grad = stage(
        sums, grad_wgate.astype(f32), grad_wup.astype(f32), grad_wdown.astype(f32), output, input_grad
    )
    columns = QUERY_COLUMNS + 2 * KEY_COLUMNS
    long_gains = sums[:, columns : columns + 2].astype(f32)
    return (
        output[None],
        input_grad[None],
        sums[:, :columns].astype(f32),
        sums[:, columns + LANES :].T.astype(f32),
        grad_wgate,
        grad_wup,
        grad_wdown,
        long_gains[:, 0],
        long_gains[:, 1],
        head_gains[:HEAD_SIZE],
        head_gains[HEAD_SIZE:],
    )


def solution(mesh):
    return jax.shard_map(
        shards,
        mesh=mesh,
        in_specs=(
            P("rows", "seq", None),
            P("rows"),
            P(),
            P(("rows", "seq"), None),
            P(None, ("rows", "seq")),
            P(("rows", "seq"), None),
            P(("rows", "seq"), None),
            P(("rows", "seq"), None),
            P(("rows", "seq")),
            P(("rows", "seq")),
            P(),
            P(),
            P("rows", "seq", None),
        ),
        out_specs=(
            P("rows", "seq", None),
            P("rows", "seq", None),
            P(("rows", "seq"), None),
            P(None, ("rows", "seq")),
            P(("rows", "seq"), None),
            P(("rows", "seq"), None),
            P(("rows", "seq"), None),
            P(("rows", "seq")),
            P(("rows", "seq")),
            P(),
            P(),
        ),
        check_vma=False,
    )
```

```python
import math
from functools import partial

import jax
import jax.numpy as jnp
from jax import lax
from jax.experimental import pallas as pl
from jax.experimental.pallas import tpu as pltpu
from jax.sharding import PartitionSpec as P

QUERY_HEADS = 20
KEY_VALUE_HEADS = 5
HEAD_SIZE = 64
CORPORA = 8
DENOM = 64
EPSILON = 1e-06
ROPE_BASE = 10000.0
QUERY_COLUMNS = QUERY_HEADS * HEAD_SIZE
KEY_COLUMNS = KEY_VALUE_HEADS * HEAD_SIZE
LANES = 128
SCORE_EXPONENT = 1.4426950408889634 * HEAD_SIZE**-0.5
SPLIT = 2
VMEM_LIMIT = 48 * 1024 * 1024

f32, bf16 = jnp.float32, jnp.bfloat16
LIGHT = pl.CostEstimate(flops=1000, bytes_accessed=1000, transcendentals=0)


def dot_nn(a, b):
    return lax.dot_general(a, b, (((1,), (0,)), ((), ())), preferred_element_type=f32)


def dot_nt(a, b):
    return lax.dot_general(a, b, (((1,), (1,)), ((), ())), preferred_element_type=f32)


def dot_tn(a, b):
    return lax.dot_general(a, b, (((0,), (0,)), ((), ())), preferred_element_type=f32)


def lanes_of(shape):
    return lax.broadcasted_iota(jnp.int32, shape, len(shape) - 1)


def head_sum(values):
    row = lax.broadcasted_iota(jnp.int32, (LANES, LANES), 0) // HEAD_SIZE
    column = lax.broadcasted_iota(jnp.int32, (LANES, LANES), 1) // HEAD_SIZE
    ones = jnp.where(row == column, 1.0, 0.0).astype(bf16)
    high = values.astype(bf16)
    low = (values - high.astype(f32)).astype(bf16)
    return dot_nn(high, ones) + dot_nn(low, ones)


def partner(values):
    first = lanes_of(values.shape) % HEAD_SIZE < HEAD_SIZE // 2
    return jnp.where(
        first,
        pltpu.roll(values, LANES - HEAD_SIZE // 2, 1),
        pltpu.roll(values, HEAD_SIZE // 2, 1),
    )


def heads_of(joint, norm_columns, gain_ref, cos_ref, sin_ref, out_ref):
    columns = joint.shape[1]
    for start in range(0, columns, LANES):
        chunk = slice(start, start + LANES)
        values = joint[:, chunk]
        scale = lax.rsqrt(head_sum(values * values) * (1.0 / HEAD_SIZE) + EPSILON)
        normed = values * scale * gain_ref[0:1, chunk]
        turned = normed * cos_ref[...] + partner(normed) * sin_ref[...]
        place = pl.program_id(0) * columns + start + lanes_of(values.shape)
        out_ref[:, chunk] = jnp.where(place < norm_columns, turned, values).astype(bf16)


def heads_forward_kernel(
    norm_columns, normed_ref, weight_ref, gain_ref, cos_ref, sin_ref, joint_ref, out_ref
):
    joint = dot_nn(normed_ref[...], weight_ref[...])
    joint_ref[...] = joint
    heads_of(joint, norm_columns, gain_ref, cos_ref, sin_ref, out_ref)


def heads_halves_kernel(
    side_ref, normed_ref, own_ref, other_ref, gain_ref, cos_ref, sin_ref, joint_ref, out_ref
):
    count, block, _ = own_ref.shape
    joint = None
    for index in range(count):
        for weight_ref, side in ((own_ref, side_ref[0]), (other_ref, 1 - side_ref[0])):
            rows = pl.ds(pl.multiple_of((2 * index + side) * block, block), block)
            term = dot_nn(normed_ref[:, rows], weight_ref[index])
            joint = term if joint is None else joint + term
    joint_ref[...] = joint
    heads_of(joint, QUERY_COLUMNS, gain_ref, cos_ref, sin_ref, out_ref)


def heads_forward_halves(normed, own, other, side, gain, cos, sin):
    tokens, width = normed.shape
    count, block, columns = own.shape
    tile = 2 * LANES
    out = pl.BlockSpec((tokens, tile), lambda i, s: (0, i))
    table = pl.BlockSpec((tokens, LANES), lambda i, s: (0, 0))
    weight = pl.BlockSpec((count, block, tile), lambda i, s: (0, 0, i))
    return pl.pallas_call(
        heads_halves_kernel,
        grid_spec=pltpu.PrefetchScalarGridSpec(
            num_scalar_prefetch=1,
            grid=(columns // tile,),
            in_specs=[
                pl.BlockSpec((tokens, width), lambda i, s: (0, 0)),
                weight,
                weight,
                pl.BlockSpec((8, tile), lambda i, s: (0, i)),
                table,
                table,
            ],
            out_specs=[out, out],
        ),
        out_shape=[
            jax.ShapeDtypeStruct((tokens, columns), f32),
            jax.ShapeDtypeStruct((tokens, columns), bf16),
        ],
        compiler_params=pltpu.CompilerParams(vmem_limit_bytes=VMEM_LIMIT),
        name="heads_forward_halves",
        cost_estimate=LIGHT,
    )(side.astype(jnp.int32).reshape(1), normed, own, other, gain, cos, sin)


def heads_forward(normed, weight, gain, cos, sin, norm_columns):
    tokens, width = normed.shape
    columns = weight.shape[1]
    tile = 2 * LANES if columns % (2 * LANES) == 0 else LANES
    out = pl.BlockSpec((tokens, tile), lambda i: (0, i))
    table = pl.BlockSpec((tokens, LANES), lambda i: (0, 0))
    return pl.pallas_call(
        partial(heads_forward_kernel, norm_columns),
        grid=(columns // tile,),
        in_specs=[
            pl.BlockSpec((tokens, width), lambda i: (0, 0)),
            pl.BlockSpec((width, tile), lambda i: (0, i)),
            pl.BlockSpec((8, tile), lambda i: (0, i)),
            table,
            table,
        ],
        out_specs=[out, out],
        out_shape=[
            jax.ShapeDtypeStruct((tokens, columns), f32),
            jax.ShapeDtypeStruct((tokens, columns), bf16),
        ],
        compiler_params=pltpu.CompilerParams(vmem_limit_bytes=VMEM_LIMIT),
        name="heads_forward",
        cost_estimate=LIGHT,
    )(normed, weight, gain, cos, sin)


def project_kernel(side_ref, mixed_ref, own_ref, other_ref, inputs_ref, out_ref):
    block = own_ref.shape[1]
    for weight_ref, side in ((own_ref, side_ref[0]), (other_ref, 1 - side_ref[0])):
        columns = pl.ds(pl.multiple_of(side * block, block), block)
        out_ref[:, columns] = inputs_ref[:, columns].astype(f32) + dot_nt(
            mixed_ref[...], weight_ref[0]
        )


def project(mixed, own, other, inputs, side):
    tokens, depth = mixed.shape
    count, block, _ = own.shape
    weight = pl.BlockSpec((1, block, depth), lambda i, s: (i, 0, 0))
    out = pl.BlockSpec((tokens, 2 * block), lambda i, s: (0, i))
    return pl.pallas_call(
        project_kernel,
        grid_spec=pltpu.PrefetchScalarGridSpec(
            num_scalar_prefetch=1,
            grid=(count,),
            in_specs=[pl.BlockSpec((tokens, depth), lambda i, s: (0, 0)), weight, weight, out],
            out_specs=out,
        ),
        out_shape=jax.ShapeDtypeStruct((tokens, 2 * count * block), f32),
        compiler_params=pltpu.CompilerParams(vmem_limit_bytes=VMEM_LIMIT),
        name="project",
        cost_estimate=LIGHT,
    )(side.astype(jnp.int32).reshape(1), mixed, own, other, inputs)


def heads_backward_kernel(
    norm_columns, grad_ref, joint_ref, gain_ref, cos_ref, sin_ref, out_ref, gain_out_ref
):
    grad = grad_ref[...].astype(f32)
    values = joint_ref[...]
    gain = gain_ref[0:1, :]
    turned = grad * cos_ref[...] - partner(grad) * sin_ref[...]
    scale = lax.rsqrt(head_sum(values * values) * (1.0 / HEAD_SIZE) + EPSILON)
    gained = turned * gain
    inner = head_sum(values * gained) * (1.0 / HEAD_SIZE)
    result = scale * gained - values * (scale * scale * scale) * inner
    place = pl.program_id(0) * LANES + lanes_of(values.shape)
    out_ref[...] = jnp.where(place < norm_columns, result, grad).astype(bf16)
    gain_out_ref[...] = jnp.broadcast_to(
        jnp.sum(turned * values * scale, axis=0, keepdims=True), gain_out_ref.shape
    )


def heads_backward(grad, joint, gain, cos, sin, norm_columns):
    tokens, columns = joint.shape
    return pl.pallas_call(
        partial(heads_backward_kernel, norm_columns),
        grid=(columns // LANES,),
        in_specs=[
            pl.BlockSpec((tokens, LANES), lambda i: (0, i)),
            pl.BlockSpec((tokens, LANES), lambda i: (0, i)),
            pl.BlockSpec((8, LANES), lambda i: (0, i)),
            pl.BlockSpec((tokens, LANES), lambda i: (0, 0)),
            pl.BlockSpec((tokens, LANES), lambda i: (0, 0)),
        ],
        out_specs=[
            pl.BlockSpec((tokens, LANES), lambda i: (0, i)),
            pl.BlockSpec((8, LANES), lambda i: (0, i)),
        ],
        out_shape=[
            jax.ShapeDtypeStruct((tokens, columns), bf16),
            jax.ShapeDtypeStruct((8, columns), f32),
        ],
        name="heads_backward",
        cost_estimate=LIGHT,
    )(grad, joint, gain, cos, sin)


def both_halves(pair, odd):
    wide = pair.astype(f32)
    first = lanes_of(wide.shape) < HEAD_SIZE
    keep = jnp.where(odd == 1, jnp.where(first, 0, 1), jnp.where(first, 1, 0)) == 1
    return jnp.where(keep, wide, pltpu.roll(wide, HEAD_SIZE, 1))


def attend_forward_kernel(place_ref, q_ref, k_ref, v_ref, out_ref, log_ref):
    group = pl.program_id(0) // 2
    place = place_ref[0]
    tokens = q_ref.shape[0]
    first = lanes_of((tokens, LANES)) < HEAD_SIZE
    pair = q_ref[...].astype(f32)
    queries = (jnp.where(first, pair, 0.0).astype(bf16), jnp.where(first, 0.0, pair).astype(bf16))

    def step(j, totals, diagonal):
        rows = pl.ds(pl.multiple_of(j * tokens, tokens), tokens)
        keys = both_halves(k_ref[rows, :], group % 2).astype(bf16)
        values = both_halves(v_ref[rows, :], (KEY_VALUE_HEADS + group) % 2)
        sides = (
            jnp.where(first, values, 1.0).astype(bf16),
            jnp.where(first, 1.0, values).astype(bf16),
        )
        result = []
        for head in range(2):
            weights = jnp.exp2(dot_nt(queries[head], keys) * SCORE_EXPONENT)
            if diagonal:
                row = lax.broadcasted_iota(jnp.int32, weights.shape, 0)
                weights = jnp.where(lanes_of(weights.shape) <= row, weights, 0.0)
            result.append(totals[head] + dot_nn(weights.astype(bf16), sides[head]))
        return tuple(result)

    zero = jnp.zeros((tokens, LANES), f32)
    totals = lax.fori_loop(0, place, lambda j, c: step(j, c, False), (zero, zero))
    totals = step(place, totals, True)
    numerator = jnp.where(first, totals[0], totals[1])
    swapped = jnp.where(first, totals[1], totals[0])
    out_ref[...] = (numerator / pltpu.roll(swapped, HEAD_SIZE, 1)).astype(bf16)
    log_ref[...] = jnp.log2(swapped)


def attend_forward(place, queries, keys_values):
    tokens = queries.shape[0]
    length = keys_values.shape[0]
    pairs = QUERY_COLUMNS // LANES
    return pl.pallas_call(
        attend_forward_kernel,
        grid_spec=pltpu.PrefetchScalarGridSpec(
            num_scalar_prefetch=1,
            grid=(pairs,),
            in_specs=[
                pl.BlockSpec((tokens, LANES), lambda i, s: (0, i)),
                pl.BlockSpec((length, LANES), lambda i, s: (0, (i // 2) // 2)),
                pl.BlockSpec((length, LANES), lambda i, s: (0, (KEY_VALUE_HEADS + i // 2) // 2)),
            ],
            out_specs=[
                pl.BlockSpec((tokens, LANES), lambda i, s: (0, i)),
                pl.BlockSpec((tokens, LANES), lambda i, s: (0, i)),
            ],
        ),
        out_shape=[
            jax.ShapeDtypeStruct((tokens, QUERY_COLUMNS), bf16),
            jax.ShapeDtypeStruct((tokens, QUERY_COLUMNS), f32),
        ],
        compiler_params=pltpu.CompilerParams(vmem_limit_bytes=VMEM_LIMIT),
        name="attend_forward",
        cost_estimate=LIGHT,
    )(place, queries, keys_values, keys_values)


def three_parts(values, lane):
    high = values.astype(bf16).astype(f32)
    rest = values - high
    middle = rest.astype(bf16).astype(f32)
    low = rest - middle
    return jnp.where(
        lane == 0, high, jnp.where(lane == 1, middle, jnp.where(lane == 2, low, 0.0))
    )


def attend_backward_kernel(
    first_group, count, place_ref, q_ref, k_ref, v_ref, out_ref, log_ref, grad_ref, dq_ref, dkv_ref, dk_sum, dv_sum
):
    pair_index = pl.program_id(0)
    local = pair_index // 2
    group = first_group + local
    place = place_ref[0]
    tokens = q_ref.shape[0]
    lane = lanes_of((tokens, LANES))
    first = lane < HEAD_SIZE
    inside = lane % HEAD_SIZE
    pair = q_ref[...].astype(f32)
    grad = grad_ref[...].astype(f32)
    delta = pltpu.roll(head_sum(grad * out_ref[...].astype(f32)), HEAD_SIZE, 1)
    logs = three_parts(log_ref[...] * (1.0 / SCORE_EXPONENT), inside)
    deltas = three_parts(delta, inside)
    minus = jnp.where(inside < 3, -1.0, 0.0)

    def sides(own, other):
        return (
            jnp.where(first, own, other).astype(bf16),
            jnp.where(first, other, own).astype(bf16),
        )

    queries = sides(pair, 0.0)
    grads = sides(grad, 0.0)
    def turned(values):
        return jnp.transpose(values.astype(f32)).astype(bf16)

    queries_log = tuple(turned(v) for v in sides(pair, logs))
    grads_delta = tuple(turned(v) for v in sides(grad, deltas))

    @pl.when(pair_index % 2 == 0)
    def _():
        dk_sum[...] = jnp.zeros_like(dk_sum)
        dv_sum[...] = jnp.zeros_like(dv_sum)

    def step(j, dq, diagonal):
        rows = pl.ds(pl.multiple_of(j * tokens, tokens), tokens)
        key_wide = both_halves(k_ref[rows, :], group % 2)
        value_wide = both_halves(v_ref[rows, :], (KEY_VALUE_HEADS + group) % 2)
        keys_turned = jnp.transpose(key_wide)[:HEAD_SIZE].astype(bf16)
        keys_log = sides(key_wide, minus)
        values_delta = sides(value_wide, minus)
        dk = dk_sum[rows, :]
        dv = dv_sum[rows, :]
        parts = list(dq)
        block = tokens // SPLIT
        for sub in range(SPLIT):
            keep = slice(sub * block, (sub + 1) * block)
            dk_part, dv_part = dk[keep], dv[keep]
            start = sub * block if diagonal else 0
            for head in range(2):
                weights = jnp.exp2(
                    dot_nn(keys_log[head][keep], queries_log[head][:, start:]) * SCORE_EXPONENT
                )
                if diagonal:
                    row = lax.broadcasted_iota(jnp.int32, weights.shape, 0)
                    weights = jnp.where(row <= lanes_of(weights.shape), weights, 0.0)
                grad_weights = dot_nn(values_delta[head][keep], grads_delta[head][:, start:])
                grad_scores = (weights * grad_weights).astype(bf16)
                dv_part = dv_part + dot_nn(weights.astype(bf16), grads[head][start:])
                dk_part = dk_part + dot_nn(grad_scores, queries[head][start:])
                term = dot_nn(keys_turned[:, keep], grad_scores)
                if start:
                    term = jnp.concatenate([jnp.zeros((HEAD_SIZE, start), f32), term], axis=1)
                parts[head] = parts[head] + term
            target = pl.ds(pl.multiple_of(j * tokens + sub * block, block), block)
            dk_sum[target, :] = dk_part
            dv_sum[target, :] = dv_part
        return tuple(parts)

    zero = jnp.zeros((HEAD_SIZE, tokens), f32)
    dq = lax.fori_loop(0, place, lambda j, c: step(j, c, False), (zero, zero))
    dq = jnp.transpose(jnp.concatenate(step(place, dq, True), axis=0))
    dq_ref[...] = (dq * HEAD_SIZE**-0.5).astype(bf16)

    @pl.when(pair_index % 2 == 1)
    def _():
        wide_lane = lanes_of(dk_sum.shape)
        for total, slot, factor in (
            (dk_sum, local, HEAD_SIZE**-0.5),
            (dv_sum, count + local, 1.0),
        ):
            both = (total[...] + pltpu.roll(total[...], HEAD_SIZE, 1)) * factor
            columns = pl.ds(pl.multiple_of(slot // 2 * LANES, LANES), LANES)
            mine = wide_lane // HEAD_SIZE == slot % 2
            dkv_ref[:, columns] = jnp.where(
                mine, both, dkv_ref[:, columns].astype(f32)
            ).astype(bf16)


def attend_backward(first, count, place, queries, keys_values, mixed, logs, grad_mixed):
    tokens = queries.shape[0]
    length = keys_values.shape[0]
    group = QUERY_HEADS // KEY_VALUE_HEADS * HEAD_SIZE
    own = pl.BlockSpec((tokens, LANES), lambda i, s: (0, 2 * first + i))
    keys = pl.BlockSpec((length, LANES), lambda i, s: (0, (first + i // 2) // 2))
    values = pl.BlockSpec(
        (length, LANES), lambda i, s: (0, (KEY_VALUE_HEADS + first + i // 2) // 2)
    )
    columns = 2 * count * HEAD_SIZE
    return pl.pallas_call(
        partial(attend_backward_kernel, first, count),
        grid_spec=pltpu.PrefetchScalarGridSpec(
            num_scalar_prefetch=1,
            grid=(2 * count,),
            in_specs=[own, keys, values, own, own, own],
            out_specs=[
                pl.BlockSpec((tokens, LANES), lambda i, s: (0, i)),
                pl.BlockSpec((length, columns), lambda i, s: (0, 0)),
            ],
            scratch_shapes=[pltpu.VMEM((length, LANES), f32), pltpu.VMEM((length, LANES), f32)],
        ),
        out_shape=[
            jax.ShapeDtypeStruct((tokens, count * group), bf16),
            jax.ShapeDtypeStruct((length, columns), bf16),
        ],
        compiler_params=pltpu.CompilerParams(vmem_limit_bytes=VMEM_LIMIT),
        name="attend_backward",
        cost_estimate=LIGHT,
    )(place, queries, keys_values, keys_values, mixed, logs, grad_mixed)


def hidden_kernel(n0_ref, n1_ref, wg_ref, wu_ref, hidden_ref, gate_ref, up_ref, n_all):
    tokens = n0_ref.shape[0]

    @pl.when(pl.program_id(0) == 0)
    def _():
        n_all[:tokens] = n0_ref[...]
        n_all[tokens:] = n1_ref[...]

    gate = dot_nn(n_all[...], wg_ref[...])
    up = dot_nn(n_all[...], wu_ref[...])
    hidden_ref[...] = (gate / (1.0 + jnp.exp(-gate)) * up).astype(bf16)
    gate_ref[...] = gate.astype(bf16)
    up_ref[...] = up.astype(bf16)


def hidden_pass(normed, wgate, wup):
    tokens, width = normed[0].shape
    columns = wgate.shape[1]
    tile = min(256, columns)
    whole = pl.BlockSpec((tokens, width), lambda i: (0, 0))
    down = pl.BlockSpec((width, tile), lambda i: (0, i))
    out = pl.BlockSpec((2 * tokens, tile), lambda i: (0, i))
    return pl.pallas_call(
        hidden_kernel,
        grid=(pl.cdiv(columns, tile),),
        in_specs=[whole] * 2 + [down] * 2,
        out_specs=[out] * 3,
        out_shape=[jax.ShapeDtypeStruct((2 * tokens, columns), bf16)] * 3,
        scratch_shapes=[pltpu.VMEM((2 * tokens, width), bf16)],
        compiler_params=pltpu.CompilerParams(vmem_limit_bytes=VMEM_LIMIT),
        name="hidden_pass",
        cost_estimate=LIGHT,
    )(*normed, wgate, wup)


def gate_kernel(n0_ref, n1_ref, wg_ref, gate_ref):
    tokens = n0_ref.shape[0]
    gate_ref[:tokens] = dot_nn(n0_ref[...], wg_ref[...]).astype(bf16)
    gate_ref[tokens:] = dot_nn(n1_ref[...], wg_ref[...]).astype(bf16)


def gate_pass(normed, wgate):
    tokens, width = normed[0].shape
    columns = wgate.shape[1]
    tile = min(256, columns)
    whole = pl.BlockSpec((tokens, width), lambda i: (0, 0))
    return pl.pallas_call(
        gate_kernel,
        grid=(pl.cdiv(columns, tile),),
        in_specs=[whole] * 2 + [pl.BlockSpec((width, tile), lambda i: (0, i))],
        out_specs=pl.BlockSpec((2 * tokens, tile), lambda i: (0, i)),
        out_shape=jax.ShapeDtypeStruct((2 * tokens, columns), bf16),
        compiler_params=pltpu.CompilerParams(vmem_limit_bytes=VMEM_LIMIT),
        name="gate_pass",
        cost_estimate=LIGHT,
    )(*normed, wgate)


def up_kernel(n0_ref, n1_ref, wu_ref, gate_ref, hidden_ref, up_ref):
    tokens = n0_ref.shape[0]
    for n_ref, rows in ((n0_ref, slice(0, tokens)), (n1_ref, slice(tokens, 2 * tokens))):
        up = dot_nn(n_ref[...], wu_ref[...])
        gate = gate_ref[rows].astype(f32)
        hidden_ref[rows] = (gate / (1.0 + jnp.exp(-gate)) * up).astype(bf16)
        up_ref[rows] = up.astype(bf16)


def up_pass(normed, wup, gate):
    tokens, width = normed[0].shape
    columns = wup.shape[1]
    tile = min(256, columns)
    whole = pl.BlockSpec((tokens, width), lambda i: (0, 0))
    out = pl.BlockSpec((2 * tokens, tile), lambda i: (0, i))
    return pl.pallas_call(
        up_kernel,
        grid=(pl.cdiv(columns, tile),),
        in_specs=[whole] * 2 + [pl.BlockSpec((width, tile), lambda i: (0, i)), out],
        out_specs=[out] * 2,
        out_shape=[jax.ShapeDtypeStruct((2 * tokens, columns), bf16)] * 2,
        compiler_params=pltpu.CompilerParams(vmem_limit_bytes=VMEM_LIMIT),
        name="up_pass",
        cost_estimate=LIGHT,
    )(*normed, wup, gate)


def gates_kernel(g0_ref, g1_ref, wd_ref, gate_ref, up_ref, gate_out_ref, up_out_ref, g_all):
    tokens = g0_ref.shape[0]

    @pl.when(pl.program_id(0) == 0)
    def _():
        g_all[:tokens] = g0_ref[...]
        g_all[tokens:] = g1_ref[...]

    grad = dot_nt(g_all[...], wd_ref[...])
    gate = gate_ref[...].astype(f32)
    up = up_ref[...].astype(f32)
    sigmoid = 1.0 / (1.0 + jnp.exp(-gate))
    gate_out_ref[...] = (grad * up * (sigmoid * (1.0 + gate * (1.0 - sigmoid)))).astype(bf16)
    up_out_ref[...] = (grad * (gate * sigmoid)).astype(bf16)


def gates_pass(grad_top, wdown, gate, up):
    tokens, width = grad_top[0].shape
    columns = gate.shape[1]
    tile = min(256, columns)
    whole = pl.BlockSpec((tokens, width), lambda i: (0, 0))
    out = pl.BlockSpec((2 * tokens, tile), lambda i: (0, i))
    return pl.pallas_call(
        gates_kernel,
        grid=(pl.cdiv(columns, tile),),
        in_specs=[whole] * 2 + [pl.BlockSpec((tile, width), lambda i: (i, 0)), out, out],
        out_specs=[out] * 2,
        out_shape=[jax.ShapeDtypeStruct((2 * tokens, columns), bf16)] * 2,
        scratch_shapes=[pltpu.VMEM((2 * tokens, width), bf16)],
        compiler_params=pltpu.CompilerParams(vmem_limit_bytes=VMEM_LIMIT),
        name="gates_pass",
        cost_estimate=LIGHT,
    )(*grad_top, wdown, gate, up)


def back_kernel(count, transposed, *refs):
    own_ref, send_ref = refs[-2:]
    tokens = own_ref.shape[0]
    dot = dot_nt if transposed else dot_nn

    def total(start):
        rows = pl.ds(start, tokens)
        result = dot(refs[0][rows, :], refs[count][...])
        for i in range(1, count):
            result = result + dot(refs[i][rows, :], refs[count + i][...])
        return result

    own_ref[...] = total(0)
    send_ref[...] = total(tokens).astype(bf16)


def back_pass(lefts, weights, transposed):
    tokens, depth = lefts[0].shape
    width = weights[0].shape[0 if transposed else 1]
    count = len(lefts)
    tile = min(512, width)
    if transposed:
        weight_spec = pl.BlockSpec((tile, depth), lambda i: (i, 0))
    else:
        weight_spec = pl.BlockSpec((depth, tile), lambda i: (0, i))
    out = pl.BlockSpec((tokens // 2, tile), lambda i: (0, i))
    return pl.pallas_call(
        partial(back_kernel, count, transposed),
        grid=(width // tile,),
        in_specs=[pl.BlockSpec((tokens, depth), lambda i: (0, 0))] * count
        + [weight_spec] * count,
        out_specs=[out, out],
        out_shape=[
            jax.ShapeDtypeStruct((tokens // 2, width), f32),
            jax.ShapeDtypeStruct((tokens // 2, width), bf16),
        ],
        compiler_params=pltpu.CompilerParams(vmem_limit_bytes=VMEM_LIMIT),
        name="back_pass",
        cost_estimate=LIGHT,
    )(*lefts, *weights)


def weight_kernel(left_count, *refs):
    lefts, rights, out_ref = refs[:left_count], refs[left_count:-1], refs[-1]
    step = min(lefts[0].shape[0], rights[0].shape[0])

    def piece(refs, start):
        index, offset = divmod(start, refs[0].shape[0])
        return refs[index][pl.ds(offset, step), :]

    total = None
    for start in range(0, left_count * lefts[0].shape[0], step):
        term = dot_tn(piece(lefts, start), piece(rights, start))
        total = term if total is None else total + term
    out_ref[...] = total.astype(bf16)


def weight_pass(lefts, rights):
    rows, columns = lefts[0].shape[1], rights[0].shape[1]
    tile = 512 if rows % 512 == 0 else 384 if rows % 384 == 0 else rows
    return pl.pallas_call(
        partial(weight_kernel, len(lefts)),
        grid=(rows // tile,),
        in_specs=[pl.BlockSpec((left.shape[0], tile), lambda i: (0, i)) for left in lefts]
        + [pl.BlockSpec(right.shape, lambda i: (0, 0)) for right in rights],
        out_specs=pl.BlockSpec((tile, columns), lambda i: (i, 0)),
        out_shape=jax.ShapeDtypeStruct((rows, columns), bf16),
        compiler_params=pltpu.CompilerParams(vmem_limit_bytes=VMEM_LIMIT),
        name="weight_pass",
        cost_estimate=LIGHT,
    )(*lefts, *rights)


def placed_kernel(side_ref, own_ref, other_ref, out_ref):
    mine = pl.program_id(0) == side_ref[0]

    @pl.when(mine)
    def _():
        for g in range(out_ref.shape[1]):
            out_ref[0, g] = own_ref[:, g]

    @pl.when(jnp.logical_not(mine))
    def _():
        for g in range(out_ref.shape[1]):
            out_ref[0, g] = other_ref[:, g]


def placed(own, other, side):
    seq, group, rows, columns = own.shape

    def entry(mine, e, g, s):
        parked = jnp.where(e == 0, 0, group // 2 - 1)
        return (0, jnp.where((e == s[0]) == mine, g, parked), 0, 0)

    return pl.pallas_call(
        placed_kernel,
        grid_spec=pltpu.PrefetchScalarGridSpec(
            num_scalar_prefetch=1,
            grid=(2, group // 2),
            in_specs=[
                pl.BlockSpec((seq, 2, rows, columns), partial(entry, True)),
                pl.BlockSpec((seq, 2, rows, columns), partial(entry, False)),
            ],
            out_specs=pl.BlockSpec(
                (1, 2, seq, rows, columns), lambda e, g, s: (e, g, 0, 0, 0)
            ),
        ),
        out_shape=jax.ShapeDtypeStruct((2, group, seq, rows, columns), own.dtype),
        compiler_params=pltpu.CompilerParams(vmem_limit_bytes=VMEM_LIMIT),
        name="placed",
        cost_estimate=LIGHT,
    )(side.astype(jnp.int32).reshape(1), own, other)


def joined_kernel(side_ref, own_ref, other_ref, out_ref):
    mine = pl.program_id(1) == side_ref[0]

    @pl.when(mine)
    def _():
        out_ref[:, 0] = own_ref[...]

    @pl.when(jnp.logical_not(mine))
    def _():
        out_ref[:, 0] = other_ref[...]


def joined(own, other, side, axis):
    shape = own.shape[:axis] + (2,) + own.shape[axis:]
    columns = own.shape[-1]
    lead = math.prod(own.shape[:axis])
    rows = math.prod(own.shape[axis:-1])
    leads, chunks = lead, 1
    while leads % 2 == 0 and leads * rows * columns > 800_000:
        leads //= 2
    while leads == 1 and rows % (32 * chunks) == 0 and rows // chunks * columns > 800_000:
        chunks *= 2
    block = rows // chunks

    def entry(mine, p, e, i, s):
        parked = jnp.where(e == 0, 0, chunks - 1)
        return (p, jnp.where((e == s[0]) == mine, i, parked), 0)

    return pl.pallas_call(
        joined_kernel,
        grid_spec=pltpu.PrefetchScalarGridSpec(
            num_scalar_prefetch=1,
            grid=(lead // leads, 2, chunks),
            in_specs=[
                pl.BlockSpec((leads, block, columns), partial(entry, True)),
                pl.BlockSpec((leads, block, columns), partial(entry, False)),
            ],
            out_specs=pl.BlockSpec((leads, 1, block, columns), lambda p, e, i, s: (p, e, i, 0)),
        ),
        out_shape=jax.ShapeDtypeStruct((lead, 2, rows, columns), own.dtype),
        compiler_params=pltpu.CompilerParams(vmem_limit_bytes=VMEM_LIMIT),
        name="joined",
        cost_estimate=LIGHT,
    )(
        side.astype(jnp.int32).reshape(1),
        own.reshape(lead, rows, columns),
        other.reshape(lead, rows, columns),
    ).reshape(shape)


def swap(values, bit):
    pairs = [(i, i ^ bit) for i in range(lax.axis_size("rows"))]
    return lax.ppermute(values, "rows", pairs)


def bit_of(bit):
    return (lax.axis_index("rows") // bit) % 2


def gather_bit(values, bit, axis):
    return joined(values, swap(values, bit), bit_of(bit), axis)


def part(values, index, axis):
    return lax.dynamic_index_in_dim(values, index, axis, keepdims=False)


def reduce_bit(values, bit, axis):
    return add_bit(values, pass_bit(values, bit, axis), bit, axis)


def outer_pairs(step, low, high):
    size = lax.axis_size("rows")
    return [
        (i, i + 4 * step)
        for i in range(size)
        if low <= i // 4 < high and 0 <= i // 4 + step < size // 4
    ]


def send_outer(values):
    count = lax.axis_size("rows") // 4
    if count == 2:
        return (swap(values, 4),)
    up, down = values, values
    ups, downs = [], []
    for t in range(1, count):
        up = lax.ppermute(up, "rows", outer_pairs(1, t - 1, count))
        down = lax.ppermute(down, "rows", outer_pairs(-1, 0, count - t + 1))
        ups.append(up)
        downs.append(down)
    return tuple(ups[::-1] + downs)


def join_outer(values, received, axis):
    count = lax.axis_size("rows") // 4
    if count == 2:
        return joined(values, received[0], bit_of(4), axis)
    place = lax.axis_index("rows") // 4
    line = jnp.stack([*received[: count - 1], values, *received[count - 1 :]], axis)
    return lax.dynamic_slice_in_dim(line, count - 1 - place, count, axis)


def gather_outer(values, axis):
    return join_outer(values, send_outer(values), axis)


def pass_outer(values, axis):
    count = lax.axis_size("rows") // 4
    place = lax.axis_index("rows") // 4

    def entry(index):
        return part(values, jnp.clip(index, 0, count - 1), axis)

    if count == 1:
        return ()
    if count == 2:
        return (swap(entry(1 - place), 4),)
    up, down = entry(place + count - 1), entry(place - count + 1)
    for t in range(1, count):
        up = lax.ppermute(up, "rows", outer_pairs(1, 0, t))
        down = lax.ppermute(down, "rows", outer_pairs(-1, count - t, count))
        if t < count - 1:
            up = (entry(place + count - 1 - t).astype(f32) + up.astype(f32)).astype(bf16)
            down = (entry(place - count + 1 + t).astype(f32) + down.astype(f32)).astype(bf16)
    return (up, down)


def add_outer(values, received, axis):
    total = part(values, lax.axis_index("rows") // 4, axis).astype(f32)
    for term in received:
        total = total + term.astype(f32)
    return total.astype(bf16)


def reduce_outer(values, axis):
    return add_outer(values, pass_outer(values, axis), axis)


def pass_bit(values, bit, axis):
    return swap(part(values, 1 - bit_of(bit), axis), bit)


def add_bit(values, received, bit, axis):
    own = part(values, bit_of(bit), axis)
    return (own.astype(f32) + received.astype(f32)).astype(bf16)


def gather_seq(values):
    return lax.all_gather(values, "seq", axis=0, tiled=False)


def reduce_seq(values):
    return lax.psum_scatter(values, "seq", scatter_dimension=0, tiled=False)


def exchange(values, axis, bit):
    size = lax.axis_size(axis)
    return lax.ppermute(values, axis, [(i, i ^ bit) for i in range(size)])


def across_group(own, send):
    return (own + swap(send, 1).astype(f32)).astype(bf16)


def stage(*values):
    return lax.optimization_barrier(values)


def mm(left, right):
    return jnp.einsum("ab,bc->ac", left, right, preferred_element_type=f32)


def mm_t(left, right):
    return jnp.einsum("ab,cb->ac", left, right, preferred_element_type=f32)


def t_mm(left, right):
    return jnp.einsum("ab,ac->bc", left, right, preferred_element_type=f32)


def norm_scale(values):
    return lax.rsqrt(jnp.mean(values * values, axis=-1, keepdims=True) + EPSILON)


def norm_backward(values, scale, gain, grad):
    gained = grad * gain
    inner = jnp.mean(values * gained, axis=-1, keepdims=True)
    result = scale * gained - values * (scale * scale * scale) * inner
    return result, jnp.sum(grad * values * scale, axis=0)


def shards(
    tokens_in,
    corpus,
    corpus_weight,
    w_qkv,
    w_out,
    w_gate,
    w_up,
    w_down,
    attn_gain,
    ffn_gain,
    q_gain,
    k_gain,
    upstream,
):
    shard_length, width = tokens_in.shape[1:]
    row_devices = lax.axis_size("rows")
    seq_devices = lax.axis_size("seq")
    outer = row_devices // 4
    d_rows = w_qkv.shape[0]
    f_rows = w_down.shape[0]
    place = lax.axis_index("seq").astype(jnp.int32)
    inputs = tokens_in[0].astype(f32)

    extra = jnp.stack(
        [
            attn_gain,
            ffn_gain,
            jnp.broadcast_to(corpus.astype(bf16), attn_gain.shape),
        ],
        axis=1,
    )
    extra = jnp.pad(extra, ((0, 0), (0, LANES - extra.shape[1])))
    kv_shard = jnp.concatenate([w_qkv[:, QUERY_COLUMNS:], extra], axis=1)
    query_shard = jnp.concatenate([w_qkv[:, :QUERY_COLUMNS], w_out.T], axis=1)
    query_shard, w_gate, w_up = stage(query_shard, w_gate, w_up)
    query_lines = gather_seq(query_shard)

    def to_group(weight):
        blocks = weight.reshape(d_rows, outer, 4, seq_devices, f_rows)
        blocks = jnp.transpose(blocks, (2, 0, 3, 1, 4))
        return blocks.reshape(2, 2, d_rows, outer * seq_devices * f_rows)

    def spread_hidden(lines, received):
        if outer == 2:
            lines = lines.reshape(seq_devices, 4, d_rows, hidden_columns)
            other = received[0].reshape(lines.shape)
            return placed(lines, other, bit_of(4)).reshape(width, hidden_columns)
        full = join_outer(lines, received, 0)
        return jnp.moveaxis(full, 1, 3).reshape(width, hidden_columns)

    gate_up = jnp.stack([to_group(w_gate), to_group(w_up)], axis=2)
    hidden_columns = gate_up.shape[-1]
    core, near = bit_of(1), bit_of(2)
    gate_up = joined(
        part(gate_up, core, 1), swap(part(gate_up, 1 - core, 1), 1), core, 1
    )
    gate_up, kv_shard = stage(gate_up, kv_shard)
    other, kv_lines, query_lines = stage(
        swap(part(gate_up, 1 - near, 0), 2), gather_seq(kv_shard), query_lines
    )
    gate_up = joined(part(gate_up, near, 0), other, near, 0)
    gate_lines = gather_seq(gate_up[:, :, 0])
    left, right = kv_lines[..., : 3 * LANES], kv_lines[..., 3 * LANES :]
    left_other, right_other = stage(send_outer(left), swap(right, 2))
    left = join_outer(left, left_other, 0)
    right = joined(right, right_other, near, 0)
    left_other, right_other = stage(swap(left, 2), send_outer(right))
    left = joined(left, left_other, near, 1)
    right = join_outer(right, right_other, 0)
    q_left, q_right = query_lines[..., :QUERY_COLUMNS], query_lines[..., QUERY_COLUMNS:]
    q_left, q_right, left, right = stage(q_left, q_right, left, right)
    q_left_other, q_right_other = send_outer(q_left), swap(q_right, 2)
    left, right = gather_bit(left, 1, 2), gather_bit(right, 1, 2)
    left, right = left.reshape(width, -1), right.reshape(width, -1)
    wkv = jnp.concatenate([left, right[:, : 2 * LANES]], axis=1)
    rows = dot_nt(jnp.eye(8, LANES, dtype=bf16), right[:, 2 * LANES :])
    attn_gain_full, ffn_gain_full, corpus_full = rows[0:1], rows[1:2], rows[2]

    position = (place * shard_length + jnp.arange(shard_length, dtype=jnp.int32)).astype(f32)
    half = HEAD_SIZE // 2
    exponent = jnp.arange(half, dtype=f32) * (-2.0 / HEAD_SIZE)
    angles = position[:, None] * jnp.power(ROPE_BASE, exponent)[None, :]
    cosine, sine = jnp.cos(angles), jnp.sin(angles)
    cos_table = jnp.concatenate([cosine] * 4, axis=1)
    sin_table = jnp.concatenate([-sine, sine] * 2, axis=1)
    wide_q = jnp.tile(q_gain.astype(f32), QUERY_HEADS)
    wide_k = jnp.concatenate(
        [jnp.tile(k_gain.astype(f32), KEY_VALUE_HEADS), jnp.ones((KEY_COLUMNS,), f32)]
    )
    wide_q = jnp.broadcast_to(wide_q[None, :], (8, QUERY_COLUMNS))
    wide_k = jnp.broadcast_to(wide_k[None, :], (8, 2 * KEY_COLUMNS))

    in_scale = norm_scale(inputs)
    normed = (inputs * in_scale * attn_gain_full).astype(bf16)
    joint_kv, own_kv = heads_forward(
        normed, wkv, wide_k, cos_table, sin_table, KEY_COLUMNS
    )
    own_kv, q_left_other, q_right_other, up_in = stage(
        own_kv, q_left_other, q_right_other, gate_up[:, :, 1]
    )
    up_lines = gather_seq(up_in)
    keys_values = gather_seq(own_kv).reshape(-1, 2 * KEY_COLUMNS)
    q_left = join_outer(q_left, q_left_other, 0)
    q_right = joined(q_right, q_right_other, near, 0)
    left_other, right_other, gate_lines, w_down = stage(
        swap(q_left, 2), send_outer(q_right), gate_lines, w_down
    )
    q_left = joined(q_left, left_other, near, 1)
    gate_other = send_outer(gate_lines)
    down_other = send_outer(w_down)
    half_rows = (2 * outer, seq_devices * d_rows, QUERY_COLUMNS)
    q_left_other = swap(q_left, 1)

    corpora = jnp.arange(CORPORA, dtype=jnp.int32)
    per_device = corpus_full.reshape(-1, d_rows)[:, 0].astype(jnp.int32)
    counts = (
        jnp.sum((per_device[:, None] == corpora[None, :]).astype(f32), axis=0) * shard_length
    )
    own_corpus = (corpus[0] == corpora).astype(f32)
    weight_row = jnp.sum(own_corpus * corpus_weight.astype(f32))
    count_row = jnp.sum(own_corpus * counts)
    factor = weight_row / DENOM * (jnp.sum(counts) / (CORPORA * count_row))
    grad_full = upstream[0].astype(f32) * factor
    grad_top, q_left, q_left_other = stage(grad_full.astype(bf16), q_left, q_left_other)

    q_halves = (q_left.reshape(half_rows), q_left_other.reshape(half_rows))
    joint_q, queries = heads_forward_halves(
        normed, *q_halves, core, wide_q, cos_table, sin_table
    )
    queries, q_right, right_other, down_other = stage(queries, q_right, right_other, down_other)
    q_right = join_outer(q_right, right_other, 0)
    down_pair = join_outer(w_down, down_other, 0)
    place_array = place.reshape(1)
    keys_values, queries, down_in = stage(keys_values, queries, down_pair)
    down_lines = gather_seq(down_in)
    mixed, logs = attend_forward(place_array, queries, keys_values)
    mixed, grad_top1, grad_top2, up_lines, wout_other = stage(
        mixed, swap(grad_top, 1), swap(grad_top, 2), up_lines, swap(q_right, 1)
    )
    middle = project(
        mixed, q_right.reshape(half_rows), wout_other.reshape(half_rows), tokens_in[0], core
    )

    ffn_scale = norm_scale(middle)
    normed_ffn = (middle * ffn_scale * ffn_gain_full).astype(bf16)
    up_other = send_outer(up_lines)
    normed_ffn, gate_other, q_right, wout_other, q_left, q_left_other = stage(
        normed_ffn, gate_other, q_right, wout_other, q_left, q_left_other
    )
    normed1 = swap(normed_ffn, 1)
    wgate = spread_hidden(gate_lines, gate_other)
    gate_near, normed2, up_other, wout_t, wq = stage(
        gate_pass((normed_ffn, normed1), wgate),
        swap(normed_ffn, 2),
        up_other,
        joined(q_right, wout_other, core, 2),
        joined(q_left, q_left_other, core, 2),
    )
    wout_t, wq = wout_t.reshape(width, -1), wq.reshape(width, -1)
    wup = spread_hidden(up_lines, up_other)
    hidden_near, up_near = up_pass((normed_ffn, normed1), wup, gate_near)
    normed3, hidden_near, grad_top3 = stage(
        swap(normed2, 1), hidden_near, swap(grad_top2, 1)
    )
    hidden_far, gate_far, up_far = hidden_pass((normed2, normed3), wgate, wup)
    normed4 = (normed_ffn, normed1, normed2, normed3)
    grad_top4 = (grad_top, grad_top1, grad_top2, grad_top3)
    wdown = down_lines.reshape(hidden_columns, width)
    gate_far, up_far = gates_pass((grad_top2, grad_top3), wdown, gate_far, up_far)
    own, send = back_pass((gate_far, up_far), (wgate, wup), True)
    grad_wdown = weight_pass((hidden_near, hidden_far), grad_top4)
    own, send, grad_wdown, wdown = stage(own, swap(send, 1), grad_wdown, wdown)
    across = (own + send.astype(f32)).astype(bf16)
    across, wdown = stage(across, wdown)
    gate_near, up_near = gates_pass((grad_top, grad_top1), wdown, gate_near, up_near)
    own, send = back_pass((gate_near, up_near), (wgate, wup), True)
    hidden_shape = (outer, 2, 2, seq_devices, d_rows, hidden_columns)
    grad_wdown = grad_wdown.reshape(seq_devices, outer, f_rows, width)
    grad_wgate = weight_pass(normed4, (gate_near, gate_far)).reshape(hidden_shape)
    across, own, send, grad_wgate, up_near = stage(
        swap(across, 2), own, send, grad_wgate, up_near
    )
    grad_wup = weight_pass(normed4, (up_near, up_far)).reshape(hidden_shape)
    send, grad_wup, down_other = stage(swap(send, 1), grad_wup, pass_outer(grad_wdown, 1))
    grad_wdown = add_outer(grad_wdown, down_other, 1)
    own = own + send.astype(f32)
    grad_normed_ffn = own + across.astype(f32)
    grad_wdown = reduce_seq(grad_wdown)

    grad_middle_part, grad_ffn_gain = norm_backward(
        middle, ffn_scale, ffn_gain_full, grad_normed_ffn
    )
    grad_middle = grad_full + grad_middle_part
    grad_branch = grad_middle.astype(bf16)
    grad_mixed = mm(grad_branch, wout_t).astype(bf16)
    attend = (place_array, queries, keys_values, mixed, logs)
    grad_q1, grad_kv1 = attend_backward(0, 2, *attend, grad_mixed)
    gate_other = pass_outer(grad_wgate, 0)
    grad_q1, grad_kv1, grad_mixed, grad_wdown, hidden_far = stage(
        grad_q1, grad_kv1, grad_mixed, grad_wdown, hidden_far
    )
    grad_kv1 = reduce_seq(grad_kv1.reshape(seq_devices, shard_length, -1))
    shape = (outer, 2, 2, seq_devices, d_rows)
    own_far, send_far = back_pass((hidden_far,), (wdown,), False)
    grad_wout, far_other, gate_other, grad_mixed = stage(
        t_mm(grad_branch, mixed).astype(bf16).reshape(*shape, QUERY_COLUMNS),
        swap(send_far, 1),
        gate_other,
        grad_mixed,
    )
    grad_gate = reduce_seq(jnp.moveaxis(add_outer(grad_wgate, gate_other, 0), 2, 0))
    across = (own_far + far_other.astype(f32)).astype(bf16)
    across, grad_mixed = stage(across, grad_mixed)
    grad_q2, grad_kv2 = attend_backward(2, 3, *attend, grad_mixed)
    grad_q2, grad_kv2, hidden_near, grad_kv1, grad_gate, wout_other, up_other, across = stage(
        grad_q2,
        grad_kv2,
        hidden_near,
        grad_kv1,
        grad_gate,
        pass_bit(grad_wout, 1, 2),
        pass_outer(grad_wup, 0),
        swap(across, 2),
    )
    grad_kv2 = reduce_seq(grad_kv2.reshape(seq_devices, shard_length, -1))

    grad_q = jnp.concatenate([grad_q1, grad_q2], axis=1)
    joint_grad_q, gain_q = heads_backward(
        grad_q, joint_q, wide_q, cos_table, sin_table, QUERY_COLUMNS
    )
    grad_wq = t_mm(normed, joint_grad_q).astype(bf16).reshape(*shape, QUERY_COLUMNS)
    grad_wout = add_bit(grad_wout, wout_other, 1, 2)
    grad_up = jnp.moveaxis(add_outer(grad_wup, up_other, 0), 2, 0)
    grad_wq = reduce_bit(grad_wq, 1, 2)
    wq_other, wout_other = pass_bit(grad_wq, 2, 1), pass_outer(grad_wout, 0)
    grad_kv2, grad_normed, grad_up = stage(grad_kv2, mm_t(joint_grad_q, wq), grad_up)
    grad_up = reduce_seq(grad_up)

    grad_kv1, grad_kv2 = (
        part_.reshape(shard_length, 2, -1) for part_ in (grad_kv1, grad_kv2)
    )
    grad_kv = jnp.concatenate([grad_kv1, grad_kv2], axis=2).reshape(shard_length, -1)
    joint_grad_kv, gain_k = heads_backward(
        grad_kv, joint_kv, wide_k, cos_table, sin_table, KEY_COLUMNS
    )
    joint_grad_kv, wq_other, wout_other = stage(joint_grad_kv, wq_other, wout_other)
    grad_wkv = t_mm(normed, joint_grad_kv).astype(bf16)
    grad_normed = grad_normed + mm_t(joint_grad_kv, wkv)
    grad_input_part, grad_attn_gain = norm_backward(
        inputs, in_scale, attn_gain_full, grad_normed
    )
    input_grad = (grad_middle + grad_input_part).astype(bf16)

    gain_rows = jnp.stack([grad_attn_gain, grad_ffn_gain]).astype(bf16)
    gain_columns = t_mm(gain_rows, jnp.eye(2, LANES, dtype=bf16)).astype(bf16)
    grad_wkv, gain_columns, hidden_near = stage(grad_wkv, gain_columns, hidden_near)
    own_near, send_near = back_pass((hidden_near,), (wdown,), False)
    grad_wq = add_bit(grad_wq, wq_other, 2, 1)
    grad_wout = add_outer(grad_wout, wout_other, 0)
    wq_other, wout_other = pass_outer(grad_wq, 0), pass_bit(grad_wout, 2, 0)
    left = grad_wkv[:, : 3 * LANES].reshape(*shape, -1)
    right = jnp.concatenate([grad_wkv[:, 3 * LANES :], gain_columns], axis=1)
    right = right.reshape(*shape, -1)
    head_gains = jnp.concatenate(
        [
            jnp.sum(gain_q[0].reshape(-1, HEAD_SIZE), axis=0),
            jnp.sum(gain_k[0, :KEY_COLUMNS].reshape(-1, HEAD_SIZE), axis=0),
        ]
    )[None]
    left, right, left_other, right_other, gains_other = stage(
        left,
        right,
        pass_bit(left, 1, 2),
        pass_bit(right, 1, 2),
        exchange(head_gains, "rows", 1),
    )
    head_gains = head_gains + gains_other
    left = add_bit(left, left_other, 1, 2)
    right = add_bit(right, right_other, 1, 2)
    left_other, right_other, wq_other, wout_other, gains_other, grad_up = stage(
        pass_bit(left, 2, 1),
        pass_outer(right, 0),
        wq_other,
        wout_other,
        exchange(head_gains, "seq", 1),
        grad_up,
    )
    head_gains = head_gains + gains_other
    left = add_bit(left, left_other, 2, 1)
    right = add_outer(right, right_other, 0)
    left_other, right_other, gains_other, near_other = stage(
        pass_outer(left, 0),
        pass_bit(right, 2, 0),
        exchange(head_gains, "rows", 2),
        swap(send_near, 1),
    )
    output = (middle + own_near + near_other.astype(f32) + across.astype(f32)).astype(bf16)
    head_gains = head_gains + gains_other
    sums = reduce_seq(
        jnp.concatenate(
            [
                add_outer(grad_wq, wq_other, 0),
                add_outer(left, left_other, 0),
                add_bit(right, right_other, 2, 0),
                add_bit(grad_wout, wout_other, 2, 0),
            ],
            axis=-1,
        )
    )
    rest = [("rows", bit) for bit in (4, 8, 16) if bit < row_devices]
    rest += [("seq", bit) for bit in (2, 4, 8) if bit < seq_devices]
    gate_up = jnp.stack([grad_gate, grad_up], axis=2)
    other, gains_other = stage(
        swap(part(gate_up, 1 - near, 0), 2), exchange(head_gains, *rest[0])
    )
    head_gains = head_gains + gains_other
    grads = joined(part(gate_up, near, 0), other, near, 0)
    for axis, bit in rest[1:]:
        head_gains = head_gains + exchange(head_gains, axis, bit)
    head_gains = head_gains[0]
    grads = joined(part(grads, core, 1), swap(part(grads, 1 - core, 1), 1), core, 1)

    def from_group(blocks):
        blocks = blocks.reshape(4, d_rows, seq_devices, outer, f_rows)
        return jnp.transpose(blocks, (1, 3, 0, 2, 4)).reshape(d_rows, -1)

    grad_wgate, grad_wup = stage(from_group(grads[:, :, 0]), from_group(grads[:, :, 1]))
    sums, grad_wgate, grad_wup, grad_wdown, output, input_grad = stage(
        sums, grad_wgate.astype(f32), grad_wup.astype(f32), grad_wdown.astype(f32), output, input_grad
    )
    columns = QUERY_COLUMNS + 2 * KEY_COLUMNS
    long_gains = sums[:, columns : columns + 2].astype(f32)
    return (
        output[None],
        input_grad[None],
        sums[:, :columns].astype(f32),
        sums[:, columns + LANES :].T.astype(f32),
        grad_wgate,
        grad_wup,
        grad_wdown,
        long_gains[:, 0],
        long_gains[:, 1],
        head_gains[:HEAD_SIZE],
        head_gains[HEAD_SIZE:],
    )


def solution(mesh):
    return jax.shard_map(
        shards,
        mesh=mesh,
        in_specs=(
            P("rows", "seq", None),
            P("rows"),
            P(),
            P(("rows", "seq"), None),
            P(None, ("rows", "seq")),
            P(("rows", "seq"), None),
            P(("rows", "seq"), None),
            P(("rows", "seq"), None),
            P(("rows", "seq")),
            P(("rows", "seq")),
            P(),
            P(),
            P("rows", "seq", None),
        ),
        out_specs=(
            P("rows", "seq", None),
            P("rows", "seq", None),
            P(("rows", "seq"), None),
            P(None, ("rows", "seq")),
            P(("rows", "seq"), None),
            P(("rows", "seq"), None),
            P(("rows", "seq"), None),
            P(("rows", "seq")),
            P(("rows", "seq")),
            P(),
            P(),
        ),
        check_vma=False,
    )
```

```python
import math
from functools import partial

import jax
import jax.numpy as jnp
from jax import lax
from jax.experimental import pallas as pl
from jax.experimental.pallas import tpu as pltpu
from jax.sharding import PartitionSpec as P

QUERY_HEADS = 20
KEY_VALUE_HEADS = 5
HEAD_SIZE = 64
CORPORA = 8
DENOM = 64
EPSILON = 1e-06
ROPE_BASE = 10000.0
QUERY_COLUMNS = QUERY_HEADS * HEAD_SIZE
KEY_COLUMNS = KEY_VALUE_HEADS * HEAD_SIZE
LANES = 128
SCORE_EXPONENT = 1.4426950408889634 * HEAD_SIZE**-0.5
SPLIT = 2
VMEM_LIMIT = 48 * 1024 * 1024

f32, bf16 = jnp.float32, jnp.bfloat16
LIGHT = pl.CostEstimate(flops=1000, bytes_accessed=1000, transcendentals=0)


def dot_nn(a, b):
    return lax.dot_general(a, b, (((1,), (0,)), ((), ())), preferred_element_type=f32)


def dot_nt(a, b):
    return lax.dot_general(a, b, (((1,), (1,)), ((), ())), preferred_element_type=f32)


def dot_tn(a, b):
    return lax.dot_general(a, b, (((0,), (0,)), ((), ())), preferred_element_type=f32)


def lanes_of(shape):
    return lax.broadcasted_iota(jnp.int32, shape, len(shape) - 1)


def head_sum(values):
    row = lax.broadcasted_iota(jnp.int32, (LANES, LANES), 0) // HEAD_SIZE
    column = lax.broadcasted_iota(jnp.int32, (LANES, LANES), 1) // HEAD_SIZE
    ones = jnp.where(row == column, 1.0, 0.0).astype(bf16)
    high = values.astype(bf16)
    low = (values - high.astype(f32)).astype(bf16)
    return dot_nn(high, ones) + dot_nn(low, ones)


def partner(values):
    first = lanes_of(values.shape) % HEAD_SIZE < HEAD_SIZE // 2
    return jnp.where(
        first,
        pltpu.roll(values, LANES - HEAD_SIZE // 2, 1),
        pltpu.roll(values, HEAD_SIZE // 2, 1),
    )


def heads_of(joint, norm_columns, gain_ref, cos_ref, sin_ref, out_ref):
    columns = joint.shape[1]
    for start in range(0, columns, LANES):
        chunk = slice(start, start + LANES)
        values = joint[:, chunk]
        scale = lax.rsqrt(head_sum(values * values) * (1.0 / HEAD_SIZE) + EPSILON)
        normed = values * scale * gain_ref[0:1, chunk]
        turned = normed * cos_ref[...] + partner(normed) * sin_ref[...]
        place = pl.program_id(0) * columns + start + lanes_of(values.shape)
        out_ref[:, chunk] = jnp.where(place < norm_columns, turned, values).astype(bf16)


def heads_forward_kernel(
    norm_columns, normed_ref, weight_ref, gain_ref, cos_ref, sin_ref, joint_ref, out_ref
):
    joint = dot_nn(normed_ref[...], weight_ref[...])
    joint_ref[...] = joint
    heads_of(joint, norm_columns, gain_ref, cos_ref, sin_ref, out_ref)


def heads_halves_kernel(
    side_ref, normed_ref, own_ref, other_ref, gain_ref, cos_ref, sin_ref, joint_ref, out_ref
):
    count, block, _ = own_ref.shape
    joint = None
    for index in range(count):
        for weight_ref, side in ((own_ref, side_ref[0]), (other_ref, 1 - side_ref[0])):
            rows = pl.ds(pl.multiple_of((2 * index + side) * block, block), block)
            term = dot_nn(normed_ref[:, rows], weight_ref[index])
            joint = term if joint is None else joint + term
    joint_ref[...] = joint
    heads_of(joint, QUERY_COLUMNS, gain_ref, cos_ref, sin_ref, out_ref)


def heads_forward_halves(normed, own, other, side, gain, cos, sin):
    tokens, width = normed.shape
    count, block, columns = own.shape
    tile = 2 * LANES
    out = pl.BlockSpec((tokens, tile), lambda i, s: (0, i))
    table = pl.BlockSpec((tokens, LANES), lambda i, s: (0, 0))
    weight = pl.BlockSpec((count, block, tile), lambda i, s: (0, 0, i))
    return pl.pallas_call(
        heads_halves_kernel,
        grid_spec=pltpu.PrefetchScalarGridSpec(
            num_scalar_prefetch=1,
            grid=(columns // tile,),
            in_specs=[
                pl.BlockSpec((tokens, width), lambda i, s: (0, 0)),
                weight,
                weight,
                pl.BlockSpec((8, tile), lambda i, s: (0, i)),
                table,
                table,
            ],
            out_specs=[out, out],
        ),
        out_shape=[
            jax.ShapeDtypeStruct((tokens, columns), f32),
            jax.ShapeDtypeStruct((tokens, columns), bf16),
        ],
        compiler_params=pltpu.CompilerParams(vmem_limit_bytes=VMEM_LIMIT),
        name="heads_forward_halves",
        cost_estimate=LIGHT,
    )(side.astype(jnp.int32).reshape(1), normed, own, other, gain, cos, sin)


def heads_forward(normed, weight, gain, cos, sin, norm_columns):
    tokens, width = normed.shape
    columns = weight.shape[1]
    tile = 2 * LANES if columns % (2 * LANES) == 0 else LANES
    out = pl.BlockSpec((tokens, tile), lambda i: (0, i))
    table = pl.BlockSpec((tokens, LANES), lambda i: (0, 0))
    return pl.pallas_call(
        partial(heads_forward_kernel, norm_columns),
        grid=(columns // tile,),
        in_specs=[
            pl.BlockSpec((tokens, width), lambda i: (0, 0)),
            pl.BlockSpec((width, tile), lambda i: (0, i)),
            pl.BlockSpec((8, tile), lambda i: (0, i)),
            table,
            table,
        ],
        out_specs=[out, out],
        out_shape=[
            jax.ShapeDtypeStruct((tokens, columns), f32),
            jax.ShapeDtypeStruct((tokens, columns), bf16),
        ],
        compiler_params=pltpu.CompilerParams(vmem_limit_bytes=VMEM_LIMIT),
        name="heads_forward",
        cost_estimate=LIGHT,
    )(normed, weight, gain, cos, sin)


def project_kernel(side_ref, mixed_ref, own_ref, other_ref, inputs_ref, out_ref):
    block = own_ref.shape[1]
    for weight_ref, side in ((own_ref, side_ref[0]), (other_ref, 1 - side_ref[0])):
        columns = pl.ds(pl.multiple_of(side * block, block), block)
        out_ref[:, columns] = inputs_ref[:, columns].astype(f32) + dot_nt(
            mixed_ref[...], weight_ref[0]
        )


def project(mixed, own, other, inputs, side):
    tokens, depth = mixed.shape
    count, block, _ = own.shape
    weight = pl.BlockSpec((1, block, depth), lambda i, s: (i, 0, 0))
    out = pl.BlockSpec((tokens, 2 * block), lambda i, s: (0, i))
    return pl.pallas_call(
        project_kernel,
        grid_spec=pltpu.PrefetchScalarGridSpec(
            num_scalar_prefetch=1,
            grid=(count,),
            in_specs=[pl.BlockSpec((tokens, depth), lambda i, s: (0, 0)), weight, weight, out],
            out_specs=out,
        ),
        out_shape=jax.ShapeDtypeStruct((tokens, 2 * count * block), f32),
        compiler_params=pltpu.CompilerParams(vmem_limit_bytes=VMEM_LIMIT),
        name="project",
        cost_estimate=LIGHT,
    )(side.astype(jnp.int32).reshape(1), mixed, own, other, inputs)


def heads_backward_kernel(
    norm_columns, grad_ref, joint_ref, gain_ref, cos_ref, sin_ref, out_ref, gain_out_ref
):
    grad = grad_ref[...].astype(f32)
    values = joint_ref[...]
    gain = gain_ref[0:1, :]
    turned = grad * cos_ref[...] - partner(grad) * sin_ref[...]
    scale = lax.rsqrt(head_sum(values * values) * (1.0 / HEAD_SIZE) + EPSILON)
    gained = turned * gain
    inner = head_sum(values * gained) * (1.0 / HEAD_SIZE)
    result = scale * gained - values * (scale * scale * scale) * inner
    place = pl.program_id(0) * LANES + lanes_of(values.shape)
    out_ref[...] = jnp.where(place < norm_columns, result, grad).astype(bf16)
    gain_out_ref[...] = jnp.broadcast_to(
        jnp.sum(turned * values * scale, axis=0, keepdims=True), gain_out_ref.shape
    )


def heads_backward(grad, joint, gain, cos, sin, norm_columns):
    tokens, columns = joint.shape
    return pl.pallas_call(
        partial(heads_backward_kernel, norm_columns),
        grid=(columns // LANES,),
        in_specs=[
            pl.BlockSpec((tokens, LANES), lambda i: (0, i)),
            pl.BlockSpec((tokens, LANES), lambda i: (0, i)),
            pl.BlockSpec((8, LANES), lambda i: (0, i)),
            pl.BlockSpec((tokens, LANES), lambda i: (0, 0)),
            pl.BlockSpec((tokens, LANES), lambda i: (0, 0)),
        ],
        out_specs=[
            pl.BlockSpec((tokens, LANES), lambda i: (0, i)),
            pl.BlockSpec((8, LANES), lambda i: (0, i)),
        ],
        out_shape=[
            jax.ShapeDtypeStruct((tokens, columns), bf16),
            jax.ShapeDtypeStruct((8, columns), f32),
        ],
        name="heads_backward",
        cost_estimate=LIGHT,
    )(grad, joint, gain, cos, sin)


def both_halves(pair, odd):
    wide = pair.astype(f32)
    first = lanes_of(wide.shape) < HEAD_SIZE
    keep = jnp.where(odd == 1, jnp.where(first, 0, 1), jnp.where(first, 1, 0)) == 1
    return jnp.where(keep, wide, pltpu.roll(wide, HEAD_SIZE, 1))


def attend_forward_kernel(place_ref, q_ref, k_ref, v_ref, out_ref, log_ref):
    group = pl.program_id(0) // 2
    place = place_ref[0]
    tokens = q_ref.shape[0]
    first = lanes_of((tokens, LANES)) < HEAD_SIZE
    pair = q_ref[...].astype(f32)
    queries = (jnp.where(first, pair, 0.0).astype(bf16), jnp.where(first, 0.0, pair).astype(bf16))

    def step(j, totals, diagonal):
        rows = pl.ds(pl.multiple_of(j * tokens, tokens), tokens)
        keys = both_halves(k_ref[rows, :], group % 2).astype(bf16)
        values = both_halves(v_ref[rows, :], (KEY_VALUE_HEADS + group) % 2)
        sides = (
            jnp.where(first, values, 1.0).astype(bf16),
            jnp.where(first, 1.0, values).astype(bf16),
        )
        result = []
        for head in range(2):
            weights = jnp.exp2(dot_nt(queries[head], keys) * SCORE_EXPONENT)
            if diagonal:
                row = lax.broadcasted_iota(jnp.int32, weights.shape, 0)
                weights = jnp.where(lanes_of(weights.shape) <= row, weights, 0.0)
            result.append(totals[head] + dot_nn(weights.astype(bf16), sides[head]))
        return tuple(result)

    zero = jnp.zeros((tokens, LANES), f32)
    totals = lax.fori_loop(0, place, lambda j, c: step(j, c, False), (zero, zero))
    totals = step(place, totals, True)
    numerator = jnp.where(first, totals[0], totals[1])
    swapped = jnp.where(first, totals[1], totals[0])
    out_ref[...] = (numerator / pltpu.roll(swapped, HEAD_SIZE, 1)).astype(bf16)
    log_ref[...] = jnp.log2(swapped)


def attend_forward(place, queries, keys_values):
    tokens = queries.shape[0]
    length = keys_values.shape[0]
    pairs = QUERY_COLUMNS // LANES
    return pl.pallas_call(
        attend_forward_kernel,
        grid_spec=pltpu.PrefetchScalarGridSpec(
            num_scalar_prefetch=1,
            grid=(pairs,),
            in_specs=[
                pl.BlockSpec((tokens, LANES), lambda i, s: (0, i)),
                pl.BlockSpec((length, LANES), lambda i, s: (0, (i // 2) // 2)),
                pl.BlockSpec((length, LANES), lambda i, s: (0, (KEY_VALUE_HEADS + i // 2) // 2)),
            ],
            out_specs=[
                pl.BlockSpec((tokens, LANES), lambda i, s: (0, i)),
                pl.BlockSpec((tokens, LANES), lambda i, s: (0, i)),
            ],
        ),
        out_shape=[
            jax.ShapeDtypeStruct((tokens, QUERY_COLUMNS), bf16),
            jax.ShapeDtypeStruct((tokens, QUERY_COLUMNS), f32),
        ],
        compiler_params=pltpu.CompilerParams(vmem_limit_bytes=VMEM_LIMIT),
        name="attend_forward",
        cost_estimate=LIGHT,
    )(place, queries, keys_values, keys_values)


def three_parts(values, lane):
    high = values.astype(bf16).astype(f32)
    rest = values - high
    middle = rest.astype(bf16).astype(f32)
    low = rest - middle
    return jnp.where(
        lane == 0, high, jnp.where(lane == 1, middle, jnp.where(lane == 2, low, 0.0))
    )


def attend_backward_kernel(
    first_group, count, place_ref, q_ref, k_ref, v_ref, out_ref, log_ref, grad_ref, dq_ref, dkv_ref, dk_sum, dv_sum
):
    pair_index = pl.program_id(0)
    local = pair_index // 2
    group = first_group + local
    place = place_ref[0]
    tokens = q_ref.shape[0]
    lane = lanes_of((tokens, LANES))
    first = lane < HEAD_SIZE
    inside = lane % HEAD_SIZE
    pair = q_ref[...].astype(f32)
    grad = grad_ref[...].astype(f32)
    delta = pltpu.roll(head_sum(grad * out_ref[...].astype(f32)), HEAD_SIZE, 1)
    logs = three_parts(log_ref[...] * (1.0 / SCORE_EXPONENT), inside)
    deltas = three_parts(delta, inside)
    minus = jnp.where(inside < 3, -1.0, 0.0)

    def sides(own, other):
        return (
            jnp.where(first, own, other).astype(bf16),
            jnp.where(first, other, own).astype(bf16),
        )

    queries = sides(pair, 0.0)
    grads = sides(grad, 0.0)
    def turned(values):
        return jnp.transpose(values.astype(f32)).astype(bf16)

    queries_log = tuple(turned(v) for v in sides(pair, logs))
    grads_delta = tuple(turned(v) for v in sides(grad, deltas))

    @pl.when(pair_index % 2 == 0)
    def _():
        dk_sum[...] = jnp.zeros_like(dk_sum)
        dv_sum[...] = jnp.zeros_like(dv_sum)

    def step(j, dq, diagonal):
        rows = pl.ds(pl.multiple_of(j * tokens, tokens), tokens)
        key_wide = both_halves(k_ref[rows, :], group % 2)
        value_wide = both_halves(v_ref[rows, :], (KEY_VALUE_HEADS + group) % 2)
        keys_turned = jnp.transpose(key_wide)[:HEAD_SIZE].astype(bf16)
        keys_log = sides(key_wide, minus)
        values_delta = sides(value_wide, minus)
        dk = dk_sum[rows, :]
        dv = dv_sum[rows, :]
        parts = list(dq)
        block = tokens // SPLIT
        for sub in range(SPLIT):
            keep = slice(sub * block, (sub + 1) * block)
            dk_part, dv_part = dk[keep], dv[keep]
            start = sub * block if diagonal else 0
            for head in range(2):
                weights = jnp.exp2(
                    dot_nn(keys_log[head][keep], queries_log[head][:, start:]) * SCORE_EXPONENT
                )
                if diagonal:
                    row = lax.broadcasted_iota(jnp.int32, weights.shape, 0)
                    weights = jnp.where(row <= lanes_of(weights.shape), weights, 0.0)
                grad_weights = dot_nn(values_delta[head][keep], grads_delta[head][:, start:])
                grad_scores = (weights * grad_weights).astype(bf16)
                dv_part = dv_part + dot_nn(weights.astype(bf16), grads[head][start:])
                dk_part = dk_part + dot_nn(grad_scores, queries[head][start:])
                term = dot_nn(keys_turned[:, keep], grad_scores)
                if start:
                    term = jnp.concatenate([jnp.zeros((HEAD_SIZE, start), f32), term], axis=1)
                parts[head] = parts[head] + term
            target = pl.ds(pl.multiple_of(j * tokens + sub * block, block), block)
            dk_sum[target, :] = dk_part
            dv_sum[target, :] = dv_part
        return tuple(parts)

    zero = jnp.zeros((HEAD_SIZE, tokens), f32)
    dq = lax.fori_loop(0, place, lambda j, c: step(j, c, False), (zero, zero))
    dq = jnp.transpose(jnp.concatenate(step(place, dq, True), axis=0))
    dq_ref[...] = (dq * HEAD_SIZE**-0.5).astype(bf16)

    @pl.when(pair_index % 2 == 1)
    def _():
        wide_lane = lanes_of(dk_sum.shape)
        for total, slot, factor in (
            (dk_sum, local, HEAD_SIZE**-0.5),
            (dv_sum, count + local, 1.0),
        ):
            both = (total[...] + pltpu.roll(total[...], HEAD_SIZE, 1)) * factor
            columns = pl.ds(pl.multiple_of(slot // 2 * LANES, LANES), LANES)
            mine = wide_lane // HEAD_SIZE == slot % 2
            dkv_ref[:, columns] = jnp.where(
                mine, both, dkv_ref[:, columns].astype(f32)
            ).astype(bf16)


def attend_backward(first, count, place, queries, keys_values, mixed, logs, grad_mixed):
    tokens = queries.shape[0]
    length = keys_values.shape[0]
    group = QUERY_HEADS // KEY_VALUE_HEADS * HEAD_SIZE
    own = pl.BlockSpec((tokens, LANES), lambda i, s: (0, 2 * first + i))
    keys = pl.BlockSpec((length, LANES), lambda i, s: (0, (first + i // 2) // 2))
    values = pl.BlockSpec(
        (length, LANES), lambda i, s: (0, (KEY_VALUE_HEADS + first + i // 2) // 2)
    )
    columns = 2 * count * HEAD_SIZE
    return pl.pallas_call(
        partial(attend_backward_kernel, first, count),
        grid_spec=pltpu.PrefetchScalarGridSpec(
            num_scalar_prefetch=1,
            grid=(2 * count,),
            in_specs=[own, keys, values, own, own, own],
            out_specs=[
                pl.BlockSpec((tokens, LANES), lambda i, s: (0, i)),
                pl.BlockSpec((length, columns), lambda i, s: (0, 0)),
            ],
            scratch_shapes=[pltpu.VMEM((length, LANES), f32), pltpu.VMEM((length, LANES), f32)],
        ),
        out_shape=[
            jax.ShapeDtypeStruct((tokens, count * group), bf16),
            jax.ShapeDtypeStruct((length, columns), bf16),
        ],
        compiler_params=pltpu.CompilerParams(vmem_limit_bytes=VMEM_LIMIT),
        name="attend_backward",
        cost_estimate=LIGHT,
    )(place, queries, keys_values, keys_values, mixed, logs, grad_mixed)


def hidden_kernel(n0_ref, n1_ref, wg_ref, wu_ref, hidden_ref, gate_ref, up_ref, n_all):
    tokens = n0_ref.shape[0]

    @pl.when(pl.program_id(0) == 0)
    def _():
        n_all[:tokens] = n0_ref[...]
        n_all[tokens:] = n1_ref[...]

    gate = dot_nn(n_all[...], wg_ref[...])
    up = dot_nn(n_all[...], wu_ref[...])
    hidden_ref[...] = (gate / (1.0 + jnp.exp(-gate)) * up).astype(bf16)
    gate_ref[...] = gate.astype(bf16)
    up_ref[...] = up.astype(bf16)


def hidden_pass(normed, wgate, wup):
    tokens, width = normed[0].shape
    columns = wgate.shape[1]
    tile = min(256, columns)
    whole = pl.BlockSpec((tokens, width), lambda i: (0, 0))
    down = pl.BlockSpec((width, tile), lambda i: (0, i))
    out = pl.BlockSpec((2 * tokens, tile), lambda i: (0, i))
    return pl.pallas_call(
        hidden_kernel,
        grid=(pl.cdiv(columns, tile),),
        in_specs=[whole] * 2 + [down] * 2,
        out_specs=[out] * 3,
        out_shape=[jax.ShapeDtypeStruct((2 * tokens, columns), bf16)] * 3,
        scratch_shapes=[pltpu.VMEM((2 * tokens, width), bf16)],
        compiler_params=pltpu.CompilerParams(vmem_limit_bytes=VMEM_LIMIT),
        name="hidden_pass",
        cost_estimate=LIGHT,
    )(*normed, wgate, wup)


def gate_kernel(n0_ref, n1_ref, wg_ref, gate_ref):
    tokens = n0_ref.shape[0]
    gate_ref[:tokens] = dot_nn(n0_ref[...], wg_ref[...]).astype(bf16)
    gate_ref[tokens:] = dot_nn(n1_ref[...], wg_ref[...]).astype(bf16)


def gate_pass(normed, wgate):
    tokens, width = normed[0].shape
    columns = wgate.shape[1]
    tile = min(256, columns)
    whole = pl.BlockSpec((tokens, width), lambda i: (0, 0))
    return pl.pallas_call(
        gate_kernel,
        grid=(pl.cdiv(columns, tile),),
        in_specs=[whole] * 2 + [pl.BlockSpec((width, tile), lambda i: (0, i))],
        out_specs=pl.BlockSpec((2 * tokens, tile), lambda i: (0, i)),
        out_shape=jax.ShapeDtypeStruct((2 * tokens, columns), bf16),
        compiler_params=pltpu.CompilerParams(vmem_limit_bytes=VMEM_LIMIT),
        name="gate_pass",
        cost_estimate=LIGHT,
    )(*normed, wgate)


def up_kernel(n0_ref, n1_ref, wu_ref, gate_ref, hidden_ref, up_ref):
    tokens = n0_ref.shape[0]
    for n_ref, rows in ((n0_ref, slice(0, tokens)), (n1_ref, slice(tokens, 2 * tokens))):
        up = dot_nn(n_ref[...], wu_ref[...])
        gate = gate_ref[rows].astype(f32)
        hidden_ref[rows] = (gate / (1.0 + jnp.exp(-gate)) * up).astype(bf16)
        up_ref[rows] = up.astype(bf16)


def up_pass(normed, wup, gate):
    tokens, width = normed[0].shape
    columns = wup.shape[1]
    tile = min(256, columns)
    whole = pl.BlockSpec((tokens, width), lambda i: (0, 0))
    out = pl.BlockSpec((2 * tokens, tile), lambda i: (0, i))
    return pl.pallas_call(
        up_kernel,
        grid=(pl.cdiv(columns, tile),),
        in_specs=[whole] * 2 + [pl.BlockSpec((width, tile), lambda i: (0, i)), out],
        out_specs=[out] * 2,
        out_shape=[jax.ShapeDtypeStruct((2 * tokens, columns), bf16)] * 2,
        compiler_params=pltpu.CompilerParams(vmem_limit_bytes=VMEM_LIMIT),
        name="up_pass",
        cost_estimate=LIGHT,
    )(*normed, wup, gate)


def gates_kernel(g0_ref, g1_ref, wd_ref, gate_ref, up_ref, gate_out_ref, up_out_ref, g_all):
    tokens = g0_ref.shape[0]

    @pl.when(pl.program_id(0) == 0)
    def _():
        g_all[:tokens] = g0_ref[...]
        g_all[tokens:] = g1_ref[...]

    grad = dot_nt(g_all[...], wd_ref[...])
    gate = gate_ref[...].astype(f32)
    up = up_ref[...].astype(f32)
    sigmoid = 1.0 / (1.0 + jnp.exp(-gate))
    gate_out_ref[...] = (grad * up * (sigmoid * (1.0 + gate * (1.0 - sigmoid)))).astype(bf16)
    up_out_ref[...] = (grad * (gate * sigmoid)).astype(bf16)


def gates_pass(grad_top, wdown, gate, up):
    tokens, width = grad_top[0].shape
    columns = gate.shape[1]
    tile = min(256, columns)
    whole = pl.BlockSpec((tokens, width), lambda i: (0, 0))
    out = pl.BlockSpec((2 * tokens, tile), lambda i: (0, i))
    return pl.pallas_call(
        gates_kernel,
        grid=(pl.cdiv(columns, tile),),
        in_specs=[whole] * 2 + [pl.BlockSpec((tile, width), lambda i: (i, 0)), out, out],
        out_specs=[out] * 2,
        out_shape=[jax.ShapeDtypeStruct((2 * tokens, columns), bf16)] * 2,
        scratch_shapes=[pltpu.VMEM((2 * tokens, width), bf16)],
        compiler_params=pltpu.CompilerParams(vmem_limit_bytes=VMEM_LIMIT),
        name="gates_pass",
        cost_estimate=LIGHT,
    )(*grad_top, wdown, gate, up)


def back_kernel(count, transposed, *refs):
    own_ref, send_ref = refs[-2:]
    tokens = own_ref.shape[0]
    dot = dot_nt if transposed else dot_nn

    def total(start):
        rows = pl.ds(start, tokens)
        result = dot(refs[0][rows, :], refs[count][...])
        for i in range(1, count):
            result = result + dot(refs[i][rows, :], refs[count + i][...])
        return result

    own_ref[...] = total(0)
    send_ref[...] = total(tokens).astype(bf16)


def back_pass(lefts, weights, transposed):
    tokens, depth = lefts[0].shape
    width = weights[0].shape[0 if transposed else 1]
    count = len(lefts)
    tile = min(512, width)
    if transposed:
        weight_spec = pl.BlockSpec((tile, depth), lambda i: (i, 0))
    else:
        weight_spec = pl.BlockSpec((depth, tile), lambda i: (0, i))
    out = pl.BlockSpec((tokens // 2, tile), lambda i: (0, i))
    return pl.pallas_call(
        partial(back_kernel, count, transposed),
        grid=(width // tile,),
        in_specs=[pl.BlockSpec((tokens, depth), lambda i: (0, 0))] * count
        + [weight_spec] * count,
        out_specs=[out, out],
        out_shape=[
            jax.ShapeDtypeStruct((tokens // 2, width), f32),
            jax.ShapeDtypeStruct((tokens // 2, width), bf16),
        ],
        compiler_params=pltpu.CompilerParams(vmem_limit_bytes=VMEM_LIMIT),
        name="back_pass",
        cost_estimate=LIGHT,
    )(*lefts, *weights)


def weight_kernel(left_count, *refs):
    lefts, rights, out_ref = refs[:left_count], refs[left_count:-1], refs[-1]
    step = min(lefts[0].shape[0], rights[0].shape[0])

    def piece(refs, start):
        index, offset = divmod(start, refs[0].shape[0])
        return refs[index][pl.ds(offset, step), :]

    total = None
    for start in range(0, left_count * lefts[0].shape[0], step):
        term = dot_tn(piece(lefts, start), piece(rights, start))
        total = term if total is None else total + term
    out_ref[...] = total.astype(bf16)


def weight_pass(lefts, rights):
    rows, columns = lefts[0].shape[1], rights[0].shape[1]
    tile = 512 if rows % 512 == 0 else 384 if rows % 384 == 0 else rows
    return pl.pallas_call(
        partial(weight_kernel, len(lefts)),
        grid=(rows // tile,),
        in_specs=[pl.BlockSpec((left.shape[0], tile), lambda i: (0, i)) for left in lefts]
        + [pl.BlockSpec(right.shape, lambda i: (0, 0)) for right in rights],
        out_specs=pl.BlockSpec((tile, columns), lambda i: (i, 0)),
        out_shape=jax.ShapeDtypeStruct((rows, columns), bf16),
        compiler_params=pltpu.CompilerParams(vmem_limit_bytes=VMEM_LIMIT),
        name="weight_pass",
        cost_estimate=LIGHT,
    )(*lefts, *rights)


def placed_kernel(side_ref, own_ref, other_ref, out_ref):
    mine = pl.program_id(0) == side_ref[0]

    @pl.when(mine)
    def _():
        for g in range(out_ref.shape[1]):
            out_ref[0, g] = own_ref[:, g]

    @pl.when(jnp.logical_not(mine))
    def _():
        for g in range(out_ref.shape[1]):
            out_ref[0, g] = other_ref[:, g]


def placed(own, other, side):
    seq, group, rows, columns = own.shape

    def entry(mine, e, g, s):
        parked = jnp.where(e == 0, 0, group // 2 - 1)
        return (0, jnp.where((e == s[0]) == mine, g, parked), 0, 0)

    return pl.pallas_call(
        placed_kernel,
        grid_spec=pltpu.PrefetchScalarGridSpec(
            num_scalar_prefetch=1,
            grid=(2, group // 2),
            in_specs=[
                pl.BlockSpec((seq, 2, rows, columns), partial(entry, True)),
                pl.BlockSpec((seq, 2, rows, columns), partial(entry, False)),
            ],
            out_specs=pl.BlockSpec(
                (1, 2, seq, rows, columns), lambda e, g, s: (e, g, 0, 0, 0)
            ),
        ),
        out_shape=jax.ShapeDtypeStruct((2, group, seq, rows, columns), own.dtype),
        compiler_params=pltpu.CompilerParams(vmem_limit_bytes=VMEM_LIMIT),
        name="placed",
        cost_estimate=LIGHT,
    )(side.astype(jnp.int32).reshape(1), own, other)


def joined_kernel(side_ref, own_ref, other_ref, out_ref):
    mine = pl.program_id(1) == side_ref[0]

    @pl.when(mine)
    def _():
        out_ref[:, 0] = own_ref[...]

    @pl.when(jnp.logical_not(mine))
    def _():
        out_ref[:, 0] = other_ref[...]


def joined(own, other, side, axis):
    shape = own.shape[:axis] + (2,) + own.shape[axis:]
    columns = own.shape[-1]
    lead = math.prod(own.shape[:axis])
    rows = math.prod(own.shape[axis:-1])
    leads, chunks = lead, 1
    while leads % 2 == 0 and leads * rows * columns > 800_000:
        leads //= 2
    while leads == 1 and rows % (32 * chunks) == 0 and rows // chunks * columns > 800_000:
        chunks *= 2
    block = rows // chunks

    def entry(mine, p, e, i, s):
        parked = jnp.where(e == 0, 0, chunks - 1)
        return (p, jnp.where((e == s[0]) == mine, i, parked), 0)

    return pl.pallas_call(
        joined_kernel,
        grid_spec=pltpu.PrefetchScalarGridSpec(
            num_scalar_prefetch=1,
            grid=(lead // leads, 2, chunks),
            in_specs=[
                pl.BlockSpec((leads, block, columns), partial(entry, True)),
                pl.BlockSpec((leads, block, columns), partial(entry, False)),
            ],
            out_specs=pl.BlockSpec((leads, 1, block, columns), lambda p, e, i, s: (p, e, i, 0)),
        ),
        out_shape=jax.ShapeDtypeStruct((lead, 2, rows, columns), own.dtype),
        compiler_params=pltpu.CompilerParams(vmem_limit_bytes=VMEM_LIMIT),
        name="joined",
        cost_estimate=LIGHT,
    )(
        side.astype(jnp.int32).reshape(1),
        own.reshape(lead, rows, columns),
        other.reshape(lead, rows, columns),
    ).reshape(shape)


def swap(values, bit):
    pairs = [(i, i ^ bit) for i in range(lax.axis_size("rows"))]
    return lax.ppermute(values, "rows", pairs)


def bit_of(bit):
    return (lax.axis_index("rows") // bit) % 2


def gather_bit(values, bit, axis):
    return joined(values, swap(values, bit), bit_of(bit), axis)


def part(values, index, axis):
    return lax.dynamic_index_in_dim(values, index, axis, keepdims=False)


def reduce_bit(values, bit, axis):
    return add_bit(values, pass_bit(values, bit, axis), bit, axis)


def outer_pairs(step, low, high):
    size = lax.axis_size("rows")
    return [
        (i, i + 4 * step)
        for i in range(size)
        if low <= i // 4 < high and 0 <= i // 4 + step < size // 4
    ]


def send_outer(values):
    count = lax.axis_size("rows") // 4
    if count == 2:
        return (swap(values, 4),)
    up, down = values, values
    ups, downs = [], []
    for t in range(1, count):
        up = lax.ppermute(up, "rows", outer_pairs(1, t - 1, count))
        down = lax.ppermute(down, "rows", outer_pairs(-1, 0, count - t + 1))
        ups.append(up)
        downs.append(down)
    return tuple(ups[::-1] + downs)


def join_outer(values, received, axis):
    count = lax.axis_size("rows") // 4
    if count == 2:
        return joined(values, received[0], bit_of(4), axis)
    place = lax.axis_index("rows") // 4
    line = jnp.stack([*received[: count - 1], values, *received[count - 1 :]], axis)
    return lax.dynamic_slice_in_dim(line, count - 1 - place, count, axis)


def gather_outer(values, axis):
    return join_outer(values, send_outer(values), axis)


def pass_outer(values, axis):
    count = lax.axis_size("rows") // 4
    place = lax.axis_index("rows") // 4

    def entry(index):
        return part(values, jnp.clip(index, 0, count - 1), axis)

    if count == 1:
        return ()
    if count == 2:
        return (swap(entry(1 - place), 4),)
    up, down = entry(place + count - 1), entry(place - count + 1)
    for t in range(1, count):
        up = lax.ppermute(up, "rows", outer_pairs(1, 0, t))
        down = lax.ppermute(down, "rows", outer_pairs(-1, count - t, count))
        if t < count - 1:
            up = (entry(place + count - 1 - t).astype(f32) + up.astype(f32)).astype(bf16)
            down = (entry(place - count + 1 + t).astype(f32) + down.astype(f32)).astype(bf16)
    return (up, down)


def add_outer(values, received, axis):
    total = part(values, lax.axis_index("rows") // 4, axis).astype(f32)
    for term in received:
        total = total + term.astype(f32)
    return total.astype(bf16)


def reduce_outer(values, axis):
    return add_outer(values, pass_outer(values, axis), axis)


def pass_bit(values, bit, axis):
    return swap(part(values, 1 - bit_of(bit), axis), bit)


def add_bit(values, received, bit, axis):
    own = part(values, bit_of(bit), axis)
    return (own.astype(f32) + received.astype(f32)).astype(bf16)


def gather_seq(values):
    return lax.all_gather(values, "seq", axis=0, tiled=False)


def reduce_seq(values):
    return lax.psum_scatter(values, "seq", scatter_dimension=0, tiled=False)


def exchange(values, axis, bit):
    size = lax.axis_size(axis)
    return lax.ppermute(values, axis, [(i, i ^ bit) for i in range(size)])


def across_group(own, send):
    return (own + swap(send, 1).astype(f32)).astype(bf16)


def stage(*values):
    return lax.optimization_barrier(values)


def mm(left, right):
    return jnp.einsum("ab,bc->ac", left, right, preferred_element_type=f32)


def mm_t(left, right):
    return jnp.einsum("ab,cb->ac", left, right, preferred_element_type=f32)


def t_mm(left, right):
    return jnp.einsum("ab,ac->bc", left, right, preferred_element_type=f32)


def norm_scale(values):
    return lax.rsqrt(jnp.mean(values * values, axis=-1, keepdims=True) + EPSILON)


def norm_backward(values, scale, gain, grad):
    gained = grad * gain
    inner = jnp.mean(values * gained, axis=-1, keepdims=True)
    result = scale * gained - values * (scale * scale * scale) * inner
    return result, jnp.sum(grad * values * scale, axis=0)


def shards(
    tokens_in,
    corpus,
    corpus_weight,
    w_qkv,
    w_out,
    w_gate,
    w_up,
    w_down,
    attn_gain,
    ffn_gain,
    q_gain,
    k_gain,
    upstream,
):
    shard_length, width = tokens_in.shape[1:]
    row_devices = lax.axis_size("rows")
    seq_devices = lax.axis_size("seq")
    outer = row_devices // 4
    d_rows = w_qkv.shape[0]
    f_rows = w_down.shape[0]
    place = lax.axis_index("seq").astype(jnp.int32)
    inputs = tokens_in[0].astype(f32)

    extra = jnp.stack(
        [
            attn_gain,
            ffn_gain,
            jnp.broadcast_to(corpus.astype(bf16), attn_gain.shape),
        ],
        axis=1,
    )
    extra = jnp.pad(extra, ((0, 0), (0, LANES - extra.shape[1])))
    kv_shard = jnp.concatenate([w_qkv[:, QUERY_COLUMNS:], extra], axis=1)
    query_shard = jnp.concatenate([w_qkv[:, :QUERY_COLUMNS], w_out.T], axis=1)
    query_shard, w_gate, w_up = stage(query_shard, w_gate, w_up)
    query_lines = gather_seq(query_shard)

    def to_group(weight):
        blocks = weight.reshape(d_rows, outer, 4, seq_devices, f_rows)
        blocks = jnp.transpose(blocks, (2, 0, 3, 1, 4))
        return blocks.reshape(2, 2, d_rows, outer * seq_devices * f_rows)

    def spread_hidden(lines, received):
        if outer == 2:
            lines = lines.reshape(seq_devices, 4, d_rows, hidden_columns)
            other = received[0].reshape(lines.shape)
            return placed(lines, other, bit_of(4)).reshape(width, hidden_columns)
        full = join_outer(lines, received, 0)
        return jnp.moveaxis(full, 1, 3).reshape(width, hidden_columns)

    gate_up = jnp.stack([to_group(w_gate), to_group(w_up)], axis=2)
    hidden_columns = gate_up.shape[-1]
    core, near = bit_of(1), bit_of(2)
    gate_up = joined(
        part(gate_up, core, 1), swap(part(gate_up, 1 - core, 1), 1), core, 1
    )
    gate_up, kv_shard = stage(gate_up, kv_shard)
    other, kv_lines, query_lines = stage(
        swap(part(gate_up, 1 - near, 0), 2), gather_seq(kv_shard), query_lines
    )
    gate_up = joined(part(gate_up, near, 0), other, near, 0)
    gate_lines = gather_seq(gate_up[:, :, 0])
    left, right = kv_lines[..., : 3 * LANES], kv_lines[..., 3 * LANES :]
    left_other, right_other = stage(send_outer(left), swap(right, 2))
    left = join_outer(left, left_other, 0)
    right = joined(right, right_other, near, 0)
    left_other, right_other = stage(swap(left, 2), send_outer(right))
    left = joined(left, left_other, near, 1)
    right = join_outer(right, right_other, 0)
    q_left, q_right = query_lines[..., :QUERY_COLUMNS], query_lines[..., QUERY_COLUMNS:]
    q_left, q_right, left, right = stage(q_left, q_right, left, right)
    q_left_other, q_right_other = send_outer(q_left), swap(q_right, 2)
    left, right = gather_bit(left, 1, 2), gather_bit(right, 1, 2)
    left, right = left.reshape(width, -1), right.reshape(width, -1)
    wkv = jnp.concatenate([left, right[:, : 2 * LANES]], axis=1)
    rows = dot_nt(jnp.eye(8, LANES, dtype=bf16), right[:, 2 * LANES :])
    attn_gain_full, ffn_gain_full, corpus_full = rows[0:1], rows[1:2], rows[2]

    position = (place * shard_length + jnp.arange(shard_length, dtype=jnp.int32)).astype(f32)
    half = HEAD_SIZE // 2
    exponent = jnp.arange(half, dtype=f32) * (-2.0 / HEAD_SIZE)
    angles = position[:, None] * jnp.power(ROPE_BASE, exponent)[None, :]
    cosine, sine = jnp.cos(angles), jnp.sin(angles)
    cos_table = jnp.concatenate([cosine] * 4, axis=1)
    sin_table = jnp.concatenate([-sine, sine] * 2, axis=1)
    wide_q = jnp.tile(q_gain.astype(f32), QUERY_HEADS)
    wide_k = jnp.concatenate(
        [jnp.tile(k_gain.astype(f32), KEY_VALUE_HEADS), jnp.ones((KEY_COLUMNS,), f32)]
    )
    wide_q = jnp.broadcast_to(wide_q[None, :], (8, QUERY_COLUMNS))
    wide_k = jnp.broadcast_to(wide_k[None, :], (8, 2 * KEY_COLUMNS))

    in_scale = norm_scale(inputs)
    normed = (inputs * in_scale * attn_gain_full).astype(bf16)
    joint_kv, own_kv = heads_forward(
        normed, wkv, wide_k, cos_table, sin_table, KEY_COLUMNS
    )
    own_kv, q_left_other, q_right_other, up_in = stage(
        own_kv, q_left_other, q_right_other, gate_up[:, :, 1]
    )
    up_lines = gather_seq(up_in)
    keys_values = gather_seq(own_kv).reshape(-1, 2 * KEY_COLUMNS)
    q_left = join_outer(q_left, q_left_other, 0)
    q_right = joined(q_right, q_right_other, near, 0)
    left_other, right_other, gate_lines, w_down = stage(
        swap(q_left, 2), send_outer(q_right), gate_lines, w_down
    )
    q_left = joined(q_left, left_other, near, 1)
    gate_other = send_outer(gate_lines)
    down_other = send_outer(w_down)
    half_rows = (2 * outer, seq_devices * d_rows, QUERY_COLUMNS)
    q_left_other = swap(q_left, 1)

    corpora = jnp.arange(CORPORA, dtype=jnp.int32)
    per_device = corpus_full.reshape(-1, d_rows)[:, 0].astype(jnp.int32)
    counts = (
        jnp.sum((per_device[:, None] == corpora[None, :]).astype(f32), axis=0) * shard_length
    )
    own_corpus = (corpus[0] == corpora).astype(f32)
    weight_row = jnp.sum(own_corpus * corpus_weight.astype(f32))
    count_row = jnp.sum(own_corpus * counts)
    factor = weight_row / DENOM * (jnp.sum(counts) / (CORPORA * count_row))
    grad_full = upstream[0].astype(f32) * factor
    grad_top, q_left, q_left_other = stage(grad_full.astype(bf16), q_left, q_left_other)

    q_halves = (q_left.reshape(half_rows), q_left_other.reshape(half_rows))
    joint_q, queries = heads_forward_halves(
        normed, *q_halves, core, wide_q, cos_table, sin_table
    )
    queries, q_right, right_other, down_other = stage(queries, q_right, right_other, down_other)
    q_right = join_outer(q_right, right_other, 0)
    down_pair = join_outer(w_down, down_other, 0)
    place_array = place.reshape(1)
    keys_values, queries, down_in = stage(keys_values, queries, down_pair)
    down_lines = gather_seq(down_in)
    mixed, logs = attend_forward(place_array, queries, keys_values)
    mixed, grad_top1, grad_top2, up_lines, wout_other = stage(
        mixed, swap(grad_top, 1), swap(grad_top, 2), up_lines, swap(q_right, 1)
    )
    middle = project(
        mixed, q_right.reshape(half_rows), wout_other.reshape(half_rows), tokens_in[0], core
    )

    ffn_scale = norm_scale(middle)
    normed_ffn = (middle * ffn_scale * ffn_gain_full).astype(bf16)
    up_other = send_outer(up_lines)
    normed_ffn, gate_other, q_right, wout_other, q_left, q_left_other = stage(
        normed_ffn, gate_other, q_right, wout_other, q_left, q_left_other
    )
    normed1 = swap(normed_ffn, 1)
    wgate = spread_hidden(gate_lines, gate_other)
    gate_near, normed2, up_other, wout_t, wq = stage(
        gate_pass((normed_ffn, normed1), wgate),
        swap(normed_ffn, 2),
        up_other,
        joined(q_right, wout_other, core, 2),
        joined(q_left, q_left_other, core, 2),
    )
    wout_t, wq = wout_t.reshape(width, -1), wq.reshape(width, -1)
    wup = spread_hidden(up_lines, up_other)
    hidden_near, up_near = up_pass((normed_ffn, normed1), wup, gate_near)
    normed3, hidden_near, grad_top3 = stage(
        swap(normed2, 1), hidden_near, swap(grad_top2, 1)
    )
    hidden_far, gate_far, up_far = hidden_pass((normed2, normed3), wgate, wup)
    normed4 = (normed_ffn, normed1, normed2, normed3)
    grad_top4 = (grad_top, grad_top1, grad_top2, grad_top3)
    wdown = down_lines.reshape(hidden_columns, width)
    gate_far, up_far = gates_pass((grad_top2, grad_top3), wdown, gate_far, up_far)
    own, send = back_pass((gate_far, up_far), (wgate, wup), True)
    grad_wdown = weight_pass((hidden_near, hidden_far), grad_top4)
    own, send, grad_wdown, wdown = stage(own, swap(send, 1), grad_wdown, wdown)
    across = (own + send.astype(f32)).astype(bf16)
    across, wdown = stage(across, wdown)
    gate_near, up_near = gates_pass((grad_top, grad_top1), wdown, gate_near, up_near)
    own, send = back_pass((gate_near, up_near), (wgate, wup), True)
    hidden_shape = (outer, 2, 2, seq_devices, d_rows, hidden_columns)
    grad_wdown = grad_wdown.reshape(seq_devices, outer, f_rows, width)
    grad_wgate = weight_pass(normed4, (gate_near, gate_far)).reshape(hidden_shape)
    across, own, send, grad_wgate, up_near = stage(
        swap(across, 2), own, send, grad_wgate, up_near
    )
    grad_wup = weight_pass(normed4, (up_near, up_far)).reshape(hidden_shape)
    send, grad_wup, down_other = stage(swap(send, 1), grad_wup, pass_outer(grad_wdown, 1))
    grad_wdown = add_outer(grad_wdown, down_other, 1)
    own = own + send.astype(f32)
    grad_normed_ffn = own + across.astype(f32)
    grad_wdown = reduce_seq(grad_wdown)

    grad_middle_part, grad_ffn_gain = norm_backward(
        middle, ffn_scale, ffn_gain_full, grad_normed_ffn
    )
    grad_middle = grad_full + grad_middle_part
    grad_branch = grad_middle.astype(bf16)
    grad_mixed = mm(grad_branch, wout_t).astype(bf16)
    attend = (place_array, queries, keys_values, mixed, logs)
    grad_q1, grad_kv1 = attend_backward(0, 2, *attend, grad_mixed)
    gate_other = pass_outer(grad_wgate, 0)
    grad_q1, grad_kv1, grad_mixed, grad_wdown, hidden_far = stage(
        grad_q1, grad_kv1, grad_mixed, grad_wdown, hidden_far
    )
    grad_kv1 = reduce_seq(grad_kv1.reshape(seq_devices, shard_length, -1))
    shape = (outer, 2, 2, seq_devices, d_rows)
    own_far, send_far = back_pass((hidden_far,), (wdown,), False)
    grad_wout, far_other, gate_other, grad_mixed = stage(
        t_mm(grad_branch, mixed).astype(bf16).reshape(*shape, QUERY_COLUMNS),
        swap(send_far, 1),
        gate_other,
        grad_mixed,
    )
    grad_gate = reduce_seq(jnp.moveaxis(add_outer(grad_wgate, gate_other, 0), 2, 0))
    across = (own_far + far_other.astype(f32)).astype(bf16)
    across, grad_mixed = stage(across, grad_mixed)
    grad_q2, grad_kv2 = attend_backward(2, 3, *attend, grad_mixed)
    grad_q2, grad_kv2, hidden_near, grad_kv1, wout_other, up_other, across = stage(
        grad_q2,
        grad_kv2,
        hidden_near,
        grad_kv1,
        pass_bit(grad_wout, 1, 2),
        pass_outer(grad_wup, 0),
        swap(across, 2),
    )
    grad_kv2 = reduce_seq(grad_kv2.reshape(seq_devices, shard_length, -1))

    grad_q = jnp.concatenate([grad_q1, grad_q2], axis=1)
    joint_grad_q, gain_q = heads_backward(
        grad_q, joint_q, wide_q, cos_table, sin_table, QUERY_COLUMNS
    )
    grad_wq = t_mm(normed, joint_grad_q).astype(bf16).reshape(*shape, QUERY_COLUMNS)
    grad_wout = add_bit(grad_wout, wout_other, 1, 2)
    grad_up = jnp.moveaxis(add_outer(grad_wup, up_other, 0), 2, 0)
    grad_wq = reduce_bit(grad_wq, 1, 2)
    wq_other, wout_other = pass_bit(grad_wq, 2, 1), pass_outer(grad_wout, 0)
    grad_kv2, grad_normed, grad_up, grad_gate = stage(
        grad_kv2, mm_t(joint_grad_q, wq), grad_up, grad_gate
    )
    grad_up = reduce_seq(grad_up)

    grad_kv1, grad_kv2 = (
        part_.reshape(shard_length, 2, -1) for part_ in (grad_kv1, grad_kv2)
    )
    grad_kv = jnp.concatenate([grad_kv1, grad_kv2], axis=2).reshape(shard_length, -1)
    joint_grad_kv, gain_k = heads_backward(
        grad_kv, joint_kv, wide_k, cos_table, sin_table, KEY_COLUMNS
    )
    joint_grad_kv, wq_other, wout_other = stage(joint_grad_kv, wq_other, wout_other)
    grad_wkv = t_mm(normed, joint_grad_kv).astype(bf16)
    grad_normed = grad_normed + mm_t(joint_grad_kv, wkv)
    grad_input_part, grad_attn_gain = norm_backward(
        inputs, in_scale, attn_gain_full, grad_normed
    )
    input_grad = (grad_middle + grad_input_part).astype(bf16)

    gain_rows = jnp.stack([grad_attn_gain, grad_ffn_gain]).astype(bf16)
    gain_columns = t_mm(gain_rows, jnp.eye(2, LANES, dtype=bf16)).astype(bf16)
    grad_wkv, gain_columns, hidden_near = stage(grad_wkv, gain_columns, hidden_near)
    own_near, send_near = back_pass((hidden_near,), (wdown,), False)
    grad_wq = add_bit(grad_wq, wq_other, 2, 1)
    grad_wout = add_outer(grad_wout, wout_other, 0)
    wq_other, wout_other = pass_outer(grad_wq, 0), pass_bit(grad_wout, 2, 0)
    left = grad_wkv[:, : 3 * LANES].reshape(*shape, -1)
    right = jnp.concatenate([grad_wkv[:, 3 * LANES :], gain_columns], axis=1)
    right = right.reshape(*shape, -1)
    head_gains = jnp.concatenate(
        [
            jnp.sum(gain_q[0].reshape(-1, HEAD_SIZE), axis=0),
            jnp.sum(gain_k[0, :KEY_COLUMNS].reshape(-1, HEAD_SIZE), axis=0),
        ]
    )[None]
    left, right, left_other, right_other, gains_other = stage(
        left,
        right,
        pass_bit(left, 1, 2),
        pass_bit(right, 1, 2),
        exchange(head_gains, "rows", 1),
    )
    head_gains = head_gains + gains_other
    left = add_bit(left, left_other, 1, 2)
    right = add_bit(right, right_other, 1, 2)
    left_other, right_other, wq_other, wout_other, gains_other, grad_up = stage(
        pass_bit(left, 2, 1),
        pass_outer(right, 0),
        wq_other,
        wout_other,
        exchange(head_gains, "seq", 1),
        grad_up,
    )
    head_gains = head_gains + gains_other
    left = add_bit(left, left_other, 2, 1)
    right = add_outer(right, right_other, 0)
    left_other, right_other, gains_other, near_other = stage(
        pass_outer(left, 0),
        pass_bit(right, 2, 0),
        exchange(head_gains, "rows", 2),
        swap(send_near, 1),
    )
    output = (middle + own_near + near_other.astype(f32) + across.astype(f32)).astype(bf16)
    head_gains = head_gains + gains_other
    sums = reduce_seq(
        jnp.concatenate(
            [
                add_outer(grad_wq, wq_other, 0),
                add_outer(left, left_other, 0),
                add_bit(right, right_other, 2, 0),
                add_bit(grad_wout, wout_other, 2, 0),
            ],
            axis=-1,
        )
    )
    rest = [("rows", bit) for bit in (4, 8, 16) if bit < row_devices]
    rest += [("seq", bit) for bit in (2, 4, 8) if bit < seq_devices]
    gate_up = jnp.stack([grad_gate, grad_up], axis=2)
    other, gains_other = stage(
        swap(part(gate_up, 1 - near, 0), 2), exchange(head_gains, *rest[0])
    )
    head_gains = head_gains + gains_other
    grads = joined(part(gate_up, near, 0), other, near, 0)
    for axis, bit in rest[1:]:
        head_gains = head_gains + exchange(head_gains, axis, bit)
    head_gains = head_gains[0]
    grads = joined(part(grads, core, 1), swap(part(grads, 1 - core, 1), 1), core, 1)

    def from_group(blocks):
        blocks = blocks.reshape(4, d_rows, seq_devices, outer, f_rows)
        return jnp.transpose(blocks, (1, 3, 0, 2, 4)).reshape(d_rows, -1)

    grad_wgate, grad_wup = stage(from_group(grads[:, :, 0]), from_group(grads[:, :, 1]))
    sums, grad_wgate, grad_wup, grad_wdown, output, input_grad = stage(
        sums, grad_wgate.astype(f32), grad_wup.astype(f32), grad_wdown.astype(f32), output, input_grad
    )
    columns = QUERY_COLUMNS + 2 * KEY_COLUMNS
    long_gains = sums[:, columns : columns + 2].astype(f32)
    return (
        output[None],
        input_grad[None],
        sums[:, :columns].astype(f32),
        sums[:, columns + LANES :].T.astype(f32),
        grad_wgate,
        grad_wup,
        grad_wdown,
        long_gains[:, 0],
        long_gains[:, 1],
        head_gains[:HEAD_SIZE],
        head_gains[HEAD_SIZE:],
    )


def solution(mesh):
    return jax.shard_map(
        shards,
        mesh=mesh,
        in_specs=(
            P("rows", "seq", None),
            P("rows"),
            P(),
            P(("rows", "seq"), None),
            P(None, ("rows", "seq")),
            P(("rows", "seq"), None),
            P(("rows", "seq"), None),
            P(("rows", "seq"), None),
            P(("rows", "seq")),
            P(("rows", "seq")),
            P(),
            P(),
            P("rows", "seq", None),
        ),
        out_specs=(
            P("rows", "seq", None),
            P("rows", "seq", None),
            P(("rows", "seq"), None),
            P(None, ("rows", "seq")),
            P(("rows", "seq"), None),
            P(("rows", "seq"), None),
            P(("rows", "seq"), None),
            P(("rows", "seq")),
            P(("rows", "seq")),
            P(),
            P(),
        ),
        check_vma=False,
    )
```

```python
import math
from functools import partial

import jax
import jax.numpy as jnp
from jax import lax
from jax.experimental import pallas as pl
from jax.experimental.pallas import tpu as pltpu
from jax.sharding import PartitionSpec as P

QUERY_HEADS = 20
KEY_VALUE_HEADS = 5
HEAD_SIZE = 64
CORPORA = 8
DENOM = 64
EPSILON = 1e-06
ROPE_BASE = 10000.0
QUERY_COLUMNS = QUERY_HEADS * HEAD_SIZE
KEY_COLUMNS = KEY_VALUE_HEADS * HEAD_SIZE
LANES = 128
SCORE_EXPONENT = 1.4426950408889634 * HEAD_SIZE**-0.5
SPLIT = 2
VMEM_LIMIT = 48 * 1024 * 1024

f32, bf16 = jnp.float32, jnp.bfloat16
LIGHT = pl.CostEstimate(flops=1000, bytes_accessed=1000, transcendentals=0)


def dot_nn(a, b):
    return lax.dot_general(a, b, (((1,), (0,)), ((), ())), preferred_element_type=f32)


def dot_nt(a, b):
    return lax.dot_general(a, b, (((1,), (1,)), ((), ())), preferred_element_type=f32)


def dot_tn(a, b):
    return lax.dot_general(a, b, (((0,), (0,)), ((), ())), preferred_element_type=f32)


def lanes_of(shape):
    return lax.broadcasted_iota(jnp.int32, shape, len(shape) - 1)


def head_sum(values):
    row = lax.broadcasted_iota(jnp.int32, (LANES, LANES), 0) // HEAD_SIZE
    column = lax.broadcasted_iota(jnp.int32, (LANES, LANES), 1) // HEAD_SIZE
    ones = jnp.where(row == column, 1.0, 0.0).astype(bf16)
    high = values.astype(bf16)
    low = (values - high.astype(f32)).astype(bf16)
    return dot_nn(high, ones) + dot_nn(low, ones)


def partner(values):
    first = lanes_of(values.shape) % HEAD_SIZE < HEAD_SIZE // 2
    return jnp.where(
        first,
        pltpu.roll(values, LANES - HEAD_SIZE // 2, 1),
        pltpu.roll(values, HEAD_SIZE // 2, 1),
    )


def heads_of(joint, norm_columns, gain_ref, cos_ref, sin_ref, out_ref):
    columns = joint.shape[1]
    for start in range(0, columns, LANES):
        chunk = slice(start, start + LANES)
        values = joint[:, chunk]
        scale = lax.rsqrt(head_sum(values * values) * (1.0 / HEAD_SIZE) + EPSILON)
        normed = values * scale * gain_ref[0:1, chunk]
        turned = normed * cos_ref[...] + partner(normed) * sin_ref[...]
        place = pl.program_id(0) * columns + start + lanes_of(values.shape)
        out_ref[:, chunk] = jnp.where(place < norm_columns, turned, values).astype(bf16)


def heads_forward_kernel(
    norm_columns, normed_ref, weight_ref, gain_ref, cos_ref, sin_ref, joint_ref, out_ref
):
    joint = dot_nn(normed_ref[...], weight_ref[...])
    joint_ref[...] = joint
    heads_of(joint, norm_columns, gain_ref, cos_ref, sin_ref, out_ref)


def heads_halves_kernel(
    side_ref, normed_ref, own_ref, other_ref, gain_ref, cos_ref, sin_ref, joint_ref, out_ref
):
    count, block, _ = own_ref.shape
    joint = None
    for index in range(count):
        for weight_ref, side in ((own_ref, side_ref[0]), (other_ref, 1 - side_ref[0])):
            rows = pl.ds(pl.multiple_of((2 * index + side) * block, block), block)
            term = dot_nn(normed_ref[:, rows], weight_ref[index])
            joint = term if joint is None else joint + term
    joint_ref[...] = joint
    heads_of(joint, QUERY_COLUMNS, gain_ref, cos_ref, sin_ref, out_ref)


def heads_forward_halves(normed, own, other, side, gain, cos, sin):
    tokens, width = normed.shape
    count, block, columns = own.shape
    tile = 2 * LANES
    out = pl.BlockSpec((tokens, tile), lambda i, s: (0, i))
    table = pl.BlockSpec((tokens, LANES), lambda i, s: (0, 0))
    weight = pl.BlockSpec((count, block, tile), lambda i, s: (0, 0, i))
    return pl.pallas_call(
        heads_halves_kernel,
        grid_spec=pltpu.PrefetchScalarGridSpec(
            num_scalar_prefetch=1,
            grid=(columns // tile,),
            in_specs=[
                pl.BlockSpec((tokens, width), lambda i, s: (0, 0)),
                weight,
                weight,
                pl.BlockSpec((8, tile), lambda i, s: (0, i)),
                table,
                table,
            ],
            out_specs=[out, out],
        ),
        out_shape=[
            jax.ShapeDtypeStruct((tokens, columns), f32),
            jax.ShapeDtypeStruct((tokens, columns), bf16),
        ],
        compiler_params=pltpu.CompilerParams(vmem_limit_bytes=VMEM_LIMIT),
        name="heads_forward_halves",
        cost_estimate=LIGHT,
    )(side.astype(jnp.int32).reshape(1), normed, own, other, gain, cos, sin)


def heads_forward(normed, weight, gain, cos, sin, norm_columns):
    tokens, width = normed.shape
    columns = weight.shape[1]
    tile = 2 * LANES if columns % (2 * LANES) == 0 else LANES
    out = pl.BlockSpec((tokens, tile), lambda i: (0, i))
    table = pl.BlockSpec((tokens, LANES), lambda i: (0, 0))
    return pl.pallas_call(
        partial(heads_forward_kernel, norm_columns),
        grid=(columns // tile,),
        in_specs=[
            pl.BlockSpec((tokens, width), lambda i: (0, 0)),
            pl.BlockSpec((width, tile), lambda i: (0, i)),
            pl.BlockSpec((8, tile), lambda i: (0, i)),
            table,
            table,
        ],
        out_specs=[out, out],
        out_shape=[
            jax.ShapeDtypeStruct((tokens, columns), f32),
            jax.ShapeDtypeStruct((tokens, columns), bf16),
        ],
        compiler_params=pltpu.CompilerParams(vmem_limit_bytes=VMEM_LIMIT),
        name="heads_forward",
        cost_estimate=LIGHT,
    )(normed, weight, gain, cos, sin)


def project_kernel(side_ref, mixed_ref, own_ref, other_ref, inputs_ref, out_ref):
    block = own_ref.shape[1]
    for weight_ref, side in ((own_ref, side_ref[0]), (other_ref, 1 - side_ref[0])):
        columns = pl.ds(pl.multiple_of(side * block, block), block)
        out_ref[:, columns] = inputs_ref[:, columns].astype(f32) + dot_nt(
            mixed_ref[...], weight_ref[0]
        )


def project(mixed, own, other, inputs, side):
    tokens, depth = mixed.shape
    count, block, _ = own.shape
    weight = pl.BlockSpec((1, block, depth), lambda i, s: (i, 0, 0))
    out = pl.BlockSpec((tokens, 2 * block), lambda i, s: (0, i))
    return pl.pallas_call(
        project_kernel,
        grid_spec=pltpu.PrefetchScalarGridSpec(
            num_scalar_prefetch=1,
            grid=(count,),
            in_specs=[pl.BlockSpec((tokens, depth), lambda i, s: (0, 0)), weight, weight, out],
            out_specs=out,
        ),
        out_shape=jax.ShapeDtypeStruct((tokens, 2 * count * block), f32),
        compiler_params=pltpu.CompilerParams(vmem_limit_bytes=VMEM_LIMIT),
        name="project",
        cost_estimate=LIGHT,
    )(side.astype(jnp.int32).reshape(1), mixed, own, other, inputs)


def heads_backward_kernel(
    norm_columns, grad_ref, joint_ref, gain_ref, cos_ref, sin_ref, out_ref, gain_out_ref
):
    grad = grad_ref[...].astype(f32)
    values = joint_ref[...]
    gain = gain_ref[0:1, :]
    turned = grad * cos_ref[...] - partner(grad) * sin_ref[...]
    scale = lax.rsqrt(head_sum(values * values) * (1.0 / HEAD_SIZE) + EPSILON)
    gained = turned * gain
    inner = head_sum(values * gained) * (1.0 / HEAD_SIZE)
    result = scale * gained - values * (scale * scale * scale) * inner
    place = pl.program_id(0) * LANES + lanes_of(values.shape)
    out_ref[...] = jnp.where(place < norm_columns, result, grad).astype(bf16)
    gain_out_ref[...] = jnp.broadcast_to(
        jnp.sum(turned * values * scale, axis=0, keepdims=True), gain_out_ref.shape
    )


def heads_backward(grad, joint, gain, cos, sin, norm_columns):
    tokens, columns = joint.shape
    return pl.pallas_call(
        partial(heads_backward_kernel, norm_columns),
        grid=(columns // LANES,),
        in_specs=[
            pl.BlockSpec((tokens, LANES), lambda i: (0, i)),
            pl.BlockSpec((tokens, LANES), lambda i: (0, i)),
            pl.BlockSpec((8, LANES), lambda i: (0, i)),
            pl.BlockSpec((tokens, LANES), lambda i: (0, 0)),
            pl.BlockSpec((tokens, LANES), lambda i: (0, 0)),
        ],
        out_specs=[
            pl.BlockSpec((tokens, LANES), lambda i: (0, i)),
            pl.BlockSpec((8, LANES), lambda i: (0, i)),
        ],
        out_shape=[
            jax.ShapeDtypeStruct((tokens, columns), bf16),
            jax.ShapeDtypeStruct((8, columns), f32),
        ],
        name="heads_backward",
        cost_estimate=LIGHT,
    )(grad, joint, gain, cos, sin)


def both_halves(pair, odd):
    wide = pair.astype(f32)
    first = lanes_of(wide.shape) < HEAD_SIZE
    keep = jnp.where(odd == 1, jnp.where(first, 0, 1), jnp.where(first, 1, 0)) == 1
    return jnp.where(keep, wide, pltpu.roll(wide, HEAD_SIZE, 1))


def attend_forward_kernel(place_ref, q_ref, k_ref, v_ref, out_ref, log_ref):
    group = pl.program_id(0) // 2
    place = place_ref[0]
    tokens = q_ref.shape[0]
    first = lanes_of((tokens, LANES)) < HEAD_SIZE
    pair = q_ref[...].astype(f32)
    queries = (jnp.where(first, pair, 0.0).astype(bf16), jnp.where(first, 0.0, pair).astype(bf16))

    def step(j, totals, diagonal):
        rows = pl.ds(pl.multiple_of(j * tokens, tokens), tokens)
        keys = both_halves(k_ref[rows, :], group % 2).astype(bf16)
        values = both_halves(v_ref[rows, :], (KEY_VALUE_HEADS + group) % 2)
        sides = (
            jnp.where(first, values, 1.0).astype(bf16),
            jnp.where(first, 1.0, values).astype(bf16),
        )
        result = []
        for head in range(2):
            weights = jnp.exp2(dot_nt(queries[head], keys) * SCORE_EXPONENT)
            if diagonal:
                row = lax.broadcasted_iota(jnp.int32, weights.shape, 0)
                weights = jnp.where(lanes_of(weights.shape) <= row, weights, 0.0)
            result.append(totals[head] + dot_nn(weights.astype(bf16), sides[head]))
        return tuple(result)

    zero = jnp.zeros((tokens, LANES), f32)
    totals = lax.fori_loop(0, place, lambda j, c: step(j, c, False), (zero, zero))
    totals = step(place, totals, True)
    numerator = jnp.where(first, totals[0], totals[1])
    swapped = jnp.where(first, totals[1], totals[0])
    out_ref[...] = (numerator / pltpu.roll(swapped, HEAD_SIZE, 1)).astype(bf16)
    log_ref[...] = jnp.log2(swapped)


def attend_forward(place, queries, keys_values):
    tokens = queries.shape[0]
    length = keys_values.shape[0]
    pairs = QUERY_COLUMNS // LANES
    return pl.pallas_call(
        attend_forward_kernel,
        grid_spec=pltpu.PrefetchScalarGridSpec(
            num_scalar_prefetch=1,
            grid=(pairs,),
            in_specs=[
                pl.BlockSpec((tokens, LANES), lambda i, s: (0, i)),
                pl.BlockSpec((length, LANES), lambda i, s: (0, (i // 2) // 2)),
                pl.BlockSpec((length, LANES), lambda i, s: (0, (KEY_VALUE_HEADS + i // 2) // 2)),
            ],
            out_specs=[
                pl.BlockSpec((tokens, LANES), lambda i, s: (0, i)),
                pl.BlockSpec((tokens, LANES), lambda i, s: (0, i)),
            ],
        ),
        out_shape=[
            jax.ShapeDtypeStruct((tokens, QUERY_COLUMNS), bf16),
            jax.ShapeDtypeStruct((tokens, QUERY_COLUMNS), f32),
        ],
        compiler_params=pltpu.CompilerParams(vmem_limit_bytes=VMEM_LIMIT),
        name="attend_forward",
        cost_estimate=LIGHT,
    )(place, queries, keys_values, keys_values)


def three_parts(values, lane):
    high = values.astype(bf16).astype(f32)
    rest = values - high
    middle = rest.astype(bf16).astype(f32)
    low = rest - middle
    return jnp.where(
        lane == 0, high, jnp.where(lane == 1, middle, jnp.where(lane == 2, low, 0.0))
    )


def attend_backward_kernel(
    first_group, count, place_ref, q_ref, k_ref, v_ref, out_ref, log_ref, grad_ref, dq_ref, dkv_ref, dk_sum, dv_sum
):
    pair_index = pl.program_id(0)
    local = pair_index // 2
    group = first_group + local
    place = place_ref[0]
    tokens = q_ref.shape[0]
    lane = lanes_of((tokens, LANES))
    first = lane < HEAD_SIZE
    inside = lane % HEAD_SIZE
    pair = q_ref[...].astype(f32)
    grad = grad_ref[...].astype(f32)
    delta = pltpu.roll(head_sum(grad * out_ref[...].astype(f32)), HEAD_SIZE, 1)
    logs = three_parts(log_ref[...] * (1.0 / SCORE_EXPONENT), inside)
    deltas = three_parts(delta, inside)
    minus = jnp.where(inside < 3, -1.0, 0.0)

    def sides(own, other):
        return (
            jnp.where(first, own, other).astype(bf16),
            jnp.where(first, other, own).astype(bf16),
        )

    queries = sides(pair, 0.0)
    grads = sides(grad, 0.0)
    def turned(values):
        return jnp.transpose(values.astype(f32)).astype(bf16)

    queries_log = tuple(turned(v) for v in sides(pair, logs))
    grads_delta = tuple(turned(v) for v in sides(grad, deltas))

    @pl.when(pair_index % 2 == 0)
    def _():
        dk_sum[...] = jnp.zeros_like(dk_sum)
        dv_sum[...] = jnp.zeros_like(dv_sum)

    def step(j, dq, diagonal):
        rows = pl.ds(pl.multiple_of(j * tokens, tokens), tokens)
        key_wide = both_halves(k_ref[rows, :], group % 2)
        value_wide = both_halves(v_ref[rows, :], (KEY_VALUE_HEADS + group) % 2)
        keys_turned = jnp.transpose(key_wide)[:HEAD_SIZE].astype(bf16)
        keys_log = sides(key_wide, minus)
        values_delta = sides(value_wide, minus)
        dk = dk_sum[rows, :]
        dv = dv_sum[rows, :]
        parts = list(dq)
        block = tokens // SPLIT
        for sub in range(SPLIT):
            keep = slice(sub * block, (sub + 1) * block)
            dk_part, dv_part = dk[keep], dv[keep]
            start = sub * block if diagonal else 0
            for head in range(2):
                weights = jnp.exp2(
                    dot_nn(keys_log[head][keep], queries_log[head][:, start:]) * SCORE_EXPONENT
                )
                if diagonal:
                    row = lax.broadcasted_iota(jnp.int32, weights.shape, 0)
                    weights = jnp.where(row <= lanes_of(weights.shape), weights, 0.0)
                grad_weights = dot_nn(values_delta[head][keep], grads_delta[head][:, start:])
                grad_scores = (weights * grad_weights).astype(bf16)
                dv_part = dv_part + dot_nn(weights.astype(bf16), grads[head][start:])
                dk_part = dk_part + dot_nn(grad_scores, queries[head][start:])
                term = dot_nn(keys_turned[:, keep], grad_scores)
                if start:
                    term = jnp.concatenate([jnp.zeros((HEAD_SIZE, start), f32), term], axis=1)
                parts[head] = parts[head] + term
            target = pl.ds(pl.multiple_of(j * tokens + sub * block, block), block)
            dk_sum[target, :] = dk_part
            dv_sum[target, :] = dv_part
        return tuple(parts)

    zero = jnp.zeros((HEAD_SIZE, tokens), f32)
    dq = lax.fori_loop(0, place, lambda j, c: step(j, c, False), (zero, zero))
    dq = jnp.transpose(jnp.concatenate(step(place, dq, True), axis=0))
    dq_ref[...] = (dq * HEAD_SIZE**-0.5).astype(bf16)

    @pl.when(pair_index % 2 == 1)
    def _():
        wide_lane = lanes_of(dk_sum.shape)
        for total, slot, factor in (
            (dk_sum, local, HEAD_SIZE**-0.5),
            (dv_sum, count + local, 1.0),
        ):
            both = (total[...] + pltpu.roll(total[...], HEAD_SIZE, 1)) * factor
            columns = pl.ds(pl.multiple_of(slot // 2 * LANES, LANES), LANES)
            mine = wide_lane // HEAD_SIZE == slot % 2
            dkv_ref[:, columns] = jnp.where(
                mine, both, dkv_ref[:, columns].astype(f32)
            ).astype(bf16)


def attend_backward(first, count, place, queries, keys_values, mixed, logs, grad_mixed):
    tokens = queries.shape[0]
    length = keys_values.shape[0]
    group = QUERY_HEADS // KEY_VALUE_HEADS * HEAD_SIZE
    own = pl.BlockSpec((tokens, LANES), lambda i, s: (0, 2 * first + i))
    keys = pl.BlockSpec((length, LANES), lambda i, s: (0, (first + i // 2) // 2))
    values = pl.BlockSpec(
        (length, LANES), lambda i, s: (0, (KEY_VALUE_HEADS + first + i // 2) // 2)
    )
    columns = 2 * count * HEAD_SIZE
    return pl.pallas_call(
        partial(attend_backward_kernel, first, count),
        grid_spec=pltpu.PrefetchScalarGridSpec(
            num_scalar_prefetch=1,
            grid=(2 * count,),
            in_specs=[own, keys, values, own, own, own],
            out_specs=[
                pl.BlockSpec((tokens, LANES), lambda i, s: (0, i)),
                pl.BlockSpec((length, columns), lambda i, s: (0, 0)),
            ],
            scratch_shapes=[pltpu.VMEM((length, LANES), f32), pltpu.VMEM((length, LANES), f32)],
        ),
        out_shape=[
            jax.ShapeDtypeStruct((tokens, count * group), bf16),
            jax.ShapeDtypeStruct((length, columns), bf16),
        ],
        compiler_params=pltpu.CompilerParams(vmem_limit_bytes=VMEM_LIMIT),
        name="attend_backward",
        cost_estimate=LIGHT,
    )(place, queries, keys_values, keys_values, mixed, logs, grad_mixed)


def hidden_kernel(n0_ref, n1_ref, wg_ref, wu_ref, hidden_ref, gate_ref, up_ref, n_all):
    tokens = n0_ref.shape[0]

    @pl.when(pl.program_id(0) == 0)
    def _():
        n_all[:tokens] = n0_ref[...]
        n_all[tokens:] = n1_ref[...]

    gate = dot_nn(n_all[...], wg_ref[...])
    up = dot_nn(n_all[...], wu_ref[...])
    hidden_ref[...] = (gate / (1.0 + jnp.exp(-gate)) * up).astype(bf16)
    gate_ref[...] = gate.astype(bf16)
    up_ref[...] = up.astype(bf16)


def hidden_pass(normed, wgate, wup):
    tokens, width = normed[0].shape
    columns = wgate.shape[1]
    tile = min(256, columns)
    whole = pl.BlockSpec((tokens, width), lambda i: (0, 0))
    down = pl.BlockSpec((width, tile), lambda i: (0, i))
    out = pl.BlockSpec((2 * tokens, tile), lambda i: (0, i))
    return pl.pallas_call(
        hidden_kernel,
        grid=(pl.cdiv(columns, tile),),
        in_specs=[whole] * 2 + [down] * 2,
        out_specs=[out] * 3,
        out_shape=[jax.ShapeDtypeStruct((2 * tokens, columns), bf16)] * 3,
        scratch_shapes=[pltpu.VMEM((2 * tokens, width), bf16)],
        compiler_params=pltpu.CompilerParams(vmem_limit_bytes=VMEM_LIMIT),
        name="hidden_pass",
        cost_estimate=LIGHT,
    )(*normed, wgate, wup)


def gate_kernel(n0_ref, n1_ref, wg_ref, gate_ref):
    tokens = n0_ref.shape[0]
    gate_ref[:tokens] = dot_nn(n0_ref[...], wg_ref[...]).astype(bf16)
    gate_ref[tokens:] = dot_nn(n1_ref[...], wg_ref[...]).astype(bf16)


def gate_pass(normed, wgate):
    tokens, width = normed[0].shape
    columns = wgate.shape[1]
    tile = min(256, columns)
    whole = pl.BlockSpec((tokens, width), lambda i: (0, 0))
    return pl.pallas_call(
        gate_kernel,
        grid=(pl.cdiv(columns, tile),),
        in_specs=[whole] * 2 + [pl.BlockSpec((width, tile), lambda i: (0, i))],
        out_specs=pl.BlockSpec((2 * tokens, tile), lambda i: (0, i)),
        out_shape=jax.ShapeDtypeStruct((2 * tokens, columns), bf16),
        compiler_params=pltpu.CompilerParams(vmem_limit_bytes=VMEM_LIMIT),
        name="gate_pass",
        cost_estimate=LIGHT,
    )(*normed, wgate)


def up_kernel(n0_ref, n1_ref, wu_ref, gate_ref, hidden_ref, up_ref):
    tokens = n0_ref.shape[0]
    for n_ref, rows in ((n0_ref, slice(0, tokens)), (n1_ref, slice(tokens, 2 * tokens))):
        up = dot_nn(n_ref[...], wu_ref[...])
        gate = gate_ref[rows].astype(f32)
        hidden_ref[rows] = (gate / (1.0 + jnp.exp(-gate)) * up).astype(bf16)
        up_ref[rows] = up.astype(bf16)


def up_pass(normed, wup, gate):
    tokens, width = normed[0].shape
    columns = wup.shape[1]
    tile = min(256, columns)
    whole = pl.BlockSpec((tokens, width), lambda i: (0, 0))
    out = pl.BlockSpec((2 * tokens, tile), lambda i: (0, i))
    return pl.pallas_call(
        up_kernel,
        grid=(pl.cdiv(columns, tile),),
        in_specs=[whole] * 2 + [pl.BlockSpec((width, tile), lambda i: (0, i)), out],
        out_specs=[out] * 2,
        out_shape=[jax.ShapeDtypeStruct((2 * tokens, columns), bf16)] * 2,
        compiler_params=pltpu.CompilerParams(vmem_limit_bytes=VMEM_LIMIT),
        name="up_pass",
        cost_estimate=LIGHT,
    )(*normed, wup, gate)


def gates_kernel(g0_ref, g1_ref, wd_ref, gate_ref, up_ref, gate_out_ref, up_out_ref, g_all):
    tokens = g0_ref.shape[0]

    @pl.when(pl.program_id(0) == 0)
    def _():
        g_all[:tokens] = g0_ref[...]
        g_all[tokens:] = g1_ref[...]

    grad = dot_nt(g_all[...], wd_ref[...])
    gate = gate_ref[...].astype(f32)
    up = up_ref[...].astype(f32)
    sigmoid = 1.0 / (1.0 + jnp.exp(-gate))
    gate_out_ref[...] = (grad * up * (sigmoid * (1.0 + gate * (1.0 - sigmoid)))).astype(bf16)
    up_out_ref[...] = (grad * (gate * sigmoid)).astype(bf16)


def gates_pass(grad_top, wdown, gate, up):
    tokens, width = grad_top[0].shape
    columns = gate.shape[1]
    tile = min(256, columns)
    whole = pl.BlockSpec((tokens, width), lambda i: (0, 0))
    out = pl.BlockSpec((2 * tokens, tile), lambda i: (0, i))
    return pl.pallas_call(
        gates_kernel,
        grid=(pl.cdiv(columns, tile),),
        in_specs=[whole] * 2 + [pl.BlockSpec((tile, width), lambda i: (i, 0)), out, out],
        out_specs=[out] * 2,
        out_shape=[jax.ShapeDtypeStruct((2 * tokens, columns), bf16)] * 2,
        scratch_shapes=[pltpu.VMEM((2 * tokens, width), bf16)],
        compiler_params=pltpu.CompilerParams(vmem_limit_bytes=VMEM_LIMIT),
        name="gates_pass",
        cost_estimate=LIGHT,
    )(*grad_top, wdown, gate, up)


def back_kernel(count, transposed, *refs):
    own_ref, send_ref = refs[-2:]
    tokens = own_ref.shape[0]
    dot = dot_nt if transposed else dot_nn

    def total(start):
        rows = pl.ds(start, tokens)
        result = dot(refs[0][rows, :], refs[count][...])
        for i in range(1, count):
            result = result + dot(refs[i][rows, :], refs[count + i][...])
        return result

    own_ref[...] = total(0)
    send_ref[...] = total(tokens).astype(bf16)


def back_pass(lefts, weights, transposed):
    tokens, depth = lefts[0].shape
    width = weights[0].shape[0 if transposed else 1]
    count = len(lefts)
    tile = min(512, width)
    if transposed:
        weight_spec = pl.BlockSpec((tile, depth), lambda i: (i, 0))
    else:
        weight_spec = pl.BlockSpec((depth, tile), lambda i: (0, i))
    out = pl.BlockSpec((tokens // 2, tile), lambda i: (0, i))
    return pl.pallas_call(
        partial(back_kernel, count, transposed),
        grid=(width // tile,),
        in_specs=[pl.BlockSpec((tokens, depth), lambda i: (0, 0))] * count
        + [weight_spec] * count,
        out_specs=[out, out],
        out_shape=[
            jax.ShapeDtypeStruct((tokens // 2, width), f32),
            jax.ShapeDtypeStruct((tokens // 2, width), bf16),
        ],
        compiler_params=pltpu.CompilerParams(vmem_limit_bytes=VMEM_LIMIT),
        name="back_pass",
        cost_estimate=LIGHT,
    )(*lefts, *weights)


def weight_kernel(left_count, *refs):
    lefts, rights, out_ref = refs[:left_count], refs[left_count:-1], refs[-1]
    step = min(lefts[0].shape[0], rights[0].shape[0])

    def piece(refs, start):
        index, offset = divmod(start, refs[0].shape[0])
        return refs[index][pl.ds(offset, step), :]

    total = None
    for start in range(0, left_count * lefts[0].shape[0], step):
        term = dot_tn(piece(lefts, start), piece(rights, start))
        total = term if total is None else total + term
    out_ref[...] = total.astype(bf16)


def weight_pass(lefts, rights):
    rows, columns = lefts[0].shape[1], rights[0].shape[1]
    tile = 512 if rows % 512 == 0 else 384 if rows % 384 == 0 else rows
    return pl.pallas_call(
        partial(weight_kernel, len(lefts)),
        grid=(rows // tile,),
        in_specs=[pl.BlockSpec((left.shape[0], tile), lambda i: (0, i)) for left in lefts]
        + [pl.BlockSpec(right.shape, lambda i: (0, 0)) for right in rights],
        out_specs=pl.BlockSpec((tile, columns), lambda i: (i, 0)),
        out_shape=jax.ShapeDtypeStruct((rows, columns), bf16),
        compiler_params=pltpu.CompilerParams(vmem_limit_bytes=VMEM_LIMIT),
        name="weight_pass",
        cost_estimate=LIGHT,
    )(*lefts, *rights)


def placed_kernel(side_ref, own_ref, other_ref, out_ref):
    mine = pl.program_id(0) == side_ref[0]

    @pl.when(mine)
    def _():
        for g in range(out_ref.shape[1]):
            out_ref[0, g] = own_ref[:, g]

    @pl.when(jnp.logical_not(mine))
    def _():
        for g in range(out_ref.shape[1]):
            out_ref[0, g] = other_ref[:, g]


def placed(own, other, side):
    seq, group, rows, columns = own.shape

    def entry(mine, e, g, s):
        parked = jnp.where(e == 0, 0, group // 2 - 1)
        return (0, jnp.where((e == s[0]) == mine, g, parked), 0, 0)

    return pl.pallas_call(
        placed_kernel,
        grid_spec=pltpu.PrefetchScalarGridSpec(
            num_scalar_prefetch=1,
            grid=(2, group // 2),
            in_specs=[
                pl.BlockSpec((seq, 2, rows, columns), partial(entry, True)),
                pl.BlockSpec((seq, 2, rows, columns), partial(entry, False)),
            ],
            out_specs=pl.BlockSpec(
                (1, 2, seq, rows, columns), lambda e, g, s: (e, g, 0, 0, 0)
            ),
        ),
        out_shape=jax.ShapeDtypeStruct((2, group, seq, rows, columns), own.dtype),
        compiler_params=pltpu.CompilerParams(vmem_limit_bytes=VMEM_LIMIT),
        name="placed",
        cost_estimate=LIGHT,
    )(side.astype(jnp.int32).reshape(1), own, other)


def joined_kernel(side_ref, own_ref, other_ref, out_ref):
    mine = pl.program_id(1) == side_ref[0]

    @pl.when(mine)
    def _():
        out_ref[:, 0] = own_ref[...]

    @pl.when(jnp.logical_not(mine))
    def _():
        out_ref[:, 0] = other_ref[...]


def joined(own, other, side, axis):
    shape = own.shape[:axis] + (2,) + own.shape[axis:]
    columns = own.shape[-1]
    lead = math.prod(own.shape[:axis])
    rows = math.prod(own.shape[axis:-1])
    leads, chunks = lead, 1
    while leads % 2 == 0 and leads * rows * columns > 800_000:
        leads //= 2
    while leads == 1 and rows % (32 * chunks) == 0 and rows // chunks * columns > 800_000:
        chunks *= 2
    block = rows // chunks

    def entry(mine, p, e, i, s):
        parked = jnp.where(e == 0, 0, chunks - 1)
        return (p, jnp.where((e == s[0]) == mine, i, parked), 0)

    return pl.pallas_call(
        joined_kernel,
        grid_spec=pltpu.PrefetchScalarGridSpec(
            num_scalar_prefetch=1,
            grid=(lead // leads, 2, chunks),
            in_specs=[
                pl.BlockSpec((leads, block, columns), partial(entry, True)),
                pl.BlockSpec((leads, block, columns), partial(entry, False)),
            ],
            out_specs=pl.BlockSpec((leads, 1, block, columns), lambda p, e, i, s: (p, e, i, 0)),
        ),
        out_shape=jax.ShapeDtypeStruct((lead, 2, rows, columns), own.dtype),
        compiler_params=pltpu.CompilerParams(vmem_limit_bytes=VMEM_LIMIT),
        name="joined",
        cost_estimate=LIGHT,
    )(
        side.astype(jnp.int32).reshape(1),
        own.reshape(lead, rows, columns),
        other.reshape(lead, rows, columns),
    ).reshape(shape)


def swap(values, bit):
    pairs = [(i, i ^ bit) for i in range(lax.axis_size("rows"))]
    return lax.ppermute(values, "rows", pairs)


def bit_of(bit):
    return (lax.axis_index("rows") // bit) % 2


def gather_bit(values, bit, axis):
    return joined(values, swap(values, bit), bit_of(bit), axis)


def part(values, index, axis):
    return lax.dynamic_index_in_dim(values, index, axis, keepdims=False)


def reduce_bit(values, bit, axis):
    return add_bit(values, pass_bit(values, bit, axis), bit, axis)


def outer_pairs(step, low, high):
    size = lax.axis_size("rows")
    return [
        (i, i + 4 * step)
        for i in range(size)
        if low <= i // 4 < high and 0 <= i // 4 + step < size // 4
    ]


def send_outer(values):
    count = lax.axis_size("rows") // 4
    if count == 2:
        return (swap(values, 4),)
    up, down = values, values
    ups, downs = [], []
    for t in range(1, count):
        up = lax.ppermute(up, "rows", outer_pairs(1, t - 1, count))
        down = lax.ppermute(down, "rows", outer_pairs(-1, 0, count - t + 1))
        ups.append(up)
        downs.append(down)
    return tuple(ups[::-1] + downs)


def join_outer(values, received, axis):
    count = lax.axis_size("rows") // 4
    if count == 2:
        return joined(values, received[0], bit_of(4), axis)
    place = lax.axis_index("rows") // 4
    line = jnp.stack([*received[: count - 1], values, *received[count - 1 :]], axis)
    return lax.dynamic_slice_in_dim(line, count - 1 - place, count, axis)


def gather_outer(values, axis):
    return join_outer(values, send_outer(values), axis)


def pass_outer(values, axis):
    count = lax.axis_size("rows") // 4
    place = lax.axis_index("rows") // 4

    def entry(index):
        return part(values, jnp.clip(index, 0, count - 1), axis)

    if count == 1:
        return ()
    if count == 2:
        return (swap(entry(1 - place), 4),)
    up, down = entry(place + count - 1), entry(place - count + 1)
    for t in range(1, count):
        up = lax.ppermute(up, "rows", outer_pairs(1, 0, t))
        down = lax.ppermute(down, "rows", outer_pairs(-1, count - t, count))
        if t < count - 1:
            up = (entry(place + count - 1 - t).astype(f32) + up.astype(f32)).astype(bf16)
            down = (entry(place - count + 1 + t).astype(f32) + down.astype(f32)).astype(bf16)
    return (up, down)


def add_outer(values, received, axis):
    total = part(values, lax.axis_index("rows") // 4, axis).astype(f32)
    for term in received:
        total = total + term.astype(f32)
    return total.astype(bf16)


def reduce_outer(values, axis):
    return add_outer(values, pass_outer(values, axis), axis)


def pass_bit(values, bit, axis):
    return swap(part(values, 1 - bit_of(bit), axis), bit)


def add_bit(values, received, bit, axis):
    own = part(values, bit_of(bit), axis)
    return (own.astype(f32) + received.astype(f32)).astype(bf16)


def gather_seq(values):
    return lax.all_gather(values, "seq", axis=0, tiled=False)


def reduce_seq(values):
    return lax.psum_scatter(values, "seq", scatter_dimension=0, tiled=False)


def exchange(values, axis, bit):
    size = lax.axis_size(axis)
    return lax.ppermute(values, axis, [(i, i ^ bit) for i in range(size)])


def across_group(own, send):
    return (own + swap(send, 1).astype(f32)).astype(bf16)


def stage(*values):
    return lax.optimization_barrier(values)


def mm(left, right):
    return jnp.einsum("ab,bc->ac", left, right, preferred_element_type=f32)


def mm_t(left, right):
    return jnp.einsum("ab,cb->ac", left, right, preferred_element_type=f32)


def t_mm(left, right):
    return jnp.einsum("ab,ac->bc", left, right, preferred_element_type=f32)


def norm_scale(values):
    return lax.rsqrt(jnp.mean(values * values, axis=-1, keepdims=True) + EPSILON)


def norm_backward(values, scale, gain, grad):
    gained = grad * gain
    inner = jnp.mean(values * gained, axis=-1, keepdims=True)
    result = scale * gained - values * (scale * scale * scale) * inner
    return result, jnp.sum(grad * values * scale, axis=0)


def shards(
    tokens_in,
    corpus,
    corpus_weight,
    w_qkv,
    w_out,
    w_gate,
    w_up,
    w_down,
    attn_gain,
    ffn_gain,
    q_gain,
    k_gain,
    upstream,
):
    shard_length, width = tokens_in.shape[1:]
    row_devices = lax.axis_size("rows")
    seq_devices = lax.axis_size("seq")
    outer = row_devices // 4
    d_rows = w_qkv.shape[0]
    f_rows = w_down.shape[0]
    place = lax.axis_index("seq").astype(jnp.int32)
    inputs = tokens_in[0].astype(f32)

    extra = jnp.stack(
        [
            attn_gain,
            ffn_gain,
            jnp.broadcast_to(corpus.astype(bf16), attn_gain.shape),
        ],
        axis=1,
    )
    extra = jnp.pad(extra, ((0, 0), (0, LANES - extra.shape[1])))
    kv_shard = jnp.concatenate([w_qkv[:, QUERY_COLUMNS:], extra], axis=1)
    query_shard = jnp.concatenate([w_qkv[:, :QUERY_COLUMNS], w_out.T], axis=1)
    query_shard, w_gate, w_up = stage(query_shard, w_gate, w_up)
    query_lines = gather_seq(query_shard)

    def to_group(weight):
        blocks = weight.reshape(d_rows, outer, 4, seq_devices, f_rows)
        blocks = jnp.transpose(blocks, (2, 0, 3, 1, 4))
        return blocks.reshape(2, 2, d_rows, outer * seq_devices * f_rows)

    def spread_hidden(lines, received):
        if outer == 2:
            lines = lines.reshape(seq_devices, 4, d_rows, hidden_columns)
            other = received[0].reshape(lines.shape)
            return placed(lines, other, bit_of(4)).reshape(width, hidden_columns)
        full = join_outer(lines, received, 0)
        return jnp.moveaxis(full, 1, 3).reshape(width, hidden_columns)

    gate_up = jnp.stack([to_group(w_gate), to_group(w_up)], axis=2)
    hidden_columns = gate_up.shape[-1]
    core, near = bit_of(1), bit_of(2)
    gate_up = joined(
        part(gate_up, core, 1), swap(part(gate_up, 1 - core, 1), 1), core, 1
    )
    gate_up, kv_shard = stage(gate_up, kv_shard)
    other, kv_lines, query_lines = stage(
        swap(part(gate_up, 1 - near, 0), 2), gather_seq(kv_shard), query_lines
    )
    gate_up = joined(part(gate_up, near, 0), other, near, 0)
    gate_lines = gather_seq(gate_up[:, :, 0])
    left, right = kv_lines[..., : 3 * LANES], kv_lines[..., 3 * LANES :]
    left_other, right_other = stage(send_outer(left), swap(right, 2))
    left = join_outer(left, left_other, 0)
    right = joined(right, right_other, near, 0)
    left_other, right_other = stage(swap(left, 2), send_outer(right))
    left = joined(left, left_other, near, 1)
    right = join_outer(right, right_other, 0)
    q_left, q_right = query_lines[..., :QUERY_COLUMNS], query_lines[..., QUERY_COLUMNS:]
    q_left, q_right, left, right = stage(q_left, q_right, left, right)
    q_left_other, q_right_other = send_outer(q_left), swap(q_right, 2)
    left, right = gather_bit(left, 1, 2), gather_bit(right, 1, 2)
    left, right = left.reshape(width, -1), right.reshape(width, -1)
    wkv = jnp.concatenate([left, right[:, : 2 * LANES]], axis=1)
    rows = dot_nt(jnp.eye(8, LANES, dtype=bf16), right[:, 2 * LANES :])
    attn_gain_full, ffn_gain_full, corpus_full = rows[0:1], rows[1:2], rows[2]

    position = (place * shard_length + jnp.arange(shard_length, dtype=jnp.int32)).astype(f32)
    half = HEAD_SIZE // 2
    exponent = jnp.arange(half, dtype=f32) * (-2.0 / HEAD_SIZE)
    angles = position[:, None] * jnp.power(ROPE_BASE, exponent)[None, :]
    cosine, sine = jnp.cos(angles), jnp.sin(angles)
    cos_table = jnp.concatenate([cosine] * 4, axis=1)
    sin_table = jnp.concatenate([-sine, sine] * 2, axis=1)
    wide_q = jnp.tile(q_gain.astype(f32), QUERY_HEADS)
    wide_k = jnp.concatenate(
        [jnp.tile(k_gain.astype(f32), KEY_VALUE_HEADS), jnp.ones((KEY_COLUMNS,), f32)]
    )
    wide_q = jnp.broadcast_to(wide_q[None, :], (8, QUERY_COLUMNS))
    wide_k = jnp.broadcast_to(wide_k[None, :], (8, 2 * KEY_COLUMNS))

    in_scale = norm_scale(inputs)
    normed = (inputs * in_scale * attn_gain_full).astype(bf16)
    joint_kv, own_kv = heads_forward(
        normed, wkv, wide_k, cos_table, sin_table, KEY_COLUMNS
    )
    own_kv, q_left_other, q_right_other, up_in = stage(
        own_kv, q_left_other, q_right_other, gate_up[:, :, 1]
    )
    up_lines = gather_seq(up_in)
    keys_values = gather_seq(own_kv).reshape(-1, 2 * KEY_COLUMNS)
    q_left = join_outer(q_left, q_left_other, 0)
    q_right = joined(q_right, q_right_other, near, 0)
    left_other, right_other, gate_lines, w_down = stage(
        swap(q_left, 2), send_outer(q_right), gate_lines, w_down
    )
    q_left = joined(q_left, left_other, near, 1)
    gate_other = send_outer(gate_lines)
    down_other = send_outer(w_down)
    half_rows = (2 * outer, seq_devices * d_rows, QUERY_COLUMNS)
    q_left_other = swap(q_left, 1)

    corpora = jnp.arange(CORPORA, dtype=jnp.int32)
    per_device = corpus_full.reshape(-1, d_rows)[:, 0].astype(jnp.int32)
    counts = (
        jnp.sum((per_device[:, None] == corpora[None, :]).astype(f32), axis=0) * shard_length
    )
    own_corpus = (corpus[0] == corpora).astype(f32)
    weight_row = jnp.sum(own_corpus * corpus_weight.astype(f32))
    count_row = jnp.sum(own_corpus * counts)
    factor = weight_row / DENOM * (jnp.sum(counts) / (CORPORA * count_row))
    grad_full = upstream[0].astype(f32) * factor
    grad_top, q_left, q_left_other = stage(grad_full.astype(bf16), q_left, q_left_other)

    q_halves = (q_left.reshape(half_rows), q_left_other.reshape(half_rows))
    joint_q, queries = heads_forward_halves(
        normed, *q_halves, core, wide_q, cos_table, sin_table
    )
    queries, q_right, right_other, down_other = stage(queries, q_right, right_other, down_other)
    q_right = join_outer(q_right, right_other, 0)
    down_pair = join_outer(w_down, down_other, 0)
    place_array = place.reshape(1)
    keys_values, queries, down_in = stage(keys_values, queries, down_pair)
    down_lines = gather_seq(down_in)
    mixed, logs = attend_forward(place_array, queries, keys_values)
    mixed, grad_top1, grad_top2, wout_other = stage(
        mixed, swap(grad_top, 1), swap(grad_top, 2), swap(q_right, 1)
    )
    middle = project(
        mixed, q_right.reshape(half_rows), wout_other.reshape(half_rows), tokens_in[0], core
    )
    middle, up_lines = stage(middle, up_lines)

    ffn_scale = norm_scale(middle)
    normed_ffn = (middle * ffn_scale * ffn_gain_full).astype(bf16)
    up_other = send_outer(up_lines)
    normed_ffn, gate_other, q_right, wout_other, q_left, q_left_other = stage(
        normed_ffn, gate_other, q_right, wout_other, q_left, q_left_other
    )
    normed1 = swap(normed_ffn, 1)
    wgate = spread_hidden(gate_lines, gate_other)
    gate_near, normed2, up_other, wout_t, wq = stage(
        gate_pass((normed_ffn, normed1), wgate),
        swap(normed_ffn, 2),
        up_other,
        joined(q_right, wout_other, core, 2),
        joined(q_left, q_left_other, core, 2),
    )
    wout_t, wq = wout_t.reshape(width, -1), wq.reshape(width, -1)
    wup = spread_hidden(up_lines, up_other)
    hidden_near, up_near = up_pass((normed_ffn, normed1), wup, gate_near)
    normed3, hidden_near, grad_top3 = stage(
        swap(normed2, 1), hidden_near, swap(grad_top2, 1)
    )
    hidden_far, gate_far, up_far = hidden_pass((normed2, normed3), wgate, wup)
    normed4 = (normed_ffn, normed1, normed2, normed3)
    grad_top4 = (grad_top, grad_top1, grad_top2, grad_top3)
    wdown = down_lines.reshape(hidden_columns, width)
    gate_far, up_far = gates_pass((grad_top2, grad_top3), wdown, gate_far, up_far)
    own, send = back_pass((gate_far, up_far), (wgate, wup), True)
    grad_wdown = weight_pass((hidden_near, hidden_far), grad_top4)
    own, send, grad_wdown, wdown = stage(own, swap(send, 1), grad_wdown, wdown)
    across = (own + send.astype(f32)).astype(bf16)
    across, wdown = stage(across, wdown)
    gate_near, up_near = gates_pass((grad_top, grad_top1), wdown, gate_near, up_near)
    own, send = back_pass((gate_near, up_near), (wgate, wup), True)
    hidden_shape = (outer, 2, 2, seq_devices, d_rows, hidden_columns)
    grad_wdown = grad_wdown.reshape(seq_devices, outer, f_rows, width)
    grad_wgate = weight_pass(normed4, (gate_near, gate_far)).reshape(hidden_shape)
    across, own, send, grad_wgate, up_near = stage(
        swap(across, 2), own, send, grad_wgate, up_near
    )
    grad_wup = weight_pass(normed4, (up_near, up_far)).reshape(hidden_shape)
    send, grad_wup, down_other = stage(swap(send, 1), grad_wup, pass_outer(grad_wdown, 1))
    grad_wdown = add_outer(grad_wdown, down_other, 1)
    own = own + send.astype(f32)
    grad_normed_ffn = own + across.astype(f32)
    grad_wdown = reduce_seq(grad_wdown)

    grad_middle_part, grad_ffn_gain = norm_backward(
        middle, ffn_scale, ffn_gain_full, grad_normed_ffn
    )
    grad_middle = grad_full + grad_middle_part
    grad_branch = grad_middle.astype(bf16)
    grad_mixed = mm(grad_branch, wout_t).astype(bf16)
    attend = (place_array, queries, keys_values, mixed, logs)
    grad_q1, grad_kv1 = attend_backward(0, 2, *attend, grad_mixed)
    gate_other = pass_outer(grad_wgate, 0)
    grad_q1, grad_kv1, grad_mixed, grad_wdown, hidden_far = stage(
        grad_q1, grad_kv1, grad_mixed, grad_wdown, hidden_far
    )
    grad_kv1 = reduce_seq(grad_kv1.reshape(seq_devices, shard_length, -1))
    shape = (outer, 2, 2, seq_devices, d_rows)
    own_far, send_far = back_pass((hidden_far,), (wdown,), False)
    grad_wout, far_other, gate_other, grad_mixed = stage(
        t_mm(grad_branch, mixed).astype(bf16).reshape(*shape, QUERY_COLUMNS),
        swap(send_far, 1),
        gate_other,
        grad_mixed,
    )
    grad_gate = reduce_seq(jnp.moveaxis(add_outer(grad_wgate, gate_other, 0), 2, 0))
    across = (own_far + far_other.astype(f32)).astype(bf16)
    across, grad_mixed = stage(across, grad_mixed)
    grad_q2, grad_kv2 = attend_backward(2, 3, *attend, grad_mixed)
    grad_q2, grad_kv2, hidden_near, grad_kv1, wout_other, up_other, across = stage(
        grad_q2,
        grad_kv2,
        hidden_near,
        grad_kv1,
        pass_bit(grad_wout, 1, 2),
        pass_outer(grad_wup, 0),
        swap(across, 2),
    )
    grad_kv2 = reduce_seq(grad_kv2.reshape(seq_devices, shard_length, -1))

    grad_q = jnp.concatenate([grad_q1, grad_q2], axis=1)
    joint_grad_q, gain_q = heads_backward(
        grad_q, joint_q, wide_q, cos_table, sin_table, QUERY_COLUMNS
    )
    grad_wq = t_mm(normed, joint_grad_q).astype(bf16).reshape(*shape, QUERY_COLUMNS)
    grad_wout = add_bit(grad_wout, wout_other, 1, 2)
    grad_up = jnp.moveaxis(add_outer(grad_wup, up_other, 0), 2, 0)
    grad_wq = reduce_bit(grad_wq, 1, 2)
    wq_other, wout_other = pass_bit(grad_wq, 2, 1), pass_outer(grad_wout, 0)
    grad_kv2, grad_normed, grad_up, grad_gate = stage(
        grad_kv2, mm_t(joint_grad_q, wq), grad_up, grad_gate
    )
    grad_up = reduce_seq(grad_up)

    grad_kv1, grad_kv2 = (
        part_.reshape(shard_length, 2, -1) for part_ in (grad_kv1, grad_kv2)
    )
    grad_kv = jnp.concatenate([grad_kv1, grad_kv2], axis=2).reshape(shard_length, -1)
    joint_grad_kv, gain_k = heads_backward(
        grad_kv, joint_kv, wide_k, cos_table, sin_table, KEY_COLUMNS
    )
    joint_grad_kv, wq_other, wout_other = stage(joint_grad_kv, wq_other, wout_other)
    grad_wkv = t_mm(normed, joint_grad_kv).astype(bf16)
    grad_normed = grad_normed + mm_t(joint_grad_kv, wkv)
    grad_input_part, grad_attn_gain = norm_backward(
        inputs, in_scale, attn_gain_full, grad_normed
    )
    input_grad = (grad_middle + grad_input_part).astype(bf16)

    gain_rows = jnp.stack([grad_attn_gain, grad_ffn_gain]).astype(bf16)
    gain_columns = t_mm(gain_rows, jnp.eye(2, LANES, dtype=bf16)).astype(bf16)
    grad_wkv, gain_columns, hidden_near = stage(grad_wkv, gain_columns, hidden_near)
    own_near, send_near = back_pass((hidden_near,), (wdown,), False)
    grad_wq = add_bit(grad_wq, wq_other, 2, 1)
    grad_wout = add_outer(grad_wout, wout_other, 0)
    wq_other, wout_other = pass_outer(grad_wq, 0), pass_bit(grad_wout, 2, 0)
    left = grad_wkv[:, : 3 * LANES].reshape(*shape, -1)
    right = jnp.concatenate([grad_wkv[:, 3 * LANES :], gain_columns], axis=1)
    right = right.reshape(*shape, -1)
    head_gains = jnp.concatenate(
        [
            jnp.sum(gain_q[0].reshape(-1, HEAD_SIZE), axis=0),
            jnp.sum(gain_k[0, :KEY_COLUMNS].reshape(-1, HEAD_SIZE), axis=0),
        ]
    )[None]
    left, right, left_other, right_other, gains_other = stage(
        left,
        right,
        pass_bit(left, 1, 2),
        pass_bit(right, 1, 2),
        exchange(head_gains, "rows", 1),
    )
    head_gains = head_gains + gains_other
    left = add_bit(left, left_other, 1, 2)
    right = add_bit(right, right_other, 1, 2)
    left_other, right_other, wq_other, wout_other, gains_other, grad_up = stage(
        pass_bit(left, 2, 1),
        pass_outer(right, 0),
        wq_other,
        wout_other,
        exchange(head_gains, "seq", 1),
        grad_up,
    )
    head_gains = head_gains + gains_other
    left = add_bit(left, left_other, 2, 1)
    right = add_outer(right, right_other, 0)
    left_other, right_other, gains_other, near_other = stage(
        pass_outer(left, 0),
        pass_bit(right, 2, 0),
        exchange(head_gains, "rows", 2),
        swap(send_near, 1),
    )
    output = (middle + own_near + near_other.astype(f32) + across.astype(f32)).astype(bf16)
    head_gains = head_gains + gains_other
    sums = reduce_seq(
        jnp.concatenate(
            [
                add_outer(grad_wq, wq_other, 0),
                add_outer(left, left_other, 0),
                add_bit(right, right_other, 2, 0),
                add_bit(grad_wout, wout_other, 2, 0),
            ],
            axis=-1,
        )
    )
    rest = [("rows", bit) for bit in (4, 8, 16) if bit < row_devices]
    rest += [("seq", bit) for bit in (2, 4, 8) if bit < seq_devices]
    gate_up = jnp.stack([grad_gate, grad_up], axis=2)
    other, gains_other = stage(
        swap(part(gate_up, 1 - near, 0), 2), exchange(head_gains, *rest[0])
    )
    head_gains = head_gains + gains_other
    grads = joined(part(gate_up, near, 0), other, near, 0)
    for axis, bit in rest[1:]:
        head_gains = head_gains + exchange(head_gains, axis, bit)
    head_gains = head_gains[0]
    grads = joined(part(grads, core, 1), swap(part(grads, 1 - core, 1), 1), core, 1)

    def from_group(blocks):
        blocks = blocks.reshape(4, d_rows, seq_devices, outer, f_rows)
        return jnp.transpose(blocks, (1, 3, 0, 2, 4)).reshape(d_rows, -1)

    grad_wgate, grad_wup = stage(from_group(grads[:, :, 0]), from_group(grads[:, :, 1]))
    sums, grad_wgate, grad_wup, grad_wdown, output, input_grad = stage(
        sums, grad_wgate.astype(f32), grad_wup.astype(f32), grad_wdown.astype(f32), output, input_grad
    )
    columns = QUERY_COLUMNS + 2 * KEY_COLUMNS
    long_gains = sums[:, columns : columns + 2].astype(f32)
    return (
        output[None],
        input_grad[None],
        sums[:, :columns].astype(f32),
        sums[:, columns + LANES :].T.astype(f32),
        grad_wgate,
        grad_wup,
        grad_wdown,
        long_gains[:, 0],
        long_gains[:, 1],
        head_gains[:HEAD_SIZE],
        head_gains[HEAD_SIZE:],
    )


def solution(mesh):
    return jax.shard_map(
        shards,
        mesh=mesh,
        in_specs=(
            P("rows", "seq", None),
            P("rows"),
            P(),
            P(("rows", "seq"), None),
            P(None, ("rows", "seq")),
            P(("rows", "seq"), None),
            P(("rows", "seq"), None),
            P(("rows", "seq"), None),
            P(("rows", "seq")),
            P(("rows", "seq")),
            P(),
            P(),
            P("rows", "seq", None),
        ),
        out_specs=(
            P("rows", "seq", None),
            P("rows", "seq", None),
            P(("rows", "seq"), None),
            P(None, ("rows", "seq")),
            P(("rows", "seq"), None),
            P(("rows", "seq"), None),
            P(("rows", "seq"), None),
            P(("rows", "seq")),
            P(("rows", "seq")),
            P(),
            P(),
        ),
        check_vma=False,
    )
```
